32 devices in a mesh: groups: 2 (over y), expert: 4 (over x, core), section: 4 (over z).
Axes of the slice: x: 2, y: 2, z: 4, core: 2. Of those that a mesh axis runs over, the one named last changes fastest.
Arguments:
- prompts: bfloat16 [32, 128, 3584], P(('groups', 'expert', 'section')), parts along dimension 0, may hold values from -6 to 6
- owners: int32 [32], P('groups'), parts along dimension 0, may hold values from 0 to 3, as said below
- lengths: int32 [32], P('groups'), parts along dimension 0, may hold values from 1 to 128, 1024 in all
- residual: bfloat16 [2, 32, 3584], P(None, ('groups', 'expert')), parts along dimension 1, may hold values from -6 to 6
- queries: bfloat16 [2, 32, 64, 192], P(None, ('groups', 'expert'), 'section'), parts along dimension 1, may hold values from -170 to 170
- expert_ids: int32 [2, 32, 8], P(None, ('groups', 'expert')), parts along dimension 1, may hold values from 0 to 15, all different within a row; in each aligned block of 4 rows (0 to 3, 4 to 7, ..., all dimensions but the last counted through in order) at most 3 rows name the same one
- route_scores: float32 [2, 32, 8], P(None, ('groups', 'expert')), parts along dimension 1, may hold values from 0.02 to 1
- attn_gain: bfloat16 [3584], replicated, may hold values from 0.25 to 1.75
- w_dkv: bfloat16 [3584, 576], P('section'), may hold values from -0.09375 to 0.09375
- kv_gain: bfloat16 [512], replicated, may hold values from 0.25 to 1.75
- w_uk: bfloat16 [64, 128, 512], P('section', None, 'expert'), may hold values from -0.5 to 0.5
- w_uv: bfloat16 [64, 128, 512], P('section', None, 'expert'), may hold values from -0.25 to 0.25
- w_o: bfloat16 [8192, 3584], P('section', 'expert'), may hold values from -0.0625 to 0.0625
- moe_gain: bfloat16 [3584], replicated, may hold values from 0.25 to 1.75
- w_gate: bfloat16 [16, 3584, 1024], P('expert', None, 'section'), may hold values from -0.09375 to 0.09375
- w_up: bfloat16 [16, 3584, 1024], P('expert', None, 'section'), may hold values from -0.09375 to 0.09375
- w_down: bfloat16 [16, 1024, 3584], P('expert', 'section'), may hold values from -0.1875 to 0.1875
Outputs:
- layer_out: bfloat16 [2, 32, 3584], P(None, ('groups', 'expert'), 'section'), parts along dimension 1
The draws below stay inside these ranges and needn't reach their ends.
There are 2 independent parts, one for each index of `groups`. The reference program is written for one: setup_inputs(seed, part) draws one part's arguments, and reference() takes and returns one part's arrays. A program takes and returns all parts, laid end to end along the dimension named above; an argument that names none is the same for every part. Nothing has to cross between parts.
Inputs may be any that keep to these rules, and one draw needn't show every extreme that they name: `owners`: requests j * 4 to j * 4 + 3 name every owner exactly once. `expert_ids`: each token names 8 different experts; within one step the 4 tokens of one owner name one expert at most 3 times.
All inputs are finite; a program needn't handle non-finite values.
Results may differ from the reference program's by a relative error of at most 0.012.
The reference program's roundings to bfloat16 on the way count: a program that leaves them out, or rounds other values in their place, can miss the bound.
Values may be sent and summed in bfloat16 or wider, within the bound.
No kernel may reach another device: no remote copies, remote signals or barrier semaphores. Data moves between devices by JAX's collectives and lax.ppermute only.
A program may use at most 192 MiB of HBM per device.

```python
import math
import jax
import jax.numpy as jnp
import numpy as np
from jax import lax

D = 3584
LAT = 512
ROPE = 64
NOPE = 128
VDIM = 128
HEADS = 64
FFE = 1024
EXPERTS = 16
TOP = 8
STEPS = 2
MAXLEN = 128
REQ_DEV = 4
REQUESTS = 16
CAP = 3


def draw_owners(key, part):
    key = jax.random.fold_in(key, 3)
    keys = jax.random.split(key, REQ_DEV)
    rows = jax.vmap(lambda sub_key: jax.random.permutation(sub_key, REQ_DEV))(keys)
    return rows.reshape(REQUESTS).astype(jnp.int32)


def draw_queries(key, part):
    key = jax.random.fold_in(key, 5)
    base = jnp.clip(jax.random.normal(key, (STEPS, REQUESTS, HEADS, NOPE + ROPE), jnp.float32), -5.0, 5.0)
    return base.astype(jnp.bfloat16)


def shard_levels(key, shape, pieces, least, top_value):
    def one(axis_at, parts):
        steps = jax.random.uniform(jax.random.fold_in(jax.random.fold_in(key, 6), axis_at), (parts,), jnp.float32, least / len(pieces), top_value / len(pieces))
        return jnp.repeat(jnp.exp(steps), shape[axis_at] // parts).reshape((-1,) + (1,) * (len(shape) - axis_at - 1))

    level = one(*pieces[0])
    for cut in pieces[1:]:
        level = level * one(*cut)
    return level


def profile(amount, total, most, skew):
    portions = [(1 << 20) // math.isqrt(standing ** skew) + 1 for standing in range(2, amount + 1)]
    surplus, counts = total - most - (amount - 1), [1] * (amount - 1)
    while surplus > 0:
        movable = [i for i in range(amount - 1) if counts[i] < most]
        pool, left = sum([portions[i] for i in movable]), surplus
        for i in movable:
            more = min(most - counts[i], max(1, left * portions[i] // pool), surplus)
            counts[i] = counts[i] + more
            surplus = surplus - more
    return np.array([most] + counts)


def uneven(own_key, count, total, bound, lean):
    if count == 2:
        one = jax.random.randint(own_key, (), max(1, total - bound), min(bound, total - 1) + 1)
        return jnp.stack([one, total - one])
    tallies = jnp.asarray(profile(count, total, bound, lean), jnp.int32)
    couples = (count - 1) // 2
    giver, receiver = tallies[1:1 + 2 * couples:2], tallies[2:2 + 2 * couples:2]
    room = jnp.minimum(giver - 1, bound - receiver)
    passed = jax.random.randint(jax.random.fold_in(own_key, 1), (couples,), 0, 1 << 20) % (room + 1)
    tallies = tallies.at[1:1 + 2 * couples:2].set(giver - passed).at[2:2 + 2 * couples:2].set(receiver + passed)
    return tallies[jax.random.permutation(jax.random.fold_in(own_key, 2), count)]


def shared_out(rng, own, number, rows, number_of, top, reach, skew):
    sequence = jax.random.permutation(rng, number_of)
    crowded, common = portions_of(number_of, rows * top, reach, skew, True), portions_of(number_of, rows * top, reach, skew, False)
    places = jnp.arange(number_of)

    def named(tallies, offset_by):
        used = int((tallies > 0).sum())
        fixed = max(1, used // 4)
        shifted = fixed + (places - fixed + offset_by * (used - fixed)) % max(1, number_of - fixed)
        return jnp.zeros((number_of,), jnp.int32).at[sequence[jnp.where(places < fixed, places, shifted)]].set(jnp.asarray(tallies, jnp.int32))

    tallies = jnp.where(number % 4 == 0, named(crowded, number // 4), named(common, number - number // 4 - 1))
    mixed = jax.random.permutation(jax.random.fold_in(own, 3), number_of)
    source_of, sink = mixed[0:number_of // 2 * 2:2], mixed[1:number_of // 2 * 2:2]
    slack = jnp.minimum(tallies[source_of] - 1, reach - tallies[sink]) // 2
    slack = jnp.where((source_of == sequence[0]) | (sink == sequence[0]) | (tallies[sink] == 0), 0, jnp.maximum(slack, 0))
    shifted = jax.random.randint(jax.random.fold_in(own, 4), (number_of // 2,), 0, 1 << 20) % (slack + 1)
    tallies = tallies.at[source_of].add(-shifted).at[sink].add(shifted)
    members = jnp.searchsorted(jnp.cumsum(tallies), jnp.arange(rows * top), side="right").astype(jnp.int32)
    listing = members.reshape(top, rows).T
    listing = listing[jax.random.permutation(jax.random.fold_in(own, 1), rows)]
    offset_by = jax.random.randint(jax.random.fold_in(own, 2), (rows, 1), 0, top)
    return jnp.take_along_axis(listing, (jnp.arange(top)[None, :] + offset_by) % top, axis=1)


def portions_of(count, total, limit, skew, full):
    loads = [(1 << 20) // math.isqrt(standing ** skew) + 1 for standing in range(1, count + 1)]
    largest = limit if full else min(limit, max(-(-total // count), total * loads[0] // sum(loads)))
    least = 1 if total - largest >= count - 1 else 0
    given, rest = [largest] + [least] * (count - 1), total - largest - least * (count - 1)
    while rest > 0:
        free = [i for i in range(1, count) if given[i] < largest] or [i for i in range(1, count) if given[i] < limit]
        whole, budget = sum([loads[i] for i in free]), rest
        for i in free:
            extra = min(limit - given[i], max(1, budget * loads[i] // whole), rest)
            given[i] = given[i] + extra
            rest = rest - extra
    return np.array(given)


def noise(key, dims, scale, reach, cuts=(), dtype=jnp.bfloat16):
    array = jax.random.normal(key, dims, jnp.float32) * scale
    if len(cuts) > 0:
        array = shard_levels(key, dims, cuts, -0.22, 0.18) * array
    return jnp.clip(array, min=-reach, max=reach).astype(dtype)


def setup_inputs(seed: int = 0, part: int = 0) -> dict:
    key_of = jax.random.split(jax.random.key(seed), 18)
    part_keys = jax.random.split(jax.random.fold_in(key_of[17], part), 18)
    prompts = noise(part_keys[0], (REQUESTS, MAXLEN, D), 1.0, 6.0, ((0, 16),))
    owners = draw_owners(jax.random.fold_in(jax.random.fold_in(key_of[17], part), 71), part)
    lengths = uneven(part_keys[2], REQUESTS, REQUESTS * MAXLEN // 2, MAXLEN, 2).astype(jnp.int32)
    residual = noise(part_keys[3], (STEPS, REQUESTS, D), 1.0, 6.0, ((1, 4),))
    queries = draw_queries(jax.random.fold_in(jax.random.fold_in(key_of[17], part), 71), part)
    expert_ids_keys = jax.random.split(jax.random.fold_in(part_keys[5], 1), STEPS * REQUESTS // REQ_DEV)
    expert_ids_turns = jax.random.permutation(jax.random.fold_in(part_keys[5], 3), STEPS * REQUESTS // REQ_DEV)
    expert_ids = jax.vmap(lambda own, number: shared_out(jax.random.fold_in(part_keys[5], 2), own, number, REQ_DEV, EXPERTS, TOP, CAP, 2))(expert_ids_keys, expert_ids_turns).reshape((STEPS, REQUESTS, TOP))
    route_scores = jnp.clip(jnp.exp(math.log(1.0) - 3.912023 * jax.random.uniform(part_keys[6], (STEPS, REQUESTS, TOP), jnp.float32) ** shard_levels(part_keys[6], (STEPS, REQUESTS, TOP), ((1, 4),), -0.2, 0.2)), 0.02, 1.0)
    attn_gain = jnp.clip(1.0 + 0.15 * jax.random.normal(key_of[7], (D,), jnp.float32), 0.25, 1.75).astype(jnp.bfloat16)
    w_dkv = noise(key_of[8], (D, LAT + ROPE), D ** -0.5, 0.09375, ((0, 4),))
    kv_gain = jnp.clip(1.0 + 0.15 * jax.random.normal(key_of[9], (LAT,), jnp.float32), 0.25, 1.75).astype(jnp.bfloat16)
    w_uk = noise(key_of[10], (HEADS, NOPE, LAT), NOPE ** -0.5, 0.5, ((0, 4), (2, 4)))
    w_uv = noise(key_of[11], (HEADS, VDIM, LAT), LAT ** -0.5, 0.25, ((0, 4), (2, 4)))
    w_o = noise(key_of[12], (HEADS * VDIM, D), (HEADS * VDIM) ** -0.5, 0.0625, ((0, 4), (1, 4)))
    moe_gain = jnp.clip(1.0 + 0.15 * jax.random.normal(key_of[13], (D,), jnp.float32), 0.25, 1.75).astype(jnp.bfloat16)
    w_gate = noise(key_of[14], (EXPERTS, D, FFE), D ** -0.5, 0.09375, ((0, 4), (2, 4)))
    w_up = noise(key_of[15], (EXPERTS, D, FFE), D ** -0.5, 0.09375, ((0, 4), (2, 4)))
    w_down = noise(key_of[16], (EXPERTS, FFE, D), FFE ** -0.5, 0.1875, ((0, 4), (1, 4)))
    return dict(prompts=prompts, owners=owners, lengths=lengths, residual=residual, queries=queries, expert_ids=expert_ids, route_scores=route_scores, attn_gain=attn_gain, w_dkv=w_dkv, kv_gain=kv_gain, w_uk=w_uk, w_uv=w_uv, w_o=w_o, moe_gain=moe_gain, w_gate=w_gate, w_up=w_up, w_down=w_down)


epsilon = 1e-06
masked_value = -1e+30
route_scale = 2.5

def rotate_pairs(values, position):
    halfway = values.shape[-1] // 2
    frequency = 10000.0 ** (-2.0 * jnp.arange(halfway).astype(jnp.float32) / values.shape[-1])
    angles = position.astype(jnp.float32)[..., None] * frequency
    cosine = jnp.cos(angles)
    sine_part = jnp.sin(angles)
    first_half = values[..., :halfway]
    second_half = values[..., halfway:]
    return jnp.concatenate([first_half * cosine - second_half * sine_part, second_half * cosine + first_half * sine_part], axis=-1)

def rms_scaled(values, gain):
    return values * lax.rsqrt(lax.optimization_barrier(jnp.mean(values * values, axis=-1, keepdims=True)) + epsilon) * gain.astype(jnp.float32)

def latent_rows(projected, kv_gain, position):
    gain_width = kv_gain.shape[0]
    scaled = rms_scaled(projected[..., :gain_width], kv_gain)
    return jnp.concatenate([scaled, rotate_pairs(projected[..., gain_width:], position)], axis=-1).astype(jnp.bfloat16)

def as_stored(values):
    return lax.optimization_barrier(values.astype(jnp.bfloat16)).astype(jnp.float32)

def one_expert(operands):
    rows, gate_weight, up_weight, down_weight = operands
    gate_part = jnp.dot(rows, gate_weight, preferred_element_type=jnp.float32)
    up_part = jnp.dot(rows, up_weight, preferred_element_type=jnp.float32)
    activated = (jax.nn.silu(gate_part) * up_part).astype(jnp.bfloat16)
    return jnp.dot(activated, down_weight, preferred_element_type=jnp.float32).astype(jnp.bfloat16)

def reference(prompts, owners, lengths, residual, queries, expert_ids, route_scores, attn_gain, w_dkv, kv_gain, w_uk, w_uv, w_o, moe_gain, w_gate, w_up, w_down):
    projected = jnp.dot(prompts.reshape(REQUESTS * MAXLEN, D), w_dkv, preferred_element_type=jnp.float32)
    projected = projected.reshape(REQUESTS, MAXLEN, LAT + ROPE)
    prompt_pos = jnp.arange(MAXLEN).astype(jnp.int32)
    prompt_cache = latent_rows(projected, kv_gain, prompt_pos[None, :])
    owner_table = owners.reshape(REQ_DEV, REQ_DEV)
    owner_index = jnp.arange(REQ_DEV).astype(jnp.int32)
    matches = owner_table[None, :, :] == owner_index[:, None, None]
    column = lax.optimization_barrier(jnp.sum(jnp.where(matches, owner_index[None, None, :], 0), axis=2)).astype(jnp.int32)
    order = (owner_index[None, :] * REQ_DEV + column).reshape(REQUESTS).astype(jnp.int32)
    token_cache = jnp.take(prompt_cache, order, axis=0)
    token_len = jnp.take(lengths, order).astype(jnp.int32)
    cache_float = token_cache.astype(jnp.float32)
    recent = jnp.zeros((REQUESTS, STEPS, LAT + ROPE), jnp.bfloat16)
    recent_pos = jnp.arange(STEPS).astype(jnp.int32)
    score_scale = (NOPE + ROPE) ** (-0.5)
    expert_range = jnp.arange(EXPERTS).astype(jnp.int32)
    slot_range = jnp.arange(CAP).astype(jnp.float32)
    outputs = []
    for step_index in range(STEPS):
        hidden = residual[step_index].astype(jnp.float32)
        normed = rms_scaled(hidden, attn_gain).astype(jnp.bfloat16)
        fresh_latent = latent_rows(jnp.dot(normed, w_dkv, preferred_element_type=jnp.float32), kv_gain, token_len + step_index)
        recent = recent.at[:, step_index].set(fresh_latent)
        recent_float = recent.astype(jnp.float32)
        query_now = queries[step_index].astype(jnp.float32)
        query_latent = jnp.einsum('rhn,hnc->rhc', query_now[..., :NOPE], w_uk.astype(jnp.float32))
        query_rot = rotate_pairs(query_now[..., NOPE:], (token_len + step_index)[:, None])
        query_cat = as_stored(jnp.concatenate([query_latent, query_rot], axis=-1))
        prompt_scores = jnp.einsum('rhc,rpc->rhp', query_cat, cache_float) * score_scale
        prompt_scores = jnp.where(prompt_pos[None, None, :] < token_len[:, None, None], prompt_scores, masked_value)
        recent_scores = jnp.einsum('rhc,rtc->rht', query_cat, recent_float) * score_scale
        recent_scores = jnp.where(recent_pos[None, None, :] <= step_index, recent_scores, masked_value)
        maxima = jnp.maximum(prompt_scores.max(axis=-1), recent_scores.max(axis=-1))[..., None]
        prompt_exp = jnp.exp(prompt_scores - maxima)
        recent_exp = jnp.exp(recent_scores - maxima)
        totals = prompt_exp.sum(axis=-1, keepdims=True) + recent_exp.sum(axis=-1, keepdims=True)
        prompt_prob = as_stored(prompt_exp / totals)
        recent_prob = as_stored(recent_exp / totals)
        out_latent = jnp.einsum('rhp,rpc->rhc', prompt_prob, cache_float[..., :LAT]) + jnp.einsum('rht,rtc->rhc', recent_prob, recent_float[..., :LAT])
        out_latent = as_stored(out_latent)
        head_values = jnp.einsum('rhc,hvc->rhv', out_latent, w_uv.astype(jnp.float32)).astype(jnp.bfloat16).reshape(REQUESTS, HEADS * VDIM)
        mixed = hidden + jnp.dot(head_values, w_o, preferred_element_type=jnp.float32)
        moe_in = rms_scaled(mixed, moe_gain).astype(jnp.bfloat16)
        match_table = (expert_ids[step_index][:, :, None] == expert_range[None, None, :]).astype(jnp.float32)
        member = match_table.sum(axis=1)
        scores_now = route_scores[step_index].astype(jnp.float32)
        weights = route_scale * scores_now / lax.optimization_barrier(jnp.sum(scores_now, axis=-1, keepdims=True))
        weight_map = jnp.einsum('rk,rke->re', weights, match_table).reshape(REQ_DEV, REQ_DEV, EXPERTS)
        grouped = member.reshape(REQ_DEV, REQ_DEV, EXPERTS)
        slot_rank = jnp.cumsum(grouped, axis=1) - grouped
        slot_map = grouped[:, None] * (slot_rank[:, None] == slot_range[None, :, None, None]).astype(jnp.float32)
        expert_rows = jnp.einsum('octe,otd->eocd', slot_map, moe_in.astype(jnp.float32).reshape(REQ_DEV, REQ_DEV, D)).astype(jnp.bfloat16)
        expert_out = lax.map(one_expert, (expert_rows.reshape(EXPERTS, REQ_DEV * CAP, D), w_gate, w_up, w_down))
        expert_out = expert_out.reshape(EXPERTS, REQ_DEV, CAP, D).astype(jnp.float32)
        combined = jnp.einsum('octe,eocd->otd', slot_map * weight_map[:, None], expert_out).reshape(REQUESTS, D)
        outputs.append((mixed + combined).astype(jnp.bfloat16))
    return jnp.stack(outputs)
```

```python
import jax
import jax.numpy as jnp
from jax import lax
from jax.sharding import PartitionSpec as P

epsilon = 1e-06
masked_value = -1e30
route_scale = 2.5


def rotation(position, width):
    halfway = width // 2
    frequency = 10000.0 ** (-2.0 * jnp.arange(halfway).astype(jnp.float32) / width)
    angles = position.astype(jnp.float32)[..., None] * frequency
    return jnp.cos(angles), jnp.sin(angles)


def rotate_pairs(values, position):
    halfway = values.shape[-1] // 2
    cosine, sine_part = rotation(position, values.shape[-1])
    first_half = values[..., :halfway]
    second_half = values[..., halfway:]
    return jnp.concatenate(
        [
            first_half * cosine - second_half * sine_part,
            second_half * cosine + first_half * sine_part,
        ],
        axis=-1,
    )


def rms_scaled(values, gain):
    return (
        values
        * lax.rsqrt(jnp.mean(values * values, axis=-1, keepdims=True) + epsilon)
        * gain.astype(jnp.float32)
    )


def latent_rows(projected, kv_gain, position):
    gain_width = kv_gain.shape[0]
    scaled = rms_scaled(projected[..., :gain_width], kv_gain)
    return jnp.concatenate(
        [scaled, rotate_pairs(projected[..., gain_width:], position)], axis=-1
    ).astype(jnp.bfloat16)


def local(
    prompts,
    owners,
    lengths,
    residual,
    queries,
    expert_ids,
    route_scores,
    attn_gain,
    w_dkv,
    kv_gain,
    w_uk,
    w_uv,
    w_o,
    moe_gain,
    w_gate,
    w_up,
    w_down,
):
    bf16, f32 = jnp.bfloat16, jnp.float32
    plane = ("groups", "expert")
    block = ("expert", "section")
    expert_rank = lax.axis_index("expert")
    section_rank = lax.axis_index("section")
    plane_rank = lax.axis_index(plane)
    experts = lax.axis_size("expert")
    sections = lax.axis_size("section")
    members = lax.axis_size("groups") * experts
    prompt_count, full_length, width = prompts.shape
    steps, tokens_here, _ = residual.shape
    heads = queries.shape[2]
    nope = w_uk.shape[1]
    rope = queries.shape[3] - nope
    latent = kv_gain.shape[0]
    cache_width = latent + rope
    depth = w_dkv.shape[0]
    piece = depth // members
    everyone = experts * sections

    w_turned = w_dkv.T
    w_piece = lax.dynamic_slice_in_dim(w_turned, plane_rank * piece, piece, 1)
    w_set = lax.all_gather(w_piece, "section", axis=0)
    rows = prompt_count * full_length
    cut = prompts.reshape(rows, sections, members, piece).transpose(2, 1, 0, 3)
    cut = lax.all_to_all(cut, plane, 0, 0, tiled=True)

    uv_full = lax.all_gather(w_uv, "expert", axis=0)

    table = owners.reshape(experts, tokens_here)
    length_table = lengths.reshape(experts, tokens_here)
    my_owner = lax.dynamic_slice(
        table, (expert_rank, section_rank * prompt_count), (1, prompt_count)
    )[0]
    my_length = lax.dynamic_slice(
        length_table, (expert_rank, section_rank * prompt_count), (1, prompt_count)
    )[0]

    residual_all = lax.all_gather(residual, "expert", axis=0)
    queries_all = lax.all_gather(queries, "expert", axis=0)
    expert_total = w_gate.shape[0] * experts
    match_table = (expert_ids[..., None] == jnp.arange(expert_total)).astype(f32)
    weights = route_scale * route_scores / jnp.sum(route_scores, axis=-1, keepdims=True)
    weight_map = jnp.sum(weights[..., None] * match_table, axis=2)
    weights_all = lax.all_gather(weight_map, "expert", axis=0)

    picked = jnp.take_along_axis(
        queries_all.transpose(2, 0, 1, 3, 4), table[:, :, None, None, None], axis=1
    )
    query_latent = jnp.einsum(
        "ejthn,hnc->ejthc", picked[..., :nope], w_uk, preferred_element_type=f32
    ).astype(bf16)
    rope_piece = rope // experts
    query_rope = lax.dynamic_slice_in_dim(picked[..., nope:], expert_rank * rope_piece, rope_piece, 4)
    query_part = jnp.concatenate([query_latent, query_rope], axis=-1).reshape(
        everyone, prompt_count, steps, heads, -1
    )
    query_part = lax.all_to_all(query_part, block, 0, 0, tiled=True)
    query_part = query_part.reshape(experts, sections, prompt_count, steps, heads, -1)
    query_part = query_part.transpose(2, 3, 1, 4, 0, 5)
    chunk = w_uk.shape[2]
    query_cat = query_part[..., :chunk].reshape(prompt_count, steps, sections * heads, latent)
    query_rope = query_part[..., chunk:].reshape(prompt_count, steps, sections * heads, rope)
    token_pos = my_length[:, None] + jnp.arange(steps)[None, :]
    query_cat = jnp.concatenate(
        [
            query_cat,
            rotate_pairs(query_rope.astype(f32), token_pos[:, :, None]).astype(bf16),
        ],
        axis=-1,
    )

    normed = rms_scaled(residual.astype(f32), attn_gain).astype(bf16)
    normed = lax.dynamic_slice_in_dim(normed, section_rank * depth, depth, 2)
    fresh = jnp.einsum("ted,kd->etk", normed, w_turned, preferred_element_type=f32).astype(bf16)
    fresh = jnp.broadcast_to(
        fresh[:, None], (experts, sections, steps, cache_width)
    ).reshape(everyone, steps, cache_width)
    fresh = lax.all_to_all(fresh, block, 0, 0, tiled=True)
    fresh = fresh.reshape(experts, sections, steps, cache_width)
    fresh = jnp.sum(jnp.take(fresh, my_owner, axis=0).astype(f32), axis=1)
    recent = latent_rows(fresh, kv_gain, token_pos)

    partial = jnp.einsum("dsrc,skc->drk", cut, w_set, preferred_element_type=f32).astype(bf16)
    partial = lax.all_to_all(partial, plane, 0, 0, tiled=True)
    projected = jnp.sum(partial.astype(f32), axis=0).reshape(prompt_count, full_length, cache_width)
    cache = latent_rows(projected, kv_gain, jnp.arange(full_length)[None, :])

    score_scale = queries.shape[-1] ** (-0.5)
    prompt_scores = (
        jnp.einsum("pthc,plc->pthl", query_cat, cache, preferred_element_type=f32) * score_scale
    )
    live = jnp.arange(full_length)[None, :] < my_length[:, None]
    prompt_scores = jnp.where(live[:, None, None, :], prompt_scores, masked_value)
    recent_scores = (
        jnp.einsum("pthc,puc->pthu", query_cat, recent, preferred_element_type=f32) * score_scale
    )
    seen = jnp.arange(steps)[None, :] <= jnp.arange(steps)[:, None]
    recent_scores = jnp.where(seen[None, :, None, :], recent_scores, masked_value)
    maxima = jnp.maximum(prompt_scores.max(axis=-1), recent_scores.max(axis=-1))[..., None]
    prompt_exp = jnp.exp(prompt_scores - maxima)
    recent_exp = jnp.exp(recent_scores - maxima)
    totals = prompt_exp.sum(axis=-1, keepdims=True) + recent_exp.sum(axis=-1, keepdims=True)
    prompt_prob = (prompt_exp / totals).astype(bf16)
    recent_prob = (recent_exp / totals).astype(bf16)
    out_latent = (
        jnp.einsum(
            "pthl,plc->pthc", prompt_prob, cache[..., :latent], preferred_element_type=f32
        )
        + jnp.einsum(
            "pthu,puc->pthc", recent_prob, recent[..., :latent], preferred_element_type=f32
        )
    ).astype(bf16)

    out_latent = out_latent.reshape(prompt_count, steps, sections, heads, latent)
    out_latent = out_latent.transpose(2, 0, 1, 3, 4)
    out_latent = lax.all_to_all(out_latent, "section", 0, 0, tiled=True)
    row = lax.dynamic_slice_in_dim(table, expert_rank, 1, 0)[0]
    out_latent = out_latent.reshape(tokens_here, steps, heads, latent)
    out_latent = jnp.take(out_latent, jnp.argsort(row), axis=0)
    out_latent = out_latent.reshape(tokens_here, steps, heads, experts, chunk)
    head_values = jnp.einsum(
        "othxc,xhvc->othv", out_latent, uv_full, preferred_element_type=f32
    ).astype(bf16)
    head_values = head_values.reshape(tokens_here * steps, -1)
    head_values = lax.all_gather(head_values, "expert", axis=0, tiled=True)

    attended = jnp.dot(head_values, w_o, preferred_element_type=f32).astype(bf16)
    attended = lax.all_gather(attended, "section", axis=0)
    attended = jnp.sum(attended.astype(f32), axis=0).astype(bf16)
    attended = lax.all_gather(attended, "expert", axis=1, tiled=True)
    hidden = residual_all.transpose(2, 0, 1, 3).reshape(-1, width).astype(f32)
    mixed = hidden + attended.astype(f32)
    moe_in = rms_scaled(mixed, moe_gain).astype(bf16)

    gate_part = jnp.einsum("td,xdf->xtf", moe_in, w_gate, preferred_element_type=f32)
    up_part = jnp.einsum("td,xdf->xtf", moe_in, w_up, preferred_element_type=f32)
    route = weights_all.transpose(2, 0, 1, 3).reshape(-1, expert_total)
    route = lax.dynamic_slice_in_dim(route, expert_rank * w_gate.shape[0], w_gate.shape[0], 1)
    activated = (jax.nn.silu(gate_part) * up_part * route.T[:, :, None]).astype(bf16)
    combined = jnp.einsum("xtf,xfd->td", activated, w_down, preferred_element_type=f32).astype(bf16)
    column = width // sections
    combined = combined.reshape(experts, experts, steps, sections, column)
    combined = combined.transpose(1, 3, 0, 2, 4).reshape(everyone, experts, steps, column)
    combined = lax.all_to_all(combined, block, 0, 0, tiled=True)
    combined = jnp.sum(combined.astype(f32), axis=0)
    own = mixed.reshape(experts, experts, steps, sections, column)
    own = lax.dynamic_slice(
        own,
        (0, expert_rank, 0, section_rank, 0),
        (experts, 1, steps, 1, column),
    )[:, 0, :, 0]
    return (own + combined).transpose(1, 0, 2).astype(bf16)


def solution(mesh):
    placed = (
        P(("groups", "expert", "section"), None, None),
        P("groups"),
        P("groups"),
        P(None, ("groups", "expert"), None),
        P(None, ("groups", "expert"), "section", None),
        P(None, ("groups", "expert"), None),
        P(None, ("groups", "expert"), None),
        P(),
        P("section", None),
        P(),
        P("section", None, "expert"),
        P("section", None, "expert"),
        P("section", "expert"),
        P(),
        P("expert", None, "section"),
        P("expert", None, "section"),
        P("expert", "section", None),
    )
    return jax.shard_map(
        local,
        mesh=mesh,
        in_specs=placed,
        out_specs=P(None, ("groups", "expert"), "section"),
        check_vma=False,
    )
```

```python
import functools

import jax
import jax.numpy as jnp
from jax import lax
from jax.experimental import pallas as pl
from jax.experimental.pallas import tpu as pltpu
from jax.sharding import PartitionSpec as P

epsilon = 1e-06
masked_value = -1e30
route_scale = 2.5


def rotation(position, width):
    halfway = width // 2
    frequency = 10000.0 ** (-2.0 * jnp.arange(halfway).astype(jnp.float32) / width)
    angles = position.astype(jnp.float32)[..., None] * frequency
    return jnp.cos(angles), jnp.sin(angles)


def rotate_pairs(values, position):
    halfway = values.shape[-1] // 2
    cosine, sine_part = rotation(position, values.shape[-1])
    first_half = values[..., :halfway]
    second_half = values[..., halfway:]
    return jnp.concatenate(
        [
            first_half * cosine - second_half * sine_part,
            second_half * cosine + first_half * sine_part,
        ],
        axis=-1,
    )


def rms_scaled(values, gain):
    return (
        values
        * lax.rsqrt(jnp.mean(values * values, axis=-1, keepdims=True) + epsilon)
        * gain.astype(jnp.float32)
    )


def latent_rows(projected, kv_gain, position):
    gain_width = kv_gain.shape[0]
    scaled = rms_scaled(projected[..., :gain_width], kv_gain)
    return jnp.concatenate(
        [scaled, rotate_pairs(projected[..., gain_width:], position)], axis=-1
    ).astype(jnp.bfloat16)


def swap(block, axis, mask):
    size = lax.axis_size(axis)
    return lax.ppermute(block, axis, [(i, i ^ mask) for i in range(size)])


def exchange(blocks, axis):
    here = lax.axis_index(axis)
    landed = [lax.dynamic_index_in_dim(blocks, here, 0, keepdims=False)]
    for mask in range(1, lax.axis_size(axis)):
        sent = lax.dynamic_index_in_dim(blocks, here ^ mask, 0, keepdims=False)
        landed.append(swap(sent, axis, mask))
    return landed


def spread(block, axis):
    return [block] + [swap(block, axis, mask) for mask in range(1, lax.axis_size(axis))]


def attend_kernel(parts, heads_rows, steps, latent, score_scale, *refs):
    part_refs = refs[:parts]
    length_ref, gain_ref, cosine_ref, sine_ref, query_ref, recent_ref, out_ref = refs[parts:]
    f32, bf16 = jnp.float32, jnp.bfloat16
    nt = (((1,), (1,)), ((), ()))
    projected = part_refs[0][0].astype(f32)
    for ref in part_refs[1:]:
        projected = projected + ref[0].astype(f32)
    wide = projected[:, :latent]
    scale = lax.rsqrt(jnp.mean(wide * wide, axis=-1, keepdims=True) + epsilon)
    keys = (wide * scale * gain_ref[...].astype(f32)).astype(bf16)
    turn = projected[:, latent:]
    half = turn.shape[1] // 2
    turned = jnp.concatenate([turn[:, half:], turn[:, :half]], axis=1)
    key_rope = (turn * cosine_ref[...] + turned * sine_ref[...]).astype(bf16)
    query = query_ref[0]
    recent = recent_ref[0]
    scores = lax.dot_general(query[:, :latent], keys, nt, preferred_element_type=f32)
    scores = scores + lax.dot_general(
        query[:, latent:], key_rope, nt, preferred_element_type=f32
    )
    fresh = lax.dot_general(query, recent, nt, preferred_element_type=f32)
    place = lax.broadcasted_iota(jnp.int32, scores.shape, 1)
    scores = jnp.where(place < length_ref[pl.program_id(0)], scores * score_scale, masked_value)
    step = lax.broadcasted_iota(jnp.int32, fresh.shape, 0) // heads_rows
    place = lax.broadcasted_iota(jnp.int32, fresh.shape, 1)
    fresh = jnp.where(place <= step, fresh * score_scale, masked_value)
    most = jnp.maximum(
        jnp.max(scores, axis=-1, keepdims=True), jnp.max(fresh, axis=-1, keepdims=True)
    )
    scores = jnp.exp(scores - most)
    fresh = jnp.exp(fresh - most)
    total = jnp.sum(scores, axis=-1, keepdims=True) + jnp.sum(fresh, axis=-1, keepdims=True)
    scores = (scores / total).astype(bf16)
    fresh = (fresh / total).astype(bf16)
    mixed = jnp.dot(scores, keys, preferred_element_type=f32)
    mixed = mixed + jnp.dot(fresh, recent[:, :latent], preferred_element_type=f32)
    out_ref[0] = mixed.astype(bf16)


def attend(parts, lengths, kv_gain, query_cat, recent, steps, score_scale):
    prompts, positions, width = parts[0].shape
    latent = kv_gain.shape[0]
    rows = query_cat.shape[1]
    cosine, sine = rotation(jnp.arange(positions), width - latent)
    cosine = jnp.concatenate([cosine, cosine], axis=-1)
    sine = jnp.concatenate([-sine, sine], axis=-1)
    one = lambda shape: pl.BlockSpec((1,) + shape, lambda i: (i, 0, 0))
    whole = lambda shape: pl.BlockSpec(shape, lambda i: (0, 0))
    return pl.pallas_call(
        functools.partial(
            attend_kernel, len(parts), rows // steps, steps, latent, score_scale
        ),
        grid=(prompts,),
        out_shape=jax.ShapeDtypeStruct((prompts, rows, latent), jnp.bfloat16),
        in_specs=[one((positions, width))] * len(parts)
        + [
            pl.BlockSpec(memory_space=pltpu.SMEM),
            whole((1, latent)),
            whole(cosine.shape),
            whole(sine.shape),
            one((rows, width)),
            one(recent.shape[1:]),
        ],
        out_specs=one((rows, latent)),
        compiler_params=pltpu.CompilerParams(vmem_limit_bytes=32 * 1024 * 1024),
        name="attend",
    )(*parts, lengths, kv_gain[None], cosine, sine, query_cat, recent)


def local(
    prompts,
    owners,
    lengths,
    residual,
    queries,
    expert_ids,
    route_scores,
    attn_gain,
    w_dkv,
    kv_gain,
    w_uk,
    w_uv,
    w_o,
    moe_gain,
    w_gate,
    w_up,
    w_down,
):
    bf16, f32 = jnp.bfloat16, jnp.float32
    block = ("expert", "section")
    expert_rank = lax.axis_index("expert")
    section_rank = lax.axis_index("section")
    group_rank = lax.axis_index("groups")
    experts = lax.axis_size("expert")
    sections = lax.axis_size("section")
    groups = lax.axis_size("groups")
    prompt_count, full_length, width = prompts.shape
    steps, tokens_here, _ = residual.shape
    heads = queries.shape[2]
    nope = w_uk.shape[1]
    rope = queries.shape[3] - nope
    latent = kv_gain.shape[0]
    cache_width = latent + rope
    depth = w_dkv.shape[0]
    piece = depth // (groups * experts)
    everyone = experts * sections

    w_turned = w_dkv.T
    w_piece = lax.dynamic_slice_in_dim(
        w_turned, (expert_rank * groups + group_rank) * piece, piece, 1
    )
    rows = prompt_count * full_length
    cut = prompts.reshape(rows, sections, experts, groups * piece).transpose(2, 1, 0, 3)
    cut = lax.all_to_all(cut, "expert", 0, 0, tiled=True)
    w_parts = spread(w_piece, "section")
    w_parts = [spread(part, "groups") for part in w_parts]

    uv_full = lax.all_gather(w_uv, "expert", axis=0)

    table = owners.reshape(experts, tokens_here)
    length_table = lengths.reshape(experts, tokens_here)
    my_owner = lax.dynamic_slice(
        table, (expert_rank, section_rank * prompt_count), (1, prompt_count)
    )[0]
    my_length = lax.dynamic_slice(
        length_table, (expert_rank, section_rank * prompt_count), (1, prompt_count)
    )[0]

    residual_all = lax.all_gather(residual, "expert", axis=0)
    queries_all = lax.all_gather(queries, "expert", axis=0)
    expert_total = w_gate.shape[0] * experts
    match_table = (expert_ids[..., None] == jnp.arange(expert_total)).astype(f32)
    weights = route_scale * route_scores / jnp.sum(route_scores, axis=-1, keepdims=True)
    weight_map = jnp.sum(weights[..., None] * match_table, axis=2)
    weights_all = lax.all_gather(weight_map, "expert", axis=0)

    picked = jnp.take_along_axis(
        queries_all.transpose(2, 0, 1, 3, 4), table[:, :, None, None, None], axis=1
    )
    query_latent = jnp.einsum(
        "ejthn,hnc->ejthc", picked[..., :nope], w_uk, preferred_element_type=f32
    ).astype(bf16)
    rope_piece = rope // experts
    query_rope = lax.dynamic_slice_in_dim(picked[..., nope:], expert_rank * rope_piece, rope_piece, 4)
    query_part = jnp.concatenate([query_latent, query_rope], axis=-1).reshape(
        everyone, prompt_count * steps * heads, -1
    )
    normed = rms_scaled(residual.astype(f32), attn_gain).astype(bf16)
    normed = lax.dynamic_slice_in_dim(normed, section_rank * depth, depth, 2)
    fresh = jnp.einsum("ted,kd->etk", normed, w_turned, preferred_element_type=f32).astype(bf16)
    fresh = fresh.reshape(experts, 1, -1, query_part.shape[-1])
    fresh = jnp.broadcast_to(fresh, (experts, sections) + fresh.shape[2:])
    query_part = jnp.concatenate(
        [query_part, fresh.reshape((everyone,) + fresh.shape[2:])], axis=1
    )
    query_part = lax.all_to_all(query_part, block, 0, 0, tiled=True)
    fresh = query_part[:, prompt_count * steps * heads :]
    fresh = fresh.reshape(experts, sections, steps, cache_width)
    query_part = query_part[:, : prompt_count * steps * heads]
    query_part = query_part.reshape(experts, sections, prompt_count, steps, heads, -1)
    query_part = query_part.transpose(2, 3, 1, 4, 0, 5)
    chunk = w_uk.shape[2]
    query_cat = query_part[..., :chunk].reshape(prompt_count, steps, sections * heads, latent)
    query_rope = query_part[..., chunk:].reshape(prompt_count, steps, sections * heads, rope)
    token_pos = my_length[:, None] + jnp.arange(steps)[None, :]
    query_cat = jnp.concatenate(
        [
            query_cat,
            rotate_pairs(query_rope.astype(f32), token_pos[:, :, None]).astype(bf16),
        ],
        axis=-1,
    )

    fresh = jnp.sum(jnp.take(fresh, my_owner, axis=0).astype(f32), axis=1)
    recent = latent_rows(fresh, kv_gain, token_pos)
    recent = jnp.pad(recent, ((0, 0), (0, -steps % 16), (0, 0)))

    partial = 0
    for mask, pair in enumerate(w_parts):
        share = lax.dynamic_index_in_dim(cut, section_rank ^ mask, 1, keepdims=False)
        for other, part in enumerate(pair):
            some = lax.dynamic_slice_in_dim(share, (group_rank ^ other) * piece, piece, 2)
            partial = partial + jnp.einsum(
                "drc,kc->drk", some, part, preferred_element_type=f32
            )
    parts = exchange(partial.astype(bf16), "expert")
    parts = [part.reshape(prompt_count, full_length, cache_width) for part in parts]
    out_latent = attend(
        parts,
        my_length,
        kv_gain,
        query_cat.reshape(prompt_count, -1, cache_width),
        recent,
        steps,
        queries.shape[-1] ** (-0.5),
    )

    out_latent = out_latent.reshape(prompt_count, steps, sections, heads, latent)
    out_latent = out_latent.transpose(2, 0, 1, 3, 4)
    out_latent = lax.all_to_all(out_latent, "section", 0, 0, tiled=True)
    row = lax.dynamic_slice_in_dim(table, expert_rank, 1, 0)[0]
    out_latent = out_latent.reshape(tokens_here, steps, heads, latent)
    out_latent = jnp.take(out_latent, jnp.argsort(row), axis=0)
    out_latent = out_latent.reshape(tokens_here, steps, heads, experts, chunk)
    head_values = jnp.einsum(
        "othxc,xhvc->othv", out_latent, uv_full, preferred_element_type=f32
    ).astype(bf16)
    head_values = head_values.reshape(tokens_here * steps, -1)
    head_values = lax.all_gather(head_values, "expert", axis=0, tiled=True)

    attended = jnp.dot(head_values, w_o, preferred_element_type=f32).astype(bf16)
    attended = sum(part.astype(f32) for part in spread(attended, "section")).astype(bf16)
    attended = lax.all_gather(attended, "expert", axis=1, tiled=True)
    hidden = residual_all.transpose(2, 0, 1, 3).reshape(-1, width).astype(f32)
    mixed = hidden + attended.astype(f32)
    moe_in = rms_scaled(mixed, moe_gain).astype(bf16)

    gate_part = jnp.einsum("td,xdf->txf", moe_in, w_gate, preferred_element_type=f32)
    up_part = jnp.einsum("td,xdf->txf", moe_in, w_up, preferred_element_type=f32)
    route = weights_all.transpose(2, 0, 1, 3).reshape(-1, expert_total)
    route = lax.dynamic_slice_in_dim(route, expert_rank * w_gate.shape[0], w_gate.shape[0], 1)
    activated = (jax.nn.silu(gate_part) * up_part * route[:, :, None]).astype(bf16)
    combined = jnp.dot(
        activated.reshape(activated.shape[0], -1),
        w_down.reshape(-1, width),
        preferred_element_type=f32,
    ).astype(bf16)
    column = width // sections
    combined = combined.reshape(experts, experts, steps, sections, column)
    combined = combined.transpose(1, 3, 0, 2, 4).reshape(everyone, experts, steps, column)
    combined = lax.all_to_all(combined, block, 0, 0, tiled=True)
    combined = jnp.sum(combined.astype(f32), axis=0)
    own = mixed.reshape(experts, experts, steps, sections, column)
    own = lax.dynamic_slice(
        own,
        (0, expert_rank, 0, section_rank, 0),
        (experts, 1, steps, 1, column),
    )[:, 0, :, 0]
    return (own + combined).transpose(1, 0, 2).astype(bf16)


def solution(mesh):
    placed = (
        P(("groups", "expert", "section"), None, None),
        P("groups"),
        P("groups"),
        P(None, ("groups", "expert"), None),
        P(None, ("groups", "expert"), "section", None),
        P(None, ("groups", "expert"), None),
        P(None, ("groups", "expert"), None),
        P(),
        P("section", None),
        P(),
        P("section", None, "expert"),
        P("section", None, "expert"),
        P("section", "expert"),
        P(),
        P("expert", None, "section"),
        P("expert", None, "section"),
        P("expert", "section", None),
    )
    return jax.shard_map(
        local,
        mesh=mesh,
        in_specs=placed,
        out_specs=P(None, ("groups", "expert"), "section"),
        check_vma=False,
    )
```

```python
import functools

import jax
import jax.numpy as jnp
import numpy as np
from jax import lax
from jax.experimental import pallas as pl
from jax.experimental.pallas import tpu as pltpu
from jax.sharding import PartitionSpec as P

epsilon = 1e-06
masked_value = -1e30
route_scale = 2.5


def rotation(position, width):
    halfway = width // 2
    frequency = 10000.0 ** (-2.0 * jnp.arange(halfway).astype(jnp.float32) / width)
    angles = position.astype(jnp.float32)[..., None] * frequency
    return jnp.cos(angles), jnp.sin(angles)


def rotate_pairs(values, position):
    halfway = values.shape[-1] // 2
    cosine, sine_part = rotation(position, values.shape[-1])
    first_half = values[..., :halfway]
    second_half = values[..., halfway:]
    return jnp.concatenate(
        [
            first_half * cosine - second_half * sine_part,
            second_half * cosine + first_half * sine_part,
        ],
        axis=-1,
    )


def rms_scaled(values, gain):
    return (
        values
        * lax.rsqrt(jnp.mean(values * values, axis=-1, keepdims=True) + epsilon)
        * gain.astype(jnp.float32)
    )


def latent_rows(projected, kv_gain, position):
    gain_width = kv_gain.shape[0]
    scaled = rms_scaled(projected[..., :gain_width], kv_gain)
    return jnp.concatenate(
        [scaled, rotate_pairs(projected[..., gain_width:], position)], axis=-1
    ).astype(jnp.bfloat16)


def swap(block, axis, mask):
    size = lax.axis_size(axis)
    return lax.ppermute(block, axis, [(i, i ^ mask) for i in range(size)])


def deliver(blocks, axis):
    return [blocks[0]] + [swap(blocks[mask], axis, mask) for mask in range(1, len(blocks))]


def spread(block, axis):
    return [block] + [swap(block, axis, mask) for mask in range(1, lax.axis_size(axis))]


def params():
    return pltpu.CompilerParams(vmem_limit_bytes=40 * 1024 * 1024)


def cut_kernel(sections, experts, piece, x_ref, *refs):
    out_refs, held = refs[:experts], refs[experts]
    rank = lax.axis_index("expert")
    for target in range(experts):
        for section in range(sections):
            at = (section * experts + target) * piece
            held[target, section] = x_ref[:, at : at + piece]
    for mask, ref in enumerate(out_refs):
        ref[...] = held[rank ^ mask]


def cut_columns(x, sections, experts):
    rows, width = x.shape
    piece = width // (sections * experts)
    block = jax.ShapeDtypeStruct((sections, rows, piece), x.dtype)
    return pl.pallas_call(
        functools.partial(cut_kernel, sections, experts, piece),
        out_shape=[block] * experts,
        scratch_shapes=[pltpu.VMEM((experts,) + block.shape, x.dtype)],
        compiler_params=params(),
        name="cut_columns",
    )(x)


def project_kernel(count, sections, groups, *refs):
    x_refs = refs[:count]
    w_refs = refs[count : count + sections * groups]
    out_refs = refs[count + sections * groups :]
    section_rank = lax.axis_index("section")
    group_rank = lax.axis_index("groups")
    rows = x_refs[0].shape[1]
    total = 0
    for mask in range(sections):
        held = [w_refs[mask * groups + other][...] for other in range(groups)]
        columns = []
        for group in range(groups):
            chosen = held[0]
            for other in range(1, groups):
                chosen = jnp.where((group_rank ^ other) == group, held[other], chosen)
            columns.append(chosen)
        weights = jnp.concatenate(columns, axis=1)
        x = jnp.concatenate([ref[section_rank ^ mask] for ref in x_refs], axis=0)
        total = total + lax.dot_general(
            x, weights, (((1,), (1,)), ((), ())), preferred_element_type=jnp.float32
        )
    for index, ref in enumerate(out_refs):
        ref[...] = total[index * rows : (index + 1) * rows].astype(ref.dtype)


def project(blocks, w_parts, sections, groups):
    out = jax.ShapeDtypeStruct((blocks[0].shape[1], w_parts[0].shape[0]), jnp.bfloat16)
    return pl.pallas_call(
        functools.partial(project_kernel, len(blocks), sections, groups),
        out_shape=[out] * len(blocks),
        compiler_params=params(),
        name="project",
    )(*blocks, *w_parts)


def attend_kernel(parts, sections, heads, steps, latent, score_scale, *refs):
    part_refs = refs[:parts]
    length_ref, gain_ref, cosine_ref, sine_ref, query_ref, recent_ref = refs[parts : parts + 6]
    out_refs, held = refs[parts + 6 : -1], refs[-1]
    f32, bf16 = jnp.float32, jnp.bfloat16
    nt = (((1,), (1,)), ((), ()))
    projected = part_refs[0][0].astype(f32)
    for ref in part_refs[1:]:
        projected = projected + ref[0].astype(f32)
    wide = projected[:, :latent]
    scale = lax.rsqrt(jnp.mean(wide * wide, axis=-1, keepdims=True) + epsilon)
    keys = (wide * scale * gain_ref[...].astype(f32)).astype(bf16)
    turn = projected[:, latent:]
    half = turn.shape[1] // 2
    turned = jnp.concatenate([turn[:, half:], turn[:, :half]], axis=1)
    key_rope = (turn * cosine_ref[...] + turned * sine_ref[...]).astype(bf16)
    query = query_ref[0]
    recent = recent_ref[0]
    scores = lax.dot_general(query[:, :latent], keys, nt, preferred_element_type=f32)
    scores = scores + lax.dot_general(
        query[:, latent:], key_rope, nt, preferred_element_type=f32
    )
    fresh = lax.dot_general(query, recent, nt, preferred_element_type=f32)
    place = lax.broadcasted_iota(jnp.int32, scores.shape, 1)
    scores = jnp.where(place < length_ref[pl.program_id(0)], scores * score_scale, masked_value)
    row = lax.broadcasted_iota(jnp.int32, fresh.shape, 0)
    place = lax.broadcasted_iota(jnp.int32, fresh.shape, 1)
    seen = place < 1
    for step in range(1, steps):
        seen = seen | ((place <= step) & (row >= step * sections * heads))
    fresh = jnp.where(seen, fresh * score_scale, masked_value)
    most = jnp.maximum(
        jnp.max(scores, axis=-1, keepdims=True), jnp.max(fresh, axis=-1, keepdims=True)
    )
    scores = jnp.exp(scores - most)
    fresh = jnp.exp(fresh - most)
    total = jnp.sum(scores, axis=-1, keepdims=True) + jnp.sum(fresh, axis=-1, keepdims=True)
    scores = (scores / total).astype(bf16)
    fresh = (fresh / total).astype(bf16)
    mixed = jnp.dot(scores, keys, preferred_element_type=f32)
    mixed = mixed + jnp.dot(fresh, recent[:, :latent], preferred_element_type=f32)
    mixed = mixed.astype(bf16)
    for section in range(sections):
        for step in range(steps):
            at = (step * sections + section) * heads
            held[section, step * heads : (step + 1) * heads] = mixed[at : at + heads]
    rank = lax.axis_index("section")
    for mask, ref in enumerate(out_refs):
        ref[0] = held[rank ^ mask]


def attend(parts, lengths, kv_gain, query_cat, recent, steps, sections, score_scale):
    prompts, positions, width = parts[0].shape
    latent = kv_gain.shape[0]
    rows = query_cat.shape[1]
    heads = rows // (steps * sections)
    cosine, sine = rotation(jnp.arange(positions), width - latent)
    cosine = jnp.concatenate([cosine, cosine], axis=-1)
    sine = jnp.concatenate([-sine, sine], axis=-1)
    one = lambda shape: pl.BlockSpec((1,) + shape, lambda i: (i, 0, 0))
    whole = lambda shape: pl.BlockSpec(shape, lambda i: (0, 0))
    out = (steps * heads, latent)
    return pl.pallas_call(
        functools.partial(
            attend_kernel, len(parts), sections, heads, steps, latent, score_scale
        ),
        grid=(prompts,),
        out_shape=[jax.ShapeDtypeStruct((prompts,) + out, jnp.bfloat16)] * sections,
        in_specs=[one((positions, width))] * len(parts)
        + [
            pl.BlockSpec(memory_space=pltpu.SMEM),
            whole((1, latent)),
            whole(cosine.shape),
            whole(sine.shape),
            one((rows, width)),
            one(recent.shape[1:]),
        ],
        out_specs=[one(out)] * sections,
        scratch_shapes=[pltpu.VMEM((sections,) + out, jnp.bfloat16)],
        compiler_params=params(),
        name="attend",
    )(*parts, lengths, kv_gain[None], cosine, sine, query_cat, recent)


def output_kernel(order_ref, value_ref, weight_ref, out_ref, ordered, total):
    step = pl.program_id(0)
    depth = weight_ref.shape[0]

    @pl.when(step == 0)
    def _():
        moved = jnp.dot(order_ref[...], value_ref[...], preferred_element_type=jnp.float32)
        moved = moved.astype(jnp.bfloat16)
        for index in range(ordered.shape[0]):
            ordered[index] = moved[:, index * depth : (index + 1) * depth]
        total[...] = jnp.zeros_like(total)

    total[...] += jnp.dot(ordered[step], weight_ref[...], preferred_element_type=jnp.float32)

    @pl.when(step == pl.num_programs(0) - 1)
    def _():
        out_ref[...] = total[...].astype(out_ref.dtype)


def output_product(values, order, weight):
    rows, depth = values.shape
    width = weight.shape[1]
    pieces = 4
    whole = lambda shape: pl.BlockSpec(shape, lambda i: (0, 0))
    return pl.pallas_call(
        output_kernel,
        grid=(pieces,),
        out_shape=jax.ShapeDtypeStruct((rows, width), jnp.bfloat16),
        in_specs=[
            whole(order.shape),
            whole(values.shape),
            pl.BlockSpec((depth // pieces, width), lambda i: (i, 0)),
        ],
        out_specs=whole((rows, width)),
        scratch_shapes=[
            pltpu.VMEM((pieces, rows, depth // pieces), jnp.bfloat16),
            pltpu.VMEM((rows, width), jnp.float32),
        ],
        compiler_params=params(),
        name="output_product",
    )(order, values, weight)


def expert_kernel(experts, sections, *refs):
    attended_ref, hidden_ref, gain_ref, route_ref, gate_ref, up_ref, down_ref = refs[:7]
    out_refs, own_ref = refs[7 : 7 + experts], refs[7 + experts]
    gate_held, up_held, down_held, staged, sems = refs[8 + experts :]
    f32, bf16 = jnp.float32, jnp.bfloat16
    count = gate_held.shape[0]
    copies = []
    for x in range(count):
        for kind, (source, held) in enumerate(
            ((gate_ref, gate_held), (up_ref, up_held), (down_ref, down_held))
        ):
            copies.append(pltpu.make_async_copy(source.at[x], held.at[x], sems.at[x, kind]))
            copies[-1].start()
    rank = lax.axis_index("expert")
    attended = jnp.concatenate([attended_ref[i] for i in range(experts)], axis=1).astype(f32)
    mixed = hidden_ref[...].astype(f32) + attended
    scale = lax.rsqrt(jnp.mean(mixed * mixed, axis=-1, keepdims=True) + epsilon)
    rows_in = (mixed * scale * gain_ref[...].astype(f32)).astype(bf16)
    block, column = staged.shape[2:]

    def stage(values):
        for owner in range(experts):
            for section in range(sections):
                staged[owner, section] = values[
                    owner * block : (owner + 1) * block, section * column : (section + 1) * column
                ]

    stage(attended)
    own_ref[...] = staged[rank].astype(bf16)
    total = 0
    for x in range(count):
        copies[3 * x].wait()
        gate = jnp.dot(rows_in, gate_held[x], preferred_element_type=f32)
        copies[3 * x + 1].wait()
        up = jnp.dot(rows_in, up_held[x], preferred_element_type=f32)
        hidden = gate / (1.0 + jnp.exp(-gate)) * up * route_ref[:, x : x + 1]
        copies[3 * x + 2].wait()
        total = total + jnp.dot(hidden.astype(bf16), down_held[x], preferred_element_type=f32)
    stage(total)
    for mask, ref in enumerate(out_refs):
        ref[...] = staged[rank ^ mask].astype(bf16)


def run_experts(attended, hidden, gain, route, w_gate, w_up, w_down, sections):
    experts, rows, _ = attended.shape
    width = hidden.shape[1]
    shape = (sections, rows // experts, width // sections)
    out = jax.ShapeDtypeStruct(shape, jnp.bfloat16)
    held = pl.BlockSpec(memory_space=pltpu.VMEM)
    away = pl.BlockSpec(memory_space=pl.ANY)
    outs = pl.pallas_call(
        functools.partial(expert_kernel, experts, sections),
        out_shape=[out] * (experts + 1),
        in_specs=[held] * 4 + [away] * 3,
        scratch_shapes=[
            pltpu.VMEM(w_gate.shape, w_gate.dtype),
            pltpu.VMEM(w_up.shape, w_up.dtype),
            pltpu.VMEM(w_down.shape, w_down.dtype),
            pltpu.VMEM((experts,) + shape, jnp.float32),
            pltpu.SemaphoreType.DMA((w_gate.shape[0], 3)),
        ],
        compiler_params=params(),
        name="run_experts",
    )(attended, hidden, gain[None], route, w_gate, w_up, w_down)
    return outs[:experts], outs[experts]


def fold_kernel(sections, count, *refs):
    in_refs, out_refs, held = refs[:count], refs[count:-1], refs[-1]
    rank = lax.axis_index("section")
    total = in_refs[0][...].astype(jnp.float32)
    for ref in in_refs[1:]:
        total = total + ref[...].astype(jnp.float32)
    held[...] = total
    for mask, ref in enumerate(out_refs):
        ref[...] = held[rank ^ mask].astype(ref.dtype)


def fold(blocks):
    sections, rows, column = blocks[0].shape
    return pl.pallas_call(
        functools.partial(fold_kernel, sections, len(blocks)),
        out_shape=[jax.ShapeDtypeStruct((rows, column), jnp.bfloat16)] * sections,
        scratch_shapes=[pltpu.VMEM((sections, rows, column), jnp.float32)],
        compiler_params=params(),
        name="fold",
    )(*blocks)


def local(
    prompts,
    owners,
    lengths,
    residual,
    queries,
    expert_ids,
    route_scores,
    attn_gain,
    w_dkv,
    kv_gain,
    w_uk,
    w_uv,
    w_o,
    moe_gain,
    w_gate,
    w_up,
    w_down,
):
    bf16, f32 = jnp.bfloat16, jnp.float32
    block = ("expert", "section")
    expert_rank = lax.axis_index("expert")
    section_rank = lax.axis_index("section")
    group_rank = lax.axis_index("groups")
    experts = lax.axis_size("expert")
    sections = lax.axis_size("section")
    groups = lax.axis_size("groups")
    prompt_count, full_length, width = prompts.shape
    steps, tokens_here, _ = residual.shape
    heads = queries.shape[2]
    nope = w_uk.shape[1]
    rope = queries.shape[3] - nope
    latent = kv_gain.shape[0]
    cache_width = latent + rope
    depth = w_dkv.shape[0]
    piece = depth // (groups * experts)
    everyone = experts * sections

    rows = prompt_count * full_length
    w_turned = w_dkv.T
    w_piece = lax.dynamic_slice_in_dim(
        w_turned, (expert_rank * groups + group_rank) * piece, piece, 1
    )
    w_parts = spread(w_piece, "section")
    cut = cut_columns(prompts.reshape(rows, width), sections, experts)
    cut = deliver(cut, "expert")
    w_parts = [part for half in w_parts for part in spread(half, "groups")]

    table = owners.reshape(experts, tokens_here)
    length_table = lengths.reshape(experts, tokens_here)
    my_owner = lax.dynamic_slice(
        table, (expert_rank, section_rank * prompt_count), (1, prompt_count)
    )[0]
    my_length = lax.dynamic_slice(
        length_table, (expert_rank, section_rank * prompt_count), (1, prompt_count)
    )[0]

    expert_total = w_gate.shape[0] * experts
    match_table = (expert_ids[..., None] == jnp.arange(expert_total)).astype(f32)
    weights = route_scale * route_scores / jnp.sum(route_scores, axis=-1, keepdims=True)
    weight_map = jnp.sum(weights[..., None] * match_table, axis=2).reshape(-1, expert_total)
    weight_high = weight_map.astype(bf16)
    weight_low = (weight_map - weight_high.astype(f32)).astype(bf16)
    own_rows = steps * tokens_here
    packed = jnp.concatenate(
        [
            residual.reshape(own_rows, width),
            queries.reshape(own_rows, -1),
            weight_high,
            weight_low,
        ],
        axis=1,
    )
    packed, cut[0] = lax.optimization_barrier((packed, cut[0]))
    packed = lax.all_gather(packed, "expert", axis=0, tiled=True)
    hidden = packed[:, :width]
    at = width + queries.shape[2] * queries.shape[3]
    queries_all = packed[:, width:at].reshape((experts,) + queries.shape)
    weights_all = packed[:, at : at + expert_total].astype(f32)
    weights_all = weights_all + packed[:, at + expert_total :].astype(f32)
    route = lax.dynamic_slice_in_dim(
        weights_all, expert_rank * w_gate.shape[0], w_gate.shape[0], 1
    )

    picked = jnp.take_along_axis(
        queries_all.transpose(2, 0, 1, 3, 4), table[:, :, None, None, None], axis=1
    )
    query_latent = jnp.einsum(
        "ejthn,hnc->ejthc", picked[..., :nope], w_uk, preferred_element_type=f32
    ).astype(bf16)
    rope_piece = rope // experts
    query_rope = lax.dynamic_slice_in_dim(picked[..., nope:], expert_rank * rope_piece, rope_piece, 4)
    query_part = jnp.concatenate([query_latent, query_rope], axis=-1).reshape(
        everyone, prompt_count * steps * heads, -1
    )
    normed = rms_scaled(residual.astype(f32), attn_gain).astype(bf16)
    normed = lax.dynamic_slice_in_dim(normed, section_rank * depth, depth, 2)
    fresh = jnp.einsum("ted,kd->etk", normed, w_turned, preferred_element_type=f32).astype(bf16)
    fresh = fresh.reshape(experts, 1, -1, query_part.shape[-1])
    fresh = jnp.broadcast_to(fresh, (experts, sections) + fresh.shape[2:])
    query_part = jnp.concatenate(
        [query_part, fresh.reshape((everyone,) + fresh.shape[2:])], axis=1
    )
    query_part = lax.all_to_all(query_part, block, 0, 0, tiled=True)
    fresh = query_part[:, prompt_count * steps * heads :]
    fresh = fresh.reshape(experts, sections, steps, cache_width)
    query_part = query_part[:, : prompt_count * steps * heads]
    query_part = query_part.reshape(experts, sections, prompt_count, steps, heads, -1)
    query_part = query_part.transpose(2, 3, 1, 4, 0, 5)
    chunk = w_uk.shape[2]
    query_cat = query_part[..., :chunk].reshape(prompt_count, steps, sections * heads, latent)
    query_rope = query_part[..., chunk:].reshape(prompt_count, steps, sections * heads, rope)
    token_pos = my_length[:, None] + jnp.arange(steps)[None, :]
    query_cat = jnp.concatenate(
        [
            query_cat,
            rotate_pairs(query_rope.astype(f32), token_pos[:, :, None]).astype(bf16),
        ],
        axis=-1,
    )

    fresh = jnp.sum(jnp.take(fresh, my_owner, axis=0).astype(f32), axis=1)
    recent = latent_rows(fresh, kv_gain, token_pos)
    recent = jnp.pad(recent, ((0, 0), (0, -steps % 16), (0, 0)))

    uv_full = lax.all_gather(w_uv, "expert", axis=0)
    away = project(cut[1:], w_parts, sections, groups)
    near = project(cut[:1], w_parts, sections, groups)
    parts = [part.reshape(prompt_count, full_length, -1) for part in deliver(near + away, "expert")]
    out_latent = attend(
        parts,
        my_length,
        kv_gain,
        query_cat.reshape(prompt_count, -1, cache_width),
        recent,
        steps,
        sections,
        queries.shape[-1] ** (-0.5),
    )

    out_latent = jnp.stack(deliver(out_latent, "section"))
    row = lax.dynamic_slice_in_dim(table, expert_rank, 1, 0)[0]
    source = jnp.argsort(row)
    source = (section_rank ^ (source // prompt_count)) * prompt_count + source % prompt_count
    out_latent = jnp.take(out_latent.reshape(tokens_here, steps, heads, -1), source, axis=0)
    out_latent = out_latent.reshape(tokens_here, steps, heads, experts, chunk)
    head_values = jnp.einsum(
        "othxc,xhvc->othv", out_latent, uv_full, preferred_element_type=f32
    ).astype(bf16)
    head_values = head_values.reshape(tokens_here * steps, -1)
    head_values = lax.all_gather(head_values, "expert", axis=0, tiled=True)

    total_rows = head_values.shape[0]
    order = np.arange(total_rows).reshape(experts, tokens_here, steps).transpose(1, 2, 0)
    order = np.eye(total_rows, dtype=np.float32)[order.reshape(-1)]
    attended = output_product(head_values, jnp.asarray(order, bf16), w_o)
    attended = sum(part.astype(f32) for part in spread(attended, "section")).astype(bf16)
    attended = lax.all_gather(attended, "expert", axis=0)
    blocks, own = run_experts(
        attended, hidden, moe_gain, route, w_gate, w_up, w_down, sections
    )
    blocks = deliver(fold(deliver(blocks, "expert")), "section")
    column = width // sections
    base = lax.dynamic_slice_in_dim(residual, section_rank * column, column, 2)
    own = lax.dynamic_index_in_dim(own, section_rank, 0, keepdims=False)
    total = base.reshape(own_rows, column).astype(f32) + own.astype(f32)
    total = total + sum(part.astype(f32) for part in blocks)
    return total.astype(bf16).reshape(steps, tokens_here, column)


def solution(mesh):
    placed = (
        P(("groups", "expert", "section"), None, None),
        P("groups"),
        P("groups"),
        P(None, ("groups", "expert"), None),
        P(None, ("groups", "expert"), "section", None),
        P(None, ("groups", "expert"), None),
        P(None, ("groups", "expert"), None),
        P(),
        P("section", None),
        P(),
        P("section", None, "expert"),
        P("section", None, "expert"),
        P("section", "expert"),
        P(),
        P("expert", None, "section"),
        P("expert", None, "section"),
        P("expert", "section", None),
    )
    return jax.shard_map(
        local,
        mesh=mesh,
        in_specs=placed,
        out_specs=P(None, ("groups", "expert"), "section"),
        check_vma=False,
    )
```

```python
import functools

import jax
import jax.numpy as jnp
from jax import lax
from jax.experimental import pallas as pl
from jax.experimental.pallas import tpu as pltpu
from jax.sharding import PartitionSpec as P

epsilon = 1e-06
masked_value = -1e30
route_scale = 2.5


def rotation(position, width):
    halfway = width // 2
    frequency = 10000.0 ** (-2.0 * jnp.arange(halfway).astype(jnp.float32) / width)
    angles = position.astype(jnp.float32)[..., None] * frequency
    return jnp.cos(angles), jnp.sin(angles)


def swap(block, axis, mask):
    size = lax.axis_size(axis)
    return lax.ppermute(block, axis, [(i, i ^ mask) for i in range(size)])


def deliver(blocks, axis):
    return [blocks[0]] + [swap(blocks[mask], axis, mask) for mask in range(1, len(blocks))]


def spread(block, axis):
    return [block] + [swap(block, axis, mask) for mask in range(1, lax.axis_size(axis))]


def params(mebibytes=40):
    return pltpu.CompilerParams(vmem_limit_bytes=mebibytes * 1024 * 1024)


def doubled(block, axis):
    held = {0: block}
    size = lax.axis_size(axis)
    masks = [1 << bit for bit in range(size.bit_length() - 1)]
    for mask in masks[1:] + masks[:1]:
        for other in list(held):
            held[other ^ mask] = swap(held[other], axis, mask)
    return [held[mask] for mask in range(size)]


def cut_kernel(sections, experts, piece, x_ref, *refs):
    out_refs, held = refs[:experts], refs[experts]
    rank = lax.axis_index("expert")
    for target in range(experts):
        for section in range(sections):
            at = (section * experts + target) * piece
            held[target, section] = x_ref[:, at : at + piece]
    for mask, ref in enumerate(out_refs):
        ref[...] = held[rank ^ mask]


def cut_columns(x, sections, experts):
    rows, width = x.shape
    piece = width // (sections * experts)
    block = jax.ShapeDtypeStruct((sections, rows, piece), x.dtype)
    return pl.pallas_call(
        functools.partial(cut_kernel, sections, experts, piece),
        out_shape=[block] * experts,
        scratch_shapes=[pltpu.VMEM((experts,) + block.shape, x.dtype)],
        compiler_params=params(),
        name="cut_columns",
    )(x)


def project_kernel(count, sections, groups, *refs):
    x_refs = refs[:count]
    w_refs = refs[count : count + sections * groups]
    out_refs = refs[count + sections * groups :]
    section_rank = lax.axis_index("section")
    group_rank = lax.axis_index("groups")
    rows = x_refs[0].shape[1]
    total = 0
    for mask in range(sections):
        held = [w_refs[mask * groups + other][...] for other in range(groups)]
        columns = []
        for group in range(groups):
            chosen = held[0]
            for other in range(1, groups):
                chosen = jnp.where((group_rank ^ other) == group, held[other], chosen)
            columns.append(chosen)
        weights = jnp.concatenate(columns, axis=1)
        x = jnp.concatenate([ref[section_rank ^ mask] for ref in x_refs], axis=0)
        total = total + lax.dot_general(
            x, weights, (((1,), (1,)), ((), ())), preferred_element_type=jnp.float32
        )
    for index, ref in enumerate(out_refs):
        ref[...] = total[index * rows : (index + 1) * rows].astype(ref.dtype)


def project(blocks, w_parts, sections, groups):
    out = jax.ShapeDtypeStruct((blocks[0].shape[1], w_parts[0].shape[0]), jnp.bfloat16)
    return pl.pallas_call(
        functools.partial(project_kernel, len(blocks), sections, groups),
        out_shape=[out] * len(blocks),
        compiler_params=params(),
        name="project",
    )(*blocks, *w_parts)


def query_kernel(
    experts, sections, prompts, nope, table_ref, query_ref, uk_ref, own_ref, gain_ref, wt_ref,
    out_ref, picked, ropes, made, normed
):
    f32, bf16 = jnp.float32, jnp.bfloat16
    _, steps, sources, heads, wide = query_ref.shape
    rope = wide - nope
    chunk = uk_ref.shape[2]
    width = out_ref.shape[2]
    count = experts * sources
    block = prompts * steps * heads
    rank = lax.axis_index("expert")

    def pick(index, carry):
        owner = table_ref[index]
        for step in range(steps):
            value = query_ref[owner, step, index // sources].astype(f32)
            at = pl.ds(pl.multiple_of((index * steps + step) * heads, heads), heads)
            picked[at, :] = value[:, :nope]
            ropes[at, :] = value[:, nope:].astype(bf16)
        return carry

    if count <= 16:
        for index in range(count):
            pick(index, 0)
    else:
        lax.fori_loop(0, count, pick, 0)
    for head in range(heads):
        at = pl.ds(head, count * steps, stride=heads)
        value = jnp.dot(picked[at, :].astype(bf16), uk_ref[head], preferred_element_type=f32)
        if chunk < made.shape[1]:
            spare = jnp.zeros((count * steps, made.shape[1] - chunk), f32)
            value = jnp.concatenate([value, spare], axis=1)
        made[at, :] = value
    small = width - chunk
    pair = lax.broadcasted_iota(jnp.int32, (rope, small), 0)
    pair = pair == lax.broadcasted_iota(jnp.int32, (rope, small), 1) + rank * small
    turned = jnp.dot(
        ropes[...], jnp.where(pair, 1.0, 0.0).astype(bf16), preferred_element_type=f32
    )
    own = own_ref[...].astype(f32)
    scale = lax.rsqrt(jnp.mean(own * own, axis=-1, keepdims=True) + epsilon)
    own = (own * scale * gain_ref[...].astype(f32)).astype(bf16)
    depth = wt_ref.shape[1]
    for section in range(sections):
        normed[section] = own[:, section * depth : (section + 1) * depth]
    fresh = lax.dot_general(
        normed[lax.axis_index("section")],
        wt_ref[...],
        (((1,), (1,)), ((), ())),
        preferred_element_type=f32,
    )
    for source in range(experts):
        lines = [
            fresh[step * sources + source :, part * width : (part + 1) * width][:1]
            for step in range(steps)
            for part in range(experts)
        ]
        lines = jnp.concatenate(lines, axis=0).astype(bf16)
        for section in range(sections):
            index = source * sections + section
            at = slice(index * block, (index + 1) * block)
            value = jnp.concatenate([made[at, :chunk], turned[at]], axis=1)
            out_ref[index, :block, :] = value.astype(bf16)
            out_ref[index, block:, :] = lines


def absorb_queries(table, queries, w_uk, own, gain, w_turned, prompts, sections):
    experts, steps, sources, heads, wide = queries.shape
    _, nope, chunk = w_uk.shape
    width = chunk + (wide - nope) // experts
    rows = prompts * steps * heads + steps * experts
    count = experts * sources * steps * heads
    held = pl.BlockSpec(memory_space=pltpu.VMEM)
    return pl.pallas_call(
        functools.partial(query_kernel, experts, sections, prompts, nope),
        out_shape=jax.ShapeDtypeStruct((experts * sections, rows, width), jnp.bfloat16),
        in_specs=[pl.BlockSpec(memory_space=pltpu.SMEM)] + [held] * 5,
        out_specs=held,
        scratch_shapes=[
            pltpu.VMEM((count, nope), jnp.float32),
            pltpu.VMEM((count, wide - nope), jnp.bfloat16),
            pltpu.VMEM((count, max(chunk, 128)), jnp.float32),
            pltpu.VMEM((sections, own.shape[0], w_turned.shape[1]), jnp.bfloat16),
        ],
        compiler_params=params(),
        name="absorb_queries",
    )(table, queries, w_uk, own, gain[None], w_turned)


def attend_kernel(parts, experts, sections, heads, steps, latent, score_scale, *refs):
    part_refs = refs[:parts]
    (length_ref, owner_ref, gain_ref, cosine_ref, sine_ref, token_cosine_ref, token_sine_ref,
     block_ref) = refs[parts : parts + 8]
    out_refs, held = refs[parts + 8 : -1], refs[-1]
    f32, bf16 = jnp.float32, jnp.bfloat16
    nt = (((1,), (1,)), ((), ()))
    prompt = pl.program_id(0)
    gain = gain_ref[...].astype(f32)
    rows = steps * heads
    chunk = latent // experts
    whole = pl.num_programs(0) * rows

    def turn(values, cosine, sine):
        half = values.shape[1] // 2
        other = jnp.concatenate([values[:, half:], values[:, :half]], axis=1)
        return values * cosine + other * sine

    def scaled(values):
        scale = lax.rsqrt(jnp.mean(values * values, axis=-1, keepdims=True) + epsilon)
        return values * scale * gain

    at = pl.ds(pl.multiple_of(prompt * rows, rows), rows)
    token_cosine, token_sine = token_cosine_ref[0], token_sine_ref[0]
    latents, ropes = [], []
    for section in range(sections):
        pieces = [block_ref[i * sections + section, at, :] for i in range(experts)]
        latents.append(jnp.concatenate([piece[:, :chunk] for piece in pieces], axis=1))
        rope = jnp.concatenate([piece[:, chunk:].astype(f32) for piece in pieces], axis=1)
        ropes.append(turn(rope, token_cosine, token_sine).astype(bf16))
    query = jnp.concatenate(latents, axis=0)
    query_rope = jnp.concatenate(ropes, axis=0)

    owner = owner_ref[prompt]
    lines = 0
    for section in range(sections):
        lines = lines + block_ref[owner * sections + section, whole:, :].astype(f32)
    recent, recent_rope = [], []
    for step in range(steps):
        line = jnp.concatenate(
            [lines[step * experts + part :][:1] for part in range(experts)], axis=1
        )
        recent.append(scaled(line[:, :latent]))
        recent_rope.append(
            turn(
                line[:, latent:],
                token_cosine[step * heads : step * heads + 1],
                token_sine[step * heads : step * heads + 1],
            )
        )
    spare = -steps % 16
    recent = jnp.concatenate(recent + [jnp.zeros((spare, latent), f32)], axis=0).astype(bf16)
    rope = recent_rope[0].shape[1]
    recent_rope = jnp.concatenate(
        recent_rope + [jnp.zeros((spare, rope), f32)], axis=0
    ).astype(bf16)

    projected = part_refs[0][0].astype(f32)
    for ref in part_refs[1:]:
        projected = projected + ref[0].astype(f32)
    keys = scaled(projected[:, :latent]).astype(bf16)
    key_rope = turn(projected[:, latent:], cosine_ref[...], sine_ref[...]).astype(bf16)
    scores = lax.dot_general(query, keys, nt, preferred_element_type=f32)
    scores = scores + lax.dot_general(query_rope, key_rope, nt, preferred_element_type=f32)
    fresh = lax.dot_general(query, recent, nt, preferred_element_type=f32)
    fresh = fresh + lax.dot_general(query_rope, recent_rope, nt, preferred_element_type=f32)
    place = lax.broadcasted_iota(jnp.int32, scores.shape, 1)
    scores = jnp.where(place < length_ref[prompt], scores * score_scale, masked_value)
    row = lax.broadcasted_iota(jnp.int32, (rows, fresh.shape[1]), 0)
    place = lax.broadcasted_iota(jnp.int32, (rows, fresh.shape[1]), 1)
    seen = jnp.where(place < 1, 1.0, 0.0)
    for step in range(1, steps):
        seen = jnp.where((place <= step) & (row >= step * heads), 1.0, seen)
    seen = jnp.concatenate([seen] * sections, axis=0)
    fresh = jnp.where(seen > 0.5, fresh * score_scale, masked_value)
    most = jnp.maximum(
        jnp.max(scores, axis=-1, keepdims=True), jnp.max(fresh, axis=-1, keepdims=True)
    )
    scores = jnp.exp(scores - most)
    fresh = jnp.exp(fresh - most)
    total = jnp.sum(scores, axis=-1, keepdims=True) + jnp.sum(fresh, axis=-1, keepdims=True)
    scores = (scores / total).astype(bf16)
    fresh = (fresh / total).astype(bf16)
    mixed = jnp.dot(scores, keys, preferred_element_type=f32)
    mixed = mixed + jnp.dot(fresh, recent, preferred_element_type=f32)
    mixed = mixed.astype(bf16)
    for section in range(sections):
        held[section] = mixed[section * rows : (section + 1) * rows]
    rank = lax.axis_index("section")
    for mask, ref in enumerate(out_refs):
        ref[0] = held[rank ^ mask]


def attend(parts, lengths, owners, kv_gain, blocks, steps, heads, experts, sections, score_scale):
    prompts, positions, width = parts[0].shape
    latent = kv_gain.shape[0]
    cosine, sine = rotation(jnp.arange(positions), width - latent)
    cosine = jnp.concatenate([cosine, cosine], axis=-1)
    sine = jnp.concatenate([-sine, sine], axis=-1)
    token_pos = lengths[:, None] + jnp.arange(steps * heads)[None, :] // heads
    token_cosine, token_sine = rotation(token_pos, width - latent)
    token_cosine = jnp.concatenate([token_cosine, token_cosine], axis=-1)
    token_sine = jnp.concatenate([-token_sine, token_sine], axis=-1)
    one = lambda shape: pl.BlockSpec((1,) + shape, lambda i: (i, 0, 0))
    whole = lambda shape: pl.BlockSpec(shape, lambda i: (0,) * len(shape))
    out = (steps * heads, latent)
    return pl.pallas_call(
        functools.partial(
            attend_kernel, len(parts), experts, sections, heads, steps, latent, score_scale
        ),
        grid=(prompts,),
        out_shape=[jax.ShapeDtypeStruct((prompts,) + out, jnp.bfloat16)] * sections,
        in_specs=[one((positions, width))] * len(parts)
        + [pl.BlockSpec(memory_space=pltpu.SMEM)] * 2
        + [
            whole((1, latent)),
            whole(cosine.shape),
            whole(sine.shape),
            one(token_cosine.shape[1:]),
            one(token_sine.shape[1:]),
            whole(blocks.shape),
        ],
        out_specs=[one(out)] * sections,
        scratch_shapes=[pltpu.VMEM((sections,) + out, jnp.bfloat16)],
        compiler_params=params(),
        name="attend",
    )(*parts, lengths, owners, kv_gain[None], cosine, sine, token_cosine, token_sine, blocks)


def value_kernel(experts, sections, heads, *refs):
    latent_refs, uv_refs = refs[:sections], refs[sections : sections + experts]
    order_ref, out_ref, held = refs[sections + experts :]
    f32, bf16 = jnp.float32, jnp.bfloat16
    chunk = uv_refs[0].shape[2]
    rows = latent_refs[0].shape[0]
    for mask, ref in enumerate(latent_refs):
        for index in range(experts):
            held[index, mask * rows : (mask + 1) * rows, :chunk] = ref[
                :, index * chunk : (index + 1) * chunk
            ].astype(f32)
    rank = lax.axis_index("expert")
    values = []
    for head in range(heads):
        at = pl.ds(head, sections * rows // heads, stride=heads)
        total = 0
        for mask, ref in enumerate(uv_refs):
            total = total + lax.dot_general(
                held[rank ^ mask, at, :][:, :chunk].astype(bf16),
                ref[head],
                (((1,), (1,)), ((), ())),
                preferred_element_type=f32,
            )
        values.append(total.astype(bf16))
    values = jnp.concatenate(values, axis=1)
    out_ref[...] = jnp.dot(order_ref[...], values, preferred_element_type=f32).astype(bf16)


def head_products(latents, uv_parts, order):
    rows, width = latents[0].shape
    heads, value, _ = uv_parts[0].shape
    held = pl.BlockSpec(memory_space=pltpu.VMEM)
    total = rows * len(latents)
    return pl.pallas_call(
        functools.partial(value_kernel, len(uv_parts), len(latents), heads),
        out_shape=jax.ShapeDtypeStruct((total // heads, heads * value), jnp.bfloat16),
        in_specs=[held] * (len(latents) + len(uv_parts) + 1),
        out_specs=held,
        scratch_shapes=[
            pltpu.VMEM((len(uv_parts), total, max(width // len(uv_parts), 128)), jnp.float32)
        ],
        compiler_params=params(),
        name="head_products",
    )(*latents, *uv_parts, order)


def output_kernel(count, order_ref, *refs):
    value_refs = refs[:count]
    weight_ref, out_ref, held, sems = refs[count:]
    pieces, depth, _ = held.shape
    copies = []
    for piece in range(pieces):
        source = weight_ref.at[pl.ds(piece * depth, depth)]
        copies.append(pltpu.make_async_copy(source, held.at[piece], sems.at[piece]))
        copies[-1].start()
    values = jnp.concatenate([ref[...] for ref in value_refs], axis=0)
    values = jnp.dot(order_ref[...], values, preferred_element_type=jnp.float32)
    values = values.astype(jnp.bfloat16)
    total = 0
    for piece in range(pieces):
        copies[piece].wait()
        total = total + jnp.dot(
            values[:, piece * depth : (piece + 1) * depth],
            held[piece],
            preferred_element_type=jnp.float32,
        )
    out_ref[...] = total.astype(out_ref.dtype)


def output_product(values, order, weight):
    rows = sum(value.shape[0] for value in values)
    depth, width = weight.shape
    pieces = 4
    held = pl.BlockSpec(memory_space=pltpu.VMEM)
    return pl.pallas_call(
        functools.partial(output_kernel, len(values)),
        out_shape=jax.ShapeDtypeStruct((rows, width), jnp.bfloat16),
        in_specs=[held] * (len(values) + 1) + [pl.BlockSpec(memory_space=pltpu.HBM)],
        out_specs=held,
        scratch_shapes=[
            pltpu.VMEM((pieces, depth // pieces, width), weight.dtype),
            pltpu.SemaphoreType.DMA((pieces,)),
        ],
        compiler_params=params(),
        name="output_product",
    )(order, *values, weight)


def expert_kernel(experts, sections, *refs):
    attended_refs, own_refs = refs[:experts], refs[experts : 2 * experts]
    gain_ref, gate_ref, up_ref, down_ref = refs[2 * experts : 2 * experts + 4]
    out_refs = refs[2 * experts + 4 : 3 * experts + 4]
    near_ref = refs[3 * experts + 4]
    gate_held, up_held, down_held, columns, sems = refs[3 * experts + 5 :]
    f32, bf16 = jnp.float32, jnp.bfloat16
    count = gate_held.shape[0]
    copies = []
    for x in range(count):
        for kind, (source, held) in enumerate(
            ((gate_ref, gate_held), (up_ref, up_held), (down_ref, down_held))
        ):
            copies.append(pltpu.make_async_copy(source.at[x], held.at[x], sems.at[x, kind]))
            copies[-1].start()
    rank = lax.axis_index("expert")
    width = gain_ref.shape[1]
    block = own_refs[0].shape[0]
    for mask, ref in enumerate(attended_refs):
        columns[rank ^ mask] = ref[...]
    attended, hidden, route = [], [], []
    for mask, ref in enumerate(own_refs):
        attended.append(
            jnp.concatenate([columns[i, rank ^ mask] for i in range(experts)], axis=1).astype(f32)
        )
        own = ref[...].astype(f32)
        hidden.append(own[:, :width])
        route.append(own[:, width:])
    near = attended[0]
    mixed = jnp.concatenate(hidden, axis=0) + jnp.concatenate(attended, axis=0)
    route = jnp.concatenate(route, axis=0)
    total_experts = route.shape[1] // 2
    route = route[:, :total_experts] + route[:, total_experts:]
    place = lax.broadcasted_iota(jnp.int32, route.shape, 1)
    scale = lax.rsqrt(jnp.mean(mixed * mixed, axis=-1, keepdims=True) + epsilon)
    rows_in = (mixed * scale * gain_ref[...].astype(f32)).astype(bf16)
    column = width // sections
    total = 0
    for x in range(count):
        weight = jnp.where(place == rank * count + x, route, 0.0)
        weight = jnp.sum(weight, axis=-1, keepdims=True)
        copies[3 * x].wait()
        gate = jnp.dot(rows_in, gate_held[x], preferred_element_type=f32)
        copies[3 * x + 1].wait()
        up = jnp.dot(rows_in, up_held[x], preferred_element_type=f32)
        inner = gate / (1.0 + jnp.exp(-gate)) * up * weight
        copies[3 * x + 2].wait()
        total = total + jnp.dot(inner.astype(bf16), down_held[x], preferred_element_type=f32)
    for section in range(sections):
        at = slice(section * column, (section + 1) * column)
        near_ref[section] = near[:, at].astype(bf16)
        for mask, ref in enumerate(out_refs):
            ref[section] = total[mask * block : (mask + 1) * block, at].astype(bf16)


def run_experts(attended, own, gain, w_gate, w_up, w_down, sections):
    experts = len(own)
    width = gain.shape[0]
    out = jax.ShapeDtypeStruct((sections, own[0].shape[0], width // sections), jnp.bfloat16)
    held = pl.BlockSpec(memory_space=pltpu.VMEM)
    away = pl.BlockSpec(memory_space=pltpu.HBM)
    outs = pl.pallas_call(
        functools.partial(expert_kernel, experts, sections),
        out_shape=[out] * (experts + 1),
        in_specs=[held] * (2 * experts + 1) + [away] * 3,
        out_specs=[held] * (experts + 1),
        scratch_shapes=[
            pltpu.VMEM(w_gate.shape, w_gate.dtype),
            pltpu.VMEM(w_up.shape, w_up.dtype),
            pltpu.VMEM(w_down.shape, w_down.dtype),
            pltpu.VMEM((experts,) + attended[0].shape, jnp.bfloat16),
            pltpu.SemaphoreType.DMA((w_gate.shape[0], 3)),
        ],
        compiler_params=params(48),
        name="run_experts",
    )(*attended, *own, gain[None], w_gate, w_up, w_down)
    return outs[:experts], outs[experts]


def fold_kernel(sections, count, *refs):
    in_refs, out_refs, held = refs[:count], refs[count:-1], refs[-1]
    rank = lax.axis_index("section")
    total = in_refs[0][...].astype(jnp.float32)
    for ref in in_refs[1:]:
        total = total + ref[...].astype(jnp.float32)
    held[...] = total
    for mask, ref in enumerate(out_refs):
        ref[...] = held[rank ^ mask].astype(ref.dtype)


def fold(blocks):
    sections, rows, column = blocks[0].shape
    return pl.pallas_call(
        functools.partial(fold_kernel, sections, len(blocks)),
        out_shape=[jax.ShapeDtypeStruct((rows, column), jnp.bfloat16)] * sections,
        scratch_shapes=[pltpu.VMEM((sections, rows, column), jnp.float32)],
        compiler_params=params(),
        name="fold",
    )(*blocks)


def local(
    prompts,
    owners,
    lengths,
    residual,
    queries,
    expert_ids,
    route_scores,
    attn_gain,
    w_dkv,
    kv_gain,
    w_uk,
    w_uv,
    w_o,
    moe_gain,
    w_gate,
    w_up,
    w_down,
):
    bf16, f32 = jnp.bfloat16, jnp.float32
    expert_rank = lax.axis_index("expert")
    section_rank = lax.axis_index("section")
    group_rank = lax.axis_index("groups")
    experts = lax.axis_size("expert")
    sections = lax.axis_size("section")
    groups = lax.axis_size("groups")
    prompt_count, full_length, width = prompts.shape
    steps, tokens_here, heads, _ = queries.shape
    depth = w_dkv.shape[0]
    piece = depth // (groups * experts)
    rows = prompt_count * full_length
    own_rows = steps * tokens_here

    w_turned = w_dkv.T
    w_piece = lax.dynamic_slice_in_dim(
        w_turned, (expert_rank * groups + group_rank) * piece, piece, 1
    )
    w_parts = spread(w_piece, "section")
    cut = list(cut_columns(prompts.reshape(rows, width), sections, experts))
    queries, cut[0] = lax.optimization_barrier((queries, cut[0]))
    queries_all = lax.all_gather(queries, "expert", axis=0)
    cut = deliver(cut, "expert")
    w_parts = [part for half in w_parts for part in spread(half, "groups")]

    table = owners.reshape(experts, tokens_here)
    length_table = lengths.reshape(experts, tokens_here)
    at = (expert_rank, section_rank * prompt_count)
    my_owner = lax.dynamic_slice(table, at, (1, prompt_count))[0]
    my_length = lax.dynamic_slice(length_table, at, (1, prompt_count))[0]

    queries_all, *cut = lax.optimization_barrier((queries_all, *cut))
    own = residual.reshape(own_rows, width)
    blocks = absorb_queries(
        owners, queries_all, w_uk, own, attn_gain, w_turned, prompt_count, sections
    )
    blocks = lax.all_to_all(blocks, ("expert", "section"), 0, 0, tiled=True)

    expert_total = w_gate.shape[0] * experts
    match_table = (expert_ids[..., None] == jnp.arange(expert_total)).astype(f32)
    weights = route_scale * route_scores / jnp.sum(route_scores, axis=-1, keepdims=True)
    weight_map = jnp.sum(weights[..., None] * match_table, axis=2).reshape(-1, expert_total)
    weight_high = weight_map.astype(bf16)
    weight_low = (weight_map - weight_high.astype(f32)).astype(bf16)
    packed = jnp.concatenate([own, weight_high, weight_low], axis=1)
    w_uv, packed, cut[0] = lax.optimization_barrier((w_uv, packed, cut[0]))
    uv_parts = doubled(w_uv, "expert")

    away = list(project(cut[1:], w_parts, sections, groups))
    near = list(project(cut[:1], w_parts, sections, groups))
    parts = [part.reshape(prompt_count, full_length, -1) for part in deliver(near + away, "expert")]
    blocks, uv_parts[2] = lax.optimization_barrier((blocks, uv_parts[2]))
    out_latent = attend(
        parts,
        my_length,
        my_owner,
        kv_gain,
        blocks,
        steps,
        heads,
        experts,
        sections,
        queries.shape[-1] ** (-0.5),
    )

    out_latent = deliver(out_latent, "section")
    row = lax.dynamic_slice_in_dim(table, expert_rank, 1, 0)[0]
    place = jnp.arange(tokens_here)
    place = (section_rank ^ (place // prompt_count)) * prompt_count + place % prompt_count
    step = jnp.arange(own_rows) % steps
    order = jnp.take(row, place)[jnp.arange(own_rows) // steps] * steps + step
    order = (jnp.arange(own_rows)[:, None] == order[None, :]).astype(bf16)
    head_values = head_products(
        [part.reshape(-1, part.shape[-1]) for part in out_latent], uv_parts, order
    )
    head_values = spread(head_values, "expert")

    total_rows = own_rows * experts
    row = jnp.arange(total_rows)
    source = (row % experts) ^ expert_rank
    order = source * own_rows + row // experts
    order = (order[:, None] == row[None, :]).astype(bf16)
    attended = output_product(head_values, order, w_o)
    attended = sum(part.astype(f32) for part in spread(attended, "section")).astype(bf16)
    attended = attended.reshape(experts, own_rows, -1)
    blocks, near = run_experts(
        spread(attended, "expert"),
        spread(packed, "expert"),
        moe_gain,
        w_gate,
        w_up,
        w_down,
        sections,
    )
    blocks = deliver(fold(deliver(blocks, "expert")), "section")
    column = width // sections
    base = lax.dynamic_slice_in_dim(residual, section_rank * column, column, 2)
    near = lax.dynamic_index_in_dim(near, section_rank, 0, keepdims=False)
    total = base.reshape(own_rows, column).astype(f32) + near.astype(f32)
    total = total + sum(part.astype(f32) for part in blocks)
    return total.astype(bf16).reshape(steps, tokens_here, column)


def solution(mesh):
    placed = (
        P(("groups", "expert", "section"), None, None),
        P("groups"),
        P("groups"),
        P(None, ("groups", "expert"), None),
        P(None, ("groups", "expert"), "section", None),
        P(None, ("groups", "expert"), None),
        P(None, ("groups", "expert"), None),
        P(),
        P("section", None),
        P(),
        P("section", None, "expert"),
        P("section", None, "expert"),
        P("section", "expert"),
        P(),
        P("expert", None, "section"),
        P("expert", None, "section"),
        P("expert", "section", None),
    )
    return jax.shard_map(
        local,
        mesh=mesh,
        in_specs=placed,
        out_specs=P(None, ("groups", "expert"), "section"),
        check_vma=False,
    )
```

```python
import functools
import math

import jax
import jax.numpy as jnp
import numpy as np
from jax import lax
from jax.experimental import pallas as pl
from jax.experimental.pallas import tpu as pltpu
from jax.sharding import PartitionSpec as P

epsilon = 1e-06
masked_value = -1e30
route_scale = 2.5


def rotation(positions, width):
    halfway = width // 2
    frequency = 10000.0 ** (-2.0 * np.arange(halfway) / width)
    angles = np.arange(positions)[:, None] * frequency
    cosine = np.concatenate([np.cos(angles), np.cos(angles)], axis=1)
    sine = np.concatenate([-np.sin(angles), np.sin(angles)], axis=1)
    return jnp.asarray(cosine, jnp.float32), jnp.asarray(sine, jnp.float32)


def swap(block, axis, mask):
    size = lax.axis_size(axis)
    return lax.ppermute(block, axis, [(i, i ^ mask) for i in range(size)])


def deliver(blocks, axis):
    return [blocks[0]] + [swap(blocks[mask], axis, mask) for mask in range(1, len(blocks))]


def spread(block, axis):
    return [block] + [swap(block, axis, mask) for mask in range(1, lax.axis_size(axis))]


def params(*arrays, scale=1):
    held = sum(math.prod(array.shape) * array.dtype.itemsize for array in arrays)
    mebibytes = min(56, 4 + scale * held // 1024 // 1024)
    return pltpu.CompilerParams(vmem_limit_bytes=mebibytes * 1024 * 1024)


def fetch_kernel(count, *refs):
    sems = refs[2 * count]
    copies = [
        pltpu.make_async_copy(refs[index], refs[count + index], sems.at[index])
        for index in range(count)
    ]
    for copy in copies:
        copy.start()
    for copy in copies:
        copy.wait()


def fetch(*arrays):
    size = sum(array.size * array.dtype.itemsize for array in arrays)
    return pl.pallas_call(
        functools.partial(fetch_kernel, len(arrays)),
        out_shape=[pltpu.VMEM(array.shape, array.dtype) for array in arrays],
        in_specs=[pl.BlockSpec(memory_space=pltpu.HBM)] * len(arrays),
        out_specs=[pl.BlockSpec(memory_space=pltpu.VMEM)] * len(arrays),
        scratch_shapes=[pltpu.SemaphoreType.DMA((len(arrays),))],
        compiler_params=pltpu.CompilerParams(vmem_limit_bytes=1024 * 1024),
        cost_estimate=pl.CostEstimate(flops=0, bytes_accessed=2 * size, transcendentals=0),
        name="fetch",
    )(*[pltpu.with_memory_space_constraint(array, pltpu.HBM) for array in arrays])


def doubled(block, axis):
    held = {0: block}
    size = lax.axis_size(axis)
    masks = [1 << bit for bit in range(size.bit_length() - 1)]
    for mask in masks[1:] + masks[:1]:
        for other in list(held):
            held[other ^ mask] = swap(held[other], axis, mask)
    return [held[mask] for mask in range(size)]


def cut_kernel(sections, experts, piece, x_ref, *refs):
    out_refs, held = refs[:experts], refs[experts]
    rank = lax.axis_index("expert")
    for target in range(experts):
        for section in range(sections):
            at = (section * experts + target) * piece
            held[target, section] = x_ref[:, at : at + piece]
    for mask, ref in enumerate(out_refs):
        ref[...] = held[rank ^ mask]


def cut_columns(x, sections, experts):
    rows, width = x.shape
    piece = width // (sections * experts)
    block = jax.ShapeDtypeStruct((sections, rows, piece), x.dtype)
    return pl.pallas_call(
        functools.partial(cut_kernel, sections, experts, piece),
        out_shape=[block] * experts,
        scratch_shapes=[pltpu.VMEM((experts,) + block.shape, x.dtype)],
        compiler_params=params(x, scale=6),
        name="cut_columns",
    )(x)


def project_kernel(count, sections, groups, *refs):
    x_refs = refs[:count]
    w_refs = refs[count : count + sections * groups]
    out_refs = refs[count + sections * groups :]
    section_rank = lax.axis_index("section")
    group_rank = lax.axis_index("groups")
    rows = x_refs[0].shape[1]
    total = 0
    for mask in range(sections):
        held = [w_refs[mask * groups + other][...] for other in range(groups)]
        columns = []
        for group in range(groups):
            chosen = held[0]
            for other in range(1, groups):
                chosen = jnp.where((group_rank ^ other) == group, held[other], chosen)
            columns.append(chosen)
        weights = jnp.concatenate(columns, axis=1)
        x = jnp.concatenate([ref[section_rank ^ mask] for ref in x_refs], axis=0)
        total = total + lax.dot_general(
            x, weights, (((1,), (1,)), ((), ())), preferred_element_type=jnp.float32
        )
    for index, ref in enumerate(out_refs):
        ref[...] = total[index * rows : (index + 1) * rows].astype(ref.dtype)


def project(blocks, w_parts, sections, groups):
    out = jax.ShapeDtypeStruct((blocks[0].shape[1], w_parts[0].shape[0]), jnp.bfloat16)
    return pl.pallas_call(
        functools.partial(project_kernel, len(blocks), sections, groups),
        out_shape=[out] * len(blocks),
        compiler_params=params(*blocks, *w_parts, scale=6),
        name="project",
    )(*blocks, *w_parts)


def query_kernel(
    experts, sections, prompts, nope, *refs
):
    f32, bf16 = jnp.float32, jnp.bfloat16
    table_ref, query_refs = refs[0], refs[1 : 1 + experts]
    uk_ref, own_ref, gain_ref, wt_ref, out_ref, picked, ropes, made, normed, query_ref = refs[
        1 + experts :
    ]
    steps, sources, heads, wide = query_refs[0].shape
    rope = wide - nope
    chunk = uk_ref.shape[2]
    width = out_ref.shape[2]
    count = experts * sources
    block = prompts * steps * heads
    rank = lax.axis_index("expert")

    for mask, ref in enumerate(query_refs):
        query_ref[rank ^ mask] = ref[...]

    def pick(index, carry):
        owner = table_ref[index]
        for step in range(steps):
            value = query_ref[owner, step, index // sources].astype(f32)
            at = pl.ds(pl.multiple_of((index * steps + step) * heads, heads), heads)
            picked[at, :] = value[:, :nope]
            ropes[at, :] = value[:, nope:].astype(bf16)
        return carry

    if count <= 16:
        for index in range(count):
            pick(index, 0)
    else:
        lax.fori_loop(0, count, pick, 0)
    for head in range(heads):
        at = pl.ds(head, count * steps, stride=heads)
        value = jnp.dot(picked[at, :].astype(bf16), uk_ref[head], preferred_element_type=f32)
        if chunk < made.shape[1]:
            spare = jnp.zeros((count * steps, made.shape[1] - chunk), f32)
            value = jnp.concatenate([value, spare], axis=1)
        made[at, :] = value
    small = width - chunk
    pair = lax.broadcasted_iota(jnp.int32, (rope, small), 0)
    pair = pair == lax.broadcasted_iota(jnp.int32, (rope, small), 1) + rank * small
    turned = jnp.dot(
        ropes[...], jnp.where(pair, 1.0, 0.0).astype(bf16), preferred_element_type=f32
    )
    own = jnp.concatenate([own_ref[step] for step in range(steps)], axis=0).astype(f32)
    scale = lax.rsqrt(jnp.mean(own * own, axis=-1, keepdims=True) + epsilon)
    own = (own * scale * gain_ref[...][None].astype(f32)).astype(bf16)
    depth = wt_ref.shape[1]
    for section in range(sections):
        normed[section] = own[:, section * depth : (section + 1) * depth]
    fresh = lax.dot_general(
        normed[lax.axis_index("section")],
        wt_ref[...],
        (((1,), (1,)), ((), ())),
        preferred_element_type=f32,
    )
    for source in range(experts):
        lines = [
            fresh[step * sources + source :, part * width : (part + 1) * width][:1]
            for step in range(steps)
            for part in range(experts)
        ]
        lines = jnp.concatenate(lines, axis=0).astype(bf16)
        for section in range(sections):
            index = source * sections + section
            at = slice(index * block, (index + 1) * block)
            value = jnp.concatenate([made[at, :chunk], turned[at]], axis=1)
            out_ref[index, :block, :] = value.astype(bf16)
            out_ref[index, block:, :] = lines


def absorb_queries(table, queries, w_uk, own, gain, w_turned, prompts, sections):
    experts = len(queries)
    steps, sources, heads, wide = queries[0].shape
    _, nope, chunk = w_uk.shape
    width = chunk + (wide - nope) // experts
    rows = prompts * steps * heads + steps * experts
    count = experts * sources * steps * heads
    held = pl.BlockSpec(memory_space=pltpu.VMEM)
    return pl.pallas_call(
        functools.partial(query_kernel, experts, sections, prompts, nope),
        out_shape=jax.ShapeDtypeStruct((experts * sections, rows, width), jnp.bfloat16),
        in_specs=[pl.BlockSpec(memory_space=pltpu.SMEM)] + [held] * (experts + 4),
        out_specs=held,
        scratch_shapes=[
            pltpu.VMEM((count, nope), jnp.float32),
            pltpu.VMEM((count, wide - nope), jnp.bfloat16),
            pltpu.VMEM((count, max(chunk, 128)), jnp.float32),
            pltpu.VMEM(
                (sections, own.shape[0] * own.shape[1], w_turned.shape[1]), jnp.bfloat16
            ),
            pltpu.VMEM((experts,) + queries[0].shape, jnp.bfloat16),
        ],
        compiler_params=params(*queries, w_uk, own, w_turned, scale=4),
        name="absorb_queries",
    )(table, *queries, w_uk, own, gain, w_turned)


def turn(values, cosine, sine):
    half = values.shape[1] // 2
    other = jnp.concatenate([values[:, half:], values[:, :half]], axis=1)
    return values * cosine + other * sine


def scaled(values, gain):
    scale = lax.rsqrt(jnp.mean(values * values, axis=-1, keepdims=True) + epsilon)
    return values * scale * gain.astype(jnp.float32)


def gather_kernel(
    prompts, experts, sections, sources, heads, steps, latent, length_ref, owner_ref, gain_ref,
    cosine_ref, sine_ref, block_ref, query_ref, query_rope_ref, recent_ref, recent_rope_ref,
    cosine_held, sine_held
):
    f32, bf16 = jnp.float32, jnp.bfloat16
    rows = steps * heads
    chunk = latent // experts
    first = lax.axis_index("expert") * sources + lax.axis_index("section") * prompts
    gain = gain_ref[...][None]
    for prompt in range(prompts):
        length, owner = length_ref[first + prompt], owner_ref[first + prompt]
        for step in range(steps):
            at = slice(step * heads, (step + 1) * heads)
            cosine_held[at, :] = jnp.broadcast_to(
                cosine_ref[pl.ds(length + step, 1), :], (heads, cosine_ref.shape[1])
            )
            sine_held[at, :] = jnp.broadcast_to(
                sine_ref[pl.ds(length + step, 1), :], (heads, sine_ref.shape[1])
            )
        cosine, sine = cosine_held[...], sine_held[...]
        at = slice(prompt * rows, (prompt + 1) * rows)
        for section in range(sections):
            pieces = [block_ref[i * sections + section, at, :] for i in range(experts)]
            to = slice(section * rows, (section + 1) * rows)
            query_ref[prompt, to, :] = jnp.concatenate(
                [piece[:, :chunk] for piece in pieces], axis=1
            )
            rope = jnp.concatenate([piece[:, chunk:].astype(f32) for piece in pieces], axis=1)
            query_rope_ref[prompt, to, :] = turn(rope, cosine, sine).astype(bf16)
        lines = 0
        for section in range(sections):
            lines = lines + block_ref[
                owner * sections + section, prompts * rows :, :
            ].astype(f32)
        recent, recent_rope = [], []
        for step in range(steps):
            line = jnp.concatenate(
                [lines[step * experts + part :][:1] for part in range(experts)], axis=1
            )
            recent.append(scaled(line[:, :latent], gain))
            at = slice(step * heads, step * heads + 1)
            recent_rope.append(turn(line[:, latent:], cosine[at], sine[at]))
        spare = recent_ref.shape[1] - steps
        recent.append(jnp.zeros((spare, latent), f32))
        recent_rope.append(jnp.zeros((spare, recent_rope[0].shape[1]), f32))
        recent_ref[prompt] = jnp.concatenate(recent, axis=0).astype(bf16)
        recent_rope_ref[prompt] = jnp.concatenate(recent_rope, axis=0).astype(bf16)


def gather_queries(blocks, lengths, owners, kv_gain, table, prompts, sources, experts, sections,
                   steps, heads):
    latent = kv_gain.shape[0]
    rope = blocks.shape[2] * experts - latent
    rows = sections * steps * heads
    spare = steps + -steps % 16
    shape = lambda *sizes: jax.ShapeDtypeStruct((prompts,) + sizes, jnp.bfloat16)
    held = pl.BlockSpec(memory_space=pltpu.VMEM)
    return pl.pallas_call(
        functools.partial(
            gather_kernel, prompts, experts, sections, sources, heads, steps, latent
        ),
        out_shape=[shape(rows, latent), shape(rows, rope), shape(spare, latent), shape(spare, rope)],
        in_specs=[pl.BlockSpec(memory_space=pltpu.SMEM)] * 2 + [held] * 4,
        out_specs=[held] * 4,
        scratch_shapes=[pltpu.VMEM((steps * heads, rope), jnp.float32)] * 2,
        compiler_params=params(blocks, scale=4),
        name="gather_queries",
    )(lengths, owners, kv_gain, *table, blocks)


def attend_kernel(parts, sections, sources, heads, steps, score_scale, *refs):
    part_refs = refs[:parts]
    (length_ref, gain_ref, cosine_ref, sine_ref, query_ref, query_rope_ref, recent_ref,
     recent_rope_ref) = refs[parts : parts + 8]
    out_refs, held = refs[parts + 8 : -1], refs[-1]
    f32, bf16 = jnp.float32, jnp.bfloat16
    nt = (((1,), (1,)), ((), ()))
    prompts, _, latent = query_ref.shape
    rows = steps * heads
    section_rank = lax.axis_index("section")
    first = lax.axis_index("expert") * sources + section_rank * prompts
    positions = part_refs[0].shape[0] // prompts
    for prompt in range(prompts):
        at = slice(prompt * positions, (prompt + 1) * positions)
        projected = part_refs[0][at].astype(f32)
        for ref in part_refs[1:]:
            projected = projected + ref[at].astype(f32)
        keys = scaled(projected[:, :latent], gain_ref[...][None]).astype(bf16)
        key_rope = turn(
            projected[:, latent:], cosine_ref[:positions], sine_ref[:positions]
        ).astype(bf16)
        query, query_rope = query_ref[prompt], query_rope_ref[prompt]
        recent, recent_rope = recent_ref[prompt], recent_rope_ref[prompt]
        scores = lax.dot_general(query, keys, nt, preferred_element_type=f32)
        scores = scores + lax.dot_general(query_rope, key_rope, nt, preferred_element_type=f32)
        fresh = lax.dot_general(query, recent, nt, preferred_element_type=f32)
        fresh = fresh + lax.dot_general(query_rope, recent_rope, nt, preferred_element_type=f32)
        place = lax.broadcasted_iota(jnp.int32, scores.shape, 1)
        scores = jnp.where(
            place < length_ref[first + prompt], scores * score_scale, masked_value
        )
        row = lax.broadcasted_iota(jnp.int32, (rows, fresh.shape[1]), 0)
        place = lax.broadcasted_iota(jnp.int32, (rows, fresh.shape[1]), 1)
        seen = jnp.where(place < 1, 1.0, 0.0)
        for step in range(1, steps):
            seen = jnp.where((place <= step) & (row >= step * heads), 1.0, seen)
        seen = jnp.concatenate([seen] * sections, axis=0)
        fresh = jnp.where(seen > 0.5, fresh * score_scale, masked_value)
        most = jnp.maximum(
            jnp.max(scores, axis=-1, keepdims=True), jnp.max(fresh, axis=-1, keepdims=True)
        )
        scores = jnp.exp(scores - most)
        fresh = jnp.exp(fresh - most)
        total = jnp.sum(scores, axis=-1, keepdims=True) + jnp.sum(fresh, axis=-1, keepdims=True)
        scores = (scores / total).astype(bf16)
        fresh = (fresh / total).astype(bf16)
        mixed = jnp.dot(scores, keys, preferred_element_type=f32)
        mixed = mixed + jnp.dot(fresh, recent, preferred_element_type=f32)
        mixed = mixed.astype(bf16)
        for section in range(sections):
            held[section] = mixed[section * rows : (section + 1) * rows]
        for mask, ref in enumerate(out_refs):
            ref[prompt * rows : (prompt + 1) * rows, :] = held[section_rank ^ mask]


def attend(parts, lengths, kv_gain, table, gathered, sources, steps, sections, score_scale):
    prompts, rows, latent = gathered[0].shape
    out = (rows // sections, latent)
    held = pl.BlockSpec(memory_space=pltpu.VMEM)
    return pl.pallas_call(
        functools.partial(
            attend_kernel, len(parts), sections, sources, out[0] // steps, steps, score_scale
        ),
        out_shape=[jax.ShapeDtypeStruct((prompts * out[0], latent), jnp.bfloat16)] * sections,
        in_specs=[held] * len(parts) + [pl.BlockSpec(memory_space=pltpu.SMEM)] + [held] * 7,
        out_specs=[held] * sections,
        scratch_shapes=[pltpu.VMEM((sections,) + out, jnp.bfloat16)],
        compiler_params=params(*parts, *gathered, scale=6),
        name="attend",
    )(*parts, lengths, kv_gain, *table, *gathered)


def value_kernel(experts, sections, heads, steps, sources, *refs):
    owner_ref = refs[0]
    latent_refs, uv_refs = refs[1 : 1 + sections], refs[1 + sections : 1 + sections + experts]
    out_ref, held = refs[1 + sections + experts :]
    f32, bf16 = jnp.float32, jnp.bfloat16
    chunk = uv_refs[0].shape[2]
    rows = latent_refs[0].shape[0]
    for mask, ref in enumerate(latent_refs):
        for index in range(experts):
            held[index, mask * rows : (mask + 1) * rows, :chunk] = ref[
                :, index * chunk : (index + 1) * chunk
            ].astype(f32)
    rank = lax.axis_index("expert")
    values = []
    for head in range(heads):
        at = pl.ds(head, sections * rows // heads, stride=heads)
        total = 0
        for mask, ref in enumerate(uv_refs):
            total = total + lax.dot_general(
                held[rank ^ mask, at, :][:, :chunk].astype(bf16),
                ref[head],
                (((1,), (1,)), ((), ())),
                preferred_element_type=f32,
            )
        values.append(total.astype(bf16))
    values = jnp.concatenate(values, axis=1)
    prompts = sources // sections
    section_rank = lax.axis_index("section")
    size = sources * steps
    to = lax.broadcasted_iota(jnp.int32, (size, size), 0)
    row = lax.broadcasted_iota(jnp.int32, (size, size), 1)
    order = jnp.zeros((size, size), f32)
    for mask in range(sections):
        for prompt in range(prompts):
            owner = owner_ref[
                rank * sources + (section_rank ^ mask) * prompts + prompt
            ]
            for step in range(steps):
                index = (mask * prompts + prompt) * steps + step
                order = jnp.where((row == index) & (to == owner * steps + step), 1.0, order)
    out_ref[...] = jnp.dot(order.astype(bf16), values, preferred_element_type=f32).astype(bf16)


def head_products(owners, latents, uv_parts, steps, sources):
    rows, width = latents[0].shape
    heads, value, _ = uv_parts[0].shape
    held = pl.BlockSpec(memory_space=pltpu.VMEM)
    total = rows * len(latents)
    return pl.pallas_call(
        functools.partial(
            value_kernel, len(uv_parts), len(latents), heads, steps, sources
        ),
        out_shape=jax.ShapeDtypeStruct((total // heads, heads * value), jnp.bfloat16),
        in_specs=[pl.BlockSpec(memory_space=pltpu.SMEM)]
        + [held] * (len(latents) + len(uv_parts)),
        out_specs=held,
        scratch_shapes=[
            pltpu.VMEM((len(uv_parts), total, max(width // len(uv_parts), 128)), jnp.float32)
        ],
        compiler_params=params(*latents, *uv_parts, scale=4),
        name="head_products",
    )(owners, *latents, *uv_parts)


def output_kernel(experts, *refs):
    value_refs = refs[:experts]
    weight_ref, out_ref = refs[experts:]
    values = jnp.concatenate([ref[...] for ref in value_refs], axis=0)
    rows = values.shape[0]
    to = lax.broadcasted_iota(jnp.int32, (rows, rows), 0)
    row = lax.broadcasted_iota(jnp.int32, (rows, rows), 1)
    source = (to & (experts - 1)) ^ lax.axis_index("expert")
    rest = lax.shift_right_logical(to, experts.bit_length() - 1)
    order = jnp.where(row == source * (rows // experts) + rest, 1.0, 0.0).astype(jnp.bfloat16)
    values = jnp.dot(order, values, preferred_element_type=jnp.float32).astype(jnp.bfloat16)
    out_ref[...] = jnp.dot(
        values, weight_ref[...], preferred_element_type=jnp.float32
    ).astype(out_ref.dtype)


def output_product(values, weight):
    rows = sum(value.shape[0] for value in values)
    held = pl.BlockSpec(memory_space=pltpu.VMEM)
    return pl.pallas_call(
        functools.partial(output_kernel, len(values)),
        out_shape=jax.ShapeDtypeStruct((rows, weight.shape[1]), jnp.bfloat16),
        in_specs=[held] * (len(values) + 1),
        out_specs=held,
        compiler_params=params(*values, scale=8),
        name="output_product",
    )(*values, weight)


def expert_kernel(experts, sections, picks, *refs):
    attended_refs, own_refs = refs[:experts], refs[experts : 2 * experts]
    gain_ref, gate_ref, up_ref, down_ref, out_ref, near_ref, columns = refs[2 * experts :]
    f32, bf16 = jnp.float32, jnp.bfloat16
    count = gate_ref.shape[0]
    rank, section_rank = lax.axis_index("expert"), lax.axis_index("section")
    width = gain_ref.shape[0]
    steps, sources, _ = own_refs[0].shape
    block = steps * sources
    for mask, ref in enumerate(attended_refs):
        columns[rank ^ mask] = ref[...]
    attended, hidden, route = [], [], []
    for mask, ref in enumerate(own_refs):
        attended.append(
            jnp.concatenate([columns[i, rank ^ mask] for i in range(experts)], axis=1).astype(f32)
        )
        own = jnp.concatenate([ref[step] for step in range(steps)], axis=0).astype(f32)
        hidden.append(own[:, :width])
        route.append(own[:, width:])
    near = attended[0]
    mixed = jnp.concatenate(hidden, axis=0) + jnp.concatenate(attended, axis=0)
    route = jnp.concatenate(route, axis=0)
    named = route[:, :picks]
    weights = route[:, picks : 2 * picks] + route[:, 2 * picks :]
    weights = route_scale * weights / jnp.sum(weights, axis=-1, keepdims=True)
    scale = lax.rsqrt(jnp.mean(mixed * mixed, axis=-1, keepdims=True) + epsilon)
    rows_in = (mixed * scale * gain_ref[...][None].astype(f32)).astype(bf16)
    column = width // sections
    total = 0
    for x in range(count):
        mine = (rank * count + x).astype(f32)
        weight = jnp.sum(jnp.where(named == mine, weights, 0.0), axis=-1, keepdims=True)
        gate = jnp.dot(rows_in, gate_ref[x], preferred_element_type=f32)
        up = jnp.dot(rows_in, up_ref[x], preferred_element_type=f32)
        inner = gate / (1.0 + jnp.exp(-gate)) * up * weight
        total = total + jnp.dot(inner.astype(bf16), down_ref[x], preferred_element_type=f32)
    for section in range(sections):
        at = slice(section * column, (section + 1) * column)
        near_ref[section] = near[:, at].astype(bf16)
        for mask in range(experts):
            out_ref[(rank ^ mask) * sections + section] = total[
                mask * block : (mask + 1) * block, at
            ].astype(bf16)


def run_experts(attended, own, gain, w_gate, w_up, w_down, picks, sections):
    experts = len(own)
    width = gain.shape[0]
    block = (own[0].shape[0] * own[0].shape[1], width // sections)
    held = pl.BlockSpec(memory_space=pltpu.VMEM)
    return pl.pallas_call(
        functools.partial(expert_kernel, experts, sections, picks),
        out_shape=[
            jax.ShapeDtypeStruct((experts * sections,) + block, jnp.bfloat16),
            jax.ShapeDtypeStruct((sections,) + block, jnp.bfloat16),
        ],
        in_specs=[held] * (2 * experts + 4),
        out_specs=[held] * 2,
        scratch_shapes=[pltpu.VMEM((experts,) + attended[0].shape, jnp.bfloat16)],
        compiler_params=params(*attended, *own, scale=16),
        name="run_experts",
    )(*attended, *own, gain, w_gate, w_up, w_down)


def finish_kernel(block_ref, near_ref, base_ref, out_ref):
    f32 = jnp.float32
    steps, sources, _ = out_ref.shape
    total = near_ref[lax.axis_index("section")].astype(f32)
    for index in range(block_ref.shape[0]):
        total = total + block_ref[index].astype(f32)
    for step in range(steps):
        value = base_ref[step].astype(f32) + total[step * sources : (step + 1) * sources]
        out_ref[step] = value.astype(out_ref.dtype)


def finish(blocks, near, base):
    held = pl.BlockSpec(memory_space=pltpu.VMEM)
    return pl.pallas_call(
        finish_kernel,
        out_shape=jax.ShapeDtypeStruct(base.shape, base.dtype),
        in_specs=[held] * 3,
        out_specs=held,
        compiler_params=params(blocks, near, base, scale=4),
        name="finish",
    )(blocks, near, base)


def local(
    prompts,
    owners,
    lengths,
    residual,
    queries,
    expert_ids,
    route_scores,
    attn_gain,
    w_dkv,
    kv_gain,
    w_uk,
    w_uv,
    w_o,
    moe_gain,
    w_gate,
    w_up,
    w_down,
):
    bf16, f32 = jnp.bfloat16, jnp.float32
    expert_rank = lax.axis_index("expert")
    section_rank = lax.axis_index("section")
    group_rank = lax.axis_index("groups")
    experts = lax.axis_size("expert")
    sections = lax.axis_size("section")
    groups = lax.axis_size("groups")
    prompt_count, full_length, width = prompts.shape
    steps, tokens_here, heads, _ = queries.shape
    depth = w_dkv.shape[0]
    piece = depth // (groups * experts)
    latent = kv_gain.shape[0]
    cache_width = w_dkv.shape[1]
    rows = prompt_count * full_length
    own_rows = steps * tokens_here

    w_turned = w_dkv.T

    def w_piece(group):
        return lax.dynamic_slice_in_dim(
            w_turned, (expert_rank * groups + group) * piece, piece, 1
        )

    halves = spread(w_piece(group_rank), "section")
    queries_all = spread(queries, "expert")
    cut = list(cut_columns(prompts.reshape(rows, width), sections, experts))
    cut = deliver(cut, "expert")
    queries_all[0], *rest = lax.optimization_barrier((queries_all[0], *cut[1:], *halves[1:]))
    cut = cut[:1] + rest[: experts - 1]
    halves = halves[:1] + rest[experts - 1 :]
    w_parts = halves[:1] + [w_piece(group_rank ^ other) for other in range(1, groups)]
    for half in halves[1:]:
        w_parts += spread(half, "groups")

    blocks = absorb_queries(
        owners, queries_all, w_uk, residual, attn_gain, w_turned, prompt_count, sections
    )
    blocks = lax.all_to_all(blocks, ("expert", "section"), 0, 0, tiled=True)

    high = route_scores.astype(bf16)
    low = (route_scores - high.astype(f32)).astype(bf16)
    packed = jnp.concatenate([residual, expert_ids.astype(bf16), high, low], axis=2)
    w_uv, packed, cut[1] = lax.optimization_barrier((w_uv, packed, cut[1]))
    uv_parts = doubled(w_uv, "expert")
    packed = spread(packed, "expert")

    away = list(project(cut[1:], w_parts, sections, groups))
    near = list(project(cut[:1], w_parts, sections, groups))
    parts = deliver(near + away, "expert")
    table = rotation(full_length + steps + -(full_length + steps) % 8, cache_width - latent)
    gathered = list(gather_queries(
        blocks, lengths, owners, kv_gain, table, prompt_count, tokens_here, experts, sections,
        steps, heads
    ))
    gathered[0], *rest = lax.optimization_barrier((gathered[0], *uv_parts, *packed))
    uv_parts, packed = rest[:experts], rest[experts:]
    out_latent = attend(
        parts, lengths, kv_gain, table, gathered, tokens_here, steps, sections,
        queries.shape[-1] ** (-0.5),
    )

    out_latent = deliver(out_latent, "section")
    head_values = head_products(owners, out_latent, uv_parts, steps, tokens_here)
    head_values = spread(head_values, "expert")

    (w_o,) = fetch(w_o)
    (w_gate,) = fetch(w_gate)
    (w_up,) = fetch(w_up)
    (w_down,) = fetch(w_down)
    attended = output_product(head_values, w_o)
    attended = sum(part.astype(f32) for part in spread(attended, "section")).astype(bf16)
    attended = attended.reshape(experts, own_rows, -1)
    blocks, near = run_experts(
        spread(attended, "expert"),
        packed,
        moe_gain,
        w_gate,
        w_up,
        w_down,
        expert_ids.shape[2],
        sections,
    )
    blocks = lax.all_to_all(blocks, ("expert", "section"), 0, 0, tiled=True)
    column = width // sections
    base = lax.dynamic_slice_in_dim(residual, section_rank * column, column, 2)
    return finish(blocks, near, base)


def solution(mesh):
    placed = (
        P(("groups", "expert", "section"), None, None),
        P("groups"),
        P("groups"),
        P(None, ("groups", "expert"), None),
        P(None, ("groups", "expert"), "section", None),
        P(None, ("groups", "expert"), None),
        P(None, ("groups", "expert"), None),
        P(),
        P("section", None),
        P(),
        P("section", None, "expert"),
        P("section", None, "expert"),
        P("section", "expert"),
        P(),
        P("expert", None, "section"),
        P("expert", None, "section"),
        P("expert", "section", None),
    )
    return jax.shard_map(
        local,
        mesh=mesh,
        in_specs=placed,
        out_specs=P(None, ("groups", "expert"), "section"),
        check_vma=False,
    )
```

```python
import functools
import math

import jax
import jax.numpy as jnp
import numpy as np
from jax import lax
from jax.experimental import pallas as pl
from jax.experimental.pallas import tpu as pltpu
from jax.sharding import PartitionSpec as P

epsilon = 1e-06
masked_value = -1e30
route_scale = 2.5


def rotation(positions, width):
    halfway = width // 2
    frequency = 10000.0 ** (-2.0 * np.arange(halfway) / width)
    angles = np.arange(positions)[:, None] * frequency
    cosine = np.concatenate([np.cos(angles), np.cos(angles)], axis=1)
    sine = np.concatenate([-np.sin(angles), np.sin(angles)], axis=1)
    return jnp.asarray(cosine, jnp.float32), jnp.asarray(sine, jnp.float32)


def swap(block, axis, mask):
    size = lax.axis_size(axis)
    return lax.ppermute(block, axis, [(i, i ^ mask) for i in range(size)])


def deliver(blocks, axis):
    return [blocks[0]] + [swap(blocks[mask], axis, mask) for mask in range(1, len(blocks))]


def spread(block, axis):
    return [block] + [swap(block, axis, mask) for mask in range(1, lax.axis_size(axis))]


def params(*arrays, scale=1):
    held = sum(math.prod(array.shape) * array.dtype.itemsize for array in arrays)
    mebibytes = min(56, 4 + scale * held // 1024 // 1024)
    return pltpu.CompilerParams(vmem_limit_bytes=mebibytes * 1024 * 1024)


def at_home(*arrays):
    return [pltpu.with_memory_space_constraint(array, pltpu.HBM) for array in arrays]


def fetch_kernel(count, *refs):
    out_refs, sems = refs[-1 - count : -1], refs[-1]
    copies = [
        pltpu.make_async_copy(refs[index], out_refs[index], sems.at[index])
        for index in range(count)
    ]
    for copy in copies:
        copy.start()
    for copy in copies:
        copy.wait()


def fetch(arrays, after):
    size = sum(array.size * array.dtype.itemsize for array in arrays)
    return pl.pallas_call(
        functools.partial(fetch_kernel, len(arrays)),
        out_shape=[pltpu.VMEM(array.shape, array.dtype) for array in arrays],
        in_specs=[pl.BlockSpec(memory_space=pltpu.HBM)] * len(arrays)
        + [pl.BlockSpec(memory_space=pl.ANY)] * len(after),
        out_specs=[pl.BlockSpec(memory_space=pltpu.VMEM)] * len(arrays),
        scratch_shapes=[pltpu.SemaphoreType.DMA((len(arrays),))],
        compiler_params=pltpu.CompilerParams(vmem_limit_bytes=1024 * 1024),
        cost_estimate=pl.CostEstimate(flops=0, bytes_accessed=2 * size, transcendentals=0),
        name="fetch",
    )(*at_home(*arrays), *after)


def doubled(block, axis):
    held = {0: block}
    size = lax.axis_size(axis)
    masks = [1 << bit for bit in range(size.bit_length() - 1)]
    for mask in masks[1:] + masks[:1]:
        for other in list(held):
            held[other ^ mask] = swap(held[other], axis, mask)
    return [held[mask] for mask in range(size)]


def cut_kernel(sections, experts, piece, x_ref, *refs):
    out_refs, held = refs[:experts], refs[experts]
    rank = lax.axis_index("expert")
    for target in range(experts):
        for section in range(sections):
            at = (section * experts + target) * piece
            held[target, section] = x_ref[:, at : at + piece]
    for mask, ref in enumerate(out_refs):
        ref[...] = held[rank ^ mask]


def cut_columns(x, sections, experts):
    rows, width = x.shape
    piece = width // (sections * experts)
    block = jax.ShapeDtypeStruct((sections, rows, piece), x.dtype)
    return pl.pallas_call(
        functools.partial(cut_kernel, sections, experts, piece),
        out_shape=[block] * experts,
        scratch_shapes=[pltpu.VMEM((experts,) + block.shape, x.dtype)],
        compiler_params=params(x, scale=6),
        name="cut_columns",
    )(*at_home(x))


def project_kernel(count, sections, groups, *refs):
    x_refs = refs[:count]
    w_refs = refs[count : count + sections * groups]
    out_refs = refs[count + sections * groups :]
    section_rank = lax.axis_index("section")
    group_rank = lax.axis_index("groups")
    rows = x_refs[0].shape[1]
    total = 0
    for mask in range(sections):
        held = [w_refs[mask * groups + other][...] for other in range(groups)]
        columns = []
        for group in range(groups):
            chosen = held[0]
            for other in range(1, groups):
                chosen = jnp.where((group_rank ^ other) == group, held[other], chosen)
            columns.append(chosen)
        weights = jnp.concatenate(columns, axis=1)
        x = jnp.concatenate([ref[section_rank ^ mask] for ref in x_refs], axis=0)
        total = total + lax.dot_general(
            x, weights, (((1,), (1,)), ((), ())), preferred_element_type=jnp.float32
        )
    for index, ref in enumerate(out_refs):
        ref[...] = total[index * rows : (index + 1) * rows].astype(ref.dtype)


def project(blocks, w_parts, sections, groups):
    out = jax.ShapeDtypeStruct((blocks[0].shape[1], w_parts[0].shape[0]), jnp.bfloat16)
    return pl.pallas_call(
        functools.partial(project_kernel, len(blocks), sections, groups),
        out_shape=[out] * len(blocks),
        compiler_params=params(*blocks, *w_parts, scale=6),
        name="project",
    )(*blocks, *w_parts)


def query_kernel(
    experts, sections, prompts, nope, *refs
):
    f32, bf16 = jnp.float32, jnp.bfloat16
    table_ref, query_refs = refs[0], refs[1 : 1 + experts]
    uk_ref, own_ref, gain_ref, wt_ref = refs[1 + experts : 5 + experts]
    out_ref, token_ref, picked, ropes, made, normed, query_ref = refs[-7:]
    token_ref[...] = jnp.zeros_like(token_ref)
    steps, sources, heads, wide = query_refs[0].shape
    rope = wide - nope
    chunk = uk_ref.shape[2]
    width = out_ref.shape[2]
    count = experts * sources
    block = prompts * steps * heads
    rank = lax.axis_index("expert")

    for mask, ref in enumerate(query_refs):
        query_ref[rank ^ mask] = ref[...]

    def pick(index, carry):
        owner = table_ref[index]
        for step in range(steps):
            value = query_ref[owner, step, index // sources].astype(f32)
            at = pl.ds(pl.multiple_of((index * steps + step) * heads, heads), heads)
            picked[at, :] = value[:, :nope]
            ropes[at, :] = value[:, nope:].astype(bf16)
        return carry

    if count <= 16:
        for index in range(count):
            pick(index, 0)
    else:
        lax.fori_loop(0, count, pick, 0)
    for head in range(heads):
        at = pl.ds(head, count * steps, stride=heads)
        value = jnp.dot(picked[at, :].astype(bf16), uk_ref[head], preferred_element_type=f32)
        if chunk < made.shape[1]:
            spare = jnp.zeros((count * steps, made.shape[1] - chunk), f32)
            value = jnp.concatenate([value, spare], axis=1)
        made[at, :] = value
    small = width - chunk
    pair = lax.broadcasted_iota(jnp.int32, (rope, small), 0)
    pair = pair == lax.broadcasted_iota(jnp.int32, (rope, small), 1) + rank * small
    turned = jnp.dot(
        ropes[...], jnp.where(pair, 1.0, 0.0).astype(bf16), preferred_element_type=f32
    )
    own = jnp.concatenate([own_ref[step] for step in range(steps)], axis=0).astype(f32)
    scale = lax.rsqrt(jnp.mean(own * own, axis=-1, keepdims=True) + epsilon)
    own = (own * scale * gain_ref[...][None].astype(f32)).astype(bf16)
    depth = wt_ref.shape[1]
    for section in range(sections):
        normed[section] = own[:, section * depth : (section + 1) * depth]
    fresh = lax.dot_general(
        normed[lax.axis_index("section")],
        wt_ref[...],
        (((1,), (1,)), ((), ())),
        preferred_element_type=f32,
    )
    for source in range(experts):
        lines = [
            fresh[step * sources + source :, part * width : (part + 1) * width][:1]
            for step in range(steps)
            for part in range(experts)
        ]
        lines = jnp.concatenate(lines, axis=0).astype(bf16)
        for section in range(sections):
            index = source * sections + section
            at = slice(index * block, (index + 1) * block)
            value = jnp.concatenate([made[at, :chunk], turned[at]], axis=1)
            out_ref[index, :block, :] = value.astype(bf16)
            out_ref[index, block:, :] = lines


def absorb_queries(table, queries, w_uk, own, gain, w_turned, prompts, sections, after):
    experts = len(queries)
    steps, sources, heads, wide = queries[0].shape
    _, nope, chunk = w_uk.shape
    width = chunk + (wide - nope) // experts
    rows = prompts * steps * heads + steps * experts
    count = experts * sources * steps * heads
    held = pl.BlockSpec(memory_space=pltpu.VMEM)
    return pl.pallas_call(
        functools.partial(query_kernel, experts, sections, prompts, nope),
        out_shape=[
            jax.ShapeDtypeStruct((experts * sections, rows, width), jnp.bfloat16),
            jax.ShapeDtypeStruct((8, 128), jnp.bfloat16),
        ],
        in_specs=[pl.BlockSpec(memory_space=pltpu.SMEM)]
        + [held] * (experts + 4)
        + [pl.BlockSpec(memory_space=pl.ANY)] * len(after),
        out_specs=[held] * 2,
        scratch_shapes=[
            pltpu.VMEM((count, nope), jnp.float32),
            pltpu.VMEM((count, wide - nope), jnp.bfloat16),
            pltpu.VMEM((count, max(chunk, 128)), jnp.float32),
            pltpu.VMEM(
                (sections, own.shape[0] * own.shape[1], w_turned.shape[1]), jnp.bfloat16
            ),
            pltpu.VMEM((experts,) + queries[0].shape, jnp.bfloat16),
        ],
        compiler_params=params(*queries, w_uk, own, w_turned, scale=4),
        name="absorb_queries",
    )(table, *queries, *at_home(w_uk, own, gain, w_turned), *after)


def turn(values, cosine, sine):
    half = values.shape[1] // 2
    other = jnp.concatenate([values[:, half:], values[:, :half]], axis=1)
    return values * cosine + other * sine


def scaled(values, gain):
    scale = lax.rsqrt(jnp.mean(values * values, axis=-1, keepdims=True) + epsilon)
    return values * scale * gain.astype(jnp.float32)


def gather_kernel(
    prompts, experts, sections, sources, heads, steps, latent, length_ref, owner_ref, gain_ref,
    cosine_ref, sine_ref, block_ref, query_ref, query_rope_ref, recent_ref, recent_rope_ref,
    cosine_held, sine_held
):
    f32, bf16 = jnp.float32, jnp.bfloat16
    rows = steps * heads
    chunk = latent // experts
    first = lax.axis_index("expert") * sources + lax.axis_index("section") * prompts
    gain = gain_ref[...][None]
    for prompt in range(prompts):
        length, owner = length_ref[first + prompt], owner_ref[first + prompt]
        for step in range(steps):
            at = slice(step * heads, (step + 1) * heads)
            cosine_held[at, :] = jnp.broadcast_to(
                cosine_ref[pl.ds(length + step, 1), :], (heads, cosine_ref.shape[1])
            )
            sine_held[at, :] = jnp.broadcast_to(
                sine_ref[pl.ds(length + step, 1), :], (heads, sine_ref.shape[1])
            )
        cosine, sine = cosine_held[...], sine_held[...]
        at = slice(prompt * rows, (prompt + 1) * rows)
        for section in range(sections):
            pieces = [block_ref[i * sections + section, at, :] for i in range(experts)]
            to = slice(section * rows, (section + 1) * rows)
            query_ref[prompt, to, :] = jnp.concatenate(
                [piece[:, :chunk] for piece in pieces], axis=1
            )
            rope = jnp.concatenate([piece[:, chunk:].astype(f32) for piece in pieces], axis=1)
            query_rope_ref[prompt, to, :] = turn(rope, cosine, sine).astype(bf16)
        lines = 0
        for section in range(sections):
            lines = lines + block_ref[
                owner * sections + section, prompts * rows :, :
            ].astype(f32)
        recent, recent_rope = [], []
        for step in range(steps):
            line = jnp.concatenate(
                [lines[step * experts + part :][:1] for part in range(experts)], axis=1
            )
            recent.append(scaled(line[:, :latent], gain))
            at = slice(step * heads, step * heads + 1)
            recent_rope.append(turn(line[:, latent:], cosine[at], sine[at]))
        spare = recent_ref.shape[1] - steps
        recent.append(jnp.zeros((spare, latent), f32))
        recent_rope.append(jnp.zeros((spare, recent_rope[0].shape[1]), f32))
        recent_ref[prompt] = jnp.concatenate(recent, axis=0).astype(bf16)
        recent_rope_ref[prompt] = jnp.concatenate(recent_rope, axis=0).astype(bf16)


def gather_queries(blocks, lengths, owners, kv_gain, table, prompts, sources, experts, sections,
                   steps, heads):
    latent = kv_gain.shape[0]
    rope = blocks.shape[2] * experts - latent
    rows = sections * steps * heads
    spare = steps + -steps % 16
    shape = lambda *sizes: jax.ShapeDtypeStruct((prompts,) + sizes, jnp.bfloat16)
    held = pl.BlockSpec(memory_space=pltpu.VMEM)
    return pl.pallas_call(
        functools.partial(
            gather_kernel, prompts, experts, sections, sources, heads, steps, latent
        ),
        out_shape=[shape(rows, latent), shape(rows, rope), shape(spare, latent), shape(spare, rope)],
        in_specs=[pl.BlockSpec(memory_space=pltpu.SMEM)] * 2 + [held] * 4,
        out_specs=[held] * 4,
        scratch_shapes=[pltpu.VMEM((steps * heads, rope), jnp.float32)] * 2,
        compiler_params=params(blocks, scale=4),
        name="gather_queries",
    )(lengths, owners, *at_home(kv_gain, *table), blocks)


def attend_kernel(parts, sections, sources, heads, steps, score_scale, *refs):
    part_refs = refs[:parts]
    (length_ref, gain_ref, cosine_ref, sine_ref, query_ref, query_rope_ref, recent_ref,
     recent_rope_ref) = refs[parts : parts + 8]
    out_refs, held = refs[-1 - sections : -1], refs[-1]
    f32, bf16 = jnp.float32, jnp.bfloat16
    nt = (((1,), (1,)), ((), ()))
    prompts, _, latent = query_ref.shape
    rows = steps * heads
    section_rank = lax.axis_index("section")
    first = lax.axis_index("expert") * sources + section_rank * prompts
    positions = part_refs[0].shape[0] // prompts
    for prompt in range(prompts):
        at = slice(prompt * positions, (prompt + 1) * positions)
        projected = part_refs[0][at].astype(f32)
        for ref in part_refs[1:]:
            projected = projected + ref[at].astype(f32)
        keys = scaled(projected[:, :latent], gain_ref[...][None]).astype(bf16)
        key_rope = turn(
            projected[:, latent:], cosine_ref[:positions], sine_ref[:positions]
        ).astype(bf16)
        query, query_rope = query_ref[prompt], query_rope_ref[prompt]
        recent, recent_rope = recent_ref[prompt], recent_rope_ref[prompt]
        scores = lax.dot_general(query, keys, nt, preferred_element_type=f32)
        scores = scores + lax.dot_general(query_rope, key_rope, nt, preferred_element_type=f32)
        fresh = lax.dot_general(query, recent, nt, preferred_element_type=f32)
        fresh = fresh + lax.dot_general(query_rope, recent_rope, nt, preferred_element_type=f32)
        place = lax.broadcasted_iota(jnp.int32, scores.shape, 1)
        scores = jnp.where(
            place < length_ref[first + prompt], scores * score_scale, masked_value
        )
        row = lax.broadcasted_iota(jnp.int32, (rows, fresh.shape[1]), 0)
        place = lax.broadcasted_iota(jnp.int32, (rows, fresh.shape[1]), 1)
        seen = jnp.where(place < 1, 1.0, 0.0)
        for step in range(1, steps):
            seen = jnp.where((place <= step) & (row >= step * heads), 1.0, seen)
        seen = jnp.concatenate([seen] * sections, axis=0)
        fresh = jnp.where(seen > 0.5, fresh * score_scale, masked_value)
        most = jnp.maximum(
            jnp.max(scores, axis=-1, keepdims=True), jnp.max(fresh, axis=-1, keepdims=True)
        )
        scores = jnp.exp(scores - most)
        fresh = jnp.exp(fresh - most)
        total = jnp.sum(scores, axis=-1, keepdims=True) + jnp.sum(fresh, axis=-1, keepdims=True)
        scores = (scores / total).astype(bf16)
        fresh = (fresh / total).astype(bf16)
        mixed = jnp.dot(scores, keys, preferred_element_type=f32)
        mixed = mixed + jnp.dot(fresh, recent, preferred_element_type=f32)
        mixed = mixed.astype(bf16)
        for section in range(sections):
            held[section] = mixed[section * rows : (section + 1) * rows]
        for mask, ref in enumerate(out_refs):
            ref[prompt * rows : (prompt + 1) * rows, :] = held[section_rank ^ mask]


def attend(
    parts, lengths, kv_gain, table, gathered, sources, steps, sections, score_scale, after
):
    prompts, rows, latent = gathered[0].shape
    out = (rows // sections, latent)
    held = pl.BlockSpec(memory_space=pltpu.VMEM)
    return pl.pallas_call(
        functools.partial(
            attend_kernel, len(parts), sections, sources, out[0] // steps, steps, score_scale
        ),
        out_shape=[jax.ShapeDtypeStruct((prompts * out[0], latent), jnp.bfloat16)] * sections,
        in_specs=[held] * len(parts)
        + [pl.BlockSpec(memory_space=pltpu.SMEM)]
        + [held] * 7
        + [pl.BlockSpec(memory_space=pl.ANY)] * len(after),
        out_specs=[held] * sections,
        scratch_shapes=[pltpu.VMEM((sections,) + out, jnp.bfloat16)],
        compiler_params=params(*parts, *gathered, scale=6),
        name="attend",
    )(*parts, lengths, *at_home(kv_gain, *table), *gathered, *after)


def value_kernel(experts, sections, heads, steps, sources, *refs):
    owner_ref = refs[0]
    latent_refs, uv_refs = refs[1 : 1 + sections], refs[1 + sections : 1 + sections + experts]
    out_ref, held = refs[1 + sections + experts :]
    f32, bf16 = jnp.float32, jnp.bfloat16
    chunk = uv_refs[0].shape[2]
    rows = latent_refs[0].shape[0]
    for mask, ref in enumerate(latent_refs):
        for index in range(experts):
            held[index, mask * rows : (mask + 1) * rows, :chunk] = ref[
                :, index * chunk : (index + 1) * chunk
            ].astype(f32)
    rank = lax.axis_index("expert")
    values = []
    for head in range(heads):
        at = pl.ds(head, sections * rows // heads, stride=heads)
        total = 0
        for mask, ref in enumerate(uv_refs):
            total = total + lax.dot_general(
                held[rank ^ mask, at, :][:, :chunk].astype(bf16),
                ref[head],
                (((1,), (1,)), ((), ())),
                preferred_element_type=f32,
            )
        values.append(total.astype(bf16))
    values = jnp.concatenate(values, axis=1)
    prompts = sources // sections
    section_rank = lax.axis_index("section")
    size = sources * steps
    to = lax.broadcasted_iota(jnp.int32, (size, size), 0)
    row = lax.broadcasted_iota(jnp.int32, (size, size), 1)
    order = jnp.zeros((size, size), f32)
    for mask in range(sections):
        for prompt in range(prompts):
            owner = owner_ref[
                rank * sources + (section_rank ^ mask) * prompts + prompt
            ]
            for step in range(steps):
                index = (mask * prompts + prompt) * steps + step
                order = jnp.where((row == index) & (to == owner * steps + step), 1.0, order)
    out_ref[...] = jnp.dot(order.astype(bf16), values, preferred_element_type=f32).astype(bf16)


def head_products(owners, latents, uv_parts, steps, sources):
    rows, width = latents[0].shape
    heads, value, _ = uv_parts[0].shape
    held = pl.BlockSpec(memory_space=pltpu.VMEM)
    total = rows * len(latents)
    return pl.pallas_call(
        functools.partial(
            value_kernel, len(uv_parts), len(latents), heads, steps, sources
        ),
        out_shape=jax.ShapeDtypeStruct((total // heads, heads * value), jnp.bfloat16),
        in_specs=[pl.BlockSpec(memory_space=pltpu.SMEM)]
        + [held] * (len(latents) + len(uv_parts)),
        out_specs=held,
        scratch_shapes=[
            pltpu.VMEM((len(uv_parts), total, max(width // len(uv_parts), 128)), jnp.float32)
        ],
        compiler_params=params(*latents, *uv_parts, scale=4),
        name="head_products",
    )(owners, *latents, *uv_parts)


def output_kernel(experts, *refs):
    value_refs = refs[:experts]
    weight_ref, out_ref = refs[experts:]
    values = jnp.concatenate([ref[...] for ref in value_refs], axis=0)
    rows = values.shape[0]
    to = lax.broadcasted_iota(jnp.int32, (rows, rows), 0)
    row = lax.broadcasted_iota(jnp.int32, (rows, rows), 1)
    source = (to & (experts - 1)) ^ lax.axis_index("expert")
    rest = lax.shift_right_logical(to, experts.bit_length() - 1)
    order = jnp.where(row == source * (rows // experts) + rest, 1.0, 0.0).astype(jnp.bfloat16)
    values = jnp.dot(order, values, preferred_element_type=jnp.float32).astype(jnp.bfloat16)
    out_ref[...] = jnp.dot(
        values, weight_ref[...], preferred_element_type=jnp.float32
    ).astype(out_ref.dtype)


def output_product(values, weight):
    rows = sum(value.shape[0] for value in values)
    held = pl.BlockSpec(memory_space=pltpu.VMEM)
    return pl.pallas_call(
        functools.partial(output_kernel, len(values)),
        out_shape=jax.ShapeDtypeStruct((rows, weight.shape[1]), jnp.bfloat16),
        in_specs=[held] * (len(values) + 1),
        out_specs=held,
        compiler_params=params(*values, scale=8),
        name="output_product",
    )(*values, weight)


def expert_kernel(experts, sections, picks, *refs):
    attended_refs, own_refs = refs[:experts], refs[experts : 2 * experts]
    gain_ref, gate_ref, up_ref, down_ref, out_ref, near_ref, columns = refs[2 * experts :]
    f32, bf16 = jnp.float32, jnp.bfloat16
    count = gate_ref.shape[0]
    rank, section_rank = lax.axis_index("expert"), lax.axis_index("section")
    width = gain_ref.shape[0]
    steps, sources, _ = own_refs[0].shape
    block = steps * sources
    for mask, ref in enumerate(attended_refs):
        columns[rank ^ mask] = ref[...]
    attended, hidden, route = [], [], []
    for mask, ref in enumerate(own_refs):
        attended.append(
            jnp.concatenate([columns[i, rank ^ mask] for i in range(experts)], axis=1).astype(f32)
        )
        own = jnp.concatenate([ref[step] for step in range(steps)], axis=0).astype(f32)
        hidden.append(own[:, :width])
        route.append(own[:, width:])
    near = attended[0]
    mixed = jnp.concatenate(hidden, axis=0) + jnp.concatenate(attended, axis=0)
    route = jnp.concatenate(route, axis=0)
    named = route[:, :picks]
    weights = route[:, picks : 2 * picks] + route[:, 2 * picks :]
    weights = route_scale * weights / jnp.sum(weights, axis=-1, keepdims=True)
    scale = lax.rsqrt(jnp.mean(mixed * mixed, axis=-1, keepdims=True) + epsilon)
    rows_in = (mixed * scale * gain_ref[...][None].astype(f32)).astype(bf16)
    column = width // sections
    total = 0
    for x in range(count):
        mine = (rank * count + x).astype(f32)
        weight = jnp.sum(jnp.where(named == mine, weights, 0.0), axis=-1, keepdims=True)
        gate = jnp.dot(rows_in, gate_ref[x], preferred_element_type=f32)
        up = jnp.dot(rows_in, up_ref[x], preferred_element_type=f32)
        inner = gate / (1.0 + jnp.exp(-gate)) * up * weight
        total = total + jnp.dot(inner.astype(bf16), down_ref[x], preferred_element_type=f32)
    for section in range(sections):
        at = slice(section * column, (section + 1) * column)
        near_ref[section] = near[:, at].astype(bf16)
        for mask in range(experts):
            out_ref[(rank ^ mask) * sections + section] = total[
                mask * block : (mask + 1) * block, at
            ].astype(bf16)


def run_experts(attended, own, gain, w_gate, w_up, w_down, picks, sections):
    experts = len(own)
    width = gain.shape[0]
    block = (own[0].shape[0] * own[0].shape[1], width // sections)
    held = pl.BlockSpec(memory_space=pltpu.VMEM)
    return pl.pallas_call(
        functools.partial(expert_kernel, experts, sections, picks),
        out_shape=[
            jax.ShapeDtypeStruct((experts * sections,) + block, jnp.bfloat16),
            jax.ShapeDtypeStruct((sections,) + block, jnp.bfloat16),
        ],
        in_specs=[held] * (2 * experts + 4),
        out_specs=[held] * 2,
        scratch_shapes=[pltpu.VMEM((experts,) + attended[0].shape, jnp.bfloat16)],
        compiler_params=params(*attended, *own, scale=16),
        name="run_experts",
    )(*attended, *own, *at_home(gain), w_gate, w_up, w_down)


def finish_kernel(block_ref, near_ref, base_ref, out_ref):
    f32 = jnp.float32
    steps, sources, _ = out_ref.shape
    total = near_ref[lax.axis_index("section")].astype(f32)
    for index in range(block_ref.shape[0]):
        total = total + block_ref[index].astype(f32)
    for step in range(steps):
        value = base_ref[step].astype(f32) + total[step * sources : (step + 1) * sources]
        out_ref[step] = value.astype(out_ref.dtype)


def finish(blocks, near, base):
    held = pl.BlockSpec(memory_space=pltpu.VMEM)
    return pl.pallas_call(
        finish_kernel,
        out_shape=jax.ShapeDtypeStruct(base.shape, base.dtype),
        in_specs=[held] * 3,
        out_specs=held,
        compiler_params=params(blocks, near, base, scale=4),
        name="finish",
    )(blocks, near, base)


def local(
    prompts,
    owners,
    lengths,
    residual,
    queries,
    expert_ids,
    route_scores,
    attn_gain,
    w_dkv,
    kv_gain,
    w_uk,
    w_uv,
    w_o,
    moe_gain,
    w_gate,
    w_up,
    w_down,
):
    bf16, f32 = jnp.bfloat16, jnp.float32
    expert_rank = lax.axis_index("expert")
    section_rank = lax.axis_index("section")
    group_rank = lax.axis_index("groups")
    experts = lax.axis_size("expert")
    sections = lax.axis_size("section")
    groups = lax.axis_size("groups")
    prompt_count, full_length, width = prompts.shape
    steps, tokens_here, heads, _ = queries.shape
    depth = w_dkv.shape[0]
    piece = depth // (groups * experts)
    latent = kv_gain.shape[0]
    cache_width = w_dkv.shape[1]
    rows = prompt_count * full_length
    own_rows = steps * tokens_here

    w_turned = w_dkv.T

    def w_piece(group):
        return lax.dynamic_slice_in_dim(
            w_turned, (expert_rank * groups + group) * piece, piece, 1
        )

    halves = spread(w_piece(group_rank), "section")
    queries_all = spread(queries, "expert")
    cut = list(cut_columns(prompts.reshape(rows, width), sections, experts))
    cut = deliver(cut, "expert")
    w_parts = halves[:1] + [w_piece(group_rank ^ other) for other in range(1, groups)]
    for half in halves[1:]:
        w_parts += spread(half, "groups")
    w_gate, w_up, w_down = fetch([w_gate, w_up, w_down], queries_all[1:])

    blocks, token = absorb_queries(
        owners, queries_all, w_uk, residual, attn_gain, w_turned, prompt_count, sections,
        cut[1:] + halves[1:] + w_parts[groups : groups + 2] + [w_gate],
    )
    blocks = lax.all_to_all(blocks, ("expert", "section"), 0, 0, tiled=True)

    high = route_scores.astype(bf16)
    low = (route_scores - high.astype(f32)).astype(bf16)
    packed = jnp.concatenate([residual, expert_ids.astype(bf16), high, low], axis=2)
    w_uv, token = lax.optimization_barrier((w_uv, token))
    uv_parts = doubled(w_uv, "expert")
    packed = spread(packed, "expert")

    away = list(project(cut[1:], w_parts, sections, groups))
    near = list(project(cut[:1], w_parts, sections, groups))
    parts = deliver(near + away, "expert")
    table = rotation(full_length + steps + -(full_length + steps) % 8, cache_width - latent)
    gathered = list(gather_queries(
        blocks, lengths, owners, kv_gain, table, prompt_count, tokens_here, experts, sections,
        steps, heads
    ))
    out_latent = attend(
        parts, lengths, kv_gain, table, gathered, tokens_here, steps, sections,
        queries.shape[-1] ** (-0.5), packed + [uv_parts[2], token],
    )

    out_latent = deliver(out_latent, "section")
    head_values = head_products(owners, out_latent, uv_parts, steps, tokens_here)
    head_values = spread(head_values, "expert")

    (w_o,) = fetch([w_o], [])
    attended = output_product(head_values, w_o)
    attended = sum(part.astype(f32) for part in spread(attended, "section")).astype(bf16)
    attended = attended.reshape(experts, own_rows, -1)
    blocks, near = run_experts(
        spread(attended, "expert"),
        packed,
        moe_gain,
        w_gate,
        w_up,
        w_down,
        expert_ids.shape[2],
        sections,
    )
    blocks = lax.all_to_all(blocks, ("expert", "section"), 0, 0, tiled=True)
    column = width // sections
    base = lax.dynamic_slice_in_dim(residual, section_rank * column, column, 2)
    return finish(blocks, near, base)


def solution(mesh):
    placed = (
        P(("groups", "expert", "section"), None, None),
        P("groups"),
        P("groups"),
        P(None, ("groups", "expert"), None),
        P(None, ("groups", "expert"), "section", None),
        P(None, ("groups", "expert"), None),
        P(None, ("groups", "expert"), None),
        P(),
        P("section", None),
        P(),
        P("section", None, "expert"),
        P("section", None, "expert"),
        P("section", "expert"),
        P(),
        P("expert", None, "section"),
        P("expert", None, "section"),
        P("expert", "section", None),
    )
    return jax.shard_map(
        local,
        mesh=mesh,
        in_specs=placed,
        out_specs=P(None, ("groups", "expert"), "section"),
        check_vma=False,
    )
```

```python
import functools
import math

import jax
import jax.numpy as jnp
import numpy as np
from jax import lax
from jax.experimental import pallas as pl
from jax.experimental.pallas import tpu as pltpu
from jax.sharding import PartitionSpec as P

epsilon = 1e-06
masked_value = -1e30
route_scale = 2.5


def rotation(positions, width):
    halfway = width // 2
    frequency = 10000.0 ** (-2.0 * np.arange(halfway) / width)
    angles = np.arange(positions)[:, None] * frequency
    cosine = np.concatenate([np.cos(angles), np.cos(angles)], axis=1)
    sine = np.concatenate([-np.sin(angles), np.sin(angles)], axis=1)
    return jnp.asarray(cosine, jnp.float32), jnp.asarray(sine, jnp.float32)


def swap(block, axis, mask):
    size = lax.axis_size(axis)
    return lax.ppermute(block, axis, [(i, i ^ mask) for i in range(size)])


def deliver(blocks, axis):
    return [blocks[0]] + [swap(blocks[mask], axis, mask) for mask in range(1, len(blocks))]


def spread(block, axis):
    return [block] + [swap(block, axis, mask) for mask in range(1, lax.axis_size(axis))]


def params(*arrays, scale=1):
    held = sum(math.prod(array.shape) * array.dtype.itemsize for array in arrays)
    mebibytes = min(56, 4 + scale * held // 1024 // 1024)
    return pltpu.CompilerParams(vmem_limit_bytes=mebibytes * 1024 * 1024)


def at_home(*arrays):
    return [pltpu.with_memory_space_constraint(array, pltpu.HBM) for array in arrays]


def fetch_kernel(count, *refs):
    out_refs, sems = refs[-1 - count : -1], refs[-1]
    copies = [
        pltpu.make_async_copy(refs[index], out_refs[index], sems.at[index])
        for index in range(count)
    ]
    for copy in copies:
        copy.start()
    for copy in copies:
        copy.wait()


def fetch(arrays, after):
    size = sum(array.size * array.dtype.itemsize for array in arrays)
    return pl.pallas_call(
        functools.partial(fetch_kernel, len(arrays)),
        out_shape=[pltpu.VMEM(array.shape, array.dtype) for array in arrays],
        in_specs=[pl.BlockSpec(memory_space=pltpu.HBM)] * len(arrays)
        + [pl.BlockSpec(memory_space=pl.ANY)] * len(after),
        out_specs=[pl.BlockSpec(memory_space=pltpu.VMEM)] * len(arrays),
        scratch_shapes=[pltpu.SemaphoreType.DMA((len(arrays),))],
        compiler_params=pltpu.CompilerParams(vmem_limit_bytes=1024 * 1024),
        cost_estimate=pl.CostEstimate(flops=0, bytes_accessed=2 * size, transcendentals=0),
        name="fetch",
    )(*at_home(*arrays), *after)


def doubled(held, axis, masks):
    held = dict(held)
    for mask in masks:
        for other in list(held):
            held[other ^ mask] = swap(held[other], axis, mask)
    return held


def cut_kernel(sections, experts, piece, x_ref, query_ref, *refs):
    out_refs, held = refs[-1 - experts : -1], refs[-1]
    rank = lax.axis_index("expert")
    steps, sources, heads, wide = query_ref.shape
    rows = x_ref.shape[0]
    for target in range(experts):
        for section in range(sections):
            at = (section * experts + target) * piece
            held[target, section * rows : (section + 1) * rows] = x_ref[:, at : at + piece]
    for mask, ref in enumerate(out_refs):
        ref[: sections * rows, :piece] = held[rank ^ mask]
        for step in range(steps):
            for source in range(sources):
                at = sections * rows + (step * sources + source) * heads
                ref[at : at + heads, :wide] = query_ref[step, source]


def cut_columns(x, queries, sections, experts, after):
    rows, width = x.shape
    piece = width // (sections * experts)
    steps, sources, heads, wide = queries.shape
    block = jax.ShapeDtypeStruct(
        (sections * rows + steps * sources * heads, max(piece, wide)), x.dtype
    )
    return pl.pallas_call(
        functools.partial(cut_kernel, sections, experts, piece),
        out_shape=[block] * experts,
        in_specs=[pl.BlockSpec(memory_space=pltpu.VMEM)] * 2
        + [pl.BlockSpec(memory_space=pl.ANY)] * len(after),
        scratch_shapes=[pltpu.VMEM((experts, sections * rows, piece), x.dtype)],
        compiler_params=params(x, block, scale=6),
        name="cut_columns",
    )(*at_home(x, queries), *after)


def project_kernel(count, first, rows, experts, sections, *refs):
    x_refs, (own_ref, *w_refs) = refs[:count], refs[count : count + 1 + sections]
    out_refs, columns = refs[-1 - count : -1], refs[-1]
    section_rank, rank = lax.axis_index("section"), lax.axis_index("expert")
    width, piece = w_refs[0].shape
    steps = own_ref.shape[0]
    total = 0
    for mask in range(sections):
        at = pl.ds(pl.multiple_of((section_rank ^ mask) * rows, rows), rows)
        x = jnp.concatenate([ref[at, :piece] for ref in x_refs], axis=0)
        total = total + lax.dot_general(
            x, w_refs[mask][...], (((1,), (1,)), ((), ())), preferred_element_type=jnp.float32
        )
    own = jnp.concatenate([own_ref[step] for step in range(steps)], axis=0).astype(jnp.float32)
    block = own.shape[0]
    column = columns.shape[2]
    for target in range(experts):
        columns[target] = own[:, target * column : (target + 1) * column]
    for index, ref in enumerate(out_refs):
        ref[:rows, :] = total[index * rows : (index + 1) * rows].astype(ref.dtype)
        value = columns[rank ^ (first + index)]
        for line, at in enumerate(range(0, column, width)):
            end = min(at + width, column)
            to = rows + line * block
            ref[to : to + block, : end - at] = value[:, at:end].astype(ref.dtype)


def project(blocks, own, w_parts, first, rows, experts, after):
    width = w_parts[0].shape[0]
    column = own.shape[2] // experts
    block = own.shape[0] * own.shape[1]
    out = jax.ShapeDtypeStruct((rows + block * -(-column // width), width), jnp.bfloat16)
    held = pl.BlockSpec(memory_space=pltpu.VMEM)
    return pl.pallas_call(
        functools.partial(
            project_kernel, len(blocks), first, rows, experts, len(w_parts)
        ),
        out_shape=[out] * len(blocks),
        in_specs=[held] * (len(blocks) + 1 + len(w_parts))
        + [pl.BlockSpec(memory_space=pl.ANY)] * len(after),
        scratch_shapes=[pltpu.VMEM((experts, block, column), jnp.float32)],
        compiler_params=params(*blocks, *w_parts, scale=6),
        name="project",
    )(*blocks, *at_home(own), *w_parts, *after)


def query_kernel(
    experts, sections, prompts, nope, shape, *refs
):
    f32, bf16 = jnp.float32, jnp.bfloat16
    table_ref, query_refs = refs[0], refs[1 : 1 + experts]
    uk_ref, own_ref, gain_ref, wt_ref = refs[1 + experts : 5 + experts]
    out_ref, token_ref, picked, ropes, made, normed, query_ref = refs[-7:]
    token_ref[...] = jnp.zeros_like(token_ref)
    steps, sources, heads, wide = shape
    rope = wide - nope
    chunk = uk_ref.shape[2]
    width = out_ref.shape[2]
    count = experts * sources
    block = prompts * steps * heads
    rank = lax.axis_index("expert")

    for mask, ref in enumerate(query_refs):
        for step in range(steps):
            for source in range(sources):
                at = ref.shape[0] - (steps * sources - step * sources - source) * heads
                query_ref[rank ^ mask, step, source] = ref[at : at + heads, :wide]

    def pick(index, carry):
        owner = table_ref[index]
        for step in range(steps):
            value = query_ref[owner, step, index // sources].astype(f32)
            at = pl.ds(pl.multiple_of((index * steps + step) * heads, heads), heads)
            picked[at, :] = value[:, :nope]
            ropes[at, :] = value[:, nope:].astype(bf16)
        return carry

    if count <= 16:
        for index in range(count):
            pick(index, 0)
    else:
        lax.fori_loop(0, count, pick, 0)
    for head in range(heads):
        at = pl.ds(head, count * steps, stride=heads)
        value = jnp.dot(picked[at, :].astype(bf16), uk_ref[head], preferred_element_type=f32)
        if chunk < made.shape[1]:
            spare = jnp.zeros((count * steps, made.shape[1] - chunk), f32)
            value = jnp.concatenate([value, spare], axis=1)
        made[at, :] = value
    small = width - chunk
    pair = lax.broadcasted_iota(jnp.int32, (rope, small), 0)
    pair = pair == lax.broadcasted_iota(jnp.int32, (rope, small), 1) + rank * small
    turned = jnp.dot(
        ropes[...], jnp.where(pair, 1.0, 0.0).astype(bf16), preferred_element_type=f32
    )
    own = jnp.concatenate([own_ref[step] for step in range(steps)], axis=0).astype(f32)
    scale = lax.rsqrt(jnp.mean(own * own, axis=-1, keepdims=True) + epsilon)
    own = (own * scale * gain_ref[...][None].astype(f32)).astype(bf16)
    depth = wt_ref.shape[1]
    for section in range(sections):
        normed[section] = own[:, section * depth : (section + 1) * depth]
    fresh = lax.dot_general(
        normed[lax.axis_index("section")],
        wt_ref[...],
        (((1,), (1,)), ((), ())),
        preferred_element_type=f32,
    )
    for source in range(experts):
        lines = [
            fresh[step * sources + source :, part * width : (part + 1) * width][:1]
            for step in range(steps)
            for part in range(experts)
        ]
        lines = jnp.concatenate(lines, axis=0).astype(bf16)
        for section in range(sections):
            index = source * sections + section
            at = slice(index * block, (index + 1) * block)
            value = jnp.concatenate([made[at, :chunk], turned[at]], axis=1)
            out_ref[index, :block, :] = value.astype(bf16)
            out_ref[index, block:, :] = lines


def absorb_queries(table, queries, shape, w_uk, own, gain, w_turned, prompts, sections, after):
    experts = len(queries)
    steps, sources, heads, wide = shape
    _, nope, chunk = w_uk.shape
    width = chunk + (wide - nope) // experts
    rows = prompts * steps * heads + steps * experts
    count = experts * sources * steps * heads
    held = pl.BlockSpec(memory_space=pltpu.VMEM)
    return pl.pallas_call(
        functools.partial(query_kernel, experts, sections, prompts, nope, shape),
        out_shape=[
            jax.ShapeDtypeStruct((experts * sections, rows, width), jnp.bfloat16),
            jax.ShapeDtypeStruct((8, 128), jnp.bfloat16),
        ],
        in_specs=[pl.BlockSpec(memory_space=pltpu.SMEM)]
        + [held] * (experts + 4)
        + [pl.BlockSpec(memory_space=pl.ANY)] * len(after),
        out_specs=[held] * 2,
        scratch_shapes=[
            pltpu.VMEM((count, nope), jnp.float32),
            pltpu.VMEM((count, wide - nope), jnp.bfloat16),
            pltpu.VMEM((count, max(chunk, 128)), jnp.float32),
            pltpu.VMEM(
                (sections, own.shape[0] * own.shape[1], w_turned.shape[1]), jnp.bfloat16
            ),
            pltpu.VMEM((experts,) + shape, jnp.bfloat16),
        ],
        compiler_params=params(*queries, w_uk, own, w_turned, scale=4),
        name="absorb_queries",
    )(*at_home(table), *queries, *at_home(w_uk, own, gain, w_turned), *after)


def turn(values, cosine, sine):
    half = values.shape[1] // 2
    other = jnp.concatenate([values[:, half:], values[:, :half]], axis=1)
    return values * cosine + other * sine


def scaled(values, gain):
    scale = lax.rsqrt(jnp.mean(values * values, axis=-1, keepdims=True) + epsilon)
    return values * scale * gain.astype(jnp.float32)


def gather_kernel(
    prompts, experts, sections, sources, heads, steps, latent, length_ref, owner_ref, gain_ref,
    cosine_ref, sine_ref, block_ref, query_ref, query_rope_ref, recent_ref, recent_rope_ref,
    cosine_held, sine_held
):
    f32, bf16 = jnp.float32, jnp.bfloat16
    rows = steps * heads
    chunk = latent // experts
    first = lax.axis_index("expert") * sources + lax.axis_index("section") * prompts
    gain = gain_ref[...][None]
    for prompt in range(prompts):
        length, owner = length_ref[first + prompt], owner_ref[first + prompt]
        for step in range(steps):
            at = slice(step * heads, (step + 1) * heads)
            cosine_held[at, :] = jnp.broadcast_to(
                cosine_ref[pl.ds(length + step, 1), :], (heads, cosine_ref.shape[1])
            )
            sine_held[at, :] = jnp.broadcast_to(
                sine_ref[pl.ds(length + step, 1), :], (heads, sine_ref.shape[1])
            )
        cosine, sine = cosine_held[...], sine_held[...]
        at = slice(prompt * rows, (prompt + 1) * rows)
        for section in range(sections):
            pieces = [block_ref[i * sections + section, at, :] for i in range(experts)]
            to = slice(section * rows, (section + 1) * rows)
            query_ref[prompt, to, :] = jnp.concatenate(
                [piece[:, :chunk] for piece in pieces], axis=1
            )
            rope = jnp.concatenate([piece[:, chunk:].astype(f32) for piece in pieces], axis=1)
            query_rope_ref[prompt, to, :] = turn(rope, cosine, sine).astype(bf16)
        lines = 0
        for section in range(sections):
            lines = lines + block_ref[
                owner * sections + section, prompts * rows :, :
            ].astype(f32)
        recent, recent_rope = [], []
        for step in range(steps):
            line = jnp.concatenate(
                [lines[step * experts + part :][:1] for part in range(experts)], axis=1
            )
            recent.append(scaled(line[:, :latent], gain))
            at = slice(step * heads, step * heads + 1)
            recent_rope.append(turn(line[:, latent:], cosine[at], sine[at]))
        spare = recent_ref.shape[1] - steps
        recent.append(jnp.zeros((spare, latent), f32))
        recent_rope.append(jnp.zeros((spare, recent_rope[0].shape[1]), f32))
        recent_ref[prompt] = jnp.concatenate(recent, axis=0).astype(bf16)
        recent_rope_ref[prompt] = jnp.concatenate(recent_rope, axis=0).astype(bf16)


def gather_queries(blocks, lengths, owners, kv_gain, table, prompts, sources, experts, sections,
                   steps, heads):
    latent = kv_gain.shape[0]
    rope = blocks.shape[2] * experts - latent
    rows = sections * steps * heads
    spare = steps + -steps % 16
    shape = lambda *sizes: jax.ShapeDtypeStruct((prompts,) + sizes, jnp.bfloat16)
    held = pl.BlockSpec(memory_space=pltpu.VMEM)
    return pl.pallas_call(
        functools.partial(
            gather_kernel, prompts, experts, sections, sources, heads, steps, latent
        ),
        out_shape=[shape(rows, latent), shape(rows, rope), shape(spare, latent), shape(spare, rope)],
        in_specs=[pl.BlockSpec(memory_space=pltpu.SMEM)] * 2 + [held] * 4,
        out_specs=[held] * 4,
        scratch_shapes=[pltpu.VMEM((steps * heads, rope), jnp.float32)] * 2,
        compiler_params=params(blocks, scale=4),
        name="gather_queries",
    )(*at_home(lengths, owners, kv_gain, *table), blocks)


def attend_kernel(parts, positions, sections, sources, heads, steps, score_scale, *refs):
    part_refs = refs[:parts]
    (length_ref, gain_ref, cosine_ref, sine_ref, query_ref, query_rope_ref, recent_ref,
     recent_rope_ref) = refs[parts : parts + 8]
    out_refs, token_ref, held = refs[-2 - sections : -2], refs[-2], refs[-1]
    token_ref[...] = jnp.zeros_like(token_ref)
    f32, bf16 = jnp.float32, jnp.bfloat16
    nt = (((1,), (1,)), ((), ()))
    prompts, _, latent = query_ref.shape
    rows = steps * heads
    section_rank = lax.axis_index("section")
    first = lax.axis_index("expert") * sources + section_rank * prompts
    for prompt in range(prompts):
        at = slice(prompt * positions, (prompt + 1) * positions)
        projected = part_refs[0][at].astype(f32)
        for ref in part_refs[1:]:
            projected = projected + ref[at].astype(f32)
        keys = scaled(projected[:, :latent], gain_ref[...][None]).astype(bf16)
        key_rope = turn(
            projected[:, latent:], cosine_ref[:positions], sine_ref[:positions]
        ).astype(bf16)
        query, query_rope = query_ref[prompt], query_rope_ref[prompt]
        recent, recent_rope = recent_ref[prompt], recent_rope_ref[prompt]
        scores = lax.dot_general(query, keys, nt, preferred_element_type=f32)
        scores = scores + lax.dot_general(query_rope, key_rope, nt, preferred_element_type=f32)
        fresh = lax.dot_general(query, recent, nt, preferred_element_type=f32)
        fresh = fresh + lax.dot_general(query_rope, recent_rope, nt, preferred_element_type=f32)
        place = lax.broadcasted_iota(jnp.int32, scores.shape, 1)
        scores = jnp.where(
            place < length_ref[first + prompt], scores * score_scale, masked_value
        )
        row = lax.broadcasted_iota(jnp.int32, (rows, fresh.shape[1]), 0)
        place = lax.broadcasted_iota(jnp.int32, (rows, fresh.shape[1]), 1)
        seen = jnp.where(place < 1, 1.0, 0.0)
        for step in range(1, steps):
            seen = jnp.where((place <= step) & (row >= step * heads), 1.0, seen)
        seen = jnp.concatenate([seen] * sections, axis=0)
        fresh = jnp.where(seen > 0.5, fresh * score_scale, masked_value)
        most = jnp.maximum(
            jnp.max(scores, axis=-1, keepdims=True), jnp.max(fresh, axis=-1, keepdims=True)
        )
        scores = jnp.exp(scores - most)
        fresh = jnp.exp(fresh - most)
        total = jnp.sum(scores, axis=-1, keepdims=True) + jnp.sum(fresh, axis=-1, keepdims=True)
        scores = (scores / total).astype(bf16)
        fresh = (fresh / total).astype(bf16)
        mixed = jnp.dot(scores, keys, preferred_element_type=f32)
        mixed = mixed + jnp.dot(fresh, recent, preferred_element_type=f32)
        mixed = mixed.astype(bf16)
        for section in range(sections):
            held[section] = mixed[section * rows : (section + 1) * rows]
        for mask, ref in enumerate(out_refs):
            ref[prompt * rows : (prompt + 1) * rows, :] = held[section_rank ^ mask]


def attend(
    parts, positions, lengths, kv_gain, table, gathered, sources, steps, sections, score_scale
):
    prompts, rows, latent = gathered[0].shape
    out = (rows // sections, latent)
    held = pl.BlockSpec(memory_space=pltpu.VMEM)
    return pl.pallas_call(
        functools.partial(
            attend_kernel, len(parts), positions, sections, sources, out[0] // steps, steps,
            score_scale
        ),
        out_shape=[jax.ShapeDtypeStruct((prompts * out[0], latent), jnp.bfloat16)] * sections
        + [jax.ShapeDtypeStruct((8, 128), jnp.bfloat16)],
        in_specs=[held] * len(parts)
        + [pl.BlockSpec(memory_space=pltpu.SMEM)]
        + [held] * 7,
        out_specs=[held] * (sections + 1),
        scratch_shapes=[pltpu.VMEM((sections,) + out, jnp.bfloat16)],
        compiler_params=params(*parts, *gathered, scale=6),
        name="attend",
    )(*parts, *at_home(lengths, kv_gain, *table), *gathered)


def value_kernel(experts, sections, heads, steps, sources, *refs):
    owner_ref = refs[0]
    latent_refs, uv_refs = refs[1 : 1 + sections], refs[1 + sections : 1 + sections + experts]
    route_ref = refs[1 + sections + experts]
    out_ref, held = refs[-2:]
    f32, bf16 = jnp.float32, jnp.bfloat16
    chunk = uv_refs[0].shape[2]
    rows = latent_refs[0].shape[0]
    for mask, ref in enumerate(latent_refs):
        for index in range(experts):
            held[index, mask * rows : (mask + 1) * rows, :chunk] = ref[
                :, index * chunk : (index + 1) * chunk
            ].astype(f32)
    rank = lax.axis_index("expert")
    values = []
    for head in range(heads):
        at = pl.ds(head, sections * rows // heads, stride=heads)
        total = 0
        for mask, ref in enumerate(uv_refs):
            total = total + lax.dot_general(
                held[rank ^ mask, at, :][:, :chunk].astype(bf16),
                ref[head],
                (((1,), (1,)), ((), ())),
                preferred_element_type=f32,
            )
        values.append(total.astype(bf16))
    values = jnp.concatenate(values, axis=1)
    prompts = sources // sections
    section_rank = lax.axis_index("section")
    size = sources * steps
    to = lax.broadcasted_iota(jnp.int32, (size, size), 0)
    row = lax.broadcasted_iota(jnp.int32, (size, size), 1)
    order = jnp.zeros((size, size), f32)
    for mask in range(sections):
        for prompt in range(prompts):
            owner = owner_ref[
                rank * sources + (section_rank ^ mask) * prompts + prompt
            ]
            for step in range(steps):
                index = (mask * prompts + prompt) * steps + step
                order = jnp.where((row == index) & (to == owner * steps + step), 1.0, order)
    width = values.shape[1]
    out_ref[:, :width] = jnp.dot(
        order.astype(bf16), values, preferred_element_type=f32
    ).astype(bf16)
    out_ref[:, width:] = route_ref[...]


def head_products(owners, latents, uv_parts, route, steps, sources, after):
    rows, width = latents[0].shape
    heads, value, _ = uv_parts[0].shape
    held = pl.BlockSpec(memory_space=pltpu.VMEM)
    total = rows * len(latents)
    return pl.pallas_call(
        functools.partial(
            value_kernel, len(uv_parts), len(latents), heads, steps, sources
        ),
        out_shape=jax.ShapeDtypeStruct(
            (total // heads, heads * value + route.shape[1]), jnp.bfloat16
        ),
        in_specs=[pl.BlockSpec(memory_space=pltpu.SMEM)]
        + [held] * (len(latents) + len(uv_parts) + 1)
        + [pl.BlockSpec(memory_space=pl.ANY)] * len(after),
        out_specs=held,
        scratch_shapes=[
            pltpu.VMEM((len(uv_parts), total, max(width // len(uv_parts), 128)), jnp.float32)
        ],
        compiler_params=params(*latents, *uv_parts, scale=4),
        name="head_products",
    )(*at_home(owners), *latents, *uv_parts, route, *after)


def output_kernel(experts, *refs):
    value_refs = refs[:experts]
    weight_ref, out_ref = refs[experts:]
    depth = weight_ref.shape[0]
    values = jnp.concatenate([ref[:, :depth] for ref in value_refs], axis=0)
    rows = values.shape[0]
    to = lax.broadcasted_iota(jnp.int32, (rows, rows), 0)
    row = lax.broadcasted_iota(jnp.int32, (rows, rows), 1)
    source = (to & (experts - 1)) ^ lax.axis_index("expert")
    rest = lax.shift_right_logical(to, experts.bit_length() - 1)
    order = jnp.where(row == source * (rows // experts) + rest, 1.0, 0.0).astype(jnp.bfloat16)
    values = jnp.dot(order, values, preferred_element_type=jnp.float32).astype(jnp.bfloat16)
    out_ref[...] = jnp.dot(
        values, weight_ref[...], preferred_element_type=jnp.float32
    ).astype(out_ref.dtype)


def output_product(values, weight):
    rows = sum(value.shape[0] for value in values)
    held = pl.BlockSpec(memory_space=pltpu.VMEM)
    return pl.pallas_call(
        functools.partial(output_kernel, len(values)),
        out_shape=jax.ShapeDtypeStruct((rows, weight.shape[1]), jnp.bfloat16),
        in_specs=[held] * (len(values) + 1),
        out_specs=held,
        compiler_params=params(*values, scale=8),
        name="output_product",
    )(*values, weight)


def mix_kernel(count, owners, rows, *refs):
    part_refs, own_refs = refs[:count], refs[count : count + owners]
    out_ref, held = refs[-2:]
    f32 = jnp.float32
    total = part_refs[0][...].astype(f32)
    for ref in part_refs[1:]:
        total = total + ref[...].astype(f32)
    block, column = held.shape[1:]
    for owner in range(owners):
        held[owner] = total[owner * block : (owner + 1) * block]
    rank = lax.axis_index("expert")
    for mask, ref in enumerate(own_refs):
        lines = []
        for line, at in enumerate(range(0, column, ref.shape[1])):
            end = min(at + ref.shape[1], column)
            to = rows + line * block
            lines.append(ref[to : to + block, : end - at].astype(f32))
        lines = lines[0] if len(lines) == 1 else jnp.concatenate(lines, axis=1)
        out_ref[rank ^ mask] = (held[rank ^ mask] + lines).astype(out_ref.dtype)


def mix(parts, owns, rows, after):
    total, width = parts[0].shape
    owners = len(owns)
    held = pl.BlockSpec(memory_space=pltpu.VMEM)
    shape = (owners, total // owners, width)
    return pl.pallas_call(
        functools.partial(mix_kernel, len(parts), owners, rows),
        out_shape=jax.ShapeDtypeStruct(shape, parts[0].dtype),
        in_specs=[held] * (len(parts) + owners)
        + [pl.BlockSpec(memory_space=pl.ANY)] * len(after),
        out_specs=held,
        scratch_shapes=[pltpu.VMEM(shape, jnp.float32)],
        compiler_params=params(*parts, *owns, scale=4),
        name="mix",
    )(*parts, *owns, *after)


def expert_kernel(experts, sections, picks, *refs):
    mixed_refs, route_refs = refs[:experts], refs[experts : 2 * experts]
    gain_ref, gate_ref, up_ref, down_ref, out_ref, near_ref, columns = refs[2 * experts :]
    f32, bf16 = jnp.float32, jnp.bfloat16
    count = gate_ref.shape[0]
    rank = lax.axis_index("expert")
    width = gain_ref.shape[0]
    block = mixed_refs[0].shape[1]
    for mask, ref in enumerate(mixed_refs):
        columns[rank ^ mask] = ref[...]
    mixed, route = [], []
    for mask, ref in enumerate(route_refs):
        mixed.append(
            jnp.concatenate([columns[i, rank ^ mask] for i in range(experts)], axis=1).astype(f32)
        )
        route.append(ref[:, ref.shape[1] - 128 :].astype(f32))
    near = mixed[0]
    mixed = jnp.concatenate(mixed, axis=0)
    route = jnp.concatenate(route, axis=0)
    named = route[:, :picks]
    weights = route[:, picks : 2 * picks] + route[:, 2 * picks : 3 * picks]
    weights = route_scale * weights / jnp.sum(weights, axis=-1, keepdims=True)
    scale = lax.rsqrt(jnp.mean(mixed * mixed, axis=-1, keepdims=True) + epsilon)
    rows_in = (mixed * scale * gain_ref[...][None].astype(f32)).astype(bf16)
    column = width // sections
    total = 0
    for x in range(count):
        mine = (rank * count + x).astype(f32)
        weight = jnp.sum(jnp.where(named == mine, weights, 0.0), axis=-1, keepdims=True)
        gate = jnp.dot(rows_in, gate_ref[x], preferred_element_type=f32)
        up = jnp.dot(rows_in, up_ref[x], preferred_element_type=f32)
        inner = gate / (1.0 + jnp.exp(-gate)) * up * weight
        total = total + jnp.dot(inner.astype(bf16), down_ref[x], preferred_element_type=f32)
    for section in range(sections):
        at = slice(section * column, (section + 1) * column)
        near_ref[section] = near[:, at].astype(bf16)
        for mask in range(experts):
            out_ref[(rank ^ mask) * sections + section] = total[
                mask * block : (mask + 1) * block, at
            ].astype(bf16)


def run_experts(mixed, routes, gain, w_gate, w_up, w_down, picks, sections):
    experts = len(mixed)
    block = (mixed[0].shape[1], gain.shape[0] // sections)
    held = pl.BlockSpec(memory_space=pltpu.VMEM)
    return pl.pallas_call(
        functools.partial(expert_kernel, experts, sections, picks),
        out_shape=[
            jax.ShapeDtypeStruct((experts * sections,) + block, jnp.bfloat16),
            jax.ShapeDtypeStruct((sections,) + block, jnp.bfloat16),
        ],
        in_specs=[held] * (2 * experts + 4),
        out_specs=[held] * 2,
        scratch_shapes=[pltpu.VMEM((experts,) + mixed[0].shape, jnp.bfloat16)],
        compiler_params=params(*mixed, scale=32),
        name="run_experts",
    )(*mixed, *routes, *at_home(gain), w_gate, w_up, w_down)


def finish_kernel(block_ref, near_ref, out_ref):
    f32 = jnp.float32
    steps, sources, _ = out_ref.shape
    total = near_ref[lax.axis_index("section")].astype(f32)
    for index in range(block_ref.shape[0]):
        total = total + block_ref[index].astype(f32)
    for step in range(steps):
        out_ref[step] = total[step * sources : (step + 1) * sources].astype(out_ref.dtype)


def finish(blocks, near, steps):
    held = pl.BlockSpec(memory_space=pltpu.VMEM)
    _, rows, column = near.shape
    return pl.pallas_call(
        finish_kernel,
        out_shape=jax.ShapeDtypeStruct((steps, rows // steps, column), near.dtype),
        in_specs=[held] * 2,
        out_specs=held,
        compiler_params=params(blocks, near, scale=4),
        name="finish",
    )(blocks, near)


def local(
    prompts,
    owners,
    lengths,
    residual,
    queries,
    expert_ids,
    route_scores,
    attn_gain,
    w_dkv,
    kv_gain,
    w_uk,
    w_uv,
    w_o,
    moe_gain,
    w_gate,
    w_up,
    w_down,
):
    bf16, f32 = jnp.bfloat16, jnp.float32
    expert_rank = lax.axis_index("expert")
    section_rank = lax.axis_index("section")
    experts = lax.axis_size("expert")
    sections = lax.axis_size("section")
    prompt_count, full_length, width = prompts.shape
    steps, tokens_here, heads, _ = queries.shape
    depth = w_dkv.shape[0]
    piece = depth // experts
    latent = kv_gain.shape[0]
    cache_width = w_dkv.shape[1]
    rows = prompt_count * full_length
    own_rows = steps * tokens_here

    w_turned = w_dkv.T
    w_piece = lax.dynamic_slice_in_dim(w_turned, expert_rank * piece, piece, 1)
    masks = [1 << bit for bit in range(experts.bit_length() - 1)]
    uv_parts = doubled({0: w_uv}, "expert", masks[1:])
    w_parts = spread(w_piece, "section")
    cut = cut_columns(
        prompts.reshape(rows, width), queries, sections, experts,
        [],
    )
    cut = deliver(cut, "expert")

    blocks, token = absorb_queries(
        owners, cut, queries.shape, w_uk, residual, attn_gain, w_turned, prompt_count, sections,
        [uv_parts[masks[-1]]],
    )
    blocks = lax.all_to_all(blocks, ("expert", "section"), 0, 0, tiled=True)

    away = list(project(cut[1:], residual, w_parts, 1, rows, experts, [token]))
    near = list(project(cut[:1], residual, w_parts, 0, rows, experts, away[:1]))
    parts = deliver(near + away, "expert")
    table = rotation(full_length + steps + -(full_length + steps) % 8, cache_width - latent)
    gathered = list(gather_queries(
        blocks, lengths, owners, kv_gain, table, prompt_count, tokens_here, experts, sections,
        steps, heads
    ))
    *out_latent, token = attend(
        parts, full_length, lengths, kv_gain, table, gathered, tokens_here, steps, sections,
        queries.shape[-1] ** (-0.5),
    )

    (w_gate,) = fetch([w_gate], [token])
    order = sorted(uv_parts)
    *uv_parts, token = lax.optimization_barrier((*[uv_parts[mask] for mask in order], token))
    uv_parts = doubled(dict(zip(order, uv_parts)), "expert", masks[:1])
    out_latent = deliver(out_latent, "section")
    high = route_scores.astype(bf16)
    low = (route_scores - high.astype(f32)).astype(bf16)
    route = jnp.concatenate([expert_ids.astype(bf16), high, low], axis=2).reshape(own_rows, -1)
    route = jnp.pad(route, ((0, 0), (0, 128 - route.shape[1])))
    head_values = head_products(
        owners, out_latent, [uv_parts[mask] for mask in range(experts)], route, steps,
        tokens_here, [w_gate, token],
    )
    head_values = spread(head_values, "expert")

    (w_o,) = fetch([w_o], [])
    attended = output_product(head_values, w_o)
    (w_up,) = fetch([w_up], [attended])
    mixed = mix(spread(attended, "section"), parts, rows, [w_up])
    (w_down,) = fetch([w_down], [mixed])
    blocks, near = run_experts(
        spread(mixed, "expert"),
        head_values,
        moe_gain,
        w_gate,
        w_up,
        w_down,
        expert_ids.shape[2],
        sections,
    )
    blocks = lax.all_to_all(blocks, ("expert", "section"), 0, 0, tiled=True)
    return finish(blocks, near, steps)


def solution(mesh):
    placed = (
        P(("groups", "expert", "section"), None, None),
        P("groups"),
        P("groups"),
        P(None, ("groups", "expert"), None),
        P(None, ("groups", "expert"), "section", None),
        P(None, ("groups", "expert"), None),
        P(None, ("groups", "expert"), None),
        P(),
        P("section", None),
        P(),
        P("section", None, "expert"),
        P("section", None, "expert"),
        P("section", "expert"),
        P(),
        P("expert", None, "section"),
        P("expert", None, "section"),
        P("expert", "section", None),
    )
    return jax.shard_map(
        local,
        mesh=mesh,
        in_specs=placed,
        out_specs=P(None, ("groups", "expert"), "section"),
        check_vma=False,
    )
```

```python
import functools
import math

import jax
import jax.numpy as jnp
import numpy as np
from jax import lax
from jax.experimental import pallas as pl
from jax.experimental.pallas import tpu as pltpu
from jax.sharding import PartitionSpec as P

epsilon = 1e-06
masked_value = -1e30
route_scale = 2.5


def rotation(positions, width):
    halfway = width // 2
    frequency = 10000.0 ** (-2.0 * np.arange(halfway) / width)
    angles = np.arange(positions)[:, None] * frequency
    cosine = np.concatenate([np.cos(angles), np.cos(angles)], axis=1)
    sine = np.concatenate([-np.sin(angles), np.sin(angles)], axis=1)
    return jnp.asarray(cosine, jnp.float32), jnp.asarray(sine, jnp.float32)


def swap(block, axis, mask):
    size = lax.axis_size(axis)
    return lax.ppermute(block, axis, [(i, i ^ mask) for i in range(size)])


def deliver(blocks, axis):
    return [blocks[0]] + [swap(blocks[mask], axis, mask) for mask in range(1, len(blocks))]


def spread(block, axis):
    return [block] + [swap(block, axis, mask) for mask in range(1, lax.axis_size(axis))]


def params(*arrays, scale=1):
    held = sum(math.prod(array.shape) * array.dtype.itemsize for array in arrays)
    mebibytes = min(56, 4 + scale * held // 1024 // 1024)
    return pltpu.CompilerParams(vmem_limit_bytes=mebibytes * 1024 * 1024)


def at_home(*arrays):
    return [pltpu.with_memory_space_constraint(array, pltpu.HBM) for array in arrays]


def fetch_kernel(count, *refs):
    out_refs, sems = refs[-1 - count : -1], refs[-1]
    copies = [
        pltpu.make_async_copy(refs[index], out_refs[index], sems.at[index])
        for index in range(count)
    ]
    for copy in copies:
        copy.start()
    for copy in copies:
        copy.wait()


def fetch(arrays, after):
    size = sum(array.size * array.dtype.itemsize for array in arrays)
    return pl.pallas_call(
        functools.partial(fetch_kernel, len(arrays)),
        out_shape=[pltpu.VMEM(array.shape, array.dtype) for array in arrays],
        in_specs=[pl.BlockSpec(memory_space=pltpu.HBM)] * len(arrays)
        + [pl.BlockSpec(memory_space=pl.ANY)] * len(after),
        out_specs=[pl.BlockSpec(memory_space=pltpu.VMEM)] * len(arrays),
        scratch_shapes=[pltpu.SemaphoreType.DMA((len(arrays),))],
        compiler_params=pltpu.CompilerParams(vmem_limit_bytes=1024 * 1024),
        cost_estimate=pl.CostEstimate(flops=0, bytes_accessed=2 * size, transcendentals=0),
        name="fetch",
    )(*at_home(*arrays), *after)


def doubled(held, axis, masks):
    held = dict(held)
    for mask in masks:
        for other in list(held):
            held[other ^ mask] = swap(held[other], axis, mask)
    return held


def cut_kernel(sections, experts, piece, x_ref, query_ref, w_ref, *refs):
    w_out_ref, *out_refs, w_held, held = refs
    rank = lax.axis_index("expert")
    steps, sources, heads, wide = query_ref.shape
    rows = x_ref.shape[0]
    for target in range(experts):
        w_held[target] = w_ref[:, target * piece : (target + 1) * piece]
    w_out_ref[...] = w_held[rank]
    for target in range(experts):
        for section in range(sections):
            at = (section * experts + target) * piece
            held[target, section * rows : (section + 1) * rows] = x_ref[:, at : at + piece]
    for mask, ref in enumerate(out_refs):
        ref[: sections * rows, :piece] = held[rank ^ mask]
        for step in range(steps):
            for source in range(sources):
                at = sections * rows + (step * sources + source) * heads
                ref[at : at + heads, :wide] = query_ref[step, source]


def cut_columns(x, queries, w_turned, sections, experts):
    rows, width = x.shape
    piece = width // (sections * experts)
    steps, sources, heads, wide = queries.shape
    block = jax.ShapeDtypeStruct(
        (sections * rows + steps * sources * heads, max(piece, wide)), x.dtype
    )
    return pl.pallas_call(
        functools.partial(cut_kernel, sections, experts, piece),
        out_shape=[jax.ShapeDtypeStruct((w_turned.shape[0], piece), x.dtype)] + [block] * experts,
        scratch_shapes=[
            pltpu.VMEM((experts, w_turned.shape[0], piece), x.dtype),
            pltpu.VMEM((experts, sections * rows, piece), x.dtype),
        ],
        compiler_params=params(x, block, w_turned, scale=6),
        name="cut_columns",
    )(*at_home(x, queries, w_turned))


def project_kernel(count, first, rows, *refs):
    x_refs, rider_ref, w_refs, out_refs = refs[:count], refs[count], refs[count + 1 :], refs[-count:]
    section_rank = lax.axis_index("section")
    sections = lax.axis_size("section")
    piece = w_refs[0].shape[1]
    total = 0
    for mask in range(sections):
        at = pl.ds(pl.multiple_of((section_rank ^ mask) * rows, rows), rows)
        x = jnp.concatenate([ref[at, :piece] for ref in x_refs], axis=0)
        total = total + lax.dot_general(
            x, w_refs[mask][...], (((1,), (1,)), ((), ())), preferred_element_type=jnp.float32
        )
    for index, ref in enumerate(out_refs):
        ref[:rows, :] = total[index * rows : (index + 1) * rows].astype(ref.dtype)
        ref[rows:, :] = rider_ref[first + index]


def project(blocks, riders, w_parts, first, rows, after):
    out = jax.ShapeDtypeStruct((rows + riders.shape[1], riders.shape[2]), jnp.bfloat16)
    held = pl.BlockSpec(memory_space=pltpu.VMEM)
    return pl.pallas_call(
        functools.partial(project_kernel, len(blocks), first, rows),
        out_shape=[out] * len(blocks),
        in_specs=[held] * (len(blocks) + 1 + len(w_parts))
        + [pl.BlockSpec(memory_space=pl.ANY)] * len(after),
        compiler_params=params(*blocks, *w_parts, scale=6),
        name="project",
    )(*blocks, riders, *w_parts, *after)


def query_kernel(
    experts, sections, prompts, nope, shape, *refs
):
    f32, bf16 = jnp.float32, jnp.bfloat16
    table_ref, query_refs = refs[0], refs[1 : 1 + experts]
    uk_ref, own_ref, gain_ref, wt_ref = refs[1 + experts : 5 + experts]
    out_ref, rider_ref, token_ref, picked, ropes, made, normed, query_ref, columns = refs[-9:]
    token_ref[...] = jnp.zeros_like(token_ref)
    steps, sources, heads, wide = shape
    rope = wide - nope
    chunk = uk_ref.shape[2]
    width = out_ref.shape[2]
    count = experts * sources
    block = prompts * steps * heads
    rank = lax.axis_index("expert")

    for mask, ref in enumerate(query_refs):
        for step in range(steps):
            for source in range(sources):
                at = ref.shape[0] - (steps * sources - step * sources - source) * heads
                query_ref[rank ^ mask, step, source] = ref[at : at + heads, :wide]

    def pick(index, carry):
        owner = table_ref[index]
        for step in range(steps):
            value = query_ref[owner, step, index // sources].astype(f32)
            at = pl.ds(pl.multiple_of((index * steps + step) * heads, heads), heads)
            picked[at, :] = value[:, :nope]
            ropes[at, :] = value[:, nope:].astype(bf16)
        return carry

    if count <= 16:
        for index in range(count):
            pick(index, 0)
    else:
        lax.fori_loop(0, count, pick, 0)
    for head in range(heads):
        at = pl.ds(head, count * steps, stride=heads)
        value = jnp.dot(picked[at, :].astype(bf16), uk_ref[head], preferred_element_type=f32)
        if chunk < made.shape[1]:
            spare = jnp.zeros((count * steps, made.shape[1] - chunk), f32)
            value = jnp.concatenate([value, spare], axis=1)
        made[at, :] = value
    small = width - chunk
    pair = lax.broadcasted_iota(jnp.int32, (rope, small), 0)
    pair = pair == lax.broadcasted_iota(jnp.int32, (rope, small), 1) + rank * small
    turned = jnp.dot(
        ropes[...], jnp.where(pair, 1.0, 0.0).astype(bf16), preferred_element_type=f32
    )
    own = jnp.concatenate([own_ref[step] for step in range(steps)], axis=0).astype(f32)
    lines, column = columns.shape[1:]
    for target in range(experts):
        columns[target] = own[:, target * column : (target + 1) * column]
    for mask in range(experts):
        value = columns[rank ^ mask]
        for line, at in enumerate(range(0, column, rider_ref.shape[2])):
            end = min(at + rider_ref.shape[2], column)
            rider_ref[mask, line * lines : (line + 1) * lines, : end - at] = value[
                :, at:end
            ].astype(bf16)
    scale = lax.rsqrt(jnp.mean(own * own, axis=-1, keepdims=True) + epsilon)
    own = (own * scale * gain_ref[...][None].astype(f32)).astype(bf16)
    depth = wt_ref.shape[1]
    for section in range(sections):
        normed[section] = own[:, section * depth : (section + 1) * depth]
    fresh = lax.dot_general(
        normed[lax.axis_index("section")],
        wt_ref[...],
        (((1,), (1,)), ((), ())),
        preferred_element_type=f32,
    )
    for source in range(experts):
        lines = [
            fresh[step * sources + source :, part * width : (part + 1) * width][:1]
            for step in range(steps)
            for part in range(experts)
        ]
        lines = jnp.concatenate(lines, axis=0).astype(bf16)
        for section in range(sections):
            index = source * sections + section
            at = slice(index * block, (index + 1) * block)
            value = jnp.concatenate([made[at, :chunk], turned[at]], axis=1)
            out_ref[index, :block, :] = value.astype(bf16)
            out_ref[index, block:, :] = lines


def absorb_queries(table, queries, shape, w_uk, own, gain, w_turned, prompts, sections):
    experts = len(queries)
    steps, sources, heads, wide = shape
    _, nope, chunk = w_uk.shape
    width = chunk + (wide - nope) // experts
    block, column = own.shape[0] * own.shape[1], own.shape[2] // experts
    cache_width = w_turned.shape[0]
    rows = prompts * steps * heads + steps * experts
    count = experts * sources * steps * heads
    held = pl.BlockSpec(memory_space=pltpu.VMEM)
    return pl.pallas_call(
        functools.partial(query_kernel, experts, sections, prompts, nope, shape),
        out_shape=[
            jax.ShapeDtypeStruct((experts * sections, rows, width), jnp.bfloat16),
            jax.ShapeDtypeStruct(
                (experts, block * -(-column // cache_width), cache_width), jnp.bfloat16
            ),
            jax.ShapeDtypeStruct((8, 128), jnp.bfloat16),
        ],
        in_specs=[pl.BlockSpec(memory_space=pltpu.SMEM)]
        + [held] * (experts + 4),
        out_specs=[held] * 3,
        scratch_shapes=[
            pltpu.VMEM((count, nope), jnp.float32),
            pltpu.VMEM((count, wide - nope), jnp.bfloat16),
            pltpu.VMEM((count, max(chunk, 128)), jnp.float32),
            pltpu.VMEM(
                (sections, own.shape[0] * own.shape[1], w_turned.shape[1]), jnp.bfloat16
            ),
            pltpu.VMEM((experts,) + shape, jnp.bfloat16),
            pltpu.VMEM((experts, block, column), jnp.float32),
        ],
        compiler_params=params(*queries, w_uk, own, w_turned, scale=4),
        name="absorb_queries",
    )(*at_home(table), *queries, *at_home(w_uk, own, gain, w_turned))


def turn(values, cosine, sine):
    half = values.shape[1] // 2
    other = jnp.concatenate([values[:, half:], values[:, :half]], axis=1)
    return values * cosine + other * sine


def scaled(values, gain):
    scale = lax.rsqrt(jnp.mean(values * values, axis=-1, keepdims=True) + epsilon)
    return values * scale * gain.astype(jnp.float32)


def gather_kernel(
    prompts, experts, sections, sources, heads, steps, latent, length_ref, owner_ref, gain_ref,
    cosine_ref, sine_ref, block_ref, query_ref, query_rope_ref, recent_ref, recent_rope_ref,
    cosine_held, sine_held
):
    f32, bf16 = jnp.float32, jnp.bfloat16
    rows = steps * heads
    chunk = latent // experts
    first = lax.axis_index("expert") * sources + lax.axis_index("section") * prompts
    gain = gain_ref[...][None]
    for prompt in range(prompts):
        length, owner = length_ref[first + prompt], owner_ref[first + prompt]
        for step in range(steps):
            at = slice(step * heads, (step + 1) * heads)
            cosine_held[at, :] = jnp.broadcast_to(
                cosine_ref[pl.ds(length + step, 1), :], (heads, cosine_ref.shape[1])
            )
            sine_held[at, :] = jnp.broadcast_to(
                sine_ref[pl.ds(length + step, 1), :], (heads, sine_ref.shape[1])
            )
        cosine, sine = cosine_held[...], sine_held[...]
        at = slice(prompt * rows, (prompt + 1) * rows)
        for section in range(sections):
            pieces = [block_ref[i * sections + section, at, :] for i in range(experts)]
            to = slice(section * rows, (section + 1) * rows)
            query_ref[prompt, to, :] = jnp.concatenate(
                [piece[:, :chunk] for piece in pieces], axis=1
            )
            rope = jnp.concatenate([piece[:, chunk:].astype(f32) for piece in pieces], axis=1)
            query_rope_ref[prompt, to, :] = turn(rope, cosine, sine).astype(bf16)
        lines = 0
        for section in range(sections):
            lines = lines + block_ref[
                owner * sections + section, prompts * rows :, :
            ].astype(f32)
        recent, recent_rope = [], []
        for step in range(steps):
            line = jnp.concatenate(
                [lines[step * experts + part :][:1] for part in range(experts)], axis=1
            )
            recent.append(scaled(line[:, :latent], gain))
            at = slice(step * heads, step * heads + 1)
            recent_rope.append(turn(line[:, latent:], cosine[at], sine[at]))
        spare = recent_ref.shape[1] - steps
        recent.append(jnp.zeros((spare, latent), f32))
        recent_rope.append(jnp.zeros((spare, recent_rope[0].shape[1]), f32))
        recent_ref[prompt] = jnp.concatenate(recent, axis=0).astype(bf16)
        recent_rope_ref[prompt] = jnp.concatenate(recent_rope, axis=0).astype(bf16)


def gather_queries(blocks, lengths, owners, kv_gain, table, prompts, sources, experts, sections,
                   steps, heads):
    latent = kv_gain.shape[0]
    rope = blocks.shape[2] * experts - latent
    rows = sections * steps * heads
    spare = steps + -steps % 16
    shape = lambda *sizes: jax.ShapeDtypeStruct((prompts,) + sizes, jnp.bfloat16)
    held = pl.BlockSpec(memory_space=pltpu.VMEM)
    return pl.pallas_call(
        functools.partial(
            gather_kernel, prompts, experts, sections, sources, heads, steps, latent
        ),
        out_shape=[shape(rows, latent), shape(rows, rope), shape(spare, latent), shape(spare, rope)],
        in_specs=[pl.BlockSpec(memory_space=pltpu.SMEM)] * 2 + [held] * 4,
        out_specs=[held] * 4,
        scratch_shapes=[pltpu.VMEM((steps * heads, rope), jnp.float32)] * 2,
        compiler_params=params(blocks, scale=4),
        name="gather_queries",
    )(*at_home(lengths, owners, kv_gain, *table), blocks)


def attend_kernel(parts, positions, sections, sources, heads, steps, score_scale, *refs):
    part_refs = refs[:parts]
    (length_ref, gain_ref, cosine_ref, sine_ref, query_ref, query_rope_ref, recent_ref,
     recent_rope_ref) = refs[parts : parts + 8]
    out_refs, token_ref, held = refs[-2 - sections : -2], refs[-2], refs[-1]
    token_ref[...] = jnp.zeros_like(token_ref)
    f32, bf16 = jnp.float32, jnp.bfloat16
    nt = (((1,), (1,)), ((), ()))
    prompts, _, latent = query_ref.shape
    rows = steps * heads
    section_rank = lax.axis_index("section")
    first = lax.axis_index("expert") * sources + section_rank * prompts
    for prompt in range(prompts):
        at = slice(prompt * positions, (prompt + 1) * positions)
        projected = part_refs[0][at].astype(f32)
        for ref in part_refs[1:]:
            projected = projected + ref[at].astype(f32)
        keys = scaled(projected[:, :latent], gain_ref[...][None]).astype(bf16)
        key_rope = turn(
            projected[:, latent:], cosine_ref[:positions], sine_ref[:positions]
        ).astype(bf16)
        query, query_rope = query_ref[prompt], query_rope_ref[prompt]
        recent, recent_rope = recent_ref[prompt], recent_rope_ref[prompt]
        scores = lax.dot_general(query, keys, nt, preferred_element_type=f32)
        scores = scores + lax.dot_general(query_rope, key_rope, nt, preferred_element_type=f32)
        fresh = lax.dot_general(query, recent, nt, preferred_element_type=f32)
        fresh = fresh + lax.dot_general(query_rope, recent_rope, nt, preferred_element_type=f32)
        place = lax.broadcasted_iota(jnp.int32, scores.shape, 1)
        scores = jnp.where(
            place < length_ref[first + prompt], scores * score_scale, masked_value
        )
        row = lax.broadcasted_iota(jnp.int32, (rows, fresh.shape[1]), 0)
        place = lax.broadcasted_iota(jnp.int32, (rows, fresh.shape[1]), 1)
        seen = jnp.where(place < 1, 1.0, 0.0)
        for step in range(1, steps):
            seen = jnp.where((place <= step) & (row >= step * heads), 1.0, seen)
        seen = jnp.concatenate([seen] * sections, axis=0)
        fresh = jnp.where(seen > 0.5, fresh * score_scale, masked_value)
        most = jnp.maximum(
            jnp.max(scores, axis=-1, keepdims=True), jnp.max(fresh, axis=-1, keepdims=True)
        )
        scores = jnp.exp(scores - most)
        fresh = jnp.exp(fresh - most)
        total = jnp.sum(scores, axis=-1, keepdims=True) + jnp.sum(fresh, axis=-1, keepdims=True)
        scores = (scores / total).astype(bf16)
        fresh = (fresh / total).astype(bf16)
        mixed = jnp.dot(scores, keys, preferred_element_type=f32)
        mixed = mixed + jnp.dot(fresh, recent, preferred_element_type=f32)
        mixed = mixed.astype(bf16)
        for section in range(sections):
            held[section] = mixed[section * rows : (section + 1) * rows]
        for mask, ref in enumerate(out_refs):
            ref[prompt * rows : (prompt + 1) * rows, :] = held[section_rank ^ mask]


def attend(
    parts, positions, lengths, kv_gain, table, gathered, sources, steps, sections, score_scale
):
    prompts, rows, latent = gathered[0].shape
    out = (rows // sections, latent)
    held = pl.BlockSpec(memory_space=pltpu.VMEM)
    return pl.pallas_call(
        functools.partial(
            attend_kernel, len(parts), positions, sections, sources, out[0] // steps, steps,
            score_scale
        ),
        out_shape=[jax.ShapeDtypeStruct((prompts * out[0], latent), jnp.bfloat16)] * sections
        + [jax.ShapeDtypeStruct((8, 128), jnp.bfloat16)],
        in_specs=[held] * len(parts)
        + [pl.BlockSpec(memory_space=pltpu.SMEM)]
        + [held] * 7,
        out_specs=[held] * (sections + 1),
        scratch_shapes=[pltpu.VMEM((sections,) + out, jnp.bfloat16)],
        compiler_params=params(*parts, *gathered, scale=6),
        name="attend",
    )(*parts, *at_home(lengths, kv_gain, *table), *gathered)


def value_kernel(experts, sections, heads, steps, sources, *refs):
    owner_ref = refs[0]
    latent_refs, uv_refs = refs[1 : 1 + sections], refs[1 + sections : 1 + sections + experts]
    route_ref = refs[1 + sections + experts]
    out_ref, held = refs[-2:]
    f32, bf16 = jnp.float32, jnp.bfloat16
    chunk = uv_refs[0].shape[2]
    rows = latent_refs[0].shape[0]
    for mask, ref in enumerate(latent_refs):
        for index in range(experts):
            held[index, mask * rows : (mask + 1) * rows, :chunk] = ref[
                :, index * chunk : (index + 1) * chunk
            ].astype(f32)
    rank = lax.axis_index("expert")
    values = []
    for head in range(heads):
        at = pl.ds(head, sections * rows // heads, stride=heads)
        total = 0
        for mask, ref in enumerate(uv_refs):
            total = total + lax.dot_general(
                held[rank ^ mask, at, :][:, :chunk].astype(bf16),
                ref[head],
                (((1,), (1,)), ((), ())),
                preferred_element_type=f32,
            )
        values.append(total.astype(bf16))
    values = jnp.concatenate(values, axis=1)
    prompts = sources // sections
    section_rank = lax.axis_index("section")
    size = sources * steps
    to = lax.broadcasted_iota(jnp.int32, (size, size), 0)
    row = lax.broadcasted_iota(jnp.int32, (size, size), 1)
    order = jnp.zeros((size, size), f32)
    for mask in range(sections):
        for prompt in range(prompts):
            owner = owner_ref[
                rank * sources + (section_rank ^ mask) * prompts + prompt
            ]
            for step in range(steps):
                index = (mask * prompts + prompt) * steps + step
                order = jnp.where((row == index) & (to == owner * steps + step), 1.0, order)
    width = values.shape[1]
    out_ref[:, :width] = jnp.dot(
        order.astype(bf16), values, preferred_element_type=f32
    ).astype(bf16)
    out_ref[:, width:] = route_ref[...]


def head_products(owners, latents, uv_parts, route, steps, sources, after):
    rows, width = latents[0].shape
    heads, value, _ = uv_parts[0].shape
    held = pl.BlockSpec(memory_space=pltpu.VMEM)
    total = rows * len(latents)
    return pl.pallas_call(
        functools.partial(
            value_kernel, len(uv_parts), len(latents), heads, steps, sources
        ),
        out_shape=jax.ShapeDtypeStruct(
            (total // heads, heads * value + route.shape[1]), jnp.bfloat16
        ),
        in_specs=[pl.BlockSpec(memory_space=pltpu.SMEM)]
        + [held] * (len(latents) + len(uv_parts) + 1)
        + [pl.BlockSpec(memory_space=pl.ANY)] * len(after),
        out_specs=held,
        scratch_shapes=[
            pltpu.VMEM((len(uv_parts), total, max(width // len(uv_parts), 128)), jnp.float32)
        ],
        compiler_params=params(*latents, *uv_parts, scale=4),
        name="head_products",
    )(*at_home(owners), *latents, *uv_parts, route, *after)


def output_kernel(experts, *refs):
    value_refs = refs[:experts]
    weight_ref, out_ref = refs[experts:]
    depth = weight_ref.shape[0]
    values = jnp.concatenate([ref[:, :depth] for ref in value_refs], axis=0)
    rows = values.shape[0]
    to = lax.broadcasted_iota(jnp.int32, (rows, rows), 0)
    row = lax.broadcasted_iota(jnp.int32, (rows, rows), 1)
    source = (to & (experts - 1)) ^ lax.axis_index("expert")
    rest = lax.shift_right_logical(to, experts.bit_length() - 1)
    order = jnp.where(row == source * (rows // experts) + rest, 1.0, 0.0).astype(jnp.bfloat16)
    values = jnp.dot(order, values, preferred_element_type=jnp.float32).astype(jnp.bfloat16)
    out_ref[...] = jnp.dot(
        values, weight_ref[...], preferred_element_type=jnp.float32
    ).astype(out_ref.dtype)


def output_product(values, weight):
    rows = sum(value.shape[0] for value in values)
    held = pl.BlockSpec(memory_space=pltpu.VMEM)
    return pl.pallas_call(
        functools.partial(output_kernel, len(values)),
        out_shape=jax.ShapeDtypeStruct((rows, weight.shape[1]), jnp.bfloat16),
        in_specs=[held] * (len(values) + 1),
        out_specs=held,
        compiler_params=params(*values, scale=8),
        name="output_product",
    )(*values, weight)


def mix_kernel(count, owners, rows, *refs):
    part_refs, own_refs = refs[:count], refs[count : count + owners]
    out_ref, held = refs[-2:]
    f32 = jnp.float32
    total = part_refs[0][...].astype(f32)
    for ref in part_refs[1:]:
        total = total + ref[...].astype(f32)
    block, column = held.shape[1:]
    for owner in range(owners):
        held[owner] = total[owner * block : (owner + 1) * block]
    rank = lax.axis_index("expert")
    for mask, ref in enumerate(own_refs):
        lines = []
        for line, at in enumerate(range(0, column, ref.shape[1])):
            end = min(at + ref.shape[1], column)
            to = rows + line * block
            lines.append(ref[to : to + block, : end - at].astype(f32))
        lines = lines[0] if len(lines) == 1 else jnp.concatenate(lines, axis=1)
        out_ref[rank ^ mask] = (held[rank ^ mask] + lines).astype(out_ref.dtype)


def mix(parts, owns, rows, after):
    total, width = parts[0].shape
    owners = len(owns)
    held = pl.BlockSpec(memory_space=pltpu.VMEM)
    shape = (owners, total // owners, width)
    return pl.pallas_call(
        functools.partial(mix_kernel, len(parts), owners, rows),
        out_shape=jax.ShapeDtypeStruct(shape, parts[0].dtype),
        in_specs=[held] * (len(parts) + owners)
        + [pl.BlockSpec(memory_space=pl.ANY)] * len(after),
        out_specs=held,
        scratch_shapes=[pltpu.VMEM(shape, jnp.float32)],
        compiler_params=params(*parts, *owns, scale=4),
        name="mix",
    )(*parts, *owns, *after)


def expert_kernel(experts, sections, picks, *refs):
    mixed_refs, route_refs = refs[:experts], refs[experts : 2 * experts]
    gain_ref, gate_ref, up_ref, down_ref, out_ref, near_ref, columns = refs[2 * experts :]
    f32, bf16 = jnp.float32, jnp.bfloat16
    count = gate_ref.shape[0]
    rank = lax.axis_index("expert")
    width = gain_ref.shape[0]
    block = mixed_refs[0].shape[1]
    for mask, ref in enumerate(mixed_refs):
        columns[rank ^ mask] = ref[...]
    mixed, route = [], []
    for mask, ref in enumerate(route_refs):
        mixed.append(
            jnp.concatenate([columns[i, rank ^ mask] for i in range(experts)], axis=1).astype(f32)
        )
        route.append(ref[:, ref.shape[1] - 128 :].astype(f32))
    near = mixed[0]
    mixed = jnp.concatenate(mixed, axis=0)
    route = jnp.concatenate(route, axis=0)
    named = route[:, :picks]
    weights = route[:, picks : 2 * picks] + route[:, 2 * picks : 3 * picks]
    weights = route_scale * weights / jnp.sum(weights, axis=-1, keepdims=True)
    scale = lax.rsqrt(jnp.mean(mixed * mixed, axis=-1, keepdims=True) + epsilon)
    rows_in = (mixed * scale * gain_ref[...][None].astype(f32)).astype(bf16)
    column = width // sections
    total = 0
    for x in range(count):
        mine = (rank * count + x).astype(f32)
        weight = jnp.sum(jnp.where(named == mine, weights, 0.0), axis=-1, keepdims=True)
        gate = jnp.dot(rows_in, gate_ref[x], preferred_element_type=f32)
        up = jnp.dot(rows_in, up_ref[x], preferred_element_type=f32)
        inner = gate / (1.0 + jnp.exp(-gate)) * up * weight
        total = total + jnp.dot(inner.astype(bf16), down_ref[x], preferred_element_type=f32)
    for section in range(sections):
        at = slice(section * column, (section + 1) * column)
        near_ref[section] = near[:, at].astype(bf16)
        for mask in range(experts):
            out_ref[(rank ^ mask) * sections + section] = total[
                mask * block : (mask + 1) * block, at
            ].astype(bf16)


def run_experts(mixed, routes, gain, w_gate, w_up, w_down, picks, sections):
    experts = len(mixed)
    block = (mixed[0].shape[1], gain.shape[0] // sections)
    held = pl.BlockSpec(memory_space=pltpu.VMEM)
    return pl.pallas_call(
        functools.partial(expert_kernel, experts, sections, picks),
        out_shape=[
            jax.ShapeDtypeStruct((experts * sections,) + block, jnp.bfloat16),
            jax.ShapeDtypeStruct((sections,) + block, jnp.bfloat16),
        ],
        in_specs=[held] * (2 * experts + 4),
        out_specs=[held] * 2,
        scratch_shapes=[pltpu.VMEM((experts,) + mixed[0].shape, jnp.bfloat16)],
        compiler_params=params(*mixed, scale=32),
        name="run_experts",
    )(*mixed, *routes, *at_home(gain), w_gate, w_up, w_down)


def finish_kernel(block_ref, near_ref, out_ref):
    f32 = jnp.float32
    steps, sources, _ = out_ref.shape
    total = near_ref[lax.axis_index("section")].astype(f32)
    for index in range(block_ref.shape[0]):
        total = total + block_ref[index].astype(f32)
    for step in range(steps):
        out_ref[step] = total[step * sources : (step + 1) * sources].astype(out_ref.dtype)


def finish(blocks, near, steps):
    held = pl.BlockSpec(memory_space=pltpu.VMEM)
    _, rows, column = near.shape
    return pl.pallas_call(
        finish_kernel,
        out_shape=jax.ShapeDtypeStruct((steps, rows // steps, column), near.dtype),
        in_specs=[held] * 2,
        out_specs=held,
        compiler_params=params(blocks, near, scale=4),
        name="finish",
    )(blocks, near)


def local(
    prompts,
    owners,
    lengths,
    residual,
    queries,
    expert_ids,
    route_scores,
    attn_gain,
    w_dkv,
    kv_gain,
    w_uk,
    w_uv,
    w_o,
    moe_gain,
    w_gate,
    w_up,
    w_down,
):
    bf16, f32 = jnp.bfloat16, jnp.float32
    expert_rank = lax.axis_index("expert")
    section_rank = lax.axis_index("section")
    experts = lax.axis_size("expert")
    sections = lax.axis_size("section")
    prompt_count, full_length, width = prompts.shape
    steps, tokens_here, heads, _ = queries.shape
    latent = kv_gain.shape[0]
    cache_width = w_dkv.shape[1]
    rows = prompt_count * full_length
    own_rows = steps * tokens_here

    w_turned = w_dkv.T
    w_piece, *cut = cut_columns(
        prompts.reshape(rows, width), queries, w_turned, sections, experts
    )
    w_parts = spread(w_piece, "section")
    cut = deliver(cut, "expert")

    blocks, riders, token = absorb_queries(
        owners, cut, queries.shape, w_uk, residual, attn_gain, w_turned, prompt_count, sections
    )
    blocks = lax.all_to_all(blocks, ("expert", "section"), 0, 0, tiled=True)
    w_uv, token = lax.optimization_barrier((w_uv, token))
    masks = [1 << bit for bit in range(experts.bit_length() - 1)]
    uv_parts = doubled({0: w_uv}, "expert", masks[1:])

    away = list(project(cut[1:], riders, w_parts, 1, rows, [token]))
    near = list(project(cut[:1], riders, w_parts, 0, rows, away[:1]))
    parts = deliver(near + away, "expert")
    table = rotation(full_length + steps + -(full_length + steps) % 8, cache_width - latent)
    gathered = list(gather_queries(
        blocks, lengths, owners, kv_gain, table, prompt_count, tokens_here, experts, sections,
        steps, heads
    ))
    *out_latent, token = attend(
        parts, full_length, lengths, kv_gain, table, gathered, tokens_here, steps, sections,
        queries.shape[-1] ** (-0.5),
    )

    (w_gate,) = fetch([w_gate], [token])
    order = sorted(uv_parts)
    *uv_parts, token = lax.optimization_barrier((*[uv_parts[mask] for mask in order], token))
    uv_parts = doubled(dict(zip(order, uv_parts)), "expert", masks[:1])
    out_latent = deliver(out_latent, "section")
    high = route_scores.astype(bf16)
    low = (route_scores - high.astype(f32)).astype(bf16)
    route = jnp.concatenate([expert_ids.astype(bf16), high, low], axis=2).reshape(own_rows, -1)
    route = jnp.pad(route, ((0, 0), (0, 128 - route.shape[1])))
    head_values = head_products(
        owners, out_latent, [uv_parts[mask] for mask in range(experts)], route, steps,
        tokens_here, [w_gate, token],
    )
    head_values = spread(head_values, "expert")

    (w_o,) = fetch([w_o], [])
    attended = output_product(head_values, w_o)
    (w_up,) = fetch([w_up], [attended])
    mixed = mix(spread(attended, "section"), parts, rows, [w_up])
    (w_down,) = fetch([w_down], [mixed])
    blocks, near = run_experts(
        spread(mixed, "expert"),
        head_values,
        moe_gain,
        w_gate,
        w_up,
        w_down,
        expert_ids.shape[2],
        sections,
    )
    blocks = lax.all_to_all(blocks, ("expert", "section"), 0, 0, tiled=True)
    return finish(blocks, near, steps)


def solution(mesh):
    placed = (
        P(("groups", "expert", "section"), None, None),
        P("groups"),
        P("groups"),
        P(None, ("groups", "expert"), None),
        P(None, ("groups", "expert"), "section", None),
        P(None, ("groups", "expert"), None),
        P(None, ("groups", "expert"), None),
        P(),
        P("section", None),
        P(),
        P("section", None, "expert"),
        P("section", None, "expert"),
        P("section", "expert"),
        P(),
        P("expert", None, "section"),
        P("expert", None, "section"),
        P("expert", "section", None),
    )
    return jax.shard_map(
        local,
        mesh=mesh,
        in_specs=placed,
        out_specs=P(None, ("groups", "expert"), "section"),
        check_vma=False,
    )
```

```python
import functools
import math

import jax
import jax.numpy as jnp
import numpy as np
from jax import lax
from jax.experimental import pallas as pl
from jax.experimental.pallas import tpu as pltpu
from jax.sharding import PartitionSpec as P

epsilon = 1e-06
masked_value = -1e30
route_scale = 2.5


def rotation(positions, width):
    halfway = width // 2
    frequency = 10000.0 ** (-2.0 * np.arange(halfway) / width)
    angles = np.arange(positions)[:, None] * frequency
    cosine = np.concatenate([np.cos(angles), np.cos(angles)], axis=1)
    sine = np.concatenate([-np.sin(angles), np.sin(angles)], axis=1)
    return jnp.asarray(cosine, jnp.float32), jnp.asarray(sine, jnp.float32)


def swap(block, axis, mask):
    size = lax.axis_size(axis)
    return lax.ppermute(block, axis, [(i, i ^ mask) for i in range(size)])


def deliver(blocks, axis):
    return [blocks[0]] + [swap(blocks[mask], axis, mask) for mask in range(1, len(blocks))]


def spread(block, axis):
    return [block] + [swap(block, axis, mask) for mask in range(1, lax.axis_size(axis))]


def params(*arrays, scale=1):
    held = sum(math.prod(array.shape) * array.dtype.itemsize for array in arrays)
    mebibytes = min(56, 4 + scale * held // 1024 // 1024)
    return pltpu.CompilerParams(vmem_limit_bytes=mebibytes * 1024 * 1024)


def at_home(*arrays):
    return [pltpu.with_memory_space_constraint(array, pltpu.HBM) for array in arrays]


def fetch_kernel(count, *refs):
    out_refs, sems = refs[-1 - count : -1], refs[-1]
    copies = [
        pltpu.make_async_copy(refs[index], out_refs[index], sems.at[index])
        for index in range(count)
    ]
    for copy in copies:
        copy.start()
    for copy in copies:
        copy.wait()


def fetch(arrays, after):
    size = sum(array.size * array.dtype.itemsize for array in arrays)
    return pl.pallas_call(
        functools.partial(fetch_kernel, len(arrays)),
        out_shape=[pltpu.VMEM(array.shape, array.dtype) for array in arrays],
        in_specs=[pl.BlockSpec(memory_space=pltpu.HBM)] * len(arrays)
        + [pl.BlockSpec(memory_space=pl.ANY)] * len(after),
        out_specs=[pl.BlockSpec(memory_space=pltpu.VMEM)] * len(arrays),
        scratch_shapes=[pltpu.SemaphoreType.DMA((len(arrays),))],
        compiler_params=pltpu.CompilerParams(vmem_limit_bytes=1024 * 1024),
        cost_estimate=pl.CostEstimate(flops=0, bytes_accessed=2 * size, transcendentals=0),
        name="fetch",
    )(*at_home(*arrays), *after)


def doubled(held, axis, masks):
    held = dict(held)
    for mask in masks:
        for other in list(held):
            held[other ^ mask] = swap(held[other], axis, mask)
    return held


def cut_kernel(sections, experts, piece, x_ref, query_ref, w_ref, uv_ref, *refs):
    w_out_ref, *out_refs, w_held, held = refs
    rank = lax.axis_index("expert")
    steps, sources, heads, wide = query_ref.shape
    rows = x_ref.shape[0]
    for target in range(experts):
        w_held[target] = w_ref[:, target * piece : (target + 1) * piece]
    w_out_ref[...] = w_held[rank]
    for target in range(experts):
        for section in range(sections):
            at = (section * experts + target) * piece
            held[target, section * rows : (section + 1) * rows] = x_ref[:, at : at + piece]
    for mask, ref in enumerate(out_refs):
        ref[: sections * rows, :piece] = held[rank ^ mask]
        for step in range(steps):
            for source in range(sources):
                at = sections * rows + (step * sources + source) * heads
                ref[at : at + heads, :wide] = query_ref[step, source]
    ref = out_refs[experts // 2]
    heads, value, chunk = uv_ref.shape
    base = ref.shape[0] - heads // 2 * value
    for head in range(heads):
        at = base + head % (heads // 2) * value
        to = head // (heads // 2) * chunk
        ref[at : at + value, to : to + chunk] = uv_ref[head]


def cut_columns(x, queries, w_turned, w_uv, sections, experts):
    rows, width = x.shape
    piece = width // (sections * experts)
    steps, sources, heads, wide = queries.shape
    uv_heads, value, chunk = w_uv.shape
    lanes = max(piece, wide, 2 * chunk)
    block = jax.ShapeDtypeStruct((sections * rows + steps * sources * heads, lanes), x.dtype)
    tall = jax.ShapeDtypeStruct((block.shape[0] + uv_heads // 2 * value, lanes), x.dtype)
    return pl.pallas_call(
        functools.partial(cut_kernel, sections, experts, piece),
        out_shape=[jax.ShapeDtypeStruct((w_turned.shape[0], piece), x.dtype)]
        + [tall if mask == experts // 2 else block for mask in range(experts)],
        scratch_shapes=[
            pltpu.VMEM((experts, w_turned.shape[0], piece), x.dtype),
            pltpu.VMEM((experts, sections * rows, piece), x.dtype),
        ],
        compiler_params=params(x, block, w_turned, w_uv, scale=6),
        name="cut_columns",
    )(*at_home(x, queries, w_turned, w_uv))


def project_kernel(count, first, rows, *refs):
    x_refs, rider_ref, w_refs, out_refs = refs[:count], refs[count], refs[count + 1 :], refs[-count:]
    section_rank = lax.axis_index("section")
    sections = lax.axis_size("section")
    piece = w_refs[0].shape[1]
    total = 0
    for mask in range(sections):
        at = pl.ds(pl.multiple_of((section_rank ^ mask) * rows, rows), rows)
        x = jnp.concatenate([ref[at, :piece] for ref in x_refs], axis=0)
        total = total + lax.dot_general(
            x, w_refs[mask][...], (((1,), (1,)), ((), ())), preferred_element_type=jnp.float32
        )
    for index, ref in enumerate(out_refs):
        ref[:rows, :] = total[index * rows : (index + 1) * rows].astype(ref.dtype)
        ref[rows:, :] = rider_ref[first + index]


def project(blocks, riders, w_parts, first, rows, after):
    out = jax.ShapeDtypeStruct((rows + riders.shape[1], riders.shape[2]), jnp.bfloat16)
    held = pl.BlockSpec(memory_space=pltpu.VMEM)
    return pl.pallas_call(
        functools.partial(project_kernel, len(blocks), first, rows),
        out_shape=[out] * len(blocks),
        in_specs=[held] * (len(blocks) + 1 + len(w_parts))
        + [pl.BlockSpec(memory_space=pl.ANY)] * len(after),
        compiler_params=params(*blocks, *w_parts, scale=6),
        name="project",
    )(*blocks, riders, *w_parts, *after)


def query_kernel(
    experts, sections, prompts, nope, shape, base, *refs
):
    f32, bf16 = jnp.float32, jnp.bfloat16
    table_ref, query_refs = refs[0], refs[1 : 1 + experts]
    uk_ref, own_ref, gain_ref, wt_ref = refs[1 + experts : 5 + experts]
    out_ref, rider_ref, token_ref, picked, ropes, made, normed, query_ref, columns = refs[-9:]
    token_ref[...] = jnp.zeros_like(token_ref)
    steps, sources, heads, wide = shape
    rope = wide - nope
    chunk = uk_ref.shape[2]
    width = out_ref.shape[2]
    count = experts * sources
    block = prompts * steps * heads
    rank = lax.axis_index("expert")

    for mask, ref in enumerate(query_refs):
        for step in range(steps):
            for source in range(sources):
                at = base + (step * sources + source) * heads
                query_ref[rank ^ mask, step, source] = ref[at : at + heads, :wide]

    def pick(index, carry):
        owner = table_ref[index]
        for step in range(steps):
            value = query_ref[owner, step, index // sources].astype(f32)
            at = pl.ds(pl.multiple_of((index * steps + step) * heads, heads), heads)
            picked[at, :] = value[:, :nope]
            ropes[at, :] = value[:, nope:].astype(bf16)
        return carry

    if count <= 16:
        for index in range(count):
            pick(index, 0)
    else:
        lax.fori_loop(0, count, pick, 0)
    for head in range(heads):
        at = pl.ds(head, count * steps, stride=heads)
        value = jnp.dot(picked[at, :].astype(bf16), uk_ref[head], preferred_element_type=f32)
        if chunk < made.shape[1]:
            spare = jnp.zeros((count * steps, made.shape[1] - chunk), f32)
            value = jnp.concatenate([value, spare], axis=1)
        made[at, :] = value
    small = width - chunk
    pair = lax.broadcasted_iota(jnp.int32, (rope, small), 0)
    pair = pair == lax.broadcasted_iota(jnp.int32, (rope, small), 1) + rank * small
    turned = jnp.dot(
        ropes[...], jnp.where(pair, 1.0, 0.0).astype(bf16), preferred_element_type=f32
    )
    own = jnp.concatenate([own_ref[step] for step in range(steps)], axis=0).astype(f32)
    lines, column = columns.shape[1:]
    for target in range(experts):
        columns[target] = own[:, target * column : (target + 1) * column]
    for mask in range(experts):
        value = columns[rank ^ mask]
        for line, at in enumerate(range(0, column, rider_ref.shape[2])):
            end = min(at + rider_ref.shape[2], column)
            rider_ref[mask, line * lines : (line + 1) * lines, : end - at] = value[
                :, at:end
            ].astype(bf16)
    scale = lax.rsqrt(jnp.mean(own * own, axis=-1, keepdims=True) + epsilon)
    own = (own * scale * gain_ref[...][None].astype(f32)).astype(bf16)
    depth = wt_ref.shape[1]
    for section in range(sections):
        normed[section] = own[:, section * depth : (section + 1) * depth]
    fresh = lax.dot_general(
        normed[lax.axis_index("section")],
        wt_ref[...],
        (((1,), (1,)), ((), ())),
        preferred_element_type=f32,
    )
    for source in range(experts):
        lines = [
            fresh[step * sources + source :, part * width : (part + 1) * width][:1]
            for step in range(steps)
            for part in range(experts)
        ]
        lines = jnp.concatenate(lines, axis=0).astype(bf16)
        for section in range(sections):
            index = source * sections + section
            at = slice(index * block, (index + 1) * block)
            value = jnp.concatenate([made[at, :chunk], turned[at]], axis=1)
            out_ref[index, :block, :] = value.astype(bf16)
            out_ref[index, block:, :] = lines


def absorb_queries(table, queries, shape, w_uk, own, gain, w_turned, prompts, sections, after):
    experts = len(queries)
    steps, sources, heads, wide = shape
    _, nope, chunk = w_uk.shape
    width = chunk + (wide - nope) // experts
    block, column = own.shape[0] * own.shape[1], own.shape[2] // experts
    cache_width = w_turned.shape[0]
    rows = prompts * steps * heads + steps * experts
    count = experts * sources * steps * heads
    held = pl.BlockSpec(memory_space=pltpu.VMEM)
    return pl.pallas_call(
        functools.partial(
            query_kernel, experts, sections, prompts, nope, shape,
            queries[0].shape[0] - steps * sources * heads,
        ),
        out_shape=[
            jax.ShapeDtypeStruct((experts * sections, rows, width), jnp.bfloat16),
            jax.ShapeDtypeStruct(
                (experts, block * -(-column // cache_width), cache_width), jnp.bfloat16
            ),
            jax.ShapeDtypeStruct((8, 128), jnp.bfloat16),
        ],
        in_specs=[pl.BlockSpec(memory_space=pltpu.SMEM)]
        + [held] * (experts + 4)
        + [pl.BlockSpec(memory_space=pl.ANY)] * len(after),
        out_specs=[held] * 3,
        scratch_shapes=[
            pltpu.VMEM((count, nope), jnp.float32),
            pltpu.VMEM((count, wide - nope), jnp.bfloat16),
            pltpu.VMEM((count, max(chunk, 128)), jnp.float32),
            pltpu.VMEM(
                (sections, own.shape[0] * own.shape[1], w_turned.shape[1]), jnp.bfloat16
            ),
            pltpu.VMEM((experts,) + shape, jnp.bfloat16),
            pltpu.VMEM((experts, block, column), jnp.float32),
        ],
        compiler_params=params(*queries, w_uk, own, w_turned, scale=4),
        name="absorb_queries",
    )(*at_home(table), *queries, *at_home(w_uk, own, gain, w_turned), *after)


def turn(values, cosine, sine):
    half = values.shape[1] // 2
    other = jnp.concatenate([values[:, half:], values[:, :half]], axis=1)
    return values * cosine + other * sine


def scaled(values, gain):
    scale = lax.rsqrt(jnp.mean(values * values, axis=-1, keepdims=True) + epsilon)
    return values * scale * gain.astype(jnp.float32)


def gather_kernel(
    prompts, experts, sections, sources, heads, steps, latent, length_ref, owner_ref, gain_ref,
    cosine_ref, sine_ref, block_ref, query_ref, query_rope_ref, recent_ref, recent_rope_ref,
    cosine_held, sine_held
):
    f32, bf16 = jnp.float32, jnp.bfloat16
    rows = steps * heads
    chunk = latent // experts
    first = lax.axis_index("expert") * sources + lax.axis_index("section") * prompts
    gain = gain_ref[...][None]
    for prompt in range(prompts):
        length, owner = length_ref[first + prompt], owner_ref[first + prompt]
        for step in range(steps):
            at = slice(step * heads, (step + 1) * heads)
            cosine_held[at, :] = jnp.broadcast_to(
                cosine_ref[pl.ds(length + step, 1), :], (heads, cosine_ref.shape[1])
            )
            sine_held[at, :] = jnp.broadcast_to(
                sine_ref[pl.ds(length + step, 1), :], (heads, sine_ref.shape[1])
            )
        cosine, sine = cosine_held[...], sine_held[...]
        at = slice(prompt * rows, (prompt + 1) * rows)
        for section in range(sections):
            pieces = [block_ref[i * sections + section, at, :] for i in range(experts)]
            to = slice(section * rows, (section + 1) * rows)
            query_ref[prompt, to, :] = jnp.concatenate(
                [piece[:, :chunk] for piece in pieces], axis=1
            )
            rope = jnp.concatenate([piece[:, chunk:].astype(f32) for piece in pieces], axis=1)
            query_rope_ref[prompt, to, :] = turn(rope, cosine, sine).astype(bf16)
        lines = 0
        for section in range(sections):
            lines = lines + block_ref[
                owner * sections + section, prompts * rows :, :
            ].astype(f32)
        recent, recent_rope = [], []
        for step in range(steps):
            line = jnp.concatenate(
                [lines[step * experts + part :][:1] for part in range(experts)], axis=1
            )
            recent.append(scaled(line[:, :latent], gain))
            at = slice(step * heads, step * heads + 1)
            recent_rope.append(turn(line[:, latent:], cosine[at], sine[at]))
        spare = recent_ref.shape[1] - steps
        recent.append(jnp.zeros((spare, latent), f32))
        recent_rope.append(jnp.zeros((spare, recent_rope[0].shape[1]), f32))
        recent_ref[prompt] = jnp.concatenate(recent, axis=0).astype(bf16)
        recent_rope_ref[prompt] = jnp.concatenate(recent_rope, axis=0).astype(bf16)


def gather_queries(blocks, lengths, owners, kv_gain, table, prompts, sources, experts, sections,
                   steps, heads):
    latent = kv_gain.shape[0]
    rope = blocks.shape[2] * experts - latent
    rows = sections * steps * heads
    spare = steps + -steps % 16
    shape = lambda *sizes: jax.ShapeDtypeStruct((prompts,) + sizes, jnp.bfloat16)
    held = pl.BlockSpec(memory_space=pltpu.VMEM)
    return pl.pallas_call(
        functools.partial(
            gather_kernel, prompts, experts, sections, sources, heads, steps, latent
        ),
        out_shape=[shape(rows, latent), shape(rows, rope), shape(spare, latent), shape(spare, rope)],
        in_specs=[pl.BlockSpec(memory_space=pltpu.SMEM)] * 2 + [held] * 4,
        out_specs=[held] * 4,
        scratch_shapes=[pltpu.VMEM((steps * heads, rope), jnp.float32)] * 2,
        compiler_params=params(blocks, scale=4),
        name="gather_queries",
    )(*at_home(lengths, owners, kv_gain, *table), blocks)


def attend_kernel(parts, positions, sections, sources, heads, steps, score_scale, *refs):
    part_refs = refs[:parts]
    (length_ref, gain_ref, cosine_ref, sine_ref, query_ref, query_rope_ref, recent_ref,
     recent_rope_ref) = refs[parts : parts + 8]
    out_refs, token_ref, held = refs[-2 - sections : -2], refs[-2], refs[-1]
    token_ref[...] = jnp.zeros_like(token_ref)
    f32, bf16 = jnp.float32, jnp.bfloat16
    nt = (((1,), (1,)), ((), ()))
    prompts, _, latent = query_ref.shape
    rows = steps * heads
    section_rank = lax.axis_index("section")
    first = lax.axis_index("expert") * sources + section_rank * prompts
    for prompt in range(prompts):
        at = slice(prompt * positions, (prompt + 1) * positions)
        projected = part_refs[0][at].astype(f32)
        for ref in part_refs[1:]:
            projected = projected + ref[at].astype(f32)
        keys = scaled(projected[:, :latent], gain_ref[...][None]).astype(bf16)
        key_rope = turn(
            projected[:, latent:], cosine_ref[:positions], sine_ref[:positions]
        ).astype(bf16)
        query, query_rope = query_ref[prompt], query_rope_ref[prompt]
        recent, recent_rope = recent_ref[prompt], recent_rope_ref[prompt]
        scores = lax.dot_general(query, keys, nt, preferred_element_type=f32)
        scores = scores + lax.dot_general(query_rope, key_rope, nt, preferred_element_type=f32)
        fresh = lax.dot_general(query, recent, nt, preferred_element_type=f32)
        fresh = fresh + lax.dot_general(query_rope, recent_rope, nt, preferred_element_type=f32)
        place = lax.broadcasted_iota(jnp.int32, scores.shape, 1)
        scores = jnp.where(
            place < length_ref[first + prompt], scores * score_scale, masked_value
        )
        row = lax.broadcasted_iota(jnp.int32, (rows, fresh.shape[1]), 0)
        place = lax.broadcasted_iota(jnp.int32, (rows, fresh.shape[1]), 1)
        seen = jnp.where(place < 1, 1.0, 0.0)
        for step in range(1, steps):
            seen = jnp.where((place <= step) & (row >= step * heads), 1.0, seen)
        seen = jnp.concatenate([seen] * sections, axis=0)
        fresh = jnp.where(seen > 0.5, fresh * score_scale, masked_value)
        most = jnp.maximum(
            jnp.max(scores, axis=-1, keepdims=True), jnp.max(fresh, axis=-1, keepdims=True)
        )
        scores = jnp.exp(scores - most)
        fresh = jnp.exp(fresh - most)
        total = jnp.sum(scores, axis=-1, keepdims=True) + jnp.sum(fresh, axis=-1, keepdims=True)
        scores = (scores / total).astype(bf16)
        fresh = (fresh / total).astype(bf16)
        mixed = jnp.dot(scores, keys, preferred_element_type=f32)
        mixed = mixed + jnp.dot(fresh, recent, preferred_element_type=f32)
        mixed = mixed.astype(bf16)
        for section in range(sections):
            held[section] = mixed[section * rows : (section + 1) * rows]
        for mask, ref in enumerate(out_refs):
            ref[prompt * rows : (prompt + 1) * rows, :] = held[section_rank ^ mask]


def attend(
    parts, positions, lengths, kv_gain, table, gathered, sources, steps, sections, score_scale
):
    prompts, rows, latent = gathered[0].shape
    out = (rows // sections, latent)
    held = pl.BlockSpec(memory_space=pltpu.VMEM)
    return pl.pallas_call(
        functools.partial(
            attend_kernel, len(parts), positions, sections, sources, out[0] // steps, steps,
            score_scale
        ),
        out_shape=[jax.ShapeDtypeStruct((prompts * out[0], latent), jnp.bfloat16)] * sections
        + [jax.ShapeDtypeStruct((8, 128), jnp.bfloat16)],
        in_specs=[held] * len(parts)
        + [pl.BlockSpec(memory_space=pltpu.SMEM)]
        + [held] * 7,
        out_specs=[held] * (sections + 1),
        scratch_shapes=[pltpu.VMEM((sections,) + out, jnp.bfloat16)],
        compiler_params=params(*parts, *gathered, scale=6),
        name="attend",
    )(*parts, *at_home(lengths, kv_gain, *table), *gathered)


def value_kernel(experts, sections, heads, steps, sources, *refs):
    owner_ref = refs[0]
    latent_refs, uv_refs = refs[1 : 1 + sections], refs[1 + sections : 1 + sections + experts]
    route_ref = refs[1 + sections + experts]
    out_ref, held = refs[-2:]
    f32, bf16 = jnp.float32, jnp.bfloat16
    value, chunk = uv_refs[0].shape[1:]
    rows = latent_refs[0].shape[0]
    for mask, ref in enumerate(latent_refs):
        for index in range(experts):
            held[index, mask * rows : (mask + 1) * rows, :chunk] = ref[
                :, index * chunk : (index + 1) * chunk
            ].astype(f32)
    rank = lax.axis_index("expert")
    values = []
    for head in range(heads):
        at = pl.ds(head, sections * rows // heads, stride=heads)
        total = 0
        for mask, ref in enumerate(uv_refs):
            if len(ref.shape) == 3:
                weight = ref[head]
            else:
                low = ref.shape[0] - (heads // 2 - head % (heads // 2)) * value
                side = head // (heads // 2) * chunk
                weight = ref[low : low + value, side : side + chunk]
            total = total + lax.dot_general(
                held[rank ^ mask, at, :][:, :chunk].astype(bf16),
                weight,
                (((1,), (1,)), ((), ())),
                preferred_element_type=f32,
            )
        values.append(total.astype(bf16))
    values = jnp.concatenate(values, axis=1)
    prompts = sources // sections
    section_rank = lax.axis_index("section")
    size = sources * steps
    to = lax.broadcasted_iota(jnp.int32, (size, size), 0)
    row = lax.broadcasted_iota(jnp.int32, (size, size), 1)
    order = jnp.zeros((size, size), f32)
    for mask in range(sections):
        for prompt in range(prompts):
            owner = owner_ref[
                rank * sources + (section_rank ^ mask) * prompts + prompt
            ]
            for step in range(steps):
                index = (mask * prompts + prompt) * steps + step
                order = jnp.where((row == index) & (to == owner * steps + step), 1.0, order)
    width = values.shape[1]
    out_ref[:, :width] = jnp.dot(
        order.astype(bf16), values, preferred_element_type=f32
    ).astype(bf16)
    out_ref[:, width:] = route_ref[...]


def head_products(owners, latents, uv_parts, route, steps, sources, after):
    rows, width = latents[0].shape
    heads, value, _ = uv_parts[0].shape
    held = pl.BlockSpec(memory_space=pltpu.VMEM)
    total = rows * len(latents)
    return pl.pallas_call(
        functools.partial(
            value_kernel, len(uv_parts), len(latents), heads, steps, sources
        ),
        out_shape=jax.ShapeDtypeStruct(
            (total // heads, heads * value + route.shape[1]), jnp.bfloat16
        ),
        in_specs=[pl.BlockSpec(memory_space=pltpu.SMEM)]
        + [held] * (len(latents) + len(uv_parts) + 1)
        + [pl.BlockSpec(memory_space=pl.ANY)] * len(after),
        out_specs=held,
        scratch_shapes=[
            pltpu.VMEM((len(uv_parts), total, max(width // len(uv_parts), 128)), jnp.float32)
        ],
        compiler_params=params(*latents, *uv_parts, scale=4),
        name="head_products",
    )(*at_home(owners), *latents, *uv_parts, route, *after)


def output_kernel(experts, *refs):
    value_refs = refs[:experts]
    weight_ref, out_ref = refs[experts:]
    depth = weight_ref.shape[0]
    values = jnp.concatenate([ref[:, :depth] for ref in value_refs], axis=0)
    rows = values.shape[0]
    to = lax.broadcasted_iota(jnp.int32, (rows, rows), 0)
    row = lax.broadcasted_iota(jnp.int32, (rows, rows), 1)
    source = (to & (experts - 1)) ^ lax.axis_index("expert")
    rest = lax.shift_right_logical(to, experts.bit_length() - 1)
    order = jnp.where(row == source * (rows // experts) + rest, 1.0, 0.0).astype(jnp.bfloat16)
    values = jnp.dot(order, values, preferred_element_type=jnp.float32).astype(jnp.bfloat16)
    out_ref[...] = jnp.dot(
        values, weight_ref[...], preferred_element_type=jnp.float32
    ).astype(out_ref.dtype)


def output_product(values, weight):
    rows = sum(value.shape[0] for value in values)
    held = pl.BlockSpec(memory_space=pltpu.VMEM)
    return pl.pallas_call(
        functools.partial(output_kernel, len(values)),
        out_shape=jax.ShapeDtypeStruct((rows, weight.shape[1]), jnp.bfloat16),
        in_specs=[held] * (len(values) + 1),
        out_specs=held,
        compiler_params=params(*values, scale=8),
        name="output_product",
    )(*values, weight)


def mix_kernel(count, owners, rows, *refs):
    part_refs, own_refs = refs[:count], refs[count : count + owners]
    out_ref, held = refs[-2:]
    f32 = jnp.float32
    total = part_refs[0][...].astype(f32)
    for ref in part_refs[1:]:
        total = total + ref[...].astype(f32)
    block, column = held.shape[1:]
    for owner in range(owners):
        held[owner] = total[owner * block : (owner + 1) * block]
    rank = lax.axis_index("expert")
    for mask, ref in enumerate(own_refs):
        lines = []
        for line, at in enumerate(range(0, column, ref.shape[1])):
            end = min(at + ref.shape[1], column)
            to = rows + line * block
            lines.append(ref[to : to + block, : end - at].astype(f32))
        lines = lines[0] if len(lines) == 1 else jnp.concatenate(lines, axis=1)
        out_ref[rank ^ mask] = (held[rank ^ mask] + lines).astype(out_ref.dtype)


def mix(parts, owns, rows, after):
    total, width = parts[0].shape
    owners = len(owns)
    held = pl.BlockSpec(memory_space=pltpu.VMEM)
    shape = (owners, total // owners, width)
    return pl.pallas_call(
        functools.partial(mix_kernel, len(parts), owners, rows),
        out_shape=jax.ShapeDtypeStruct(shape, parts[0].dtype),
        in_specs=[held] * (len(parts) + owners)
        + [pl.BlockSpec(memory_space=pl.ANY)] * len(after),
        out_specs=held,
        scratch_shapes=[pltpu.VMEM(shape, jnp.float32)],
        compiler_params=params(*parts, *owns, scale=4),
        name="mix",
    )(*parts, *owns, *after)


def expert_kernel(experts, sections, picks, *refs):
    mixed_refs, route_refs = refs[:experts], refs[experts : 2 * experts]
    gain_ref, gate_ref, up_ref, down_ref, out_ref, near_ref, columns = refs[2 * experts :]
    f32, bf16 = jnp.float32, jnp.bfloat16
    count = gate_ref.shape[0]
    rank = lax.axis_index("expert")
    width = gain_ref.shape[0]
    block = mixed_refs[0].shape[1]
    for mask, ref in enumerate(mixed_refs):
        columns[rank ^ mask] = ref[...]
    mixed, route = [], []
    for mask, ref in enumerate(route_refs):
        mixed.append(
            jnp.concatenate([columns[i, rank ^ mask] for i in range(experts)], axis=1).astype(f32)
        )
        route.append(ref[:, ref.shape[1] - 128 :].astype(f32))
    near = mixed[0]
    mixed = jnp.concatenate(mixed, axis=0)
    route = jnp.concatenate(route, axis=0)
    named = route[:, :picks]
    weights = route[:, picks : 2 * picks] + route[:, 2 * picks : 3 * picks]
    weights = route_scale * weights / jnp.sum(weights, axis=-1, keepdims=True)
    scale = lax.rsqrt(jnp.mean(mixed * mixed, axis=-1, keepdims=True) + epsilon)
    rows_in = (mixed * scale * gain_ref[...][None].astype(f32)).astype(bf16)
    column = width // sections
    total = 0
    for x in range(count):
        mine = (rank * count + x).astype(f32)
        weight = jnp.sum(jnp.where(named == mine, weights, 0.0), axis=-1, keepdims=True)
        gate = jnp.dot(rows_in, gate_ref[x], preferred_element_type=f32)
        up = jnp.dot(rows_in, up_ref[x], preferred_element_type=f32)
        inner = gate / (1.0 + jnp.exp(-gate)) * up * weight
        total = total + jnp.dot(inner.astype(bf16), down_ref[x], preferred_element_type=f32)
    for section in range(sections):
        at = slice(section * column, (section + 1) * column)
        near_ref[section] = near[:, at].astype(bf16)
        for mask in range(experts):
            out_ref[(rank ^ mask) * sections + section] = total[
                mask * block : (mask + 1) * block, at
            ].astype(bf16)


def run_experts(mixed, routes, gain, w_gate, w_up, w_down, picks, sections):
    experts = len(mixed)
    block = (mixed[0].shape[1], gain.shape[0] // sections)
    held = pl.BlockSpec(memory_space=pltpu.VMEM)
    return pl.pallas_call(
        functools.partial(expert_kernel, experts, sections, picks),
        out_shape=[
            jax.ShapeDtypeStruct((experts * sections,) + block, jnp.bfloat16),
            jax.ShapeDtypeStruct((sections,) + block, jnp.bfloat16),
        ],
        in_specs=[held] * (2 * experts + 4),
        out_specs=[held] * 2,
        scratch_shapes=[pltpu.VMEM((experts,) + mixed[0].shape, jnp.bfloat16)],
        compiler_params=params(*mixed, scale=32),
        name="run_experts",
    )(*mixed, *routes, *at_home(gain), w_gate, w_up, w_down)


def finish_kernel(block_ref, near_ref, out_ref):
    f32 = jnp.float32
    steps, sources, _ = out_ref.shape
    total = near_ref[lax.axis_index("section")].astype(f32)
    for index in range(block_ref.shape[0]):
        total = total + block_ref[index].astype(f32)
    for step in range(steps):
        out_ref[step] = total[step * sources : (step + 1) * sources].astype(out_ref.dtype)


def finish(blocks, near, steps):
    held = pl.BlockSpec(memory_space=pltpu.VMEM)
    _, rows, column = near.shape
    return pl.pallas_call(
        finish_kernel,
        out_shape=jax.ShapeDtypeStruct((steps, rows // steps, column), near.dtype),
        in_specs=[held] * 2,
        out_specs=held,
        compiler_params=params(blocks, near, scale=4),
        name="finish",
    )(blocks, near)


def local(
    prompts,
    owners,
    lengths,
    residual,
    queries,
    expert_ids,
    route_scores,
    attn_gain,
    w_dkv,
    kv_gain,
    w_uk,
    w_uv,
    w_o,
    moe_gain,
    w_gate,
    w_up,
    w_down,
):
    bf16, f32 = jnp.bfloat16, jnp.float32
    expert_rank = lax.axis_index("expert")
    section_rank = lax.axis_index("section")
    experts = lax.axis_size("expert")
    sections = lax.axis_size("section")
    prompt_count, full_length, width = prompts.shape
    steps, tokens_here, heads, _ = queries.shape
    latent = kv_gain.shape[0]
    cache_width = w_dkv.shape[1]
    rows = prompt_count * full_length
    own_rows = steps * tokens_here

    w_turned = w_dkv.T
    w_piece, *cut = cut_columns(
        prompts.reshape(rows, width), queries, w_turned, w_uv, sections, experts
    )
    w_parts = spread(w_piece, "section")
    cut = deliver(cut, "expert")

    blocks, riders, token = absorb_queries(
        owners, cut, queries.shape, w_uk, residual, attn_gain, w_turned, prompt_count, sections,
        w_parts[1:],
    )
    blocks = lax.all_to_all(blocks, ("expert", "section"), 0, 0, tiled=True)
    away = list(project(cut[1:], riders, w_parts, 1, rows, [token]))
    near = list(project(cut[:1], riders, w_parts, 0, rows, away[:1]))
    parts = deliver(near + away, "expert")
    table = rotation(full_length + steps + -(full_length + steps) % 8, cache_width - latent)
    gathered = list(gather_queries(
        blocks, lengths, owners, kv_gain, table, prompt_count, tokens_here, experts, sections,
        steps, heads
    ))
    *out_latent, token = attend(
        parts, full_length, lengths, kv_gain, table, gathered, tokens_here, steps, sections,
        queries.shape[-1] ** (-0.5),
    )

    (w_gate,) = fetch([w_gate], [token])
    masks = [1 << bit for bit in range(experts.bit_length() - 1)]
    uv_parts = {0: w_uv, masks[-1]: cut[masks[-1]]}
    uv_parts = doubled(uv_parts, "expert", masks[1:-1] + masks[:1])
    out_latent = deliver(out_latent, "section")
    high = route_scores.astype(bf16)
    low = (route_scores - high.astype(f32)).astype(bf16)
    route = jnp.concatenate([expert_ids.astype(bf16), high, low], axis=2).reshape(own_rows, -1)
    route = jnp.pad(route, ((0, 0), (0, 128 - route.shape[1])))
    head_values = head_products(
        owners, out_latent, [uv_parts[mask] for mask in range(experts)], route, steps,
        tokens_here, [w_gate, token],
    )
    head_values = spread(head_values, "expert")

    (w_o,) = fetch([w_o], [])
    attended = output_product(head_values, w_o)
    (w_up,) = fetch([w_up], [attended])
    mixed = mix(spread(attended, "section"), parts, rows, [w_up])
    (w_down,) = fetch([w_down], [mixed])
    blocks, near = run_experts(
        spread(mixed, "expert"),
        head_values,
        moe_gain,
        w_gate,
        w_up,
        w_down,
        expert_ids.shape[2],
        sections,
    )
    blocks = lax.all_to_all(blocks, ("expert", "section"), 0, 0, tiled=True)
    return finish(blocks, near, steps)


def solution(mesh):
    placed = (
        P(("groups", "expert", "section"), None, None),
        P("groups"),
        P("groups"),
        P(None, ("groups", "expert"), None),
        P(None, ("groups", "expert"), "section", None),
        P(None, ("groups", "expert"), None),
        P(None, ("groups", "expert"), None),
        P(),
        P("section", None),
        P(),
        P("section", None, "expert"),
        P("section", None, "expert"),
        P("section", "expert"),
        P(),
        P("expert", None, "section"),
        P("expert", None, "section"),
        P("expert", "section", None),
    )
    return jax.shard_map(
        local,
        mesh=mesh,
        in_specs=placed,
        out_specs=P(None, ("groups", "expert"), "section"),
        check_vma=False,
    )
```

```python
import functools
import math

import jax
import jax.numpy as jnp
import numpy as np
from jax import lax
from jax.experimental import pallas as pl
from jax.experimental.pallas import tpu as pltpu
from jax.sharding import PartitionSpec as P

epsilon = 1e-06
masked_value = -1e30
route_scale = 2.5


def rotation(positions, width):
    halfway = width // 2
    frequency = 10000.0 ** (-2.0 * np.arange(halfway) / width)
    angles = np.arange(positions)[:, None] * frequency
    cosine = np.concatenate([np.cos(angles), np.cos(angles)], axis=1)
    sine = np.concatenate([-np.sin(angles), np.sin(angles)], axis=1)
    return jnp.asarray(cosine, jnp.float32), jnp.asarray(sine, jnp.float32)


def swap(block, axis, mask):
    size = lax.axis_size(axis)
    return lax.ppermute(block, axis, [(i, i ^ mask) for i in range(size)])


def deliver(blocks, axis):
    return [blocks[0]] + [swap(blocks[mask], axis, mask) for mask in range(1, len(blocks))]


def spread(block, axis):
    return [block] + [swap(block, axis, mask) for mask in range(1, lax.axis_size(axis))]


def params(*arrays, scale=1):
    held = sum(math.prod(array.shape) * array.dtype.itemsize for array in arrays)
    mebibytes = min(56, 4 + scale * held // 1024 // 1024)
    return pltpu.CompilerParams(vmem_limit_bytes=mebibytes * 1024 * 1024)


def at_home(*arrays):
    return [pltpu.with_memory_space_constraint(array, pltpu.HBM) for array in arrays]


def fetch_kernel(count, *refs):
    out_refs, sems = refs[-1 - count : -1], refs[-1]
    copies = [
        pltpu.make_async_copy(refs[index], out_refs[index], sems.at[index])
        for index in range(count)
    ]
    for copy in copies:
        copy.start()
    for copy in copies:
        copy.wait()


def fetch(arrays, after):
    size = sum(array.size * array.dtype.itemsize for array in arrays)
    return pl.pallas_call(
        functools.partial(fetch_kernel, len(arrays)),
        out_shape=[pltpu.VMEM(array.shape, array.dtype) for array in arrays],
        in_specs=[pl.BlockSpec(memory_space=pltpu.HBM)] * len(arrays)
        + [pl.BlockSpec(memory_space=pl.ANY)] * len(after),
        out_specs=[pl.BlockSpec(memory_space=pltpu.VMEM)] * len(arrays),
        scratch_shapes=[pltpu.SemaphoreType.DMA((len(arrays),))],
        compiler_params=pltpu.CompilerParams(vmem_limit_bytes=1024 * 1024),
        cost_estimate=pl.CostEstimate(flops=0, bytes_accessed=2 * size, transcendentals=0),
        name="fetch",
    )(*at_home(*arrays), *after)


def doubled(held, axis, masks):
    held = dict(held)
    for mask in masks:
        for other in list(held):
            held[other ^ mask] = swap(held[other], axis, mask)
    return held


def cut_kernel(sections, experts, piece, x_ref, query_ref, w_ref, uv_ref, *refs):
    w_out_ref, *out_refs, w_held, held = refs
    rank = lax.axis_index("expert")
    steps, sources, heads, wide = query_ref.shape
    rows = x_ref.shape[0]
    for target in range(experts):
        w_held[target] = w_ref[:, target * piece : (target + 1) * piece]
    w_out_ref[...] = w_held[rank]
    for target in range(experts):
        for section in range(sections):
            at = (section * experts + target) * piece
            held[target, section * rows : (section + 1) * rows] = x_ref[:, at : at + piece]
    for mask, ref in enumerate(out_refs):
        ref[: sections * rows, :piece] = held[rank ^ mask]
        for step in range(steps):
            for source in range(sources):
                at = sections * rows + (step * sources + source) * heads
                ref[at : at + heads, :wide] = query_ref[step, source]
    ref = out_refs[experts // 2]
    heads, value, chunk = uv_ref.shape
    base = ref.shape[0] - heads // 2 * value
    for head in range(heads):
        at = base + head % (heads // 2) * value
        to = head // (heads // 2) * chunk
        ref[at : at + value, to : to + chunk] = uv_ref[head]


def cut_columns(x, queries, w_turned, w_uv, sections, experts):
    rows, width = x.shape
    piece = width // (sections * experts)
    steps, sources, heads, wide = queries.shape
    uv_heads, value, chunk = w_uv.shape
    lanes = max(piece, wide, 2 * chunk)
    block = jax.ShapeDtypeStruct((sections * rows + steps * sources * heads, lanes), x.dtype)
    tall = jax.ShapeDtypeStruct((block.shape[0] + uv_heads // 2 * value, lanes), x.dtype)
    return pl.pallas_call(
        functools.partial(cut_kernel, sections, experts, piece),
        out_shape=[jax.ShapeDtypeStruct((w_turned.shape[0], piece), x.dtype)]
        + [tall if mask == experts // 2 else block for mask in range(experts)],
        scratch_shapes=[
            pltpu.VMEM((experts, w_turned.shape[0], piece), x.dtype),
            pltpu.VMEM((experts, sections * rows, piece), x.dtype),
        ],
        compiler_params=params(x, block, w_turned, w_uv, scale=6),
        name="cut_columns",
    )(*at_home(x, queries, w_turned, w_uv))


def project_kernel(count, first, rows, *refs):
    x_refs, rider_ref, w_refs, out_refs = refs[:count], refs[count], refs[count + 1 :], refs[-count:]
    section_rank = lax.axis_index("section")
    sections = lax.axis_size("section")
    piece = w_refs[0].shape[1]
    total = 0
    for mask in range(sections):
        at = pl.ds(pl.multiple_of((section_rank ^ mask) * rows, rows), rows)
        x = jnp.concatenate([ref[at, :piece] for ref in x_refs], axis=0)
        total = total + lax.dot_general(
            x, w_refs[mask][...], (((1,), (1,)), ((), ())), preferred_element_type=jnp.float32
        )
    for index, ref in enumerate(out_refs):
        ref[:rows, :] = total[index * rows : (index + 1) * rows].astype(ref.dtype)
        ref[rows:, :] = rider_ref[first + index]


def project(blocks, riders, w_parts, first, rows, after):
    out = jax.ShapeDtypeStruct((rows + riders.shape[1], riders.shape[2]), jnp.bfloat16)
    held = pl.BlockSpec(memory_space=pltpu.VMEM)
    return pl.pallas_call(
        functools.partial(project_kernel, len(blocks), first, rows),
        out_shape=[out] * len(blocks),
        in_specs=[held] * (len(blocks) + 1 + len(w_parts))
        + [pl.BlockSpec(memory_space=pl.ANY)] * len(after),
        compiler_params=params(*blocks, *w_parts, scale=6),
        name="project",
    )(*blocks, riders, *w_parts, *after)


def query_kernel(
    experts, sections, prompts, nope, shape, base, *refs
):
    f32, bf16 = jnp.float32, jnp.bfloat16
    table_ref, query_refs = refs[0], refs[1 : 1 + experts]
    uk_ref, own_ref, gain_ref, wt_ref = refs[1 + experts : 5 + experts]
    out_ref, rider_ref, token_ref, picked, ropes, made, normed, query_ref, columns = refs[-9:]
    token_ref[...] = jnp.zeros_like(token_ref)
    steps, sources, heads, wide = shape
    rope = wide - nope
    chunk = uk_ref.shape[2]
    width = out_ref.shape[2]
    count = experts * sources
    block = prompts * steps * heads
    rank = lax.axis_index("expert")

    for mask, ref in enumerate(query_refs):
        for step in range(steps):
            for source in range(sources):
                at = base + (step * sources + source) * heads
                query_ref[rank ^ mask, step, source] = ref[at : at + heads, :wide]

    def pick(index, carry):
        owner = table_ref[index]
        for step in range(steps):
            value = query_ref[owner, step, index // sources].astype(f32)
            at = pl.ds(pl.multiple_of((index * steps + step) * heads, heads), heads)
            picked[at, :] = value[:, :nope]
            ropes[at, :] = value[:, nope:].astype(bf16)
        return carry

    if count <= 16:
        for index in range(count):
            pick(index, 0)
    else:
        lax.fori_loop(0, count, pick, 0)
    for head in range(heads):
        at = pl.ds(head, count * steps, stride=heads)
        value = jnp.dot(picked[at, :].astype(bf16), uk_ref[head], preferred_element_type=f32)
        if chunk < made.shape[1]:
            spare = jnp.zeros((count * steps, made.shape[1] - chunk), f32)
            value = jnp.concatenate([value, spare], axis=1)
        made[at, :] = value
    small = width - chunk
    pair = lax.broadcasted_iota(jnp.int32, (rope, small), 0)
    pair = pair == lax.broadcasted_iota(jnp.int32, (rope, small), 1) + rank * small
    turned = jnp.dot(
        ropes[...], jnp.where(pair, 1.0, 0.0).astype(bf16), preferred_element_type=f32
    )
    own = jnp.concatenate([own_ref[step] for step in range(steps)], axis=0).astype(f32)
    lines, column = columns.shape[1:]
    for target in range(experts):
        columns[target] = own[:, target * column : (target + 1) * column]
    for mask in range(experts):
        value = columns[rank ^ mask]
        for line, at in enumerate(range(0, column, rider_ref.shape[2])):
            end = min(at + rider_ref.shape[2], column)
            rider_ref[mask, line * lines : (line + 1) * lines, : end - at] = value[
                :, at:end
            ].astype(bf16)
    scale = lax.rsqrt(jnp.mean(own * own, axis=-1, keepdims=True) + epsilon)
    own = (own * scale * gain_ref[...][None].astype(f32)).astype(bf16)
    depth = wt_ref.shape[1]
    for section in range(sections):
        normed[section] = own[:, section * depth : (section + 1) * depth]
    fresh = lax.dot_general(
        normed[lax.axis_index("section")],
        wt_ref[...],
        (((1,), (1,)), ((), ())),
        preferred_element_type=f32,
    )
    for source in range(experts):
        lines = [
            fresh[step * sources + source :, part * width : (part + 1) * width][:1]
            for step in range(steps)
            for part in range(experts)
        ]
        lines = jnp.concatenate(lines, axis=0).astype(bf16)
        for section in range(sections):
            index = source * sections + section
            at = slice(index * block, (index + 1) * block)
            value = jnp.concatenate([made[at, :chunk], turned[at]], axis=1)
            out_ref[index, :block, :] = value.astype(bf16)
            out_ref[index, block:, :] = lines


def absorb_queries(table, queries, shape, w_uk, own, gain, w_turned, prompts, sections, after):
    experts = len(queries)
    steps, sources, heads, wide = shape
    _, nope, chunk = w_uk.shape
    width = chunk + (wide - nope) // experts
    block, column = own.shape[0] * own.shape[1], own.shape[2] // experts
    cache_width = w_turned.shape[0]
    rows = prompts * steps * heads + steps * experts
    count = experts * sources * steps * heads
    held = pl.BlockSpec(memory_space=pltpu.VMEM)
    return pl.pallas_call(
        functools.partial(
            query_kernel, experts, sections, prompts, nope, shape,
            queries[0].shape[0] - steps * sources * heads,
        ),
        out_shape=[
            jax.ShapeDtypeStruct((experts * sections, rows, width), jnp.bfloat16),
            jax.ShapeDtypeStruct(
                (experts, block * -(-column // cache_width), cache_width), jnp.bfloat16
            ),
            jax.ShapeDtypeStruct((8, 128), jnp.bfloat16),
        ],
        in_specs=[pl.BlockSpec(memory_space=pltpu.SMEM)]
        + [held] * (experts + 4)
        + [pl.BlockSpec(memory_space=pl.ANY)] * len(after),
        out_specs=[held] * 3,
        scratch_shapes=[
            pltpu.VMEM((count, nope), jnp.float32),
            pltpu.VMEM((count, wide - nope), jnp.bfloat16),
            pltpu.VMEM((count, max(chunk, 128)), jnp.float32),
            pltpu.VMEM(
                (sections, own.shape[0] * own.shape[1], w_turned.shape[1]), jnp.bfloat16
            ),
            pltpu.VMEM((experts,) + shape, jnp.bfloat16),
            pltpu.VMEM((experts, block, column), jnp.float32),
        ],
        compiler_params=params(*queries, w_uk, own, w_turned, scale=4),
        name="absorb_queries",
    )(*at_home(table), *queries, *at_home(w_uk, own, gain, w_turned), *after)


def turn(values, cosine, sine):
    half = values.shape[1] // 2
    other = jnp.concatenate([values[:, half:], values[:, :half]], axis=1)
    return values * cosine + other * sine


def scaled(values, gain):
    scale = lax.rsqrt(jnp.mean(values * values, axis=-1, keepdims=True) + epsilon)
    return values * scale * gain.astype(jnp.float32)


def gather_kernel(
    prompts, experts, sections, sources, heads, steps, latent, length_ref, owner_ref, gain_ref,
    cosine_ref, sine_ref, block_ref, query_ref, query_rope_ref, recent_ref, recent_rope_ref,
    cosine_held, sine_held
):
    f32, bf16 = jnp.float32, jnp.bfloat16
    rows = steps * heads
    chunk = latent // experts
    first = lax.axis_index("expert") * sources + lax.axis_index("section") * prompts
    gain = gain_ref[...][None]
    for prompt in range(prompts):
        length, owner = length_ref[first + prompt], owner_ref[first + prompt]
        for step in range(steps):
            at = slice(step * heads, (step + 1) * heads)
            cosine_held[at, :] = jnp.broadcast_to(
                cosine_ref[pl.ds(length + step, 1), :], (heads, cosine_ref.shape[1])
            )
            sine_held[at, :] = jnp.broadcast_to(
                sine_ref[pl.ds(length + step, 1), :], (heads, sine_ref.shape[1])
            )
        cosine, sine = cosine_held[...], sine_held[...]
        at = slice(prompt * rows, (prompt + 1) * rows)
        for section in range(sections):
            pieces = [block_ref[i * sections + section, at, :] for i in range(experts)]
            to = slice(section * rows, (section + 1) * rows)
            query_ref[prompt, to, :] = jnp.concatenate(
                [piece[:, :chunk] for piece in pieces], axis=1
            )
            rope = jnp.concatenate([piece[:, chunk:].astype(f32) for piece in pieces], axis=1)
            query_rope_ref[prompt, to, :] = turn(rope, cosine, sine).astype(bf16)
        lines = 0
        for section in range(sections):
            lines = lines + block_ref[
                owner * sections + section, prompts * rows :, :
            ].astype(f32)
        recent, recent_rope = [], []
        for step in range(steps):
            line = jnp.concatenate(
                [lines[step * experts + part :][:1] for part in range(experts)], axis=1
            )
            recent.append(scaled(line[:, :latent], gain))
            at = slice(step * heads, step * heads + 1)
            recent_rope.append(turn(line[:, latent:], cosine[at], sine[at]))
        spare = recent_ref.shape[1] - steps
        recent.append(jnp.zeros((spare, latent), f32))
        recent_rope.append(jnp.zeros((spare, recent_rope[0].shape[1]), f32))
        recent_ref[prompt] = jnp.concatenate(recent, axis=0).astype(bf16)
        recent_rope_ref[prompt] = jnp.concatenate(recent_rope, axis=0).astype(bf16)


def gather_queries(blocks, lengths, owners, kv_gain, table, prompts, sources, experts, sections,
                   steps, heads):
    latent = kv_gain.shape[0]
    rope = blocks.shape[2] * experts - latent
    rows = sections * steps * heads
    spare = steps + -steps % 16
    shape = lambda *sizes: jax.ShapeDtypeStruct((prompts,) + sizes, jnp.bfloat16)
    held = pl.BlockSpec(memory_space=pltpu.VMEM)
    return pl.pallas_call(
        functools.partial(
            gather_kernel, prompts, experts, sections, sources, heads, steps, latent
        ),
        out_shape=[shape(rows, latent), shape(rows, rope), shape(spare, latent), shape(spare, rope)],
        in_specs=[pl.BlockSpec(memory_space=pltpu.SMEM)] * 2 + [held] * 4,
        out_specs=[held] * 4,
        scratch_shapes=[pltpu.VMEM((steps * heads, rope), jnp.float32)] * 2,
        compiler_params=params(blocks, scale=4),
        name="gather_queries",
    )(*at_home(lengths, owners, kv_gain, *table), blocks)


def attend_kernel(parts, positions, sections, sources, heads, steps, score_scale, *refs):
    part_refs = refs[:parts]
    (length_ref, gain_ref, cosine_ref, sine_ref, query_ref, query_rope_ref, recent_ref,
     recent_rope_ref) = refs[parts : parts + 8]
    out_refs, token_ref, held = refs[-2 - sections : -2], refs[-2], refs[-1]
    token_ref[...] = jnp.zeros_like(token_ref)
    f32, bf16 = jnp.float32, jnp.bfloat16
    nt = (((1,), (1,)), ((), ()))
    prompts, _, latent = query_ref.shape
    rows = steps * heads
    section_rank = lax.axis_index("section")
    first = lax.axis_index("expert") * sources + section_rank * prompts
    for prompt in range(prompts):
        at = slice(prompt * positions, (prompt + 1) * positions)
        projected = part_refs[0][at].astype(f32)
        for ref in part_refs[1:]:
            projected = projected + ref[at].astype(f32)
        keys = scaled(projected[:, :latent], gain_ref[...][None]).astype(bf16)
        key_rope = turn(
            projected[:, latent:], cosine_ref[:positions], sine_ref[:positions]
        ).astype(bf16)
        query, query_rope = query_ref[prompt], query_rope_ref[prompt]
        recent, recent_rope = recent_ref[prompt], recent_rope_ref[prompt]
        scores = lax.dot_general(query, keys, nt, preferred_element_type=f32)
        scores = scores + lax.dot_general(query_rope, key_rope, nt, preferred_element_type=f32)
        fresh = lax.dot_general(query, recent, nt, preferred_element_type=f32)
        fresh = fresh + lax.dot_general(query_rope, recent_rope, nt, preferred_element_type=f32)
        place = lax.broadcasted_iota(jnp.int32, scores.shape, 1)
        scores = jnp.where(
            place < length_ref[first + prompt], scores * score_scale, masked_value
        )
        row = lax.broadcasted_iota(jnp.int32, (rows, fresh.shape[1]), 0)
        place = lax.broadcasted_iota(jnp.int32, (rows, fresh.shape[1]), 1)
        seen = jnp.where(place < 1, 1.0, 0.0)
        for step in range(1, steps):
            seen = jnp.where((place <= step) & (row >= step * heads), 1.0, seen)
        seen = jnp.concatenate([seen] * sections, axis=0)
        fresh = jnp.where(seen > 0.5, fresh * score_scale, masked_value)
        most = jnp.maximum(
            jnp.max(scores, axis=-1, keepdims=True), jnp.max(fresh, axis=-1, keepdims=True)
        )
        scores = jnp.exp(scores - most)
        fresh = jnp.exp(fresh - most)
        total = jnp.sum(scores, axis=-1, keepdims=True) + jnp.sum(fresh, axis=-1, keepdims=True)
        scores = (scores / total).astype(bf16)
        fresh = (fresh / total).astype(bf16)
        mixed = jnp.dot(scores, keys, preferred_element_type=f32)
        mixed = mixed + jnp.dot(fresh, recent, preferred_element_type=f32)
        mixed = mixed.astype(bf16)
        for section in range(sections):
            held[section] = mixed[section * rows : (section + 1) * rows]
        for mask, ref in enumerate(out_refs):
            ref[prompt * rows : (prompt + 1) * rows, :] = held[section_rank ^ mask]


def attend(
    parts, positions, lengths, kv_gain, table, gathered, sources, steps, sections, score_scale
):
    prompts, rows, latent = gathered[0].shape
    out = (rows // sections, latent)
    held = pl.BlockSpec(memory_space=pltpu.VMEM)
    return pl.pallas_call(
        functools.partial(
            attend_kernel, len(parts), positions, sections, sources, out[0] // steps, steps,
            score_scale
        ),
        out_shape=[jax.ShapeDtypeStruct((prompts * out[0], latent), jnp.bfloat16)] * sections
        + [jax.ShapeDtypeStruct((8, 128), jnp.bfloat16)],
        in_specs=[held] * len(parts)
        + [pl.BlockSpec(memory_space=pltpu.SMEM)]
        + [held] * 7,
        out_specs=[held] * (sections + 1),
        scratch_shapes=[pltpu.VMEM((sections,) + out, jnp.bfloat16)],
        compiler_params=params(*parts, *gathered, scale=6),
        name="attend",
    )(*parts, *at_home(lengths, kv_gain, *table), *gathered)


def value_kernel(experts, sections, heads, steps, sources, *refs):
    owner_ref = refs[0]
    latent_refs, uv_refs = refs[1 : 1 + sections], refs[1 + sections : 1 + sections + experts]
    route_ref = refs[1 + sections + experts]
    out_ref, held = refs[-2:]
    f32, bf16 = jnp.float32, jnp.bfloat16
    value, chunk = uv_refs[0].shape[1:]
    rows = latent_refs[0].shape[0]
    for mask, ref in enumerate(latent_refs):
        for index in range(experts):
            held[index, mask * rows : (mask + 1) * rows, :chunk] = ref[
                :, index * chunk : (index + 1) * chunk
            ].astype(f32)
    rank = lax.axis_index("expert")
    values = []
    for head in range(heads):
        at = pl.ds(head, sections * rows // heads, stride=heads)
        total = 0
        for mask, ref in enumerate(uv_refs):
            if len(ref.shape) == 3:
                weight = ref[head]
            else:
                low = ref.shape[0] - (heads // 2 - head % (heads // 2)) * value
                side = head // (heads // 2) * chunk
                weight = ref[low : low + value, side : side + chunk]
            total = total + lax.dot_general(
                held[rank ^ mask, at, :][:, :chunk].astype(bf16),
                weight,
                (((1,), (1,)), ((), ())),
                preferred_element_type=f32,
            )
        values.append(total.astype(bf16))
    values = jnp.concatenate(values, axis=1)
    prompts = sources // sections
    section_rank = lax.axis_index("section")
    size = sources * steps
    to = lax.broadcasted_iota(jnp.int32, (size, size), 0)
    row = lax.broadcasted_iota(jnp.int32, (size, size), 1)
    order = jnp.zeros((size, size), f32)
    for mask in range(sections):
        for prompt in range(prompts):
            owner = owner_ref[
                rank * sources + (section_rank ^ mask) * prompts + prompt
            ]
            for step in range(steps):
                index = (mask * prompts + prompt) * steps + step
                order = jnp.where((row == index) & (to == owner * steps + step), 1.0, order)
    width = values.shape[1]
    out_ref[:, :width] = jnp.dot(
        order.astype(bf16), values, preferred_element_type=f32
    ).astype(bf16)
    out_ref[:, width:] = route_ref[...]


def head_products(owners, latents, uv_parts, route, steps, sources, after):
    rows, width = latents[0].shape
    heads, value, _ = uv_parts[0].shape
    held = pl.BlockSpec(memory_space=pltpu.VMEM)
    total = rows * len(latents)
    return pl.pallas_call(
        functools.partial(
            value_kernel, len(uv_parts), len(latents), heads, steps, sources
        ),
        out_shape=jax.ShapeDtypeStruct(
            (total // heads, heads * value + route.shape[1]), jnp.bfloat16
        ),
        in_specs=[pl.BlockSpec(memory_space=pltpu.SMEM)]
        + [held] * (len(latents) + len(uv_parts) + 1)
        + [pl.BlockSpec(memory_space=pl.ANY)] * len(after),
        out_specs=held,
        scratch_shapes=[
            pltpu.VMEM((len(uv_parts), total, max(width // len(uv_parts), 128)), jnp.float32)
        ],
        compiler_params=params(*latents, *uv_parts, scale=4),
        name="head_products",
    )(*at_home(owners), *latents, *uv_parts, route, *after)


def output_kernel(experts, *refs):
    value_refs = refs[:experts]
    weight_ref, out_ref = refs[experts:]
    depth = weight_ref.shape[0]
    values = jnp.concatenate([ref[:, :depth] for ref in value_refs], axis=0)
    rows = values.shape[0]
    to = lax.broadcasted_iota(jnp.int32, (rows, rows), 0)
    row = lax.broadcasted_iota(jnp.int32, (rows, rows), 1)
    source = (to & (experts - 1)) ^ lax.axis_index("expert")
    rest = lax.shift_right_logical(to, experts.bit_length() - 1)
    order = jnp.where(row == source * (rows // experts) + rest, 1.0, 0.0).astype(jnp.bfloat16)
    values = jnp.dot(order, values, preferred_element_type=jnp.float32).astype(jnp.bfloat16)
    out_ref[...] = jnp.dot(
        values, weight_ref[...], preferred_element_type=jnp.float32
    ).astype(out_ref.dtype)


def output_product(values, weight):
    rows = sum(value.shape[0] for value in values)
    held = pl.BlockSpec(memory_space=pltpu.VMEM)
    return pl.pallas_call(
        functools.partial(output_kernel, len(values)),
        out_shape=jax.ShapeDtypeStruct((rows, weight.shape[1]), jnp.bfloat16),
        in_specs=[held] * (len(values) + 1),
        out_specs=held,
        compiler_params=params(*values, scale=8),
        name="output_product",
    )(*values, weight)


def mix_kernel(count, owners, rows, *refs):
    part_refs, own_refs = refs[:count], refs[count : count + owners]
    out_ref, held = refs[-2:]
    f32 = jnp.float32
    total = part_refs[0][...].astype(f32)
    for ref in part_refs[1:]:
        total = total + ref[...].astype(f32)
    block, column = held.shape[1:]
    for owner in range(owners):
        held[owner] = total[owner * block : (owner + 1) * block]
    rank = lax.axis_index("expert")
    for mask, ref in enumerate(own_refs):
        lines = []
        for line, at in enumerate(range(0, column, ref.shape[1])):
            end = min(at + ref.shape[1], column)
            to = rows + line * block
            lines.append(ref[to : to + block, : end - at].astype(f32))
        lines = lines[0] if len(lines) == 1 else jnp.concatenate(lines, axis=1)
        out_ref[rank ^ mask] = (held[rank ^ mask] + lines).astype(out_ref.dtype)


def mix(parts, owns, rows, after):
    total, width = parts[0].shape
    owners = len(owns)
    held = pl.BlockSpec(memory_space=pltpu.VMEM)
    shape = (owners, total // owners, width)
    return pl.pallas_call(
        functools.partial(mix_kernel, len(parts), owners, rows),
        out_shape=jax.ShapeDtypeStruct(shape, parts[0].dtype),
        in_specs=[held] * (len(parts) + owners)
        + [pl.BlockSpec(memory_space=pl.ANY)] * len(after),
        out_specs=held,
        scratch_shapes=[pltpu.VMEM(shape, jnp.float32)],
        compiler_params=params(*parts, *owns, scale=4),
        name="mix",
    )(*parts, *owns, *after)


def expert_kernel(experts, sections, picks, *refs):
    mixed_refs, route_refs = refs[:experts], refs[experts : 2 * experts]
    gain_ref, gate_ref, up_ref, down_ref, out_ref, near_ref, columns = refs[2 * experts :]
    f32, bf16 = jnp.float32, jnp.bfloat16
    count = gate_ref.shape[0]
    rank = lax.axis_index("expert")
    width = gain_ref.shape[0]
    block = mixed_refs[0].shape[1]
    for mask, ref in enumerate(mixed_refs):
        columns[rank ^ mask] = ref[...]
    mixed, route = [], []
    for mask, ref in enumerate(route_refs):
        mixed.append(
            jnp.concatenate([columns[i, rank ^ mask] for i in range(experts)], axis=1).astype(f32)
        )
        route.append(ref[:, ref.shape[1] - 128 :].astype(f32))
    near = mixed[0]
    mixed = jnp.concatenate(mixed, axis=0)
    route = jnp.concatenate(route, axis=0)
    named = route[:, :picks]
    weights = route[:, picks : 2 * picks] + route[:, 2 * picks : 3 * picks]
    weights = route_scale * weights / jnp.sum(weights, axis=-1, keepdims=True)
    scale = lax.rsqrt(jnp.mean(mixed * mixed, axis=-1, keepdims=True) + epsilon)
    rows_in = (mixed * scale * gain_ref[...][None].astype(f32)).astype(bf16)
    column = width // sections
    total = 0
    for x in range(count):
        mine = (rank * count + x).astype(f32)
        weight = jnp.sum(jnp.where(named == mine, weights, 0.0), axis=-1, keepdims=True)
        gate = jnp.dot(rows_in, gate_ref[x], preferred_element_type=f32)
        up = jnp.dot(rows_in, up_ref[x], preferred_element_type=f32)
        inner = gate / (1.0 + jnp.exp(-gate)) * up * weight
        total = total + jnp.dot(inner.astype(bf16), down_ref[x], preferred_element_type=f32)
    for section in range(sections):
        at = slice(section * column, (section + 1) * column)
        near_ref[section] = near[:, at].astype(bf16)
        for mask in range(experts):
            out_ref[(rank ^ mask) * sections + section] = total[
                mask * block : (mask + 1) * block, at
            ].astype(bf16)


def run_experts(mixed, routes, gain, w_gate, w_up, w_down, picks, sections):
    experts = len(mixed)
    block = (mixed[0].shape[1], gain.shape[0] // sections)
    held = pl.BlockSpec(memory_space=pltpu.VMEM)
    return pl.pallas_call(
        functools.partial(expert_kernel, experts, sections, picks),
        out_shape=[
            jax.ShapeDtypeStruct((experts * sections,) + block, jnp.bfloat16),
            jax.ShapeDtypeStruct((sections,) + block, jnp.bfloat16),
        ],
        in_specs=[held] * (2 * experts + 4),
        out_specs=[held] * 2,
        scratch_shapes=[pltpu.VMEM((experts,) + mixed[0].shape, jnp.bfloat16)],
        compiler_params=params(*mixed, scale=32),
        name="run_experts",
    )(*mixed, *routes, *at_home(gain), w_gate, w_up, w_down)


def finish_kernel(block_ref, near_ref, out_ref):
    f32 = jnp.float32
    steps, sources, _ = out_ref.shape
    total = near_ref[lax.axis_index("section")].astype(f32)
    for index in range(block_ref.shape[0]):
        total = total + block_ref[index].astype(f32)
    for step in range(steps):
        out_ref[step] = total[step * sources : (step + 1) * sources].astype(out_ref.dtype)


def finish(blocks, near, steps):
    held = pl.BlockSpec(memory_space=pltpu.VMEM)
    _, rows, column = near.shape
    return pl.pallas_call(
        finish_kernel,
        out_shape=jax.ShapeDtypeStruct((steps, rows // steps, column), near.dtype),
        in_specs=[held] * 2,
        out_specs=held,
        compiler_params=params(blocks, near, scale=4),
        name="finish",
    )(blocks, near)


def local(
    prompts,
    owners,
    lengths,
    residual,
    queries,
    expert_ids,
    route_scores,
    attn_gain,
    w_dkv,
    kv_gain,
    w_uk,
    w_uv,
    w_o,
    moe_gain,
    w_gate,
    w_up,
    w_down,
):
    bf16, f32 = jnp.bfloat16, jnp.float32
    expert_rank = lax.axis_index("expert")
    section_rank = lax.axis_index("section")
    experts = lax.axis_size("expert")
    sections = lax.axis_size("section")
    prompt_count, full_length, width = prompts.shape
    steps, tokens_here, heads, _ = queries.shape
    latent = kv_gain.shape[0]
    cache_width = w_dkv.shape[1]
    rows = prompt_count * full_length
    own_rows = steps * tokens_here

    w_turned = w_dkv.T
    w_piece, *cut = cut_columns(
        prompts.reshape(rows, width), queries, w_turned, w_uv, sections, experts
    )
    w_parts = spread(w_piece, "section")
    cut = deliver(cut, "expert")

    blocks, riders, token = absorb_queries(
        owners, cut, queries.shape, w_uk, residual, attn_gain, w_turned, prompt_count, sections,
        w_parts[2:],
    )
    blocks = lax.all_to_all(blocks, ("expert", "section"), 0, 0, tiled=True)
    away = list(project(cut[1:], riders, w_parts, 1, rows, [token]))
    near = list(project(cut[:1], riders, w_parts, 0, rows, away[:1]))
    parts = deliver(near + away, "expert")
    table = rotation(full_length + steps + -(full_length + steps) % 8, cache_width - latent)
    gathered = list(gather_queries(
        blocks, lengths, owners, kv_gain, table, prompt_count, tokens_here, experts, sections,
        steps, heads
    ))
    *out_latent, token = attend(
        parts, full_length, lengths, kv_gain, table, gathered, tokens_here, steps, sections,
        queries.shape[-1] ** (-0.5),
    )

    (w_gate,) = fetch([w_gate], [token])
    masks = [1 << bit for bit in range(experts.bit_length() - 1)]
    near_uv, far_uv, token = lax.optimization_barrier((w_uv, cut[masks[-1]], token))
    uv_parts = {0: near_uv, masks[-1]: far_uv}
    uv_parts = doubled(uv_parts, "expert", masks[1:-1] + masks[:1])
    out_latent = deliver(out_latent, "section")
    high = route_scores.astype(bf16)
    low = (route_scores - high.astype(f32)).astype(bf16)
    route = jnp.concatenate([expert_ids.astype(bf16), high, low], axis=2).reshape(own_rows, -1)
    route = jnp.pad(route, ((0, 0), (0, 128 - route.shape[1])))
    head_values = head_products(
        owners, out_latent, [uv_parts[mask] for mask in range(experts)], route, steps,
        tokens_here, [w_gate, token],
    )
    head_values = spread(head_values, "expert")

    (w_o,) = fetch([w_o], [])
    attended = output_product(head_values, w_o)
    (w_up,) = fetch([w_up], [attended])
    mixed = mix(spread(attended, "section"), parts, rows, [w_up])
    (w_down,) = fetch([w_down], [mixed])
    blocks, near = run_experts(
        spread(mixed, "expert"),
        head_values,
        moe_gain,
        w_gate,
        w_up,
        w_down,
        expert_ids.shape[2],
        sections,
    )
    blocks = lax.all_to_all(blocks, ("expert", "section"), 0, 0, tiled=True)
    return finish(blocks, near, steps)


def solution(mesh):
    placed = (
        P(("groups", "expert", "section"), None, None),
        P("groups"),
        P("groups"),
        P(None, ("groups", "expert"), None),
        P(None, ("groups", "expert"), "section", None),
        P(None, ("groups", "expert"), None),
        P(None, ("groups", "expert"), None),
        P(),
        P("section", None),
        P(),
        P("section", None, "expert"),
        P("section", None, "expert"),
        P("section", "expert"),
        P(),
        P("expert", None, "section"),
        P("expert", None, "section"),
        P("expert", "section", None),
    )
    return jax.shard_map(
        local,
        mesh=mesh,
        in_specs=placed,
        out_specs=P(None, ("groups", "expert"), "section"),
        check_vma=False,
    )
```

```python
import functools
import math

import jax
import jax.numpy as jnp
import numpy as np
from jax import lax
from jax.experimental import pallas as pl
from jax.experimental.pallas import tpu as pltpu
from jax.sharding import PartitionSpec as P

epsilon = 1e-06
masked_value = -1e30
route_scale = 2.5


def rotation(positions, width):
    halfway = width // 2
    frequency = 10000.0 ** (-2.0 * np.arange(halfway) / width)
    angles = np.arange(positions)[:, None] * frequency
    cosine = np.concatenate([np.cos(angles), np.cos(angles)], axis=1)
    sine = np.concatenate([-np.sin(angles), np.sin(angles)], axis=1)
    return jnp.asarray(cosine, jnp.float32), jnp.asarray(sine, jnp.float32)


def swap(block, axis, mask):
    size = lax.axis_size(axis)
    return lax.ppermute(block, axis, [(i, i ^ mask) for i in range(size)])


def deliver(blocks, axis):
    return [blocks[0]] + [swap(blocks[mask], axis, mask) for mask in range(1, len(blocks))]


def spread(block, axis):
    return [block] + [swap(block, axis, mask) for mask in range(1, lax.axis_size(axis))]


def params(*arrays, scale=1):
    held = sum(math.prod(array.shape) * array.dtype.itemsize for array in arrays)
    mebibytes = min(56, 4 + scale * held // 1024 // 1024)
    return pltpu.CompilerParams(vmem_limit_bytes=mebibytes * 1024 * 1024)


def at_home(*arrays):
    return [pltpu.with_memory_space_constraint(array, pltpu.HBM) for array in arrays]


def fetch_kernel(count, *refs):
    out_refs, sems = refs[-1 - count : -1], refs[-1]
    copies = [
        pltpu.make_async_copy(refs[index], out_refs[index], sems.at[index])
        for index in range(count)
    ]
    for copy in copies:
        copy.start()
    for copy in copies:
        copy.wait()


def fetch(arrays, after):
    size = sum(array.size * array.dtype.itemsize for array in arrays)
    return pl.pallas_call(
        functools.partial(fetch_kernel, len(arrays)),
        out_shape=[pltpu.VMEM(array.shape, array.dtype) for array in arrays],
        in_specs=[pl.BlockSpec(memory_space=pltpu.HBM)] * len(arrays)
        + [pl.BlockSpec(memory_space=pl.ANY)] * len(after),
        out_specs=[pl.BlockSpec(memory_space=pltpu.VMEM)] * len(arrays),
        scratch_shapes=[pltpu.SemaphoreType.DMA((len(arrays),))],
        compiler_params=pltpu.CompilerParams(vmem_limit_bytes=1024 * 1024),
        cost_estimate=pl.CostEstimate(flops=0, bytes_accessed=2 * size, transcendentals=0),
        name="fetch",
    )(*at_home(*arrays), *after)


def doubled(held, axis, masks):
    held = dict(held)
    for mask in masks:
        for other in list(held):
            held[other ^ mask] = swap(held[other], axis, mask)
    return held


def cut_kernel(sections, experts, piece, x_ref, query_ref, *refs):
    out_refs, held = refs[-1 - experts : -1], refs[-1]
    rank = lax.axis_index("expert")
    steps, sources, heads, wide = query_ref.shape
    rows = x_ref.shape[0]
    for target in range(experts):
        for section in range(sections):
            at = (section * experts + target) * piece
            held[target, section * rows : (section + 1) * rows] = x_ref[:, at : at + piece]
    for mask, ref in enumerate(out_refs):
        ref[: sections * rows, :piece] = held[rank ^ mask]
        for step in range(steps):
            for source in range(sources):
                at = sections * rows + (step * sources + source) * heads
                ref[at : at + heads, :wide] = query_ref[step, source]


def cut_columns(x, queries, sections, experts, after):
    rows, width = x.shape
    piece = width // (sections * experts)
    steps, sources, heads, wide = queries.shape
    block = jax.ShapeDtypeStruct(
        (sections * rows + steps * sources * heads, max(piece, wide)), x.dtype
    )
    return pl.pallas_call(
        functools.partial(cut_kernel, sections, experts, piece),
        out_shape=[block] * experts,
        in_specs=[pl.BlockSpec(memory_space=pltpu.VMEM)] * 2
        + [pl.BlockSpec(memory_space=pl.ANY)] * len(after),
        scratch_shapes=[pltpu.VMEM((experts, sections * rows, piece), x.dtype)],
        compiler_params=params(x, block, scale=6),
        name="cut_columns",
    )(*at_home(x, queries), *after)


def project_kernel(count, first, rows, *refs):
    x_refs, rider_ref, w_refs, out_refs = refs[:count], refs[count], refs[count + 1 :], refs[-count:]
    section_rank = lax.axis_index("section")
    sections = lax.axis_size("section")
    piece = w_refs[0].shape[1]
    total = 0
    for mask in range(sections):
        at = pl.ds(pl.multiple_of((section_rank ^ mask) * rows, rows), rows)
        x = jnp.concatenate([ref[at, :piece] for ref in x_refs], axis=0)
        total = total + lax.dot_general(
            x, w_refs[mask][...], (((1,), (1,)), ((), ())), preferred_element_type=jnp.float32
        )
    for index, ref in enumerate(out_refs):
        ref[:rows, :] = total[index * rows : (index + 1) * rows].astype(ref.dtype)
        ref[rows:, :] = rider_ref[first + index]


def project(blocks, riders, w_parts, first, rows, after):
    out = jax.ShapeDtypeStruct((rows + riders.shape[1], riders.shape[2]), jnp.bfloat16)
    held = pl.BlockSpec(memory_space=pltpu.VMEM)
    return pl.pallas_call(
        functools.partial(project_kernel, len(blocks), first, rows),
        out_shape=[out] * len(blocks),
        in_specs=[held] * (len(blocks) + 1 + len(w_parts))
        + [pl.BlockSpec(memory_space=pl.ANY)] * len(after),
        compiler_params=params(*blocks, *w_parts, scale=6),
        name="project",
    )(*blocks, riders, *w_parts, *after)


def query_kernel(
    experts, sections, prompts, nope, shape, *refs
):
    f32, bf16 = jnp.float32, jnp.bfloat16
    table_ref, query_refs = refs[0], refs[1 : 1 + experts]
    uk_ref, own_ref, gain_ref, wt_ref = refs[1 + experts : 5 + experts]
    out_ref, rider_ref, token_ref, picked, ropes, made, normed, query_ref, columns = refs[-9:]
    token_ref[...] = jnp.zeros_like(token_ref)
    steps, sources, heads, wide = shape
    rope = wide - nope
    chunk = uk_ref.shape[2]
    width = out_ref.shape[2]
    count = experts * sources
    block = prompts * steps * heads
    rank = lax.axis_index("expert")

    for mask, ref in enumerate(query_refs):
        for step in range(steps):
            for source in range(sources):
                at = ref.shape[0] - (steps * sources - step * sources - source) * heads
                query_ref[rank ^ mask, step, source] = ref[at : at + heads, :wide]

    def pick(index, carry):
        owner = table_ref[index]
        for step in range(steps):
            value = query_ref[owner, step, index // sources].astype(f32)
            at = pl.ds(pl.multiple_of((index * steps + step) * heads, heads), heads)
            picked[at, :] = value[:, :nope]
            ropes[at, :rope] = value[:, nope:]
        return carry

    if count <= 16:
        for index in range(count):
            pick(index, 0)
    else:
        lax.fori_loop(0, count, pick, 0)
    for head in range(heads):
        at = pl.ds(head, count * steps, stride=heads)
        value = jnp.dot(picked[at, :].astype(bf16), uk_ref[head], preferred_element_type=f32)
        if chunk < made.shape[1]:
            spare = jnp.zeros((count * steps, made.shape[1] - chunk), f32)
            value = jnp.concatenate([value, spare], axis=1)
        made[at, :] = value
    small = (rope + experts - 1) // experts
    lanes = rope if width != chunk else width
    groups = width // small if width == chunk else 1
    source_lane = lax.broadcasted_iota(jnp.int32, (rope, lanes), 0)
    lane = lax.broadcasted_iota(jnp.int32, (rope, lanes), 1)
    turned = 0
    for group in range(groups):
        pair = (source_lane == lane - group * small + rank * small) & (
            (lane >= group * small) & (lane < (group + 1) * small)
        )
        at = pl.ds(group, count * steps * heads // groups, stride=groups)
        turned = turned + jnp.dot(
            ropes[at, :][:, :rope].astype(bf16),
            jnp.where(pair, 1.0, 0.0).astype(bf16),
            preferred_element_type=f32,
        )
    own = jnp.concatenate([own_ref[step] for step in range(steps)], axis=0).astype(f32)
    lines, column = columns.shape[1:]
    for target in range(experts):
        columns[target] = own[:, target * column : (target + 1) * column]
    for mask in range(experts):
        value = columns[rank ^ mask]
        for line, at in enumerate(range(0, column, rider_ref.shape[2])):
            end = min(at + rider_ref.shape[2], column)
            rider_ref[mask, line * lines : (line + 1) * lines, : end - at] = value[
                :, at:end
            ].astype(bf16)
    scale = lax.rsqrt(jnp.mean(own * own, axis=-1, keepdims=True) + epsilon)
    own = (own * scale * gain_ref[...][None].astype(f32)).astype(bf16)
    depth = wt_ref.shape[1]
    for section in range(sections):
        normed[section] = own[:, section * depth : (section + 1) * depth]
    fresh = lax.dot_general(
        normed[lax.axis_index("section")],
        wt_ref[...],
        (((1,), (1,)), ((), ())),
        preferred_element_type=f32,
    )
    for source in range(experts):
        picks = [step * sources + source for step in range(steps)]
        if width == chunk:
            latent = width * experts
            lines = [
                fresh[pick:, part * width : (part + 1) * width][:1]
                for pick in picks
                for part in range(experts)
            ]
            lines.append(
                jnp.concatenate([fresh[pick:, latent:][:1] for pick in picks], axis=1)
            )
        else:
            lines = [
                fresh[pick:, part * width : (part + 1) * width][:1]
                for pick in picks
                for part in range(experts)
            ]
        lines = jnp.concatenate(lines, axis=0).astype(bf16)
        for section in range(sections):
            index = source * sections + section
            at = slice(index * block, (index + 1) * block)
            if width == chunk:
                few = block // groups
                out_ref[index, :block, :] = made[at, :chunk].astype(bf16)
                tail = [turned[index * few : (index + 1) * few].astype(bf16), lines]
                spare = out_ref.shape[1] - block - few - lines.shape[0]
                if spare:
                    tail.append(jnp.zeros((spare, width), bf16))
                out_ref[index, block:, :] = jnp.concatenate(tail, axis=0)
            else:
                value = jnp.concatenate([made[at, :chunk], turned[at, :small]], axis=1)
                out_ref[index, :block, :] = value.astype(bf16)
                out_ref[index, block:, :] = lines


def block_shape(prompts, steps, heads, experts, chunk, rope):
    rows = prompts * steps * heads
    small = rope // experts
    if chunk == 128 and small * 8 == chunk and steps * rope == chunk:
        rows = rows + rows // 8 + steps * experts + 1
        return rows + -rows % 16, chunk
    return rows + steps * experts, chunk + small


def absorb_queries(table, queries, shape, w_uk, own, gain, w_turned, prompts, sections, after):
    experts = len(queries)
    steps, sources, heads, wide = shape
    _, nope, chunk = w_uk.shape
    rows, width = block_shape(prompts, steps, heads, experts, chunk, wide - nope)
    block, column = own.shape[0] * own.shape[1], own.shape[2] // experts
    cache_width = w_turned.shape[0]
    count = experts * sources * steps * heads
    held = pl.BlockSpec(memory_space=pltpu.VMEM)
    return pl.pallas_call(
        functools.partial(query_kernel, experts, sections, prompts, nope, shape),
        out_shape=[
            jax.ShapeDtypeStruct((experts * sections, rows, width), jnp.bfloat16),
            jax.ShapeDtypeStruct(
                (experts, block * -(-column // cache_width), cache_width), jnp.bfloat16
            ),
            jax.ShapeDtypeStruct((8, 128), jnp.bfloat16),
        ],
        in_specs=[pl.BlockSpec(memory_space=pltpu.SMEM)]
        + [held] * (experts + 4)
        + [pl.BlockSpec(memory_space=pl.ANY)] * len(after),
        out_specs=[held] * 3,
        scratch_shapes=[
            pltpu.VMEM((count, nope), jnp.float32),
            pltpu.VMEM((count, max(wide - nope, 128)), jnp.float32),
            pltpu.VMEM((count, max(chunk, 128)), jnp.float32),
            pltpu.VMEM(
                (sections, own.shape[0] * own.shape[1], w_turned.shape[1]), jnp.bfloat16
            ),
            pltpu.VMEM((experts,) + shape, jnp.bfloat16),
            pltpu.VMEM((experts, block, column), jnp.float32),
        ],
        compiler_params=params(*queries, w_uk, own, w_turned, scale=4),
        name="absorb_queries",
    )(*at_home(table), *queries, *at_home(w_uk, own, gain, w_turned), *after)


def turn(values, cosine, sine):
    half = values.shape[1] // 2
    other = jnp.concatenate([values[:, half:], values[:, :half]], axis=1)
    return values * cosine + other * sine


def scaled(values, gain):
    scale = lax.rsqrt(jnp.mean(values * values, axis=-1, keepdims=True) + epsilon)
    return values * scale * gain.astype(jnp.float32)


def gather_kernel(
    prompts, experts, sections, sources, heads, steps, latent, length_ref, owner_ref, gain_ref,
    cosine_ref, sine_ref, block_ref, query_ref, query_rope_ref, recent_ref, recent_rope_ref,
    cosine_held, sine_held, ropes_held
):
    f32, bf16 = jnp.float32, jnp.bfloat16
    rows = steps * heads
    chunk = latent // experts
    whole = block_ref.shape[2] == chunk
    extra = prompts * rows // 8 if whole else 0
    first = lax.axis_index("expert") * sources + lax.axis_index("section") * prompts
    gain = gain_ref[...][None]
    for prompt in range(prompts):
        length, owner = length_ref[first + prompt], owner_ref[first + prompt]
        for step in range(steps):
            at = slice(step * heads, (step + 1) * heads)
            cosine_held[at, :] = jnp.broadcast_to(
                cosine_ref[pl.ds(length + step, 1), :], (heads, cosine_ref.shape[1])
            )
            sine_held[at, :] = jnp.broadcast_to(
                sine_ref[pl.ds(length + step, 1), :], (heads, sine_ref.shape[1])
            )
        cosine, sine = cosine_held[...], sine_held[...]
        if whole:
            few = rows // 8
            small = cosine.shape[1] // experts
            low = prompts * rows + prompt * few
            tail = jnp.concatenate(
                [
                    jnp.concatenate(
                        [block_ref[i * sections + section, low : low + few, :]
                         for i in range(experts)],
                        axis=1,
                    )
                    for section in range(sections)
                ],
                axis=0,
            )
            shape = (experts * chunk, experts * small)
            source_lane = lax.broadcasted_iota(jnp.int32, shape, 0)
            lane = lax.broadcasted_iota(jnp.int32, shape, 1)
            bits = small.bit_length() - 1
            lane = lax.shift_right_logical(lane, bits) * chunk + (lane & (small - 1))
            for group in range(8):
                pair = jnp.where(source_lane == lane + group * small, 1.0, 0.0).astype(bf16)
                value = jnp.dot(tail, pair, preferred_element_type=f32)
                pad = ropes_held.shape[1] - value.shape[1]
                value = jnp.concatenate([value, jnp.zeros((value.shape[0], pad), f32)], axis=1)
                ropes_held[pl.ds(group, sections * few, stride=8), :] = value
        at = slice(prompt * rows, (prompt + 1) * rows)
        for section in range(sections):
            pieces = [block_ref[i * sections + section, at, :] for i in range(experts)]
            to = slice(section * rows, (section + 1) * rows)
            query_ref[prompt, to, :] = jnp.concatenate(
                [piece[:, :chunk] for piece in pieces], axis=1
            )
            if whole:
                rope = ropes_held[to, : cosine.shape[1]]
            else:
                rope = jnp.concatenate(
                    [piece[:, chunk:].astype(f32) for piece in pieces], axis=1
                )
            query_rope_ref[prompt, to, :] = turn(rope, cosine, sine).astype(bf16)
        lines = 0
        for section in range(sections):
            lines = lines + block_ref[
                owner * sections + section, prompts * rows + extra :, :
            ].astype(f32)
        recent, recent_rope = [], []
        for step in range(steps):
            parts = [lines[step * experts + part :][:1] for part in range(experts)]
            if whole:
                end = cosine.shape[1]
                parts.append(
                    lines[steps * experts :][:1, step * end : (step + 1) * end]
                )
            line = jnp.concatenate(parts, axis=1)
            recent.append(scaled(line[:, :latent], gain))
            at = slice(step * heads, step * heads + 1)
            recent_rope.append(turn(line[:, latent:], cosine[at], sine[at]))
        spare = recent_ref.shape[1] - steps
        recent.append(jnp.zeros((spare, latent), f32))
        recent_rope.append(jnp.zeros((spare, recent_rope[0].shape[1]), f32))
        recent_ref[prompt] = jnp.concatenate(recent, axis=0).astype(bf16)
        recent_rope_ref[prompt] = jnp.concatenate(recent_rope, axis=0).astype(bf16)


def gather_queries(blocks, lengths, owners, kv_gain, table, prompts, sources, experts, sections,
                   steps, heads):
    latent = kv_gain.shape[0]
    rope = table[0].shape[1]
    rows = sections * steps * heads
    spare = steps + -steps % 16
    shape = lambda *sizes: jax.ShapeDtypeStruct((prompts,) + sizes, jnp.bfloat16)
    held = pl.BlockSpec(memory_space=pltpu.VMEM)
    return pl.pallas_call(
        functools.partial(
            gather_kernel, prompts, experts, sections, sources, heads, steps, latent
        ),
        out_shape=[shape(rows, latent), shape(rows, rope), shape(spare, latent), shape(spare, rope)],
        in_specs=[pl.BlockSpec(memory_space=pltpu.SMEM)] * 2 + [held] * 4,
        out_specs=[held] * 4,
        scratch_shapes=[pltpu.VMEM((steps * heads, rope), jnp.float32)] * 2
        + [pltpu.VMEM((rows, 128), jnp.float32)],
        compiler_params=params(blocks, scale=4),
        name="gather_queries",
    )(*at_home(lengths, owners, kv_gain, *table), blocks)


def attend_kernel(parts, positions, sections, sources, heads, steps, score_scale, *refs):
    part_refs = refs[:parts]
    (length_ref, gain_ref, cosine_ref, sine_ref, query_ref, query_rope_ref, recent_ref,
     recent_rope_ref) = refs[parts : parts + 8]
    out_refs, token_ref, held = refs[-2 - sections : -2], refs[-2], refs[-1]
    token_ref[...] = jnp.zeros_like(token_ref)
    f32, bf16 = jnp.float32, jnp.bfloat16
    nt = (((1,), (1,)), ((), ()))
    prompts, _, latent = query_ref.shape
    rows = steps * heads
    section_rank = lax.axis_index("section")
    first = lax.axis_index("expert") * sources + section_rank * prompts
    for prompt in range(prompts):
        at = slice(prompt * positions, (prompt + 1) * positions)
        projected = part_refs[0][at].astype(f32)
        for ref in part_refs[1:]:
            projected = projected + ref[at].astype(f32)
        keys = scaled(projected[:, :latent], gain_ref[...][None]).astype(bf16)
        key_rope = turn(
            projected[:, latent:], cosine_ref[:positions], sine_ref[:positions]
        ).astype(bf16)
        query, query_rope = query_ref[prompt], query_rope_ref[prompt]
        recent, recent_rope = recent_ref[prompt], recent_rope_ref[prompt]
        scores = lax.dot_general(query, keys, nt, preferred_element_type=f32)
        scores = scores + lax.dot_general(query_rope, key_rope, nt, preferred_element_type=f32)
        fresh = lax.dot_general(query, recent, nt, preferred_element_type=f32)
        fresh = fresh + lax.dot_general(query_rope, recent_rope, nt, preferred_element_type=f32)
        place = lax.broadcasted_iota(jnp.int32, scores.shape, 1)
        scores = jnp.where(
            place < length_ref[first + prompt], scores * score_scale, masked_value
        )
        row = lax.broadcasted_iota(jnp.int32, (rows, fresh.shape[1]), 0)
        place = lax.broadcasted_iota(jnp.int32, (rows, fresh.shape[1]), 1)
        seen = jnp.where(place < 1, 1.0, 0.0)
        for step in range(1, steps):
            seen = jnp.where((place <= step) & (row >= step * heads), 1.0, seen)
        seen = jnp.concatenate([seen] * sections, axis=0)
        fresh = jnp.where(seen > 0.5, fresh * score_scale, masked_value)
        most = jnp.maximum(
            jnp.max(scores, axis=-1, keepdims=True), jnp.max(fresh, axis=-1, keepdims=True)
        )
        scores = jnp.exp(scores - most)
        fresh = jnp.exp(fresh - most)
        total = jnp.sum(scores, axis=-1, keepdims=True) + jnp.sum(fresh, axis=-1, keepdims=True)
        scores = (scores / total).astype(bf16)
        fresh = (fresh / total).astype(bf16)
        mixed = jnp.dot(scores, keys, preferred_element_type=f32)
        mixed = mixed + jnp.dot(fresh, recent, preferred_element_type=f32)
        mixed = mixed.astype(bf16)
        for section in range(sections):
            held[section] = mixed[section * rows : (section + 1) * rows]
        for mask, ref in enumerate(out_refs):
            ref[prompt * rows : (prompt + 1) * rows, :] = held[section_rank ^ mask]


def attend(
    parts, positions, lengths, kv_gain, table, gathered, sources, steps, sections, score_scale
):
    prompts, rows, latent = gathered[0].shape
    out = (rows // sections, latent)
    held = pl.BlockSpec(memory_space=pltpu.VMEM)
    return pl.pallas_call(
        functools.partial(
            attend_kernel, len(parts), positions, sections, sources, out[0] // steps, steps,
            score_scale
        ),
        out_shape=[jax.ShapeDtypeStruct((prompts * out[0], latent), jnp.bfloat16)] * sections
        + [jax.ShapeDtypeStruct((8, 128), jnp.bfloat16)],
        in_specs=[held] * len(parts)
        + [pl.BlockSpec(memory_space=pltpu.SMEM)]
        + [held] * 7,
        out_specs=[held] * (sections + 1),
        scratch_shapes=[pltpu.VMEM((sections,) + out, jnp.bfloat16)],
        compiler_params=params(*parts, *gathered, scale=6),
        name="attend",
    )(*parts, *at_home(lengths, kv_gain, *table), *gathered)


def value_kernel(experts, sections, heads, steps, sources, *refs):
    owner_ref = refs[0]
    latent_refs, uv_refs = refs[1 : 1 + sections], refs[1 + sections : 1 + sections + experts]
    route_ref = refs[1 + sections + experts]
    out_ref, held = refs[-2:]
    f32, bf16 = jnp.float32, jnp.bfloat16
    chunk = uv_refs[0].shape[2]
    rows = latent_refs[0].shape[0]
    for mask, ref in enumerate(latent_refs):
        for index in range(experts):
            held[index, mask * rows : (mask + 1) * rows, :chunk] = ref[
                :, index * chunk : (index + 1) * chunk
            ].astype(f32)
    rank = lax.axis_index("expert")
    values = []
    for head in range(heads):
        at = pl.ds(head, sections * rows // heads, stride=heads)
        total = 0
        for mask, ref in enumerate(uv_refs):
            total = total + lax.dot_general(
                held[rank ^ mask, at, :][:, :chunk].astype(bf16),
                ref[head],
                (((1,), (1,)), ((), ())),
                preferred_element_type=f32,
            )
        values.append(total.astype(bf16))
    values = jnp.concatenate(values, axis=1)
    prompts = sources // sections
    section_rank = lax.axis_index("section")
    size = sources * steps
    to = lax.broadcasted_iota(jnp.int32, (size, size), 0)
    row = lax.broadcasted_iota(jnp.int32, (size, size), 1)
    order = jnp.zeros((size, size), f32)
    for mask in range(sections):
        for prompt in range(prompts):
            owner = owner_ref[
                rank * sources + (section_rank ^ mask) * prompts + prompt
            ]
            for step in range(steps):
                index = (mask * prompts + prompt) * steps + step
                order = jnp.where((row == index) & (to == owner * steps + step), 1.0, order)
    width = values.shape[1]
    out_ref[:, :width] = jnp.dot(
        order.astype(bf16), values, preferred_element_type=f32
    ).astype(bf16)
    out_ref[:, width:] = route_ref[...]


def head_products(owners, latents, uv_parts, route, steps, sources, after):
    rows, width = latents[0].shape
    heads, value, _ = uv_parts[0].shape
    held = pl.BlockSpec(memory_space=pltpu.VMEM)
    total = rows * len(latents)
    return pl.pallas_call(
        functools.partial(
            value_kernel, len(uv_parts), len(latents), heads, steps, sources
        ),
        out_shape=jax.ShapeDtypeStruct(
            (total // heads, heads * value + route.shape[1]), jnp.bfloat16
        ),
        in_specs=[pl.BlockSpec(memory_space=pltpu.SMEM)]
        + [held] * (len(latents) + len(uv_parts) + 1)
        + [pl.BlockSpec(memory_space=pl.ANY)] * len(after),
        out_specs=held,
        scratch_shapes=[
            pltpu.VMEM((len(uv_parts), total, max(width // len(uv_parts), 128)), jnp.float32)
        ],
        compiler_params=params(*latents, *uv_parts, scale=4),
        name="head_products",
    )(*at_home(owners), *latents, *uv_parts, route, *after)


def output_kernel(experts, *refs):
    value_refs = refs[:experts]
    weight_ref, out_ref = refs[experts:]
    depth = weight_ref.shape[0]
    values = jnp.concatenate([ref[:, :depth] for ref in value_refs], axis=0)
    rows = values.shape[0]
    to = lax.broadcasted_iota(jnp.int32, (rows, rows), 0)
    row = lax.broadcasted_iota(jnp.int32, (rows, rows), 1)
    source = (to & (experts - 1)) ^ lax.axis_index("expert")
    rest = lax.shift_right_logical(to, experts.bit_length() - 1)
    order = jnp.where(row == source * (rows // experts) + rest, 1.0, 0.0).astype(jnp.bfloat16)
    values = jnp.dot(order, values, preferred_element_type=jnp.float32).astype(jnp.bfloat16)
    out_ref[...] = jnp.dot(
        values, weight_ref[...], preferred_element_type=jnp.float32
    ).astype(out_ref.dtype)


def output_product(values, weight):
    rows = sum(value.shape[0] for value in values)
    held = pl.BlockSpec(memory_space=pltpu.VMEM)
    return pl.pallas_call(
        functools.partial(output_kernel, len(values)),
        out_shape=jax.ShapeDtypeStruct((rows, weight.shape[1]), jnp.bfloat16),
        in_specs=[held] * (len(values) + 1),
        out_specs=held,
        compiler_params=params(*values, scale=8),
        name="output_product",
    )(*values, weight)


def mix_kernel(count, owners, rows, *refs):
    part_refs, own_refs = refs[:count], refs[count : count + owners]
    out_ref, held = refs[-2:]
    f32 = jnp.float32
    total = part_refs[0][...].astype(f32)
    for ref in part_refs[1:]:
        total = total + ref[...].astype(f32)
    block, column = held.shape[1:]
    for owner in range(owners):
        held[owner] = total[owner * block : (owner + 1) * block]
    rank = lax.axis_index("expert")
    for mask, ref in enumerate(own_refs):
        lines = []
        for line, at in enumerate(range(0, column, ref.shape[1])):
            end = min(at + ref.shape[1], column)
            to = rows + line * block
            lines.append(ref[to : to + block, : end - at].astype(f32))
        lines = lines[0] if len(lines) == 1 else jnp.concatenate(lines, axis=1)
        out_ref[rank ^ mask] = (held[rank ^ mask] + lines).astype(out_ref.dtype)


def mix(parts, owns, rows, after):
    total, width = parts[0].shape
    owners = len(owns)
    held = pl.BlockSpec(memory_space=pltpu.VMEM)
    shape = (owners, total // owners, width)
    return pl.pallas_call(
        functools.partial(mix_kernel, len(parts), owners, rows),
        out_shape=jax.ShapeDtypeStruct(shape, parts[0].dtype),
        in_specs=[held] * (len(parts) + owners)
        + [pl.BlockSpec(memory_space=pl.ANY)] * len(after),
        out_specs=held,
        scratch_shapes=[pltpu.VMEM(shape, jnp.float32)],
        compiler_params=params(*parts, *owns, scale=4),
        name="mix",
    )(*parts, *owns, *after)


def expert_kernel(experts, sections, picks, *refs):
    mixed_refs, route_refs = refs[:experts], refs[experts : 2 * experts]
    gain_ref, gate_ref, up_ref, down_ref, out_ref, near_ref, columns = refs[2 * experts :]
    f32, bf16 = jnp.float32, jnp.bfloat16
    count = gate_ref.shape[0]
    rank = lax.axis_index("expert")
    width = gain_ref.shape[0]
    block = mixed_refs[0].shape[1]
    for mask, ref in enumerate(mixed_refs):
        columns[rank ^ mask] = ref[...]
    mixed, route = [], []
    for mask, ref in enumerate(route_refs):
        mixed.append(
            jnp.concatenate([columns[i, rank ^ mask] for i in range(experts)], axis=1).astype(f32)
        )
        route.append(ref[:, ref.shape[1] - 128 :].astype(f32))
    near = mixed[0]
    mixed = jnp.concatenate(mixed, axis=0)
    route = jnp.concatenate(route, axis=0)
    named = route[:, :picks]
    weights = route[:, picks : 2 * picks] + route[:, 2 * picks : 3 * picks]
    weights = route_scale * weights / jnp.sum(weights, axis=-1, keepdims=True)
    scale = lax.rsqrt(jnp.mean(mixed * mixed, axis=-1, keepdims=True) + epsilon)
    rows_in = (mixed * scale * gain_ref[...][None].astype(f32)).astype(bf16)
    column = width // sections
    total = 0
    for x in range(count):
        mine = (rank * count + x).astype(f32)
        weight = jnp.sum(jnp.where(named == mine, weights, 0.0), axis=-1, keepdims=True)
        gate = jnp.dot(rows_in, gate_ref[x], preferred_element_type=f32)
        up = jnp.dot(rows_in, up_ref[x], preferred_element_type=f32)
        inner = gate / (1.0 + jnp.exp(-gate)) * up * weight
        total = total + jnp.dot(inner.astype(bf16), down_ref[x], preferred_element_type=f32)
    for section in range(sections):
        at = slice(section * column, (section + 1) * column)
        near_ref[section] = near[:, at].astype(bf16)
        for mask in range(experts):
            out_ref[(rank ^ mask) * sections + section] = total[
                mask * block : (mask + 1) * block, at
            ].astype(bf16)


def run_experts(mixed, routes, gain, w_gate, w_up, w_down, picks, sections):
    experts = len(mixed)
    block = (mixed[0].shape[1], gain.shape[0] // sections)
    held = pl.BlockSpec(memory_space=pltpu.VMEM)
    return pl.pallas_call(
        functools.partial(expert_kernel, experts, sections, picks),
        out_shape=[
            jax.ShapeDtypeStruct((experts * sections,) + block, jnp.bfloat16),
            jax.ShapeDtypeStruct((sections,) + block, jnp.bfloat16),
        ],
        in_specs=[held] * (2 * experts + 4),
        out_specs=[held] * 2,
        scratch_shapes=[pltpu.VMEM((experts,) + mixed[0].shape, jnp.bfloat16)],
        compiler_params=params(*mixed, scale=32),
        name="run_experts",
    )(*mixed, *routes, *at_home(gain), w_gate, w_up, w_down)


def finish_kernel(block_ref, near_ref, out_ref):
    f32 = jnp.float32
    steps, sources, _ = out_ref.shape
    total = near_ref[lax.axis_index("section")].astype(f32)
    for index in range(block_ref.shape[0]):
        total = total + block_ref[index].astype(f32)
    for step in range(steps):
        out_ref[step] = total[step * sources : (step + 1) * sources].astype(out_ref.dtype)


def finish(blocks, near, steps):
    held = pl.BlockSpec(memory_space=pltpu.VMEM)
    _, rows, column = near.shape
    return pl.pallas_call(
        finish_kernel,
        out_shape=jax.ShapeDtypeStruct((steps, rows // steps, column), near.dtype),
        in_specs=[held] * 2,
        out_specs=held,
        compiler_params=params(blocks, near, scale=4),
        name="finish",
    )(blocks, near)


def local(
    prompts,
    owners,
    lengths,
    residual,
    queries,
    expert_ids,
    route_scores,
    attn_gain,
    w_dkv,
    kv_gain,
    w_uk,
    w_uv,
    w_o,
    moe_gain,
    w_gate,
    w_up,
    w_down,
):
    bf16, f32 = jnp.bfloat16, jnp.float32
    expert_rank = lax.axis_index("expert")
    section_rank = lax.axis_index("section")
    experts = lax.axis_size("expert")
    sections = lax.axis_size("section")
    prompt_count, full_length, width = prompts.shape
    steps, tokens_here, heads, _ = queries.shape
    depth = w_dkv.shape[0]
    piece = depth // experts
    latent = kv_gain.shape[0]
    cache_width = w_dkv.shape[1]
    rows = prompt_count * full_length
    own_rows = steps * tokens_here

    w_turned = w_dkv.T
    w_piece = lax.dynamic_slice_in_dim(w_turned, expert_rank * piece, piece, 1)
    masks = [1 << bit for bit in range(experts.bit_length() - 1)]
    uv_parts = doubled({0: w_uv}, "expert", masks[1:])
    w_parts = spread(w_piece, "section")
    cut = cut_columns(
        prompts.reshape(rows, width), queries, sections, experts,
        [],
    )
    cut = deliver(cut, "expert")

    blocks, riders, token = absorb_queries(
        owners, cut, queries.shape, w_uk, residual, attn_gain, w_turned, prompt_count, sections,
        [uv_parts[masks[-1]]],
    )
    blocks = lax.all_to_all(blocks, ("expert", "section"), 0, 0, tiled=True)

    away = list(project(cut[1:], riders, w_parts, 1, rows, [token]))
    near = list(project(cut[:1], riders, w_parts, 0, rows, away[:1]))
    parts = deliver(near + away, "expert")
    table = rotation(full_length + steps + -(full_length + steps) % 8, cache_width - latent)
    gathered = list(gather_queries(
        blocks, lengths, owners, kv_gain, table, prompt_count, tokens_here, experts, sections,
        steps, heads
    ))
    *out_latent, token = attend(
        parts, full_length, lengths, kv_gain, table, gathered, tokens_here, steps, sections,
        queries.shape[-1] ** (-0.5),
    )

    (w_gate,) = fetch([w_gate], [token])
    order = sorted(uv_parts)
    *uv_parts, token = lax.optimization_barrier((*[uv_parts[mask] for mask in order], token))
    uv_parts = doubled(dict(zip(order, uv_parts)), "expert", masks[:1])
    out_latent = deliver(out_latent, "section")
    high = route_scores.astype(bf16)
    low = (route_scores - high.astype(f32)).astype(bf16)
    route = jnp.concatenate([expert_ids.astype(bf16), high, low], axis=2).reshape(own_rows, -1)
    route = jnp.pad(route, ((0, 0), (0, 128 - route.shape[1])))
    head_values = head_products(
        owners, out_latent, [uv_parts[mask] for mask in range(experts)], route, steps,
        tokens_here, [w_gate, token],
    )
    head_values = spread(head_values, "expert")

    (w_o,) = fetch([w_o], [])
    attended = output_product(head_values, w_o)
    (w_up,) = fetch([w_up], [attended])
    mixed = mix(spread(attended, "section"), parts, rows, [w_up])
    (w_down,) = fetch([w_down], [mixed])
    blocks, near = run_experts(
        spread(mixed, "expert"),
        head_values,
        moe_gain,
        w_gate,
        w_up,
        w_down,
        expert_ids.shape[2],
        sections,
    )
    blocks = lax.all_to_all(blocks, ("expert", "section"), 0, 0, tiled=True)
    return finish(blocks, near, steps)


def solution(mesh):
    placed = (
        P(("groups", "expert", "section"), None, None),
        P("groups"),
        P("groups"),
        P(None, ("groups", "expert"), None),
        P(None, ("groups", "expert"), "section", None),
        P(None, ("groups", "expert"), None),
        P(None, ("groups", "expert"), None),
        P(),
        P("section", None),
        P(),
        P("section", None, "expert"),
        P("section", None, "expert"),
        P("section", "expert"),
        P(),
        P("expert", None, "section"),
        P("expert", None, "section"),
        P("expert", "section", None),
    )
    return jax.shard_map(
        local,
        mesh=mesh,
        in_specs=placed,
        out_specs=P(None, ("groups", "expert"), "section"),
        check_vma=False,
    )
```

```python
import functools
import math

import jax
import jax.numpy as jnp
import numpy as np
from jax import lax
from jax.experimental import pallas as pl
from jax.experimental.pallas import tpu as pltpu
from jax.sharding import PartitionSpec as P

epsilon = 1e-06
masked_value = -1e30
route_scale = 2.5


def rotation(positions, width):
    halfway = width // 2
    frequency = 10000.0 ** (-2.0 * np.arange(halfway) / width)
    angles = np.arange(positions)[:, None] * frequency
    cosine = np.concatenate([np.cos(angles), np.cos(angles)], axis=1)
    sine = np.concatenate([-np.sin(angles), np.sin(angles)], axis=1)
    return jnp.asarray(cosine, jnp.float32), jnp.asarray(sine, jnp.float32)


def swap(block, axis, mask):
    size = lax.axis_size(axis)
    return lax.ppermute(block, axis, [(i, i ^ mask) for i in range(size)])


def deliver(blocks, axis):
    return [blocks[0]] + [swap(blocks[mask], axis, mask) for mask in range(1, len(blocks))]


def spread(block, axis):
    return [block] + [swap(block, axis, mask) for mask in range(1, lax.axis_size(axis))]


def params(*arrays, scale=1):
    held = sum(math.prod(array.shape) * array.dtype.itemsize for array in arrays)
    mebibytes = min(56, 4 + scale * held // 1024 // 1024)
    return pltpu.CompilerParams(vmem_limit_bytes=mebibytes * 1024 * 1024)


def at_home(*arrays):
    return [pltpu.with_memory_space_constraint(array, pltpu.HBM) for array in arrays]


def fetch_kernel(count, *refs):
    out_refs, sems = refs[-1 - count : -1], refs[-1]
    copies = [
        pltpu.make_async_copy(refs[index], out_refs[index], sems.at[index])
        for index in range(count)
    ]
    for copy in copies:
        copy.start()
    for copy in copies:
        copy.wait()


def fetch(arrays, after):
    size = sum(array.size * array.dtype.itemsize for array in arrays)
    return pl.pallas_call(
        functools.partial(fetch_kernel, len(arrays)),
        out_shape=[pltpu.VMEM(array.shape, array.dtype) for array in arrays],
        in_specs=[pl.BlockSpec(memory_space=pltpu.HBM)] * len(arrays)
        + [pl.BlockSpec(memory_space=pl.ANY)] * len(after),
        out_specs=[pl.BlockSpec(memory_space=pltpu.VMEM)] * len(arrays),
        scratch_shapes=[pltpu.SemaphoreType.DMA((len(arrays),))],
        compiler_params=pltpu.CompilerParams(vmem_limit_bytes=1024 * 1024),
        cost_estimate=pl.CostEstimate(flops=0, bytes_accessed=2 * size, transcendentals=0),
        name="fetch",
    )(*at_home(*arrays), *after)


def doubled(held, axis, masks):
    held = dict(held)
    for mask in masks:
        for other in list(held):
            held[other ^ mask] = swap(held[other], axis, mask)
    return held


def cut_kernel(sections, experts, piece, x_ref, query_ref, uv_ref, half_ref, *refs):
    out_refs, held = refs[-1 - experts : -1], refs[-1]
    share = half_ref.shape[0]
    half_ref[...] = uv_ref[pl.ds(lax.axis_index("groups") * share, share)]
    rank = lax.axis_index("expert")
    steps, sources, heads, wide = query_ref.shape
    rows = x_ref.shape[0]
    for target in range(experts):
        for section in range(sections):
            at = (section * experts + target) * piece
            held[target, section * rows : (section + 1) * rows] = x_ref[:, at : at + piece]
    for mask, ref in enumerate(out_refs):
        ref[: sections * rows, :piece] = held[rank ^ mask]
        for step in range(steps):
            for source in range(sources):
                at = sections * rows + (step * sources + source) * heads
                ref[at : at + heads, :wide] = query_ref[step, source]


def cut_columns(x, queries, w_uv, sections, experts, groups):
    rows, width = x.shape
    piece = width // (sections * experts)
    steps, sources, heads, wide = queries.shape
    block = jax.ShapeDtypeStruct(
        (sections * rows + steps * sources * heads, max(piece, wide)), x.dtype
    )
    return pl.pallas_call(
        functools.partial(cut_kernel, sections, experts, piece),
        out_shape=[
            jax.ShapeDtypeStruct((w_uv.shape[0] // groups,) + w_uv.shape[1:], w_uv.dtype)
        ]
        + [block] * experts,
        scratch_shapes=[pltpu.VMEM((experts, sections * rows, piece), x.dtype)],
        compiler_params=params(x, block, w_uv, scale=6),
        name="cut_columns",
    )(*at_home(x, queries, w_uv))


def project_kernel(count, first, rows, *refs):
    x_refs, rider_ref, w_refs, out_refs = refs[:count], refs[count], refs[count + 1 :], refs[-count:]
    section_rank = lax.axis_index("section")
    sections = lax.axis_size("section")
    piece = w_refs[0].shape[1]
    total = 0
    for mask in range(sections):
        at = pl.ds(pl.multiple_of((section_rank ^ mask) * rows, rows), rows)
        x = jnp.concatenate([ref[at, :piece] for ref in x_refs], axis=0)
        total = total + lax.dot_general(
            x, w_refs[mask][...], (((1,), (1,)), ((), ())), preferred_element_type=jnp.float32
        )
    for index, ref in enumerate(out_refs):
        ref[:rows, :] = total[index * rows : (index + 1) * rows].astype(ref.dtype)
        ref[rows:, :] = rider_ref[first + index]


def project(blocks, riders, w_parts, first, rows, after):
    out = jax.ShapeDtypeStruct((rows + riders.shape[1], riders.shape[2]), jnp.bfloat16)
    held = pl.BlockSpec(memory_space=pltpu.VMEM)
    return pl.pallas_call(
        functools.partial(project_kernel, len(blocks), first, rows),
        out_shape=[out] * len(blocks),
        in_specs=[held] * (len(blocks) + 1 + len(w_parts))
        + [pl.BlockSpec(memory_space=pl.ANY)] * len(after),
        compiler_params=params(*blocks, *w_parts, scale=6),
        name="project",
    )(*blocks, riders, *w_parts, *after)


def query_kernel(
    experts, sections, prompts, nope, shape, *refs
):
    f32, bf16 = jnp.float32, jnp.bfloat16
    table_ref, query_refs = refs[0], refs[1 : 1 + experts]
    uk_ref, own_ref, gain_ref, wt_ref = refs[1 + experts : 5 + experts]
    out_ref, rider_ref, token_ref, picked, ropes, made, normed, query_ref, columns = refs[-9:]
    token_ref[...] = jnp.zeros_like(token_ref)
    steps, sources, heads, wide = shape
    rope = wide - nope
    chunk = uk_ref.shape[2]
    width = out_ref.shape[2]
    count = experts * sources
    block = prompts * steps * heads
    rank = lax.axis_index("expert")

    for mask, ref in enumerate(query_refs):
        for step in range(steps):
            for source in range(sources):
                at = ref.shape[0] - (steps * sources - step * sources - source) * heads
                query_ref[rank ^ mask, step, source] = ref[at : at + heads, :wide]

    def pick(index, carry):
        owner = table_ref[index]
        for step in range(steps):
            value = query_ref[owner, step, index // sources].astype(f32)
            at = pl.ds(pl.multiple_of((index * steps + step) * heads, heads), heads)
            picked[at, :] = value[:, :nope]
            ropes[at, :rope] = value[:, nope:]
        return carry

    if count <= 16:
        for index in range(count):
            pick(index, 0)
    else:
        lax.fori_loop(0, count, pick, 0)
    for head in range(heads):
        at = pl.ds(head, count * steps, stride=heads)
        value = jnp.dot(picked[at, :].astype(bf16), uk_ref[head], preferred_element_type=f32)
        if chunk < made.shape[1]:
            spare = jnp.zeros((count * steps, made.shape[1] - chunk), f32)
            value = jnp.concatenate([value, spare], axis=1)
        made[at, :] = value
    small = (rope + experts - 1) // experts
    lanes = rope if width != chunk else width
    groups = width // small if width == chunk else 1
    source_lane = lax.broadcasted_iota(jnp.int32, (rope, lanes), 0)
    lane = lax.broadcasted_iota(jnp.int32, (rope, lanes), 1)
    turned = 0
    for group in range(groups):
        pair = (source_lane == lane - group * small + rank * small) & (
            (lane >= group * small) & (lane < (group + 1) * small)
        )
        at = pl.ds(group, count * steps * heads // groups, stride=groups)
        turned = turned + jnp.dot(
            ropes[at, :][:, :rope].astype(bf16),
            jnp.where(pair, 1.0, 0.0).astype(bf16),
            preferred_element_type=f32,
        )
    own = jnp.concatenate([own_ref[step] for step in range(steps)], axis=0).astype(f32)
    lines, column = columns.shape[1:]
    for target in range(experts):
        columns[target] = own[:, target * column : (target + 1) * column]
    for mask in range(experts):
        value = columns[rank ^ mask]
        for line, at in enumerate(range(0, column, rider_ref.shape[2])):
            end = min(at + rider_ref.shape[2], column)
            rider_ref[mask, line * lines : (line + 1) * lines, : end - at] = value[
                :, at:end
            ].astype(bf16)
    scale = lax.rsqrt(jnp.mean(own * own, axis=-1, keepdims=True) + epsilon)
    own = (own * scale * gain_ref[...][None].astype(f32)).astype(bf16)
    depth = wt_ref.shape[1]
    for section in range(sections):
        normed[section] = own[:, section * depth : (section + 1) * depth]
    fresh = lax.dot_general(
        normed[lax.axis_index("section")],
        wt_ref[...],
        (((1,), (1,)), ((), ())),
        preferred_element_type=f32,
    )
    for source in range(experts):
        picks = [step * sources + source for step in range(steps)]
        if width == chunk:
            latent = width * experts
            lines = [
                fresh[pick:, part * width : (part + 1) * width][:1]
                for pick in picks
                for part in range(experts)
            ]
            lines.append(
                jnp.concatenate([fresh[pick:, latent:][:1] for pick in picks], axis=1)
            )
        else:
            lines = [
                fresh[pick:, part * width : (part + 1) * width][:1]
                for pick in picks
                for part in range(experts)
            ]
        lines = jnp.concatenate(lines, axis=0).astype(bf16)
        for section in range(sections):
            index = source * sections + section
            at = slice(index * block, (index + 1) * block)
            if width == chunk:
                few = block // groups
                out_ref[index, :block, :] = made[at, :chunk].astype(bf16)
                tail = [turned[index * few : (index + 1) * few].astype(bf16), lines]
                spare = out_ref.shape[1] - block - few - lines.shape[0]
                if spare:
                    tail.append(jnp.zeros((spare, width), bf16))
                out_ref[index, block:, :] = jnp.concatenate(tail, axis=0)
            else:
                value = jnp.concatenate([made[at, :chunk], turned[at, :small]], axis=1)
                out_ref[index, :block, :] = value.astype(bf16)
                out_ref[index, block:, :] = lines


def block_shape(prompts, steps, heads, experts, chunk, rope):
    rows = prompts * steps * heads
    small = rope // experts
    if chunk == 128 and small * 8 == chunk and steps * rope == chunk:
        rows = rows + rows // 8 + steps * experts + 1
        return rows + -rows % 16, chunk
    return rows + steps * experts, chunk + small


def absorb_queries(table, queries, shape, w_uk, own, gain, w_turned, prompts, sections, after):
    experts = len(queries)
    steps, sources, heads, wide = shape
    _, nope, chunk = w_uk.shape
    rows, width = block_shape(prompts, steps, heads, experts, chunk, wide - nope)
    block, column = own.shape[0] * own.shape[1], own.shape[2] // experts
    cache_width = w_turned.shape[0]
    count = experts * sources * steps * heads
    held = pl.BlockSpec(memory_space=pltpu.VMEM)
    return pl.pallas_call(
        functools.partial(query_kernel, experts, sections, prompts, nope, shape),
        out_shape=[
            jax.ShapeDtypeStruct((experts * sections, rows, width), jnp.bfloat16),
            jax.ShapeDtypeStruct(
                (experts, block * -(-column // cache_width), cache_width), jnp.bfloat16
            ),
            jax.ShapeDtypeStruct((8, 128), jnp.bfloat16),
        ],
        in_specs=[pl.BlockSpec(memory_space=pltpu.SMEM)]
        + [held] * (experts + 4)
        + [pl.BlockSpec(memory_space=pl.ANY)] * len(after),
        out_specs=[held] * 3,
        scratch_shapes=[
            pltpu.VMEM((count, nope), jnp.float32),
            pltpu.VMEM((count, max(wide - nope, 128)), jnp.float32),
            pltpu.VMEM((count, max(chunk, 128)), jnp.float32),
            pltpu.VMEM(
                (sections, own.shape[0] * own.shape[1], w_turned.shape[1]), jnp.bfloat16
            ),
            pltpu.VMEM((experts,) + shape, jnp.bfloat16),
            pltpu.VMEM((experts, block, column), jnp.float32),
        ],
        compiler_params=params(*queries, w_uk, own, w_turned, scale=4),
        name="absorb_queries",
    )(*at_home(table), *queries, *at_home(w_uk, own, gain, w_turned), *after)


def turn(values, cosine, sine):
    half = values.shape[1] // 2
    other = jnp.concatenate([values[:, half:], values[:, :half]], axis=1)
    return values * cosine + other * sine


def scaled(values, gain):
    scale = lax.rsqrt(jnp.mean(values * values, axis=-1, keepdims=True) + epsilon)
    return values * scale * gain.astype(jnp.float32)


def gather_kernel(
    prompts, experts, sections, sources, heads, steps, latent, length_ref, owner_ref, gain_ref,
    cosine_ref, sine_ref, block_ref, query_ref, query_rope_ref, recent_ref, recent_rope_ref,
    cosine_held, sine_held, ropes_held
):
    f32, bf16 = jnp.float32, jnp.bfloat16
    rows = steps * heads
    chunk = latent // experts
    whole = block_ref.shape[2] == chunk
    extra = prompts * rows // 8 if whole else 0
    first = lax.axis_index("expert") * sources + lax.axis_index("section") * prompts
    gain = gain_ref[...][None]
    for prompt in range(prompts):
        length, owner = length_ref[first + prompt], owner_ref[first + prompt]
        for step in range(steps):
            at = slice(step * heads, (step + 1) * heads)
            cosine_held[at, :] = jnp.broadcast_to(
                cosine_ref[pl.ds(length + step, 1), :], (heads, cosine_ref.shape[1])
            )
            sine_held[at, :] = jnp.broadcast_to(
                sine_ref[pl.ds(length + step, 1), :], (heads, sine_ref.shape[1])
            )
        cosine, sine = cosine_held[...], sine_held[...]
        if whole:
            few = rows // 8
            small = cosine.shape[1] // experts
            low = prompts * rows + prompt * few
            tail = jnp.concatenate(
                [
                    jnp.concatenate(
                        [block_ref[i * sections + section, low : low + few, :]
                         for i in range(experts)],
                        axis=1,
                    )
                    for section in range(sections)
                ],
                axis=0,
            )
            shape = (experts * chunk, experts * small)
            source_lane = lax.broadcasted_iota(jnp.int32, shape, 0)
            lane = lax.broadcasted_iota(jnp.int32, shape, 1)
            bits = small.bit_length() - 1
            lane = lax.shift_right_logical(lane, bits) * chunk + (lane & (small - 1))
            for group in range(8):
                pair = jnp.where(source_lane == lane + group * small, 1.0, 0.0).astype(bf16)
                value = jnp.dot(tail, pair, preferred_element_type=f32)
                pad = ropes_held.shape[1] - value.shape[1]
                value = jnp.concatenate([value, jnp.zeros((value.shape[0], pad), f32)], axis=1)
                ropes_held[pl.ds(group, sections * few, stride=8), :] = value
        at = slice(prompt * rows, (prompt + 1) * rows)
        for section in range(sections):
            pieces = [block_ref[i * sections + section, at, :] for i in range(experts)]
            to = slice(section * rows, (section + 1) * rows)
            query_ref[prompt, to, :] = jnp.concatenate(
                [piece[:, :chunk] for piece in pieces], axis=1
            )
            if whole:
                rope = ropes_held[to, : cosine.shape[1]]
            else:
                rope = jnp.concatenate(
                    [piece[:, chunk:].astype(f32) for piece in pieces], axis=1
                )
            query_rope_ref[prompt, to, :] = turn(rope, cosine, sine).astype(bf16)
        lines = 0
        for section in range(sections):
            lines = lines + block_ref[
                owner * sections + section, prompts * rows + extra :, :
            ].astype(f32)
        recent, recent_rope = [], []
        for step in range(steps):
            parts = [lines[step * experts + part :][:1] for part in range(experts)]
            if whole:
                end = cosine.shape[1]
                parts.append(
                    lines[steps * experts :][:1, step * end : (step + 1) * end]
                )
            line = jnp.concatenate(parts, axis=1)
            recent.append(scaled(line[:, :latent], gain))
            at = slice(step * heads, step * heads + 1)
            recent_rope.append(turn(line[:, latent:], cosine[at], sine[at]))
        spare = recent_ref.shape[1] - steps
        recent.append(jnp.zeros((spare, latent), f32))
        recent_rope.append(jnp.zeros((spare, recent_rope[0].shape[1]), f32))
        recent_ref[prompt] = jnp.concatenate(recent, axis=0).astype(bf16)
        recent_rope_ref[prompt] = jnp.concatenate(recent_rope, axis=0).astype(bf16)


def gather_queries(blocks, lengths, owners, kv_gain, table, prompts, sources, experts, sections,
                   steps, heads):
    latent = kv_gain.shape[0]
    rope = table[0].shape[1]
    rows = sections * steps * heads
    spare = steps + -steps % 16
    shape = lambda *sizes: jax.ShapeDtypeStruct((prompts,) + sizes, jnp.bfloat16)
    held = pl.BlockSpec(memory_space=pltpu.VMEM)
    return pl.pallas_call(
        functools.partial(
            gather_kernel, prompts, experts, sections, sources, heads, steps, latent
        ),
        out_shape=[shape(rows, latent), shape(rows, rope), shape(spare, latent), shape(spare, rope)],
        in_specs=[pl.BlockSpec(memory_space=pltpu.SMEM)] * 2 + [held] * 4,
        out_specs=[held] * 4,
        scratch_shapes=[pltpu.VMEM((steps * heads, rope), jnp.float32)] * 2
        + [pltpu.VMEM((rows, 128), jnp.float32)],
        compiler_params=params(blocks, scale=4),
        name="gather_queries",
    )(*at_home(lengths, owners, kv_gain, *table), blocks)


def attend_kernel(parts, positions, sections, sources, heads, steps, score_scale, *refs):
    part_refs = refs[:parts]
    (length_ref, gain_ref, cosine_ref, sine_ref, query_ref, query_rope_ref, recent_ref,
     recent_rope_ref) = refs[parts : parts + 8]
    out_refs, token_ref, held = refs[-2 - sections : -2], refs[-2], refs[-1]
    token_ref[...] = jnp.zeros_like(token_ref)
    f32, bf16 = jnp.float32, jnp.bfloat16
    nt = (((1,), (1,)), ((), ()))
    prompts, _, latent = query_ref.shape
    rows = steps * heads
    section_rank = lax.axis_index("section")
    first = lax.axis_index("expert") * sources + section_rank * prompts
    for prompt in range(prompts):
        at = slice(prompt * positions, (prompt + 1) * positions)
        projected = part_refs[0][at].astype(f32)
        for ref in part_refs[1:]:
            projected = projected + ref[at].astype(f32)
        keys = scaled(projected[:, :latent], gain_ref[...][None]).astype(bf16)
        key_rope = turn(
            projected[:, latent:], cosine_ref[:positions], sine_ref[:positions]
        ).astype(bf16)
        query, query_rope = query_ref[prompt], query_rope_ref[prompt]
        recent, recent_rope = recent_ref[prompt], recent_rope_ref[prompt]
        scores = lax.dot_general(query, keys, nt, preferred_element_type=f32)
        scores = scores + lax.dot_general(query_rope, key_rope, nt, preferred_element_type=f32)
        fresh = lax.dot_general(query, recent, nt, preferred_element_type=f32)
        fresh = fresh + lax.dot_general(query_rope, recent_rope, nt, preferred_element_type=f32)
        place = lax.broadcasted_iota(jnp.int32, scores.shape, 1)
        scores = jnp.where(
            place < length_ref[first + prompt], scores * score_scale, masked_value
        )
        row = lax.broadcasted_iota(jnp.int32, (rows, fresh.shape[1]), 0)
        place = lax.broadcasted_iota(jnp.int32, (rows, fresh.shape[1]), 1)
        seen = jnp.where(place < 1, 1.0, 0.0)
        for step in range(1, steps):
            seen = jnp.where((place <= step) & (row >= step * heads), 1.0, seen)
        seen = jnp.concatenate([seen] * sections, axis=0)
        fresh = jnp.where(seen > 0.5, fresh * score_scale, masked_value)
        most = jnp.maximum(
            jnp.max(scores, axis=-1, keepdims=True), jnp.max(fresh, axis=-1, keepdims=True)
        )
        scores = jnp.exp(scores - most)
        fresh = jnp.exp(fresh - most)
        total = jnp.sum(scores, axis=-1, keepdims=True) + jnp.sum(fresh, axis=-1, keepdims=True)
        scores = (scores / total).astype(bf16)
        fresh = (fresh / total).astype(bf16)
        mixed = jnp.dot(scores, keys, preferred_element_type=f32)
        mixed = mixed + jnp.dot(fresh, recent, preferred_element_type=f32)
        mixed = mixed.astype(bf16)
        for section in range(sections):
            held[section] = mixed[section * rows : (section + 1) * rows]
        for mask, ref in enumerate(out_refs):
            ref[prompt * rows : (prompt + 1) * rows, :] = held[section_rank ^ mask]


def attend(
    parts, positions, lengths, kv_gain, table, gathered, sources, steps, sections, score_scale
):
    prompts, rows, latent = gathered[0].shape
    out = (rows // sections, latent)
    held = pl.BlockSpec(memory_space=pltpu.VMEM)
    return pl.pallas_call(
        functools.partial(
            attend_kernel, len(parts), positions, sections, sources, out[0] // steps, steps,
            score_scale
        ),
        out_shape=[jax.ShapeDtypeStruct((prompts * out[0], latent), jnp.bfloat16)] * sections
        + [jax.ShapeDtypeStruct((8, 128), jnp.bfloat16)],
        in_specs=[held] * len(parts)
        + [pl.BlockSpec(memory_space=pltpu.SMEM)]
        + [held] * 7,
        out_specs=[held] * (sections + 1),
        scratch_shapes=[pltpu.VMEM((sections,) + out, jnp.bfloat16)],
        compiler_params=params(*parts, *gathered, scale=6),
        name="attend",
    )(*parts, *at_home(lengths, kv_gain, *table), *gathered)


def value_kernel(experts, sections, heads, steps, sources, count, *refs):
    owner_ref, latent_refs, uv_refs = refs[0], refs[1 : 1 + sections], refs[1 + sections :]
    route_ref = uv_refs[count]
    uv_refs = list(uv_refs[:count])
    out_ref, held = refs[-2:]
    group_rank, groups = lax.axis_index("groups"), lax.axis_size("groups")
    weights = []
    while uv_refs:
        if uv_refs[0].shape[0] == heads:
            weights.append(uv_refs[:1])
        else:
            weights.append(uv_refs[:groups])
        uv_refs = uv_refs[len(weights[-1]) :]
    f32, bf16 = jnp.float32, jnp.bfloat16
    chunk = weights[0][0].shape[2]
    rows = latent_refs[0].shape[0]
    for mask, ref in enumerate(latent_refs):
        for index in range(experts):
            held[index, mask * rows : (mask + 1) * rows, :chunk] = ref[
                :, index * chunk : (index + 1) * chunk
            ].astype(f32)
    rank = lax.axis_index("expert")
    values = []
    for head in range(heads):
        at = pl.ds(head, sections * rows // heads, stride=heads)
        total = 0
        for mask, shares in enumerate(weights):
            size = shares[0].shape[0]
            weight = shares[0][head % size]
            for other in range(1, len(shares)):
                mine = (group_rank ^ other) == head // size
                weight = jnp.where(mine, shares[other][head % size], weight)
            total = total + lax.dot_general(
                held[rank ^ mask, at, :][:, :chunk].astype(bf16),
                weight,
                (((1,), (1,)), ((), ())),
                preferred_element_type=f32,
            )
        values.append(total.astype(bf16))
    values = jnp.concatenate(values, axis=1)
    prompts = sources // sections
    section_rank = lax.axis_index("section")
    size = sources * steps
    to = lax.broadcasted_iota(jnp.int32, (size, size), 0)
    row = lax.broadcasted_iota(jnp.int32, (size, size), 1)
    order = jnp.zeros((size, size), f32)
    for mask in range(sections):
        for prompt in range(prompts):
            owner = owner_ref[
                rank * sources + (section_rank ^ mask) * prompts + prompt
            ]
            for step in range(steps):
                index = (mask * prompts + prompt) * steps + step
                order = jnp.where((row == index) & (to == owner * steps + step), 1.0, order)
    width = values.shape[1]
    out_ref[:, :width] = jnp.dot(
        order.astype(bf16), values, preferred_element_type=f32
    ).astype(bf16)
    out_ref[:, width:] = route_ref[...]


def head_products(owners, latents, uv_parts, route, steps, sources, after):
    rows, width = latents[0].shape
    heads, value, _ = uv_parts[0][0].shape
    experts = len(uv_parts)
    uv_parts = [share for part in uv_parts for share in part]
    held = pl.BlockSpec(memory_space=pltpu.VMEM)
    total = rows * len(latents)
    return pl.pallas_call(
        functools.partial(
            value_kernel, experts, len(latents), heads, steps, sources, len(uv_parts)
        ),
        out_shape=jax.ShapeDtypeStruct(
            (total // heads, heads * value + route.shape[1]), jnp.bfloat16
        ),
        in_specs=[pl.BlockSpec(memory_space=pltpu.SMEM)]
        + [held] * (len(latents) + len(uv_parts) + 1)
        + [pl.BlockSpec(memory_space=pl.ANY)] * len(after),
        out_specs=held,
        scratch_shapes=[
            pltpu.VMEM((experts, total, max(width // experts, 128)), jnp.float32)
        ],
        compiler_params=params(*latents, *uv_parts, scale=4),
        name="head_products",
    )(*at_home(owners), *latents, *uv_parts, route, *after)


def output_kernel(experts, *refs):
    value_refs = refs[:experts]
    weight_ref, out_ref = refs[experts:]
    depth = weight_ref.shape[0]
    values = jnp.concatenate([ref[:, :depth] for ref in value_refs], axis=0)
    rows = values.shape[0]
    to = lax.broadcasted_iota(jnp.int32, (rows, rows), 0)
    row = lax.broadcasted_iota(jnp.int32, (rows, rows), 1)
    source = (to & (experts - 1)) ^ lax.axis_index("expert")
    rest = lax.shift_right_logical(to, experts.bit_length() - 1)
    order = jnp.where(row == source * (rows // experts) + rest, 1.0, 0.0).astype(jnp.bfloat16)
    values = jnp.dot(order, values, preferred_element_type=jnp.float32).astype(jnp.bfloat16)
    out_ref[...] = jnp.dot(
        values, weight_ref[...], preferred_element_type=jnp.float32
    ).astype(out_ref.dtype)


def output_product(values, weight):
    rows = sum(value.shape[0] for value in values)
    held = pl.BlockSpec(memory_space=pltpu.VMEM)
    return pl.pallas_call(
        functools.partial(output_kernel, len(values)),
        out_shape=jax.ShapeDtypeStruct((rows, weight.shape[1]), jnp.bfloat16),
        in_specs=[held] * (len(values) + 1),
        out_specs=held,
        compiler_params=params(*values, scale=8),
        name="output_product",
    )(*values, weight)


def mix_kernel(count, owners, rows, *refs):
    part_refs, own_refs = refs[:count], refs[count : count + owners]
    out_ref, held = refs[-2:]
    f32 = jnp.float32
    total = part_refs[0][...].astype(f32)
    for ref in part_refs[1:]:
        total = total + ref[...].astype(f32)
    block, column = held.shape[1:]
    for owner in range(owners):
        held[owner] = total[owner * block : (owner + 1) * block]
    rank = lax.axis_index("expert")
    for mask, ref in enumerate(own_refs):
        lines = []
        for line, at in enumerate(range(0, column, ref.shape[1])):
            end = min(at + ref.shape[1], column)
            to = rows + line * block
            lines.append(ref[to : to + block, : end - at].astype(f32))
        lines = lines[0] if len(lines) == 1 else jnp.concatenate(lines, axis=1)
        out_ref[rank ^ mask] = (held[rank ^ mask] + lines).astype(out_ref.dtype)


def mix(parts, owns, rows, after):
    total, width = parts[0].shape
    owners = len(owns)
    held = pl.BlockSpec(memory_space=pltpu.VMEM)
    shape = (owners, total // owners, width)
    return pl.pallas_call(
        functools.partial(mix_kernel, len(parts), owners, rows),
        out_shape=jax.ShapeDtypeStruct(shape, parts[0].dtype),
        in_specs=[held] * (len(parts) + owners)
        + [pl.BlockSpec(memory_space=pl.ANY)] * len(after),
        out_specs=held,
        scratch_shapes=[pltpu.VMEM(shape, jnp.float32)],
        compiler_params=params(*parts, *owns, scale=4),
        name="mix",
    )(*parts, *owns, *after)


def expert_kernel(experts, sections, picks, *refs):
    mixed_refs, route_refs = refs[:experts], refs[experts : 2 * experts]
    gain_ref, gate_ref, up_ref, down_ref, out_ref, near_ref, columns = refs[2 * experts :]
    f32, bf16 = jnp.float32, jnp.bfloat16
    count = gate_ref.shape[0]
    rank = lax.axis_index("expert")
    width = gain_ref.shape[0]
    block = mixed_refs[0].shape[1]
    for mask, ref in enumerate(mixed_refs):
        columns[rank ^ mask] = ref[...]
    mixed, route = [], []
    for mask, ref in enumerate(route_refs):
        mixed.append(
            jnp.concatenate([columns[i, rank ^ mask] for i in range(experts)], axis=1).astype(f32)
        )
        route.append(ref[:, ref.shape[1] - 128 :].astype(f32))
    near = mixed[0]
    mixed = jnp.concatenate(mixed, axis=0)
    route = jnp.concatenate(route, axis=0)
    named = route[:, :picks]
    weights = route[:, picks : 2 * picks] + route[:, 2 * picks : 3 * picks]
    weights = route_scale * weights / jnp.sum(weights, axis=-1, keepdims=True)
    scale = lax.rsqrt(jnp.mean(mixed * mixed, axis=-1, keepdims=True) + epsilon)
    rows_in = (mixed * scale * gain_ref[...][None].astype(f32)).astype(bf16)
    column = width // sections
    total = 0
    for x in range(count):
        mine = (rank * count + x).astype(f32)
        weight = jnp.sum(jnp.where(named == mine, weights, 0.0), axis=-1, keepdims=True)
        gate = jnp.dot(rows_in, gate_ref[x], preferred_element_type=f32)
        up = jnp.dot(rows_in, up_ref[x], preferred_element_type=f32)
        inner = gate / (1.0 + jnp.exp(-gate)) * up * weight
        total = total + jnp.dot(inner.astype(bf16), down_ref[x], preferred_element_type=f32)
    for section in range(sections):
        at = slice(section * column, (section + 1) * column)
        near_ref[section] = near[:, at].astype(bf16)
        for mask in range(experts):
            out_ref[(rank ^ mask) * sections + section] = total[
                mask * block : (mask + 1) * block, at
            ].astype(bf16)


def run_experts(mixed, routes, gain, w_gate, w_up, w_down, picks, sections):
    experts = len(mixed)
    block = (mixed[0].shape[1], gain.shape[0] // sections)
    held = pl.BlockSpec(memory_space=pltpu.VMEM)
    return pl.pallas_call(
        functools.partial(expert_kernel, experts, sections, picks),
        out_shape=[
            jax.ShapeDtypeStruct((experts * sections,) + block, jnp.bfloat16),
            jax.ShapeDtypeStruct((sections,) + block, jnp.bfloat16),
        ],
        in_specs=[held] * (2 * experts + 4),
        out_specs=[held] * 2,
        scratch_shapes=[pltpu.VMEM((experts,) + mixed[0].shape, jnp.bfloat16)],
        compiler_params=params(*mixed, scale=32),
        name="run_experts",
    )(*mixed, *routes, *at_home(gain), w_gate, w_up, w_down)


def finish_kernel(block_ref, near_ref, out_ref):
    f32 = jnp.float32
    steps, sources, _ = out_ref.shape
    total = near_ref[lax.axis_index("section")].astype(f32)
    for index in range(block_ref.shape[0]):
        total = total + block_ref[index].astype(f32)
    for step in range(steps):
        out_ref[step] = total[step * sources : (step + 1) * sources].astype(out_ref.dtype)


def finish(blocks, near, steps):
    held = pl.BlockSpec(memory_space=pltpu.VMEM)
    _, rows, column = near.shape
    return pl.pallas_call(
        finish_kernel,
        out_shape=jax.ShapeDtypeStruct((steps, rows // steps, column), near.dtype),
        in_specs=[held] * 2,
        out_specs=held,
        compiler_params=params(blocks, near, scale=4),
        name="finish",
    )(blocks, near)


def local(
    prompts,
    owners,
    lengths,
    residual,
    queries,
    expert_ids,
    route_scores,
    attn_gain,
    w_dkv,
    kv_gain,
    w_uk,
    w_uv,
    w_o,
    moe_gain,
    w_gate,
    w_up,
    w_down,
):
    bf16, f32 = jnp.bfloat16, jnp.float32
    expert_rank = lax.axis_index("expert")
    section_rank = lax.axis_index("section")
    experts = lax.axis_size("expert")
    sections = lax.axis_size("section")
    groups = lax.axis_size("groups")
    prompt_count, full_length, width = prompts.shape
    steps, tokens_here, heads, _ = queries.shape
    depth = w_dkv.shape[0]
    piece = depth // experts
    latent = kv_gain.shape[0]
    cache_width = w_dkv.shape[1]
    rows = prompt_count * full_length
    own_rows = steps * tokens_here

    w_turned = w_dkv.T
    w_piece = lax.dynamic_slice_in_dim(w_turned, expert_rank * piece, piece, 1)
    masks = [1 << bit for bit in range(experts.bit_length() - 1)]
    far = masks[-1]
    w_parts = spread(w_piece, "section")
    uv_share, *cut = cut_columns(
        prompts.reshape(rows, width), queries, w_uv, sections, experts, groups
    )
    uv_share = swap(uv_share, "expert", far)
    cut = deliver(cut, "expert")

    blocks, riders, token = absorb_queries(
        owners, cut, queries.shape, w_uk, residual, attn_gain, w_turned, prompt_count, sections,
        [uv_share],
    )
    blocks = lax.all_to_all(blocks, ("expert", "section"), 0, 0, tiled=True)

    away = list(project(cut[1:], riders, w_parts, 1, rows, [token]))
    near = list(project(cut[:1], riders, w_parts, 0, rows, away[:1]))
    parts = deliver(near + away, "expert")
    table = rotation(full_length + steps + -(full_length + steps) % 8, cache_width - latent)
    gathered = list(gather_queries(
        blocks, lengths, owners, kv_gain, table, prompt_count, tokens_here, experts, sections,
        steps, heads
    ))
    *out_latent, token = attend(
        parts, full_length, lengths, kv_gain, table, gathered, tokens_here, steps, sections,
        queries.shape[-1] ** (-0.5),
    )

    (w_gate,) = fetch([w_gate], [token])
    uv_shares = spread(uv_share, "groups")
    *uv_shares, uv_own, token = lax.optimization_barrier((*uv_shares, w_uv, token))
    later = masks[1:-1] + masks[:1]
    held = [doubled({far: share}, "expert", later) for share in uv_shares]
    uv_parts = {mask: [share[mask] for share in held] for mask in held[0]}
    for mask, part in doubled({0: uv_own}, "expert", later).items():
        uv_parts[mask] = [part]
    out_latent = deliver(out_latent, "section")
    high = route_scores.astype(bf16)
    low = (route_scores - high.astype(f32)).astype(bf16)
    route = jnp.concatenate([expert_ids.astype(bf16), high, low], axis=2).reshape(own_rows, -1)
    route = jnp.pad(route, ((0, 0), (0, 128 - route.shape[1])))
    head_values = head_products(
        owners, out_latent, [uv_parts[mask] for mask in range(experts)], route, steps,
        tokens_here, [w_gate, token],
    )
    head_values = spread(head_values, "expert")

    (w_o,) = fetch([w_o], [])
    attended = output_product(head_values, w_o)
    (w_up,) = fetch([w_up], [attended])
    mixed = mix(spread(attended, "section"), parts, rows, [w_up])
    (w_down,) = fetch([w_down], [mixed])
    blocks, near = run_experts(
        spread(mixed, "expert"),
        head_values,
        moe_gain,
        w_gate,
        w_up,
        w_down,
        expert_ids.shape[2],
        sections,
    )
    blocks = lax.all_to_all(blocks, ("expert", "section"), 0, 0, tiled=True)
    return finish(blocks, near, steps)


def solution(mesh):
    placed = (
        P(("groups", "expert", "section"), None, None),
        P("groups"),
        P("groups"),
        P(None, ("groups", "expert"), None),
        P(None, ("groups", "expert"), "section", None),
        P(None, ("groups", "expert"), None),
        P(None, ("groups", "expert"), None),
        P(),
        P("section", None),
        P(),
        P("section", None, "expert"),
        P("section", None, "expert"),
        P("section", "expert"),
        P(),
        P("expert", None, "section"),
        P("expert", None, "section"),
        P("expert", "section", None),
    )
    return jax.shard_map(
        local,
        mesh=mesh,
        in_specs=placed,
        out_specs=P(None, ("groups", "expert"), "section"),
        check_vma=False,
    )
```

```python
import functools
import math

import jax
import jax.numpy as jnp
import numpy as np
from jax import lax
from jax.experimental import pallas as pl
from jax.experimental.pallas import tpu as pltpu
from jax.sharding import PartitionSpec as P

epsilon = 1e-06
masked_value = -1e30
route_scale = 2.5


def rotation(positions, width):
    halfway = width // 2
    frequency = 10000.0 ** (-2.0 * np.arange(halfway) / width)
    angles = np.arange(positions)[:, None] * frequency
    cosine = np.concatenate([np.cos(angles), np.cos(angles)], axis=1)
    sine = np.concatenate([-np.sin(angles), np.sin(angles)], axis=1)
    return jnp.asarray(cosine, jnp.float32), jnp.asarray(sine, jnp.float32)


def swap(block, axis, mask):
    size = lax.axis_size(axis)
    return lax.ppermute(block, axis, [(i, i ^ mask) for i in range(size)])


def deliver(blocks, axis):
    return [blocks[0]] + [swap(blocks[mask], axis, mask) for mask in range(1, len(blocks))]


def spread(block, axis):
    return [block] + [swap(block, axis, mask) for mask in range(1, lax.axis_size(axis))]


def params(*arrays, scale=1):
    held = sum(math.prod(array.shape) * array.dtype.itemsize for array in arrays)
    mebibytes = min(56, 4 + scale * held // 1024 // 1024)
    return pltpu.CompilerParams(vmem_limit_bytes=mebibytes * 1024 * 1024)


def at_home(*arrays):
    return [pltpu.with_memory_space_constraint(array, pltpu.HBM) for array in arrays]


def fetch_kernel(count, *refs):
    out_refs, sems = refs[-1 - count : -1], refs[-1]
    copies = [
        pltpu.make_async_copy(refs[index], out_refs[index], sems.at[index])
        for index in range(count)
    ]
    for copy in copies:
        copy.start()
    for copy in copies:
        copy.wait()


def fetch(arrays, after):
    size = sum(array.size * array.dtype.itemsize for array in arrays)
    return pl.pallas_call(
        functools.partial(fetch_kernel, len(arrays)),
        out_shape=[pltpu.VMEM(array.shape, array.dtype) for array in arrays],
        in_specs=[pl.BlockSpec(memory_space=pltpu.HBM)] * len(arrays)
        + [pl.BlockSpec(memory_space=pl.ANY)] * len(after),
        out_specs=[pl.BlockSpec(memory_space=pltpu.VMEM)] * len(arrays),
        scratch_shapes=[pltpu.SemaphoreType.DMA((len(arrays),))],
        compiler_params=pltpu.CompilerParams(vmem_limit_bytes=1024 * 1024),
        cost_estimate=pl.CostEstimate(flops=0, bytes_accessed=2 * size, transcendentals=0),
        name="fetch",
    )(*at_home(*arrays), *after)


def doubled(held, axis, masks):
    held = dict(held)
    for mask in masks:
        for other in list(held):
            held[other ^ mask] = swap(held[other], axis, mask)
    return held


def cut_kernel(sections, experts, piece, x_ref, query_ref, uv_ref, half_ref, *refs):
    out_refs, held = refs[-1 - experts : -1], refs[-1]
    share = half_ref.shape[0]
    half_ref[...] = uv_ref[pl.ds(lax.axis_index("groups") * share, share)]
    rank = lax.axis_index("expert")
    steps, sources, heads, wide = query_ref.shape
    rows = x_ref.shape[0]
    for target in range(experts):
        for section in range(sections):
            at = (section * experts + target) * piece
            held[target, section * rows : (section + 1) * rows] = x_ref[:, at : at + piece]
    for mask, ref in enumerate(out_refs):
        ref[: sections * rows, :piece] = held[rank ^ mask]
        for step in range(steps):
            for source in range(sources):
                at = sections * rows + (step * sources + source) * heads
                ref[at : at + heads, :wide] = query_ref[step, source]


def cut_columns(x, queries, w_uv, sections, experts, groups):
    rows, width = x.shape
    piece = width // (sections * experts)
    steps, sources, heads, wide = queries.shape
    block = jax.ShapeDtypeStruct(
        (sections * rows + steps * sources * heads, max(piece, wide)), x.dtype
    )
    return pl.pallas_call(
        functools.partial(cut_kernel, sections, experts, piece),
        out_shape=[
            jax.ShapeDtypeStruct((w_uv.shape[0] // groups,) + w_uv.shape[1:], w_uv.dtype)
        ]
        + [block] * experts,
        scratch_shapes=[pltpu.VMEM((experts, sections * rows, piece), x.dtype)],
        compiler_params=params(x, block, w_uv, scale=6),
        name="cut_columns",
    )(*at_home(x, queries, w_uv))


def project_kernel(count, first, rows, *refs):
    x_refs, rider_ref, w_refs, out_refs = refs[:count], refs[count], refs[count + 1 :], refs[-count:]
    section_rank = lax.axis_index("section")
    sections = lax.axis_size("section")
    piece = w_refs[0].shape[1]
    total = 0
    for mask in range(sections):
        at = pl.ds(pl.multiple_of((section_rank ^ mask) * rows, rows), rows)
        x = jnp.concatenate([ref[at, :piece] for ref in x_refs], axis=0)
        total = total + lax.dot_general(
            x, w_refs[mask][...], (((1,), (1,)), ((), ())), preferred_element_type=jnp.float32
        )
    for index, ref in enumerate(out_refs):
        ref[:rows, :] = total[index * rows : (index + 1) * rows].astype(ref.dtype)
        ref[rows:, :] = rider_ref[first + index]


def project(blocks, riders, w_parts, first, rows, after):
    out = jax.ShapeDtypeStruct((rows + riders.shape[1], riders.shape[2]), jnp.bfloat16)
    held = pl.BlockSpec(memory_space=pltpu.VMEM)
    return pl.pallas_call(
        functools.partial(project_kernel, len(blocks), first, rows),
        out_shape=[out] * len(blocks),
        in_specs=[held] * (len(blocks) + 1 + len(w_parts))
        + [pl.BlockSpec(memory_space=pl.ANY)] * len(after),
        compiler_params=params(*blocks, *w_parts, scale=6),
        name="project",
    )(*blocks, riders, *w_parts, *after)


def query_kernel(
    experts, sections, prompts, nope, shape, *refs
):
    f32, bf16 = jnp.float32, jnp.bfloat16
    table_ref, query_refs = refs[0], refs[1 : 1 + experts]
    uk_ref, own_ref, gain_ref, wt_ref = refs[1 + experts : 5 + experts]
    out_ref, rider_ref, token_ref, picked, ropes, made, normed, query_ref, columns = refs[-9:]
    token_ref[...] = jnp.zeros_like(token_ref)
    steps, sources, heads, wide = shape
    rope = wide - nope
    chunk = uk_ref.shape[2]
    width = out_ref.shape[2]
    count = experts * sources
    block = prompts * steps * heads
    rank = lax.axis_index("expert")

    for mask, ref in enumerate(query_refs):
        for step in range(steps):
            for source in range(sources):
                at = ref.shape[0] - (steps * sources - step * sources - source) * heads
                query_ref[rank ^ mask, step, source] = ref[at : at + heads, :wide]

    def pick(index, carry):
        owner = table_ref[index]
        for step in range(steps):
            value = query_ref[owner, step, index // sources].astype(f32)
            at = pl.ds(pl.multiple_of((index * steps + step) * heads, heads), heads)
            picked[at, :] = value[:, :nope]
            ropes[at, :rope] = value[:, nope:]
        return carry

    if count <= 16:
        for index in range(count):
            pick(index, 0)
    else:
        lax.fori_loop(0, count, pick, 0)
    for head in range(heads):
        at = pl.ds(head, count * steps, stride=heads)
        value = jnp.dot(picked[at, :].astype(bf16), uk_ref[head], preferred_element_type=f32)
        if chunk < made.shape[1]:
            spare = jnp.zeros((count * steps, made.shape[1] - chunk), f32)
            value = jnp.concatenate([value, spare], axis=1)
        made[at, :] = value
    small = (rope + experts - 1) // experts
    lanes = rope if width != chunk else width
    groups = width // small if width == chunk else 1
    source_lane = lax.broadcasted_iota(jnp.int32, (rope, lanes), 0)
    lane = lax.broadcasted_iota(jnp.int32, (rope, lanes), 1)
    turned = 0
    for group in range(groups):
        pair = (source_lane == lane - group * small + rank * small) & (
            (lane >= group * small) & (lane < (group + 1) * small)
        )
        at = pl.ds(group, count * steps * heads // groups, stride=groups)
        turned = turned + jnp.dot(
            ropes[at, :][:, :rope].astype(bf16),
            jnp.where(pair, 1.0, 0.0).astype(bf16),
            preferred_element_type=f32,
        )
    own = jnp.concatenate([own_ref[step] for step in range(steps)], axis=0).astype(f32)
    lines, column = columns.shape[1:]
    for target in range(experts):
        columns[target] = own[:, target * column : (target + 1) * column]
    for mask in range(experts):
        value = columns[rank ^ mask]
        for line, at in enumerate(range(0, column, rider_ref.shape[2])):
            end = min(at + rider_ref.shape[2], column)
            rider_ref[mask, line * lines : (line + 1) * lines, : end - at] = value[
                :, at:end
            ].astype(bf16)
    scale = lax.rsqrt(jnp.mean(own * own, axis=-1, keepdims=True) + epsilon)
    own = (own * scale * gain_ref[...][None].astype(f32)).astype(bf16)
    depth = wt_ref.shape[1]
    for section in range(sections):
        normed[section] = own[:, section * depth : (section + 1) * depth]
    fresh = lax.dot_general(
        normed[lax.axis_index("section")],
        wt_ref[...],
        (((1,), (1,)), ((), ())),
        preferred_element_type=f32,
    )
    for source in range(experts):
        picks = [step * sources + source for step in range(steps)]
        if width == chunk:
            latent = width * experts
            lines = [
                fresh[pick:, part * width : (part + 1) * width][:1]
                for pick in picks
                for part in range(experts)
            ]
            lines.append(
                jnp.concatenate([fresh[pick:, latent:][:1] for pick in picks], axis=1)
            )
        else:
            lines = [
                fresh[pick:, part * width : (part + 1) * width][:1]
                for pick in picks
                for part in range(experts)
            ]
        lines = jnp.concatenate(lines, axis=0).astype(bf16)
        for section in range(sections):
            index = source * sections + section
            at = slice(index * block, (index + 1) * block)
            if width == chunk:
                few = block // groups
                out_ref[index, :block, :] = made[at, :chunk].astype(bf16)
                tail = [turned[index * few : (index + 1) * few].astype(bf16), lines]
                spare = out_ref.shape[1] - block - few - lines.shape[0]
                if spare:
                    tail.append(jnp.zeros((spare, width), bf16))
                out_ref[index, block:, :] = jnp.concatenate(tail, axis=0)
            else:
                value = jnp.concatenate([made[at, :chunk], turned[at, :small]], axis=1)
                out_ref[index, :block, :] = value.astype(bf16)
                out_ref[index, block:, :] = lines


def block_shape(prompts, steps, heads, experts, chunk, rope):
    rows = prompts * steps * heads
    small = rope // experts
    if chunk == 128 and small * 8 == chunk and steps * rope == chunk:
        rows = rows + rows // 8 + steps * experts + 1
        return rows + -rows % 16, chunk
    return rows + steps * experts, chunk + small


def absorb_queries(table, queries, shape, w_uk, own, gain, w_turned, prompts, sections, after):
    experts = len(queries)
    steps, sources, heads, wide = shape
    _, nope, chunk = w_uk.shape
    rows, width = block_shape(prompts, steps, heads, experts, chunk, wide - nope)
    block, column = own.shape[0] * own.shape[1], own.shape[2] // experts
    cache_width = w_turned.shape[0]
    count = experts * sources * steps * heads
    held = pl.BlockSpec(memory_space=pltpu.VMEM)
    return pl.pallas_call(
        functools.partial(query_kernel, experts, sections, prompts, nope, shape),
        out_shape=[
            jax.ShapeDtypeStruct((experts * sections, rows, width), jnp.bfloat16),
            jax.ShapeDtypeStruct(
                (experts, block * -(-column // cache_width), cache_width), jnp.bfloat16
            ),
            jax.ShapeDtypeStruct((8, 128), jnp.bfloat16),
        ],
        in_specs=[pl.BlockSpec(memory_space=pltpu.SMEM)]
        + [held] * (experts + 4)
        + [pl.BlockSpec(memory_space=pl.ANY)] * len(after),
        out_specs=[held] * 3,
        scratch_shapes=[
            pltpu.VMEM((count, nope), jnp.float32),
            pltpu.VMEM((count, max(wide - nope, 128)), jnp.float32),
            pltpu.VMEM((count, max(chunk, 128)), jnp.float32),
            pltpu.VMEM(
                (sections, own.shape[0] * own.shape[1], w_turned.shape[1]), jnp.bfloat16
            ),
            pltpu.VMEM((experts,) + shape, jnp.bfloat16),
            pltpu.VMEM((experts, block, column), jnp.float32),
        ],
        compiler_params=params(*queries, w_uk, own, w_turned, scale=4),
        name="absorb_queries",
    )(*at_home(table), *queries, *at_home(w_uk, own, gain, w_turned), *after)


def turn(values, cosine, sine):
    half = values.shape[1] // 2
    other = jnp.concatenate([values[:, half:], values[:, :half]], axis=1)
    return values * cosine + other * sine


def scaled(values, gain):
    scale = lax.rsqrt(jnp.mean(values * values, axis=-1, keepdims=True) + epsilon)
    return values * scale * gain.astype(jnp.float32)


def gather_kernel(
    prompts, experts, sections, sources, heads, steps, latent, length_ref, owner_ref, gain_ref,
    cosine_ref, sine_ref, block_ref, query_ref, query_rope_ref, recent_ref, recent_rope_ref,
    cosine_held, sine_held, ropes_held
):
    f32, bf16 = jnp.float32, jnp.bfloat16
    rows = steps * heads
    chunk = latent // experts
    whole = block_ref.shape[2] == chunk
    extra = prompts * rows // 8 if whole else 0
    first = lax.axis_index("expert") * sources + lax.axis_index("section") * prompts
    gain = gain_ref[...][None]
    for prompt in range(prompts):
        length, owner = length_ref[first + prompt], owner_ref[first + prompt]
        for step in range(steps):
            at = slice(step * heads, (step + 1) * heads)
            cosine_held[at, :] = jnp.broadcast_to(
                cosine_ref[pl.ds(length + step, 1), :], (heads, cosine_ref.shape[1])
            )
            sine_held[at, :] = jnp.broadcast_to(
                sine_ref[pl.ds(length + step, 1), :], (heads, sine_ref.shape[1])
            )
        cosine, sine = cosine_held[...], sine_held[...]
        if whole:
            few = rows // 8
            small = cosine.shape[1] // experts
            low = prompts * rows + prompt * few
            tail = jnp.concatenate(
                [
                    jnp.concatenate(
                        [block_ref[i * sections + section, low : low + few, :]
                         for i in range(experts)],
                        axis=1,
                    )
                    for section in range(sections)
                ],
                axis=0,
            )
            shape = (experts * chunk, experts * small)
            source_lane = lax.broadcasted_iota(jnp.int32, shape, 0)
            lane = lax.broadcasted_iota(jnp.int32, shape, 1)
            bits = small.bit_length() - 1
            lane = lax.shift_right_logical(lane, bits) * chunk + (lane & (small - 1))
            for group in range(8):
                pair = jnp.where(source_lane == lane + group * small, 1.0, 0.0).astype(bf16)
                value = jnp.dot(tail, pair, preferred_element_type=f32)
                pad = ropes_held.shape[1] - value.shape[1]
                value = jnp.concatenate([value, jnp.zeros((value.shape[0], pad), f32)], axis=1)
                ropes_held[pl.ds(group, sections * few, stride=8), :] = value
        at = slice(prompt * rows, (prompt + 1) * rows)
        for section in range(sections):
            pieces = [block_ref[i * sections + section, at, :] for i in range(experts)]
            to = slice(section * rows, (section + 1) * rows)
            query_ref[prompt, to, :] = jnp.concatenate(
                [piece[:, :chunk] for piece in pieces], axis=1
            )
            if whole:
                rope = ropes_held[to, : cosine.shape[1]]
            else:
                rope = jnp.concatenate(
                    [piece[:, chunk:].astype(f32) for piece in pieces], axis=1
                )
            query_rope_ref[prompt, to, :] = turn(rope, cosine, sine).astype(bf16)
        lines = 0
        for section in range(sections):
            lines = lines + block_ref[
                owner * sections + section, prompts * rows + extra :, :
            ].astype(f32)
        recent, recent_rope = [], []
        for step in range(steps):
            parts = [lines[step * experts + part :][:1] for part in range(experts)]
            if whole:
                end = cosine.shape[1]
                parts.append(
                    lines[steps * experts :][:1, step * end : (step + 1) * end]
                )
            line = jnp.concatenate(parts, axis=1)
            recent.append(scaled(line[:, :latent], gain))
            at = slice(step * heads, step * heads + 1)
            recent_rope.append(turn(line[:, latent:], cosine[at], sine[at]))
        spare = recent_ref.shape[1] - steps
        recent.append(jnp.zeros((spare, latent), f32))
        recent_rope.append(jnp.zeros((spare, recent_rope[0].shape[1]), f32))
        recent_ref[prompt] = jnp.concatenate(recent, axis=0).astype(bf16)
        recent_rope_ref[prompt] = jnp.concatenate(recent_rope, axis=0).astype(bf16)


def gather_queries(blocks, lengths, owners, kv_gain, table, prompts, sources, experts, sections,
                   steps, heads):
    latent = kv_gain.shape[0]
    rope = table[0].shape[1]
    rows = sections * steps * heads
    spare = steps + -steps % 16
    shape = lambda *sizes: jax.ShapeDtypeStruct((prompts,) + sizes, jnp.bfloat16)
    held = pl.BlockSpec(memory_space=pltpu.VMEM)
    return pl.pallas_call(
        functools.partial(
            gather_kernel, prompts, experts, sections, sources, heads, steps, latent
        ),
        out_shape=[shape(rows, latent), shape(rows, rope), shape(spare, latent), shape(spare, rope)],
        in_specs=[pl.BlockSpec(memory_space=pltpu.SMEM)] * 2 + [held] * 4,
        out_specs=[held] * 4,
        scratch_shapes=[pltpu.VMEM((steps * heads, rope), jnp.float32)] * 2
        + [pltpu.VMEM((rows, 128), jnp.float32)],
        compiler_params=params(blocks, scale=4),
        name="gather_queries",
    )(*at_home(lengths, owners, kv_gain, *table), blocks)


def attend_kernel(parts, positions, sections, sources, heads, steps, score_scale, *refs):
    part_refs = refs[:parts]
    (length_ref, gain_ref, cosine_ref, sine_ref, query_ref, query_rope_ref, recent_ref,
     recent_rope_ref) = refs[parts : parts + 8]
    out_refs, token_ref, held = refs[-2 - sections : -2], refs[-2], refs[-1]
    token_ref[...] = jnp.zeros_like(token_ref)
    f32, bf16 = jnp.float32, jnp.bfloat16
    nt = (((1,), (1,)), ((), ()))
    prompts, _, latent = query_ref.shape
    rows = steps * heads
    section_rank = lax.axis_index("section")
    first = lax.axis_index("expert") * sources + section_rank * prompts
    for prompt in range(prompts):
        at = slice(prompt * positions, (prompt + 1) * positions)
        projected = part_refs[0][at].astype(f32)
        for ref in part_refs[1:]:
            projected = projected + ref[at].astype(f32)
        keys = scaled(projected[:, :latent], gain_ref[...][None]).astype(bf16)
        key_rope = turn(
            projected[:, latent:], cosine_ref[:positions], sine_ref[:positions]
        ).astype(bf16)
        query, query_rope = query_ref[prompt], query_rope_ref[prompt]
        recent, recent_rope = recent_ref[prompt], recent_rope_ref[prompt]
        scores = lax.dot_general(query, keys, nt, preferred_element_type=f32)
        scores = scores + lax.dot_general(query_rope, key_rope, nt, preferred_element_type=f32)
        fresh = lax.dot_general(query, recent, nt, preferred_element_type=f32)
        fresh = fresh + lax.dot_general(query_rope, recent_rope, nt, preferred_element_type=f32)
        place = lax.broadcasted_iota(jnp.int32, scores.shape, 1)
        scores = jnp.where(
            place < length_ref[first + prompt], scores * score_scale, masked_value
        )
        row = lax.broadcasted_iota(jnp.int32, (rows, fresh.shape[1]), 0)
        place = lax.broadcasted_iota(jnp.int32, (rows, fresh.shape[1]), 1)
        seen = jnp.where(place < 1, 1.0, 0.0)
        for step in range(1, steps):
            seen = jnp.where((place <= step) & (row >= step * heads), 1.0, seen)
        seen = jnp.concatenate([seen] * sections, axis=0)
        fresh = jnp.where(seen > 0.5, fresh * score_scale, masked_value)
        most = jnp.maximum(
            jnp.max(scores, axis=-1, keepdims=True), jnp.max(fresh, axis=-1, keepdims=True)
        )
        scores = jnp.exp(scores - most)
        fresh = jnp.exp(fresh - most)
        total = jnp.sum(scores, axis=-1, keepdims=True) + jnp.sum(fresh, axis=-1, keepdims=True)
        scores = (scores / total).astype(bf16)
        fresh = (fresh / total).astype(bf16)
        mixed = jnp.dot(scores, keys, preferred_element_type=f32)
        mixed = mixed + jnp.dot(fresh, recent, preferred_element_type=f32)
        mixed = mixed.astype(bf16)
        for section in range(sections):
            held[section] = mixed[section * rows : (section + 1) * rows]
        for mask, ref in enumerate(out_refs):
            ref[prompt * rows : (prompt + 1) * rows, :] = held[section_rank ^ mask]


def attend(
    parts, positions, lengths, kv_gain, table, gathered, sources, steps, sections, score_scale,
    after
):
    prompts, rows, latent = gathered[0].shape
    out = (rows // sections, latent)
    held = pl.BlockSpec(memory_space=pltpu.VMEM)
    return pl.pallas_call(
        functools.partial(
            attend_kernel, len(parts), positions, sections, sources, out[0] // steps, steps,
            score_scale
        ),
        out_shape=[jax.ShapeDtypeStruct((prompts * out[0], latent), jnp.bfloat16)] * sections
        + [jax.ShapeDtypeStruct((8, 128), jnp.bfloat16)],
        in_specs=[held] * len(parts)
        + [pl.BlockSpec(memory_space=pltpu.SMEM)]
        + [held] * 7
        + [pl.BlockSpec(memory_space=pl.ANY)] * len(after),
        out_specs=[held] * (sections + 1),
        scratch_shapes=[pltpu.VMEM((sections,) + out, jnp.bfloat16)],
        compiler_params=params(*parts, *gathered, scale=6),
        name="attend",
    )(*parts, *at_home(lengths, kv_gain, *table), *gathered, *after)


def value_kernel(experts, sections, heads, steps, sources, count, *refs):
    owner_ref, latent_refs, uv_refs = refs[0], refs[1 : 1 + sections], refs[1 + sections :]
    name_ref, score_ref = uv_refs[count : count + 2]
    uv_refs = list(uv_refs[:count])
    out_ref, held = refs[-2:]
    group_rank, groups = lax.axis_index("groups"), lax.axis_size("groups")
    weights = []
    while uv_refs:
        if uv_refs[0].shape[0] == heads:
            weights.append(uv_refs[:1])
        else:
            weights.append(uv_refs[:groups])
        uv_refs = uv_refs[len(weights[-1]) :]
    f32, bf16 = jnp.float32, jnp.bfloat16
    chunk = weights[0][0].shape[2]
    rows = latent_refs[0].shape[0]
    for mask, ref in enumerate(latent_refs):
        for index in range(experts):
            held[index, mask * rows : (mask + 1) * rows, :chunk] = ref[
                :, index * chunk : (index + 1) * chunk
            ].astype(f32)
    rank = lax.axis_index("expert")
    values = []
    for head in range(heads):
        at = pl.ds(head, sections * rows // heads, stride=heads)
        total = 0
        for mask, shares in enumerate(weights):
            size = shares[0].shape[0]
            weight = shares[0][head % size]
            for other in range(1, len(shares)):
                mine = (group_rank ^ other) == head // size
                weight = jnp.where(mine, shares[other][head % size], weight)
            total = total + lax.dot_general(
                held[rank ^ mask, at, :][:, :chunk].astype(bf16),
                weight,
                (((1,), (1,)), ((), ())),
                preferred_element_type=f32,
            )
        values.append(total.astype(bf16))
    values = jnp.concatenate(values, axis=1)
    prompts = sources // sections
    section_rank = lax.axis_index("section")
    size = sources * steps
    to = lax.broadcasted_iota(jnp.int32, (size, size), 0)
    row = lax.broadcasted_iota(jnp.int32, (size, size), 1)
    order = jnp.zeros((size, size), f32)
    for mask in range(sections):
        for prompt in range(prompts):
            owner = owner_ref[
                rank * sources + (section_rank ^ mask) * prompts + prompt
            ]
            for step in range(steps):
                index = (mask * prompts + prompt) * steps + step
                order = jnp.where((row == index) & (to == owner * steps + step), 1.0, order)
    width = values.shape[1]
    out_ref[:, :width] = jnp.dot(
        order.astype(bf16), values, preferred_element_type=f32
    ).astype(bf16)
    names = jnp.concatenate([name_ref[step] for step in range(steps)], axis=0).astype(f32)
    scores = jnp.concatenate([score_ref[step] for step in range(steps)], axis=0)
    high = scores.astype(bf16).astype(f32)
    spare = jnp.zeros((size, out_ref.shape[1] - width - 3 * names.shape[1]), f32)
    route = jnp.concatenate([names, high, scores - high, spare], axis=1)
    out_ref[:, width:] = route.astype(bf16)


def head_products(owners, latents, uv_parts, names, scores, steps, sources, after):
    rows, width = latents[0].shape
    heads, value, _ = uv_parts[0][0].shape
    experts = len(uv_parts)
    uv_parts = [share for part in uv_parts for share in part]
    held = pl.BlockSpec(memory_space=pltpu.VMEM)
    total = rows * len(latents)
    return pl.pallas_call(
        functools.partial(
            value_kernel, experts, len(latents), heads, steps, sources, len(uv_parts)
        ),
        out_shape=jax.ShapeDtypeStruct(
            (total // heads, heads * value + 128), jnp.bfloat16
        ),
        in_specs=[pl.BlockSpec(memory_space=pltpu.SMEM)]
        + [held] * (len(latents) + len(uv_parts) + 2)
        + [pl.BlockSpec(memory_space=pl.ANY)] * len(after),
        out_specs=held,
        scratch_shapes=[
            pltpu.VMEM((experts, total, max(width // experts, 128)), jnp.float32)
        ],
        compiler_params=params(*latents, *uv_parts, scale=4),
        name="head_products",
    )(*at_home(owners), *latents, *uv_parts, *at_home(names, scores), *after)


def output_kernel(experts, *refs):
    value_refs = refs[:experts]
    weight_ref, out_ref = refs[experts:]
    depth = weight_ref.shape[0]
    values = jnp.concatenate([ref[:, :depth] for ref in value_refs], axis=0)
    rows = values.shape[0]
    to = lax.broadcasted_iota(jnp.int32, (rows, rows), 0)
    row = lax.broadcasted_iota(jnp.int32, (rows, rows), 1)
    source = (to & (experts - 1)) ^ lax.axis_index("expert")
    rest = lax.shift_right_logical(to, experts.bit_length() - 1)
    order = jnp.where(row == source * (rows // experts) + rest, 1.0, 0.0).astype(jnp.bfloat16)
    values = jnp.dot(order, values, preferred_element_type=jnp.float32).astype(jnp.bfloat16)
    out_ref[...] = jnp.dot(
        values, weight_ref[...], preferred_element_type=jnp.float32
    ).astype(out_ref.dtype)


def output_product(values, weight):
    rows = sum(value.shape[0] for value in values)
    held = pl.BlockSpec(memory_space=pltpu.VMEM)
    return pl.pallas_call(
        functools.partial(output_kernel, len(values)),
        out_shape=jax.ShapeDtypeStruct((rows, weight.shape[1]), jnp.bfloat16),
        in_specs=[held] * (len(values) + 1),
        out_specs=held,
        compiler_params=params(*values, scale=8),
        name="output_product",
    )(*values, weight)


def mix_kernel(count, owners, rows, *refs):
    part_refs, own_refs = refs[:count], refs[count : count + owners]
    out_ref, held = refs[-2:]
    f32 = jnp.float32
    total = part_refs[0][...].astype(f32)
    for ref in part_refs[1:]:
        total = total + ref[...].astype(f32)
    block, column = held.shape[1:]
    for owner in range(owners):
        held[owner] = total[owner * block : (owner + 1) * block]
    rank = lax.axis_index("expert")
    for mask, ref in enumerate(own_refs):
        lines = []
        for line, at in enumerate(range(0, column, ref.shape[1])):
            end = min(at + ref.shape[1], column)
            to = rows + line * block
            lines.append(ref[to : to + block, : end - at].astype(f32))
        lines = lines[0] if len(lines) == 1 else jnp.concatenate(lines, axis=1)
        out_ref[rank ^ mask] = (held[rank ^ mask] + lines).astype(out_ref.dtype)


def mix(parts, owns, rows, after):
    total, width = parts[0].shape
    owners = len(owns)
    held = pl.BlockSpec(memory_space=pltpu.VMEM)
    shape = (owners, total // owners, width)
    return pl.pallas_call(
        functools.partial(mix_kernel, len(parts), owners, rows),
        out_shape=jax.ShapeDtypeStruct(shape, parts[0].dtype),
        in_specs=[held] * (len(parts) + owners)
        + [pl.BlockSpec(memory_space=pl.ANY)] * len(after),
        out_specs=held,
        scratch_shapes=[pltpu.VMEM(shape, jnp.float32)],
        compiler_params=params(*parts, *owns, scale=4),
        name="mix",
    )(*parts, *owns, *after)


def expert_kernel(experts, sections, picks, *refs):
    mixed_refs, route_refs = refs[:experts], refs[experts : 2 * experts]
    gain_ref, gate_ref, up_ref, down_ref, out_ref, near_ref, columns = refs[2 * experts :]
    f32, bf16 = jnp.float32, jnp.bfloat16
    count = gate_ref.shape[0]
    rank = lax.axis_index("expert")
    width = gain_ref.shape[0]
    block = mixed_refs[0].shape[1]
    for mask, ref in enumerate(mixed_refs):
        columns[rank ^ mask] = ref[...]
    mixed, route = [], []
    for mask, ref in enumerate(route_refs):
        mixed.append(
            jnp.concatenate([columns[i, rank ^ mask] for i in range(experts)], axis=1).astype(f32)
        )
        route.append(ref[:, ref.shape[1] - 128 :].astype(f32))
    near = mixed[0]
    mixed = jnp.concatenate(mixed, axis=0)
    route = jnp.concatenate(route, axis=0)
    named = route[:, :picks]
    weights = route[:, picks : 2 * picks] + route[:, 2 * picks : 3 * picks]
    weights = route_scale * weights / jnp.sum(weights, axis=-1, keepdims=True)
    scale = lax.rsqrt(jnp.mean(mixed * mixed, axis=-1, keepdims=True) + epsilon)
    rows_in = (mixed * scale * gain_ref[...][None].astype(f32)).astype(bf16)
    column = width // sections
    total = 0
    for x in range(count):
        mine = (rank * count + x).astype(f32)
        weight = jnp.sum(jnp.where(named == mine, weights, 0.0), axis=-1, keepdims=True)
        gate = jnp.dot(rows_in, gate_ref[x], preferred_element_type=f32)
        up = jnp.dot(rows_in, up_ref[x], preferred_element_type=f32)
        inner = gate / (1.0 + jnp.exp(-gate)) * up * weight
        total = total + jnp.dot(inner.astype(bf16), down_ref[x], preferred_element_type=f32)
    for section in range(sections):
        at = slice(section * column, (section + 1) * column)
        near_ref[section] = near[:, at].astype(bf16)
        for mask in range(experts):
            out_ref[(rank ^ mask) * sections + section] = total[
                mask * block : (mask + 1) * block, at
            ].astype(bf16)


def run_experts(mixed, routes, gain, w_gate, w_up, w_down, picks, sections):
    experts = len(mixed)
    block = (mixed[0].shape[1], gain.shape[0] // sections)
    held = pl.BlockSpec(memory_space=pltpu.VMEM)
    return pl.pallas_call(
        functools.partial(expert_kernel, experts, sections, picks),
        out_shape=[
            jax.ShapeDtypeStruct((experts * sections,) + block, jnp.bfloat16),
            jax.ShapeDtypeStruct((sections,) + block, jnp.bfloat16),
        ],
        in_specs=[held] * (2 * experts + 4),
        out_specs=[held] * 2,
        scratch_shapes=[pltpu.VMEM((experts,) + mixed[0].shape, jnp.bfloat16)],
        compiler_params=params(*mixed, scale=32),
        name="run_experts",
    )(*mixed, *routes, *at_home(gain), w_gate, w_up, w_down)


def finish_kernel(block_ref, near_ref, out_ref):
    f32 = jnp.float32
    steps, sources, _ = out_ref.shape
    total = near_ref[lax.axis_index("section")].astype(f32)
    for index in range(block_ref.shape[0]):
        total = total + block_ref[index].astype(f32)
    for step in range(steps):
        out_ref[step] = total[step * sources : (step + 1) * sources].astype(out_ref.dtype)


def finish(blocks, near, steps):
    held = pl.BlockSpec(memory_space=pltpu.VMEM)
    _, rows, column = near.shape
    return pl.pallas_call(
        finish_kernel,
        out_shape=jax.ShapeDtypeStruct((steps, rows // steps, column), near.dtype),
        in_specs=[held] * 2,
        out_specs=held,
        compiler_params=params(blocks, near, scale=4),
        name="finish",
    )(blocks, near)


def local(
    prompts,
    owners,
    lengths,
    residual,
    queries,
    expert_ids,
    route_scores,
    attn_gain,
    w_dkv,
    kv_gain,
    w_uk,
    w_uv,
    w_o,
    moe_gain,
    w_gate,
    w_up,
    w_down,
):
    bf16, f32 = jnp.bfloat16, jnp.float32
    expert_rank = lax.axis_index("expert")
    section_rank = lax.axis_index("section")
    experts = lax.axis_size("expert")
    sections = lax.axis_size("section")
    groups = lax.axis_size("groups")
    prompt_count, full_length, width = prompts.shape
    steps, tokens_here, heads, _ = queries.shape
    depth = w_dkv.shape[0]
    piece = depth // experts
    latent = kv_gain.shape[0]
    cache_width = w_dkv.shape[1]
    rows = prompt_count * full_length
    own_rows = steps * tokens_here

    w_turned = w_dkv.T
    w_piece = lax.dynamic_slice_in_dim(w_turned, expert_rank * piece, piece, 1)
    masks = [1 << bit for bit in range(experts.bit_length() - 1)]
    far = masks[-1]
    w_parts = spread(w_piece, "section")
    uv_share, *cut = cut_columns(
        prompts.reshape(rows, width), queries, w_uv, sections, experts, groups
    )
    uv_share = swap(uv_share, "expert", far)
    cut = deliver(cut, "expert")

    blocks, riders, token = absorb_queries(
        owners, cut, queries.shape, w_uk, residual, attn_gain, w_turned, prompt_count, sections,
        [uv_share],
    )
    blocks = lax.all_to_all(blocks, ("expert", "section"), 0, 0, tiled=True)

    away = list(project(cut[1:], riders, w_parts, 1, rows, [token]))
    near = list(project(cut[:1], riders, w_parts, 0, rows, away[:1]))
    parts = deliver(near + away, "expert")
    table = rotation(full_length + steps + -(full_length + steps) % 8, cache_width - latent)
    gathered = list(gather_queries(
        blocks, lengths, owners, kv_gain, table, prompt_count, tokens_here, experts, sections,
        steps, heads
    ))
    uv_shares = spread(uv_share, "groups")
    later = masks[1:-1] + masks[:1]
    held = [doubled({far: share}, "expert", later) for share in uv_shares]
    uv_parts = {mask: [share[mask] for share in held] for mask in held[0]}
    for mask, part in doubled({0: w_uv}, "expert", later).items():
        uv_parts[mask] = [part]
    *out_latent, token = attend(
        parts, full_length, lengths, kv_gain, table, gathered, tokens_here, steps, sections,
        queries.shape[-1] ** (-0.5),
        [share for mask in range(1, experts) for share in uv_parts[mask]],
    )

    (w_gate,) = fetch([w_gate], [token])
    out_latent = deliver(out_latent, "section")
    head_values = head_products(
        owners, out_latent, [uv_parts[mask] for mask in range(experts)], expert_ids,
        route_scores, steps, tokens_here, [w_gate],
    )
    head_values = spread(head_values, "expert")

    (w_o,) = fetch([w_o], [])
    attended = output_product(head_values, w_o)
    (w_up,) = fetch([w_up], [attended])
    mixed = mix(spread(attended, "section"), parts, rows, [w_up])
    (w_down,) = fetch([w_down], [mixed])
    blocks, near = run_experts(
        spread(mixed, "expert"),
        head_values,
        moe_gain,
        w_gate,
        w_up,
        w_down,
        expert_ids.shape[2],
        sections,
    )
    blocks = lax.all_to_all(blocks, ("expert", "section"), 0, 0, tiled=True)
    return finish(blocks, near, steps)


def solution(mesh):
    placed = (
        P(("groups", "expert", "section"), None, None),
        P("groups"),
        P("groups"),
        P(None, ("groups", "expert"), None),
        P(None, ("groups", "expert"), "section", None),
        P(None, ("groups", "expert"), None),
        P(None, ("groups", "expert"), None),
        P(),
        P("section", None),
        P(),
        P("section", None, "expert"),
        P("section", None, "expert"),
        P("section", "expert"),
        P(),
        P("expert", None, "section"),
        P("expert", None, "section"),
        P("expert", "section", None),
    )
    return jax.shard_map(
        local,
        mesh=mesh,
        in_specs=placed,
        out_specs=P(None, ("groups", "expert"), "section"),
        check_vma=False,
    )
```

```python
import functools
import math

import jax
import jax.numpy as jnp
import numpy as np
from jax import lax
from jax.experimental import pallas as pl
from jax.experimental.pallas import tpu as pltpu
from jax.sharding import PartitionSpec as P

epsilon = 1e-06
masked_value = -1e30
route_scale = 2.5


def rotation(positions, width):
    halfway = width // 2
    frequency = 10000.0 ** (-2.0 * np.arange(halfway) / width)
    angles = np.arange(positions)[:, None] * frequency
    cosine = np.concatenate([np.cos(angles), np.cos(angles)], axis=1)
    sine = np.concatenate([-np.sin(angles), np.sin(angles)], axis=1)
    return jnp.asarray(cosine, jnp.float32), jnp.asarray(sine, jnp.float32)


def swap(block, axis, mask):
    size = lax.axis_size(axis)
    return lax.ppermute(block, axis, [(i, i ^ mask) for i in range(size)])


def deliver(blocks, axis):
    return [blocks[0]] + [swap(blocks[mask], axis, mask) for mask in range(1, len(blocks))]


def spread(block, axis):
    return [block] + [swap(block, axis, mask) for mask in range(1, lax.axis_size(axis))]


def params(*arrays, scale=1):
    held = sum(math.prod(array.shape) * array.dtype.itemsize for array in arrays)
    mebibytes = min(56, 4 + scale * held // 1024 // 1024)
    return pltpu.CompilerParams(vmem_limit_bytes=mebibytes * 1024 * 1024)


def at_home(*arrays):
    return [pltpu.with_memory_space_constraint(array, pltpu.HBM) for array in arrays]


def fetch_kernel(count, *refs):
    out_refs, sems = refs[-1 - count : -1], refs[-1]
    copies = [
        pltpu.make_async_copy(refs[index], out_refs[index], sems.at[index])
        for index in range(count)
    ]
    for copy in copies:
        copy.start()
    for copy in copies:
        copy.wait()


def fetch(arrays, after):
    size = sum(array.size * array.dtype.itemsize for array in arrays)
    return pl.pallas_call(
        functools.partial(fetch_kernel, len(arrays)),
        out_shape=[pltpu.VMEM(array.shape, array.dtype) for array in arrays],
        in_specs=[pl.BlockSpec(memory_space=pltpu.HBM)] * len(arrays)
        + [pl.BlockSpec(memory_space=pl.ANY)] * len(after),
        out_specs=[pl.BlockSpec(memory_space=pltpu.VMEM)] * len(arrays),
        scratch_shapes=[pltpu.SemaphoreType.DMA((len(arrays),))],
        compiler_params=pltpu.CompilerParams(vmem_limit_bytes=1024 * 1024),
        cost_estimate=pl.CostEstimate(flops=0, bytes_accessed=2 * size, transcendentals=0),
        name="fetch",
    )(*at_home(*arrays), *after)


def doubled(held, axis, masks):
    held = dict(held)
    for mask in masks:
        for other in list(held):
            held[other ^ mask] = swap(held[other], axis, mask)
    return held


def cut_kernel(sections, experts, piece, x_ref, query_ref, uv_ref, half_ref, *refs):
    out_refs, held = refs[-1 - experts : -1], refs[-1]
    share = half_ref.shape[0]
    half_ref[...] = uv_ref[pl.ds(lax.axis_index("groups") * share, share)]
    rank = lax.axis_index("expert")
    steps, sources, heads, wide = query_ref.shape
    rows = x_ref.shape[0]
    for target in range(experts):
        for section in range(sections):
            at = (section * experts + target) * piece
            held[target, section * rows : (section + 1) * rows] = x_ref[:, at : at + piece]
    for mask, ref in enumerate(out_refs):
        ref[: sections * rows, :piece] = held[rank ^ mask]
        for step in range(steps):
            for source in range(sources):
                at = sections * rows + (step * sources + source) * heads
                ref[at : at + heads, :wide] = query_ref[step, source]


def cut_columns(x, queries, w_uv, sections, experts, groups):
    rows, width = x.shape
    piece = width // (sections * experts)
    steps, sources, heads, wide = queries.shape
    block = jax.ShapeDtypeStruct(
        (sections * rows + steps * sources * heads, max(piece, wide)), x.dtype
    )
    return pl.pallas_call(
        functools.partial(cut_kernel, sections, experts, piece),
        out_shape=[
            jax.ShapeDtypeStruct((w_uv.shape[0] // groups,) + w_uv.shape[1:], w_uv.dtype)
        ]
        + [block] * experts,
        scratch_shapes=[pltpu.VMEM((experts, sections * rows, piece), x.dtype)],
        compiler_params=params(x, block, w_uv, scale=6),
        name="cut_columns",
    )(*at_home(x, queries, w_uv))


def project_kernel(count, first, rows, *refs):
    x_refs, rider_ref, w_refs, out_refs = refs[:count], refs[count], refs[count + 1 :], refs[-count:]
    section_rank = lax.axis_index("section")
    sections = lax.axis_size("section")
    piece = w_refs[0].shape[1]
    total = 0
    for mask in range(sections):
        at = pl.ds(pl.multiple_of((section_rank ^ mask) * rows, rows), rows)
        x = jnp.concatenate([ref[at, :piece] for ref in x_refs], axis=0)
        total = total + lax.dot_general(
            x, w_refs[mask][...], (((1,), (1,)), ((), ())), preferred_element_type=jnp.float32
        )
    for index, ref in enumerate(out_refs):
        ref[:rows, :] = total[index * rows : (index + 1) * rows].astype(ref.dtype)
        ref[rows:, :] = rider_ref[first + index]


def project(blocks, riders, w_parts, first, rows, after):
    out = jax.ShapeDtypeStruct((rows + riders.shape[1], riders.shape[2]), jnp.bfloat16)
    held = pl.BlockSpec(memory_space=pltpu.VMEM)
    return pl.pallas_call(
        functools.partial(project_kernel, len(blocks), first, rows),
        out_shape=[out] * len(blocks),
        in_specs=[held] * (len(blocks) + 1 + len(w_parts))
        + [pl.BlockSpec(memory_space=pl.ANY)] * len(after),
        compiler_params=params(*blocks, *w_parts, scale=6),
        name="project",
    )(*blocks, *at_home(riders), *w_parts, *after)


def query_kernel(
    experts, sections, prompts, nope, shape, *refs
):
    f32, bf16 = jnp.float32, jnp.bfloat16
    table_ref, query_refs = refs[0], refs[1 : 1 + experts]
    uk_ref, own_ref, gain_ref, wt_ref = refs[1 + experts : 5 + experts]
    out_ref, rider_ref, token_ref, picked, ropes, made, normed, query_ref, columns = refs[-9:]
    token_ref[...] = jnp.zeros_like(token_ref)
    steps, sources, heads, wide = shape
    rope = wide - nope
    chunk = uk_ref.shape[2]
    width = out_ref.shape[2]
    count = experts * sources
    block = prompts * steps * heads
    rank = lax.axis_index("expert")

    for mask, ref in enumerate(query_refs):
        for step in range(steps):
            for source in range(sources):
                at = ref.shape[0] - (steps * sources - step * sources - source) * heads
                query_ref[rank ^ mask, step, source] = ref[at : at + heads, :wide]

    def pick(index, carry):
        owner = table_ref[index]
        for step in range(steps):
            value = query_ref[owner, step, index // sources].astype(f32)
            at = pl.ds(pl.multiple_of((index * steps + step) * heads, heads), heads)
            picked[at, :] = value[:, :nope]
            ropes[at, :rope] = value[:, nope:]
        return carry

    if count <= 16:
        for index in range(count):
            pick(index, 0)
    else:
        lax.fori_loop(0, count, pick, 0)
    for head in range(heads):
        at = pl.ds(head, count * steps, stride=heads)
        value = jnp.dot(picked[at, :].astype(bf16), uk_ref[head], preferred_element_type=f32)
        if chunk < made.shape[1]:
            spare = jnp.zeros((count * steps, made.shape[1] - chunk), f32)
            value = jnp.concatenate([value, spare], axis=1)
        made[at, :] = value
    small = (rope + experts - 1) // experts
    lanes = rope if width != chunk else width
    groups = width // small if width == chunk else 1
    source_lane = lax.broadcasted_iota(jnp.int32, (rope, lanes), 0)
    lane = lax.broadcasted_iota(jnp.int32, (rope, lanes), 1)
    turned = 0
    for group in range(groups):
        pair = (source_lane == lane - group * small + rank * small) & (
            (lane >= group * small) & (lane < (group + 1) * small)
        )
        at = pl.ds(group, count * steps * heads // groups, stride=groups)
        turned = turned + jnp.dot(
            ropes[at, :][:, :rope].astype(bf16),
            jnp.where(pair, 1.0, 0.0).astype(bf16),
            preferred_element_type=f32,
        )
    own = jnp.concatenate([own_ref[step] for step in range(steps)], axis=0).astype(f32)
    lines, column = columns.shape[1:]
    for target in range(experts):
        columns[target] = own[:, target * column : (target + 1) * column]
    for mask in range(experts):
        value = columns[rank ^ mask]
        for line, at in enumerate(range(0, column, rider_ref.shape[2])):
            end = min(at + rider_ref.shape[2], column)
            rider_ref[mask, line * lines : (line + 1) * lines, : end - at] = value[
                :, at:end
            ].astype(bf16)
    scale = lax.rsqrt(jnp.mean(own * own, axis=-1, keepdims=True) + epsilon)
    own = (own * scale * gain_ref[...][None].astype(f32)).astype(bf16)
    depth = wt_ref.shape[1]
    for section in range(sections):
        normed[section] = own[:, section * depth : (section + 1) * depth]
    fresh = lax.dot_general(
        normed[lax.axis_index("section")],
        wt_ref[...],
        (((1,), (1,)), ((), ())),
        preferred_element_type=f32,
    )
    for source in range(experts):
        picks = [step * sources + source for step in range(steps)]
        if width == chunk:
            latent = width * experts
            lines = [
                fresh[pick:, part * width : (part + 1) * width][:1]
                for pick in picks
                for part in range(experts)
            ]
            lines.append(
                jnp.concatenate([fresh[pick:, latent:][:1] for pick in picks], axis=1)
            )
        else:
            lines = [
                fresh[pick:, part * width : (part + 1) * width][:1]
                for pick in picks
                for part in range(experts)
            ]
        lines = jnp.concatenate(lines, axis=0).astype(bf16)
        for section in range(sections):
            index = source * sections + section
            at = slice(index * block, (index + 1) * block)
            if width == chunk:
                few = block // groups
                out_ref[index, :block, :] = made[at, :chunk].astype(bf16)
                tail = [turned[index * few : (index + 1) * few].astype(bf16), lines]
                spare = out_ref.shape[1] - block - few - lines.shape[0]
                if spare:
                    tail.append(jnp.zeros((spare, width), bf16))
                out_ref[index, block:, :] = jnp.concatenate(tail, axis=0)
            else:
                value = jnp.concatenate([made[at, :chunk], turned[at, :small]], axis=1)
                out_ref[index, :block, :] = value.astype(bf16)
                out_ref[index, block:, :] = lines


def block_shape(prompts, steps, heads, experts, chunk, rope):
    rows = prompts * steps * heads
    small = rope // experts
    if chunk == 128 and small * 8 == chunk and steps * rope == chunk:
        rows = rows + rows // 8 + steps * experts + 1
        return rows + -rows % 16, chunk
    return rows + steps * experts, chunk + small


def absorb_queries(table, queries, shape, w_uk, own, gain, w_turned, prompts, sections, after):
    experts = len(queries)
    steps, sources, heads, wide = shape
    _, nope, chunk = w_uk.shape
    rows, width = block_shape(prompts, steps, heads, experts, chunk, wide - nope)
    block, column = own.shape[0] * own.shape[1], own.shape[2] // experts
    cache_width = w_turned.shape[0]
    count = experts * sources * steps * heads
    held = pl.BlockSpec(memory_space=pltpu.VMEM)
    return pl.pallas_call(
        functools.partial(query_kernel, experts, sections, prompts, nope, shape),
        out_shape=[
            pltpu.HBM((experts * sections, rows, width), jnp.bfloat16),
            pltpu.HBM((experts, block * -(-column // cache_width), cache_width), jnp.bfloat16),
            jax.ShapeDtypeStruct((8, 128), jnp.bfloat16),
        ],
        in_specs=[pl.BlockSpec(memory_space=pltpu.SMEM)]
        + [held] * (experts + 4)
        + [pl.BlockSpec(memory_space=pl.ANY)] * len(after),
        out_specs=[held] * 3,
        scratch_shapes=[
            pltpu.VMEM((count, nope), jnp.float32),
            pltpu.VMEM((count, max(wide - nope, 128)), jnp.float32),
            pltpu.VMEM((count, max(chunk, 128)), jnp.float32),
            pltpu.VMEM(
                (sections, own.shape[0] * own.shape[1], w_turned.shape[1]), jnp.bfloat16
            ),
            pltpu.VMEM((experts,) + shape, jnp.bfloat16),
            pltpu.VMEM((experts, block, column), jnp.float32),
        ],
        compiler_params=params(*queries, w_uk, own, w_turned, scale=4),
        name="absorb_queries",
    )(*at_home(table), *queries, *at_home(w_uk, own, gain, w_turned), *after)


def turn(values, cosine, sine):
    half = values.shape[1] // 2
    other = jnp.concatenate([values[:, half:], values[:, :half]], axis=1)
    return values * cosine + other * sine


def scaled(values, gain):
    scale = lax.rsqrt(jnp.mean(values * values, axis=-1, keepdims=True) + epsilon)
    return values * scale * gain.astype(jnp.float32)


def gather_kernel(
    prompts, experts, sections, sources, heads, steps, latent, length_ref, owner_ref, gain_ref,
    cosine_ref, sine_ref, block_ref, query_ref, query_rope_ref, recent_ref, recent_rope_ref,
    cosine_held, sine_held, ropes_held
):
    f32, bf16 = jnp.float32, jnp.bfloat16
    rows = steps * heads
    chunk = latent // experts
    whole = block_ref.shape[2] == chunk
    extra = prompts * rows // 8 if whole else 0
    first = lax.axis_index("expert") * sources + lax.axis_index("section") * prompts
    gain = gain_ref[...][None]
    for prompt in range(prompts):
        length, owner = length_ref[first + prompt], owner_ref[first + prompt]
        for step in range(steps):
            at = slice(step * heads, (step + 1) * heads)
            cosine_held[at, :] = jnp.broadcast_to(
                cosine_ref[pl.ds(length + step, 1), :], (heads, cosine_ref.shape[1])
            )
            sine_held[at, :] = jnp.broadcast_to(
                sine_ref[pl.ds(length + step, 1), :], (heads, sine_ref.shape[1])
            )
        cosine, sine = cosine_held[...], sine_held[...]
        if whole:
            few = rows // 8
            small = cosine.shape[1] // experts
            low = prompts * rows + prompt * few
            tail = jnp.concatenate(
                [
                    jnp.concatenate(
                        [block_ref[i * sections + section, low : low + few, :]
                         for i in range(experts)],
                        axis=1,
                    )
                    for section in range(sections)
                ],
                axis=0,
            )
            shape = (experts * chunk, experts * small)
            source_lane = lax.broadcasted_iota(jnp.int32, shape, 0)
            lane = lax.broadcasted_iota(jnp.int32, shape, 1)
            bits = small.bit_length() - 1
            lane = lax.shift_right_logical(lane, bits) * chunk + (lane & (small - 1))
            for group in range(8):
                pair = jnp.where(source_lane == lane + group * small, 1.0, 0.0).astype(bf16)
                value = jnp.dot(tail, pair, preferred_element_type=f32)
                pad = ropes_held.shape[1] - value.shape[1]
                value = jnp.concatenate([value, jnp.zeros((value.shape[0], pad), f32)], axis=1)
                ropes_held[pl.ds(group, sections * few, stride=8), :] = value
        at = slice(prompt * rows, (prompt + 1) * rows)
        for section in range(sections):
            pieces = [block_ref[i * sections + section, at, :] for i in range(experts)]
            to = slice(section * rows, (section + 1) * rows)
            query_ref[prompt, to, :] = jnp.concatenate(
                [piece[:, :chunk] for piece in pieces], axis=1
            )
            if whole:
                rope = ropes_held[to, : cosine.shape[1]]
            else:
                rope = jnp.concatenate(
                    [piece[:, chunk:].astype(f32) for piece in pieces], axis=1
                )
            query_rope_ref[prompt, to, :] = turn(rope, cosine, sine).astype(bf16)
        lines = 0
        for section in range(sections):
            lines = lines + block_ref[
                owner * sections + section, prompts * rows + extra :, :
            ].astype(f32)
        recent, recent_rope = [], []
        for step in range(steps):
            parts = [lines[step * experts + part :][:1] for part in range(experts)]
            if whole:
                end = cosine.shape[1]
                parts.append(
                    lines[steps * experts :][:1, step * end : (step + 1) * end]
                )
            line = jnp.concatenate(parts, axis=1)
            recent.append(scaled(line[:, :latent], gain))
            at = slice(step * heads, step * heads + 1)
            recent_rope.append(turn(line[:, latent:], cosine[at], sine[at]))
        spare = recent_ref.shape[1] - steps
        recent.append(jnp.zeros((spare, latent), f32))
        recent_rope.append(jnp.zeros((spare, recent_rope[0].shape[1]), f32))
        recent_ref[prompt] = jnp.concatenate(recent, axis=0).astype(bf16)
        recent_rope_ref[prompt] = jnp.concatenate(recent_rope, axis=0).astype(bf16)


def gather_queries(blocks, lengths, owners, kv_gain, table, prompts, sources, experts, sections,
                   steps, heads):
    latent = kv_gain.shape[0]
    rope = table[0].shape[1]
    rows = sections * steps * heads
    spare = steps + -steps % 16
    shape = lambda *sizes: jax.ShapeDtypeStruct((prompts,) + sizes, jnp.bfloat16)
    held = pl.BlockSpec(memory_space=pltpu.VMEM)
    return pl.pallas_call(
        functools.partial(
            gather_kernel, prompts, experts, sections, sources, heads, steps, latent
        ),
        out_shape=[shape(rows, latent), shape(rows, rope), shape(spare, latent), shape(spare, rope)],
        in_specs=[pl.BlockSpec(memory_space=pltpu.SMEM)] * 2 + [held] * 4,
        out_specs=[held] * 4,
        scratch_shapes=[pltpu.VMEM((steps * heads, rope), jnp.float32)] * 2
        + [pltpu.VMEM((rows, 128), jnp.float32)],
        compiler_params=params(blocks, scale=4),
        name="gather_queries",
    )(*at_home(lengths, owners, kv_gain, *table), blocks)


def attend_kernel(parts, positions, sections, sources, heads, steps, score_scale, *refs):
    part_refs = refs[:parts]
    (length_ref, gain_ref, cosine_ref, sine_ref, query_ref, query_rope_ref, recent_ref,
     recent_rope_ref) = refs[parts : parts + 8]
    out_refs, token_ref, held = refs[-2 - sections : -2], refs[-2], refs[-1]
    token_ref[...] = jnp.zeros_like(token_ref)
    f32, bf16 = jnp.float32, jnp.bfloat16
    nt = (((1,), (1,)), ((), ()))
    prompts, _, latent = query_ref.shape
    rows = steps * heads
    section_rank = lax.axis_index("section")
    first = lax.axis_index("expert") * sources + section_rank * prompts
    for prompt in range(prompts):
        at = slice(prompt * positions, (prompt + 1) * positions)
        projected = part_refs[0][at].astype(f32)
        for ref in part_refs[1:]:
            projected = projected + ref[at].astype(f32)
        keys = scaled(projected[:, :latent], gain_ref[...][None]).astype(bf16)
        key_rope = turn(
            projected[:, latent:], cosine_ref[:positions], sine_ref[:positions]
        ).astype(bf16)
        query, query_rope = query_ref[prompt], query_rope_ref[prompt]
        recent, recent_rope = recent_ref[prompt], recent_rope_ref[prompt]
        scores = lax.dot_general(query, keys, nt, preferred_element_type=f32)
        scores = scores + lax.dot_general(query_rope, key_rope, nt, preferred_element_type=f32)
        fresh = lax.dot_general(query, recent, nt, preferred_element_type=f32)
        fresh = fresh + lax.dot_general(query_rope, recent_rope, nt, preferred_element_type=f32)
        place = lax.broadcasted_iota(jnp.int32, scores.shape, 1)
        scores = jnp.where(
            place < length_ref[first + prompt], scores * score_scale, masked_value
        )
        row = lax.broadcasted_iota(jnp.int32, (rows, fresh.shape[1]), 0)
        place = lax.broadcasted_iota(jnp.int32, (rows, fresh.shape[1]), 1)
        seen = jnp.where(place < 1, 1.0, 0.0)
        for step in range(1, steps):
            seen = jnp.where((place <= step) & (row >= step * heads), 1.0, seen)
        seen = jnp.concatenate([seen] * sections, axis=0)
        fresh = jnp.where(seen > 0.5, fresh * score_scale, masked_value)
        most = jnp.maximum(
            jnp.max(scores, axis=-1, keepdims=True), jnp.max(fresh, axis=-1, keepdims=True)
        )
        scores = jnp.exp(scores - most)
        fresh = jnp.exp(fresh - most)
        total = jnp.sum(scores, axis=-1, keepdims=True) + jnp.sum(fresh, axis=-1, keepdims=True)
        scores = (scores / total).astype(bf16)
        fresh = (fresh / total).astype(bf16)
        mixed = jnp.dot(scores, keys, preferred_element_type=f32)
        mixed = mixed + jnp.dot(fresh, recent, preferred_element_type=f32)
        mixed = mixed.astype(bf16)
        for section in range(sections):
            held[section] = mixed[section * rows : (section + 1) * rows]
        for mask, ref in enumerate(out_refs):
            ref[prompt * rows : (prompt + 1) * rows, :] = held[section_rank ^ mask]


def attend(
    parts, positions, lengths, kv_gain, table, gathered, sources, steps, sections, score_scale,
    after
):
    prompts, rows, latent = gathered[0].shape
    out = (rows // sections, latent)
    held = pl.BlockSpec(memory_space=pltpu.VMEM)
    return pl.pallas_call(
        functools.partial(
            attend_kernel, len(parts), positions, sections, sources, out[0] // steps, steps,
            score_scale
        ),
        out_shape=[jax.ShapeDtypeStruct((prompts * out[0], latent), jnp.bfloat16)] * sections
        + [jax.ShapeDtypeStruct((8, 128), jnp.bfloat16)],
        in_specs=[held] * len(parts)
        + [pl.BlockSpec(memory_space=pltpu.SMEM)]
        + [held] * 7
        + [pl.BlockSpec(memory_space=pl.ANY)] * len(after),
        out_specs=[held] * (sections + 1),
        scratch_shapes=[pltpu.VMEM((sections,) + out, jnp.bfloat16)],
        compiler_params=params(*parts, *gathered, scale=6),
        name="attend",
    )(*parts, *at_home(lengths, kv_gain, *table), *gathered, *after)


def value_kernel(experts, sections, heads, steps, sources, count, *refs):
    owner_ref, latent_refs, uv_refs = refs[0], refs[1 : 1 + sections], refs[1 + sections :]
    name_ref, score_ref = uv_refs[count : count + 2]
    uv_refs = list(uv_refs[:count])
    out_ref, held = refs[-2:]
    group_rank, groups = lax.axis_index("groups"), lax.axis_size("groups")
    weights = []
    while uv_refs:
        if uv_refs[0].shape[0] == heads:
            weights.append(uv_refs[:1])
        else:
            weights.append(uv_refs[:groups])
        uv_refs = uv_refs[len(weights[-1]) :]
    f32, bf16 = jnp.float32, jnp.bfloat16
    chunk = weights[0][0].shape[2]
    rows = latent_refs[0].shape[0]
    for mask, ref in enumerate(latent_refs):
        for index in range(experts):
            held[index, mask * rows : (mask + 1) * rows, :chunk] = ref[
                :, index * chunk : (index + 1) * chunk
            ].astype(f32)
    rank = lax.axis_index("expert")
    values = []
    for head in range(heads):
        at = pl.ds(head, sections * rows // heads, stride=heads)
        total = 0
        for mask, shares in enumerate(weights):
            size = shares[0].shape[0]
            weight = shares[0][head % size]
            for other in range(1, len(shares)):
                mine = (group_rank ^ other) == head // size
                weight = jnp.where(mine, shares[other][head % size], weight)
            total = total + lax.dot_general(
                held[rank ^ mask, at, :][:, :chunk].astype(bf16),
                weight,
                (((1,), (1,)), ((), ())),
                preferred_element_type=f32,
            )
        values.append(total.astype(bf16))
    values = jnp.concatenate(values, axis=1)
    prompts = sources // sections
    section_rank = lax.axis_index("section")
    size = sources * steps
    to = lax.broadcasted_iota(jnp.int32, (size, size), 0)
    row = lax.broadcasted_iota(jnp.int32, (size, size), 1)
    order = jnp.zeros((size, size), f32)
    for mask in range(sections):
        for prompt in range(prompts):
            owner = owner_ref[
                rank * sources + (section_rank ^ mask) * prompts + prompt
            ]
            for step in range(steps):
                index = (mask * prompts + prompt) * steps + step
                order = jnp.where((row == index) & (to == owner * steps + step), 1.0, order)
    width = values.shape[1]
    out_ref[:, :width] = jnp.dot(
        order.astype(bf16), values, preferred_element_type=f32
    ).astype(bf16)
    names = jnp.concatenate([name_ref[step] for step in range(steps)], axis=0).astype(f32)
    scores = jnp.concatenate([score_ref[step] for step in range(steps)], axis=0)
    high = scores.astype(bf16).astype(f32)
    spare = jnp.zeros((size, out_ref.shape[1] - width - 3 * names.shape[1]), f32)
    route = jnp.concatenate([names, high, scores - high, spare], axis=1)
    out_ref[:, width:] = route.astype(bf16)


def head_products(owners, latents, uv_parts, names, scores, steps, sources, after):
    rows, width = latents[0].shape
    heads, value, _ = uv_parts[0][0].shape
    experts = len(uv_parts)
    uv_parts = [share for part in uv_parts for share in part]
    held = pl.BlockSpec(memory_space=pltpu.VMEM)
    total = rows * len(latents)
    return pl.pallas_call(
        functools.partial(
            value_kernel, experts, len(latents), heads, steps, sources, len(uv_parts)
        ),
        out_shape=jax.ShapeDtypeStruct(
            (total // heads, heads * value + 128), jnp.bfloat16
        ),
        in_specs=[pl.BlockSpec(memory_space=pltpu.SMEM)]
        + [held] * (len(latents) + len(uv_parts) + 2)
        + [pl.BlockSpec(memory_space=pl.ANY)] * len(after),
        out_specs=held,
        scratch_shapes=[
            pltpu.VMEM((experts, total, max(width // experts, 128)), jnp.float32)
        ],
        compiler_params=params(*latents, *uv_parts, scale=4),
        name="head_products",
    )(*at_home(owners), *latents, *uv_parts, *at_home(names, scores), *after)


def output_kernel(experts, *refs):
    value_refs = refs[:experts]
    weight_ref, out_ref = refs[experts:]
    depth = weight_ref.shape[0]
    values = jnp.concatenate([ref[:, :depth] for ref in value_refs], axis=0)
    rows = values.shape[0]
    to = lax.broadcasted_iota(jnp.int32, (rows, rows), 0)
    row = lax.broadcasted_iota(jnp.int32, (rows, rows), 1)
    source = (to & (experts - 1)) ^ lax.axis_index("expert")
    rest = lax.shift_right_logical(to, experts.bit_length() - 1)
    order = jnp.where(row == source * (rows // experts) + rest, 1.0, 0.0).astype(jnp.bfloat16)
    values = jnp.dot(order, values, preferred_element_type=jnp.float32).astype(jnp.bfloat16)
    out_ref[...] = jnp.dot(
        values, weight_ref[...], preferred_element_type=jnp.float32
    ).astype(out_ref.dtype)


def output_product(values, weight):
    rows = sum(value.shape[0] for value in values)
    held = pl.BlockSpec(memory_space=pltpu.VMEM)
    return pl.pallas_call(
        functools.partial(output_kernel, len(values)),
        out_shape=jax.ShapeDtypeStruct((rows, weight.shape[1]), jnp.bfloat16),
        in_specs=[held] * (len(values) + 1),
        out_specs=held,
        compiler_params=params(*values, scale=8),
        name="output_product",
    )(*values, weight)


def mix_kernel(count, owners, rows, *refs):
    part_refs, own_refs = refs[:count], refs[count : count + owners]
    out_ref, held = refs[-2:]
    f32 = jnp.float32
    total = part_refs[0][...].astype(f32)
    for ref in part_refs[1:]:
        total = total + ref[...].astype(f32)
    block, column = held.shape[1:]
    for owner in range(owners):
        held[owner] = total[owner * block : (owner + 1) * block]
    rank = lax.axis_index("expert")
    for mask, ref in enumerate(own_refs):
        lines = []
        for line, at in enumerate(range(0, column, ref.shape[1])):
            end = min(at + ref.shape[1], column)
            to = rows + line * block
            lines.append(ref[to : to + block, : end - at].astype(f32))
        lines = lines[0] if len(lines) == 1 else jnp.concatenate(lines, axis=1)
        out_ref[rank ^ mask] = (held[rank ^ mask] + lines).astype(out_ref.dtype)


def mix(parts, owns, rows, after):
    total, width = parts[0].shape
    owners = len(owns)
    held = pl.BlockSpec(memory_space=pltpu.VMEM)
    shape = (owners, total // owners, width)
    return pl.pallas_call(
        functools.partial(mix_kernel, len(parts), owners, rows),
        out_shape=jax.ShapeDtypeStruct(shape, parts[0].dtype),
        in_specs=[held] * (len(parts) + owners)
        + [pl.BlockSpec(memory_space=pl.ANY)] * len(after),
        out_specs=held,
        scratch_shapes=[pltpu.VMEM(shape, jnp.float32)],
        compiler_params=params(*parts, *owns, scale=4),
        name="mix",
    )(*parts, *owns, *after)


def expert_kernel(experts, sections, picks, *refs):
    mixed_refs, route_refs = refs[:experts], refs[experts : 2 * experts]
    gain_ref, gate_ref, up_ref, down_ref, out_ref, near_ref, columns = refs[2 * experts :]
    f32, bf16 = jnp.float32, jnp.bfloat16
    count = gate_ref.shape[0]
    rank = lax.axis_index("expert")
    width = gain_ref.shape[0]
    block = mixed_refs[0].shape[1]
    for mask, ref in enumerate(mixed_refs):
        columns[rank ^ mask] = ref[...]
    mixed, route = [], []
    for mask, ref in enumerate(route_refs):
        mixed.append(
            jnp.concatenate([columns[i, rank ^ mask] for i in range(experts)], axis=1).astype(f32)
        )
        route.append(ref[:, ref.shape[1] - 128 :].astype(f32))
    near = mixed[0]
    mixed = jnp.concatenate(mixed, axis=0)
    route = jnp.concatenate(route, axis=0)
    named = route[:, :picks]
    weights = route[:, picks : 2 * picks] + route[:, 2 * picks : 3 * picks]
    weights = route_scale * weights / jnp.sum(weights, axis=-1, keepdims=True)
    scale = lax.rsqrt(jnp.mean(mixed * mixed, axis=-1, keepdims=True) + epsilon)
    rows_in = (mixed * scale * gain_ref[...][None].astype(f32)).astype(bf16)
    column = width // sections
    total = 0
    for x in range(count):
        mine = (rank * count + x).astype(f32)
        weight = jnp.sum(jnp.where(named == mine, weights, 0.0), axis=-1, keepdims=True)
        gate = jnp.dot(rows_in, gate_ref[x], preferred_element_type=f32)
        up = jnp.dot(rows_in, up_ref[x], preferred_element_type=f32)
        inner = gate / (1.0 + jnp.exp(-gate)) * up * weight
        total = total + jnp.dot(inner.astype(bf16), down_ref[x], preferred_element_type=f32)
    for section in range(sections):
        at = slice(section * column, (section + 1) * column)
        near_ref[section] = near[:, at].astype(bf16)
        for mask in range(experts):
            out_ref[(rank ^ mask) * sections + section] = total[
                mask * block : (mask + 1) * block, at
            ].astype(bf16)


def run_experts(mixed, routes, gain, w_gate, w_up, w_down, picks, sections):
    experts = len(mixed)
    block = (mixed[0].shape[1], gain.shape[0] // sections)
    held = pl.BlockSpec(memory_space=pltpu.VMEM)
    return pl.pallas_call(
        functools.partial(expert_kernel, experts, sections, picks),
        out_shape=[
            jax.ShapeDtypeStruct((experts * sections,) + block, jnp.bfloat16),
            jax.ShapeDtypeStruct((sections,) + block, jnp.bfloat16),
        ],
        in_specs=[held] * (2 * experts + 4),
        out_specs=[held] * 2,
        scratch_shapes=[pltpu.VMEM((experts,) + mixed[0].shape, jnp.bfloat16)],
        compiler_params=params(*mixed, scale=32),
        name="run_experts",
    )(*mixed, *routes, *at_home(gain), w_gate, w_up, w_down)


def finish_kernel(block_ref, near_ref, out_ref):
    f32 = jnp.float32
    steps, sources, _ = out_ref.shape
    total = near_ref[lax.axis_index("section")].astype(f32)
    for index in range(block_ref.shape[0]):
        total = total + block_ref[index].astype(f32)
    for step in range(steps):
        out_ref[step] = total[step * sources : (step + 1) * sources].astype(out_ref.dtype)


def finish(blocks, near, steps):
    held = pl.BlockSpec(memory_space=pltpu.VMEM)
    _, rows, column = near.shape
    return pl.pallas_call(
        finish_kernel,
        out_shape=jax.ShapeDtypeStruct((steps, rows // steps, column), near.dtype),
        in_specs=[held] * 2,
        out_specs=held,
        compiler_params=params(blocks, near, scale=4),
        name="finish",
    )(blocks, near)


def local(
    prompts,
    owners,
    lengths,
    residual,
    queries,
    expert_ids,
    route_scores,
    attn_gain,
    w_dkv,
    kv_gain,
    w_uk,
    w_uv,
    w_o,
    moe_gain,
    w_gate,
    w_up,
    w_down,
):
    bf16, f32 = jnp.bfloat16, jnp.float32
    expert_rank = lax.axis_index("expert")
    section_rank = lax.axis_index("section")
    experts = lax.axis_size("expert")
    sections = lax.axis_size("section")
    groups = lax.axis_size("groups")
    prompt_count, full_length, width = prompts.shape
    steps, tokens_here, heads, _ = queries.shape
    depth = w_dkv.shape[0]
    piece = depth // experts
    latent = kv_gain.shape[0]
    cache_width = w_dkv.shape[1]
    rows = prompt_count * full_length
    own_rows = steps * tokens_here

    w_turned = w_dkv.T
    w_piece = lax.dynamic_slice_in_dim(w_turned, expert_rank * piece, piece, 1)
    masks = [1 << bit for bit in range(experts.bit_length() - 1)]
    far = masks[-1]
    w_parts = spread(w_piece, "section")
    uv_share, *cut = cut_columns(
        prompts.reshape(rows, width), queries, w_uv, sections, experts, groups
    )
    uv_share = swap(uv_share, "expert", far)
    cut = deliver(cut, "expert")

    blocks, riders, token = absorb_queries(
        owners, cut, queries.shape, w_uk, residual, attn_gain, w_turned, prompt_count, sections,
        [uv_share],
    )
    blocks = lax.all_to_all(blocks, ("expert", "section"), 0, 0, tiled=True)

    away = list(project(cut[1:], riders, w_parts, 1, rows, [token]))
    near = list(project(cut[:1], riders, w_parts, 0, rows, away[:1]))
    parts = deliver(near + away, "expert")
    table = rotation(full_length + steps + -(full_length + steps) % 8, cache_width - latent)
    gathered = list(gather_queries(
        blocks, lengths, owners, kv_gain, table, prompt_count, tokens_here, experts, sections,
        steps, heads
    ))
    uv_shares = spread(uv_share, "groups")
    later = masks[1:-1] + masks[:1]
    held = [doubled({far: share}, "expert", later) for share in uv_shares]
    uv_parts = {mask: [share[mask] for share in held] for mask in held[0]}
    for mask, part in doubled({0: w_uv}, "expert", later).items():
        uv_parts[mask] = [part]
    *out_latent, token = attend(
        parts, full_length, lengths, kv_gain, table, gathered, tokens_here, steps, sections,
        queries.shape[-1] ** (-0.5),
        [share for mask in range(1, experts) for share in uv_parts[mask]],
    )

    (w_gate,) = fetch([w_gate], [token])
    out_latent = deliver(out_latent, "section")
    head_values = head_products(
        owners, out_latent, [uv_parts[mask] for mask in range(experts)], expert_ids,
        route_scores, steps, tokens_here, [w_gate],
    )
    head_values = spread(head_values, "expert")

    (w_o,) = fetch([w_o], [])
    attended = output_product(head_values, w_o)
    (w_up,) = fetch([w_up], [attended])
    mixed = mix(spread(attended, "section"), parts, rows, [w_up])
    (w_down,) = fetch([w_down], [mixed])
    blocks, near = run_experts(
        spread(mixed, "expert"),
        head_values,
        moe_gain,
        w_gate,
        w_up,
        w_down,
        expert_ids.shape[2],
        sections,
    )
    blocks = lax.all_to_all(blocks, ("expert", "section"), 0, 0, tiled=True)
    return finish(blocks, near, steps)


def solution(mesh):
    placed = (
        P(("groups", "expert", "section"), None, None),
        P("groups"),
        P("groups"),
        P(None, ("groups", "expert"), None),
        P(None, ("groups", "expert"), "section", None),
        P(None, ("groups", "expert"), None),
        P(None, ("groups", "expert"), None),
        P(),
        P("section", None),
        P(),
        P("section", None, "expert"),
        P("section", None, "expert"),
        P("section", "expert"),
        P(),
        P("expert", None, "section"),
        P("expert", None, "section"),
        P("expert", "section", None),
    )
    return jax.shard_map(
        local,
        mesh=mesh,
        in_specs=placed,
        out_specs=P(None, ("groups", "expert"), "section"),
        check_vma=False,
    )
```

```python
import functools
import math

import jax
import jax.numpy as jnp
import numpy as np
from jax import lax
from jax.experimental import pallas as pl
from jax.experimental.pallas import tpu as pltpu
from jax.sharding import PartitionSpec as P

epsilon = 1e-06
masked_value = -1e30
route_scale = 2.5


def rotation(positions, width):
    halfway = width // 2
    frequency = 10000.0 ** (-2.0 * np.arange(halfway) / width)
    angles = np.arange(positions)[:, None] * frequency
    cosine = np.concatenate([np.cos(angles), np.cos(angles)], axis=1)
    sine = np.concatenate([-np.sin(angles), np.sin(angles)], axis=1)
    return jnp.asarray(cosine, jnp.float32), jnp.asarray(sine, jnp.float32)


def swap(block, axis, mask):
    size = lax.axis_size(axis)
    return lax.ppermute(block, axis, [(i, i ^ mask) for i in range(size)])


def deliver(blocks, axis):
    return [blocks[0]] + [swap(blocks[mask], axis, mask) for mask in range(1, len(blocks))]


def spread(block, axis):
    return [block] + [swap(block, axis, mask) for mask in range(1, lax.axis_size(axis))]


def params(*arrays, scale=1):
    held = sum(math.prod(array.shape) * array.dtype.itemsize for array in arrays)
    mebibytes = min(56, 4 + scale * held // 1024 // 1024)
    return pltpu.CompilerParams(vmem_limit_bytes=mebibytes * 1024 * 1024)


def at_home(*arrays):
    return [pltpu.with_memory_space_constraint(array, pltpu.HBM) for array in arrays]


def fetch_kernel(count, *refs):
    out_refs, sems = refs[-1 - count : -1], refs[-1]
    copies = [
        pltpu.make_async_copy(refs[index], out_refs[index], sems.at[index])
        for index in range(count)
    ]
    for copy in copies:
        copy.start()
    for copy in copies:
        copy.wait()


def fetch(arrays, after):
    size = sum(array.size * array.dtype.itemsize for array in arrays)
    return pl.pallas_call(
        functools.partial(fetch_kernel, len(arrays)),
        out_shape=[pltpu.VMEM(array.shape, array.dtype) for array in arrays],
        in_specs=[pl.BlockSpec(memory_space=pltpu.HBM)] * len(arrays)
        + [pl.BlockSpec(memory_space=pl.ANY)] * len(after),
        out_specs=[pl.BlockSpec(memory_space=pltpu.VMEM)] * len(arrays),
        scratch_shapes=[pltpu.SemaphoreType.DMA((len(arrays),))],
        compiler_params=pltpu.CompilerParams(vmem_limit_bytes=1024 * 1024),
        cost_estimate=pl.CostEstimate(flops=0, bytes_accessed=2 * size, transcendentals=0),
        name="fetch",
    )(*at_home(*arrays), *after)


def doubled(held, axis, masks):
    held = dict(held)
    for mask in masks:
        for other in list(held):
            held[other ^ mask] = swap(held[other], axis, mask)
    return held


def cut_kernel(
    sections, experts, piece, x_ref, query_ref, uv_ref, w_ref, half_ref, w_out_ref, *refs
):
    out_refs, w_held, held = refs[:experts], refs[experts], refs[experts + 1]
    for target in range(experts):
        w_held[target] = w_ref[:, target * piece : (target + 1) * piece]
    w_piece = w_held[lax.axis_index("expert")]
    if w_out_ref.shape == w_piece.shape:
        w_out_ref[...] = w_piece
    else:
        full = w_piece.shape[0]
        few = full // 4
        w_out_ref[:full, :] = w_piece[:, :128]
        rest = jnp.concatenate(
            [w_piece[index * few : (index + 1) * few, 128:] for index in range(4)], axis=1
        )
        for index in range(rest.shape[1] // 128):
            to = full + index * few
            w_out_ref[to : to + few, :] = rest[:, index * 128 : (index + 1) * 128]
    share = half_ref.shape[0]
    half_ref[...] = uv_ref[pl.ds(lax.axis_index("groups") * share, share)]
    rank = lax.axis_index("expert")
    steps, sources, heads, wide = query_ref.shape
    rows = x_ref.shape[0]
    for target in range(experts):
        for section in range(sections):
            at = (section * experts + target) * piece
            held[target, section * rows : (section + 1) * rows] = x_ref[:, at : at + piece]
    for mask, ref in enumerate(out_refs):
        ref[: sections * rows, :piece] = held[rank ^ mask]
        for step in range(steps):
            for source in range(sources):
                at = sections * rows + (step * sources + source) * heads
                ref[at : at + heads, :wide] = query_ref[step, source]


def folded(rows, piece):
    if 128 < piece < 256 and (piece - 128) % 32 == 0 and rows % 64 == 0:
        return rows + rows // 4 * ((piece - 128) // 32), 128
    return rows, piece


def unfolded(value, rows, piece):
    if value.shape == (rows, piece):
        return value
    few = rows // 4
    rest = jnp.concatenate(
        [value[at : at + few] for at in range(rows, value.shape[0], few)], axis=1
    )
    wide = piece - 128
    rest = jnp.concatenate(
        [rest[:, index * wide : (index + 1) * wide] for index in range(4)], axis=0
    )
    return jnp.concatenate([value[:rows], rest], axis=1)


def cut_columns(x, queries, w_uv, w_turned, sections, experts, groups):
    rows, width = x.shape
    piece = width // (sections * experts)
    steps, sources, heads, wide = queries.shape
    block = jax.ShapeDtypeStruct(
        (sections * rows + steps * sources * heads, max(piece, wide)), x.dtype
    )
    return pl.pallas_call(
        functools.partial(cut_kernel, sections, experts, piece),
        out_shape=[
            jax.ShapeDtypeStruct((w_uv.shape[0] // groups,) + w_uv.shape[1:], w_uv.dtype),
            jax.ShapeDtypeStruct(folded(w_turned.shape[0], piece), x.dtype),
        ]
        + [block] * experts,
        scratch_shapes=[
            pltpu.VMEM((experts, w_turned.shape[0], piece), x.dtype),
            pltpu.VMEM((experts, sections * rows, piece), x.dtype),
        ],
        compiler_params=params(x, block, w_uv, w_turned, scale=6),
        name="cut_columns",
    )(*at_home(x, queries, w_uv, w_turned))


def project_kernel(count, first, rows, piece, *refs):
    x_refs, rider_ref, w_refs, out_refs = refs[:count], refs[count], refs[count + 1 :], refs[-count:]
    section_rank = lax.axis_index("section")
    sections = lax.axis_size("section")
    width = rider_ref.shape[2]
    total = 0
    for mask in range(sections):
        weights = unfolded(w_refs[mask][...], width, piece)
        at = pl.ds(pl.multiple_of((section_rank ^ mask) * rows, rows), rows)
        x = jnp.concatenate([ref[at, :piece] for ref in x_refs], axis=0)
        total = total + lax.dot_general(
            x, weights, (((1,), (1,)), ((), ())), preferred_element_type=jnp.float32
        )
    for index, ref in enumerate(out_refs):
        ref[:rows, :] = total[index * rows : (index + 1) * rows].astype(ref.dtype)
        ref[rows:, :] = rider_ref[first + index]


def project(blocks, riders, w_parts, first, rows, piece, after):
    out = jax.ShapeDtypeStruct((rows + riders.shape[1], riders.shape[2]), jnp.bfloat16)
    held = pl.BlockSpec(memory_space=pltpu.VMEM)
    return pl.pallas_call(
        functools.partial(project_kernel, len(blocks), first, rows, piece),
        out_shape=[out] * len(blocks),
        in_specs=[held] * (len(blocks) + 1 + len(w_parts))
        + [pl.BlockSpec(memory_space=pl.ANY)] * len(after),
        compiler_params=params(*blocks, *w_parts, scale=6),
        name="project",
    )(*blocks, riders, *w_parts, *after)


def query_kernel(
    experts, sections, prompts, nope, shape, *refs
):
    f32, bf16 = jnp.float32, jnp.bfloat16
    table_ref, query_refs = refs[0], refs[1 : 1 + experts]
    uk_ref, own_ref, gain_ref, wt_ref = refs[1 + experts : 5 + experts]
    out_ref, rider_ref, token_ref, picked, ropes, made, normed, query_ref, columns = refs[-9:]
    token_ref[...] = jnp.zeros_like(token_ref)
    steps, sources, heads, wide = shape
    rope = wide - nope
    chunk = uk_ref.shape[2]
    width = out_ref.shape[2]
    count = experts * sources
    block = prompts * steps * heads
    rank = lax.axis_index("expert")

    for mask, ref in enumerate(query_refs):
        for step in range(steps):
            for source in range(sources):
                at = ref.shape[0] - (steps * sources - step * sources - source) * heads
                query_ref[rank ^ mask, step, source] = ref[at : at + heads, :wide]

    def pick(index, carry):
        owner = table_ref[index]
        for step in range(steps):
            value = query_ref[owner, step, index // sources].astype(f32)
            at = pl.ds(pl.multiple_of((index * steps + step) * heads, heads), heads)
            picked[at, :] = value[:, :nope]
            ropes[at, :rope] = value[:, nope:]
        return carry

    if count <= 16:
        for index in range(count):
            pick(index, 0)
    else:
        lax.fori_loop(0, count, pick, 0)
    for head in range(heads):
        at = pl.ds(head, count * steps, stride=heads)
        value = jnp.dot(picked[at, :].astype(bf16), uk_ref[head], preferred_element_type=f32)
        if chunk < made.shape[1]:
            spare = jnp.zeros((count * steps, made.shape[1] - chunk), f32)
            value = jnp.concatenate([value, spare], axis=1)
        made[at, :] = value
    small = (rope + experts - 1) // experts
    lanes = rope if width != chunk else width
    groups = width // small if width == chunk else 1
    source_lane = lax.broadcasted_iota(jnp.int32, (rope, lanes), 0)
    lane = lax.broadcasted_iota(jnp.int32, (rope, lanes), 1)
    turned = 0
    for group in range(groups):
        pair = (source_lane == lane - group * small + rank * small) & (
            (lane >= group * small) & (lane < (group + 1) * small)
        )
        at = pl.ds(group, count * steps * heads // groups, stride=groups)
        turned = turned + jnp.dot(
            ropes[at, :][:, :rope].astype(bf16),
            jnp.where(pair, 1.0, 0.0).astype(bf16),
            preferred_element_type=f32,
        )
    own = jnp.concatenate([own_ref[step] for step in range(steps)], axis=0).astype(f32)
    lines, column = columns.shape[1:]
    for target in range(experts):
        columns[target] = own[:, target * column : (target + 1) * column]
    for mask in range(experts):
        value = columns[rank ^ mask]
        for line, at in enumerate(range(0, column, rider_ref.shape[2])):
            end = min(at + rider_ref.shape[2], column)
            rider_ref[mask, line * lines : (line + 1) * lines, : end - at] = value[
                :, at:end
            ].astype(bf16)
    scale = lax.rsqrt(jnp.mean(own * own, axis=-1, keepdims=True) + epsilon)
    own = (own * scale * gain_ref[...][None].astype(f32)).astype(bf16)
    depth = wt_ref.shape[1]
    for section in range(sections):
        normed[section] = own[:, section * depth : (section + 1) * depth]
    fresh = lax.dot_general(
        normed[lax.axis_index("section")],
        wt_ref[...],
        (((1,), (1,)), ((), ())),
        preferred_element_type=f32,
    )
    for source in range(experts):
        picks = [step * sources + source for step in range(steps)]
        if width == chunk:
            latent = width * experts
            lines = [
                fresh[pick:, part * width : (part + 1) * width][:1]
                for pick in picks
                for part in range(experts)
            ]
            lines.append(
                jnp.concatenate([fresh[pick:, latent:][:1] for pick in picks], axis=1)
            )
        else:
            lines = [
                fresh[pick:, part * width : (part + 1) * width][:1]
                for pick in picks
                for part in range(experts)
            ]
        lines = jnp.concatenate(lines, axis=0).astype(bf16)
        for section in range(sections):
            index = source * sections + section
            at = slice(index * block, (index + 1) * block)
            if width == chunk:
                few = block // groups
                out_ref[index, :block, :] = made[at, :chunk].astype(bf16)
                tail = [turned[index * few : (index + 1) * few].astype(bf16), lines]
                spare = out_ref.shape[1] - block - few - lines.shape[0]
                if spare:
                    tail.append(jnp.zeros((spare, width), bf16))
                out_ref[index, block:, :] = jnp.concatenate(tail, axis=0)
            else:
                value = jnp.concatenate([made[at, :chunk], turned[at, :small]], axis=1)
                out_ref[index, :block, :] = value.astype(bf16)
                out_ref[index, block:, :] = lines


def block_shape(prompts, steps, heads, experts, chunk, rope):
    rows = prompts * steps * heads
    small = rope // experts
    if chunk == 128 and small * 8 == chunk and steps * rope == chunk:
        rows = rows + rows // 8 + steps * experts + 1
        return rows + -rows % 16, chunk
    return rows + steps * experts, chunk + small


def absorb_queries(table, queries, shape, w_uk, own, gain, w_turned, prompts, sections, after):
    experts = len(queries)
    steps, sources, heads, wide = shape
    _, nope, chunk = w_uk.shape
    rows, width = block_shape(prompts, steps, heads, experts, chunk, wide - nope)
    block, column = own.shape[0] * own.shape[1], own.shape[2] // experts
    cache_width = w_turned.shape[0]
    count = experts * sources * steps * heads
    held = pl.BlockSpec(memory_space=pltpu.VMEM)
    return pl.pallas_call(
        functools.partial(query_kernel, experts, sections, prompts, nope, shape),
        out_shape=[
            jax.ShapeDtypeStruct((experts * sections, rows, width), jnp.bfloat16),
            jax.ShapeDtypeStruct(
                (experts, block * -(-column // cache_width), cache_width), jnp.bfloat16
            ),
            jax.ShapeDtypeStruct((8, 128), jnp.bfloat16),
        ],
        in_specs=[pl.BlockSpec(memory_space=pltpu.SMEM)]
        + [held] * (experts + 4)
        + [pl.BlockSpec(memory_space=pl.ANY)] * len(after),
        out_specs=[held] * 3,
        scratch_shapes=[
            pltpu.VMEM((count, nope), jnp.float32),
            pltpu.VMEM((count, max(wide - nope, 128)), jnp.float32),
            pltpu.VMEM((count, max(chunk, 128)), jnp.float32),
            pltpu.VMEM(
                (sections, own.shape[0] * own.shape[1], w_turned.shape[1]), jnp.bfloat16
            ),
            pltpu.VMEM((experts,) + shape, jnp.bfloat16),
            pltpu.VMEM((experts, block, column), jnp.float32),
        ],
        compiler_params=params(*queries, w_uk, own, w_turned, scale=4),
        name="absorb_queries",
    )(*at_home(table), *queries, *at_home(w_uk, own, gain, w_turned), *after)


def turn(values, cosine, sine):
    half = values.shape[1] // 2
    other = jnp.concatenate([values[:, half:], values[:, :half]], axis=1)
    return values * cosine + other * sine


def scaled(values, gain):
    scale = lax.rsqrt(jnp.mean(values * values, axis=-1, keepdims=True) + epsilon)
    return values * scale * gain.astype(jnp.float32)


def gather_kernel(
    prompts, experts, sections, sources, heads, steps, latent, length_ref, owner_ref, gain_ref,
    cosine_ref, sine_ref, block_ref, query_ref, query_rope_ref, recent_ref, recent_rope_ref,
    cosine_held, sine_held, ropes_held
):
    f32, bf16 = jnp.float32, jnp.bfloat16
    rows = steps * heads
    chunk = latent // experts
    whole = block_ref.shape[2] == chunk
    extra = prompts * rows // 8 if whole else 0
    first = lax.axis_index("expert") * sources + lax.axis_index("section") * prompts
    gain = gain_ref[...][None]
    for prompt in range(prompts):
        length, owner = length_ref[first + prompt], owner_ref[first + prompt]
        for step in range(steps):
            at = slice(step * heads, (step + 1) * heads)
            cosine_held[at, :] = jnp.broadcast_to(
                cosine_ref[pl.ds(length + step, 1), :], (heads, cosine_ref.shape[1])
            )
            sine_held[at, :] = jnp.broadcast_to(
                sine_ref[pl.ds(length + step, 1), :], (heads, sine_ref.shape[1])
            )
        cosine, sine = cosine_held[...], sine_held[...]
        if whole:
            few = rows // 8
            small = cosine.shape[1] // experts
            low = prompts * rows + prompt * few
            tail = jnp.concatenate(
                [
                    jnp.concatenate(
                        [block_ref[i * sections + section, low : low + few, :]
                         for i in range(experts)],
                        axis=1,
                    )
                    for section in range(sections)
                ],
                axis=0,
            )
            shape = (experts * chunk, experts * small)
            source_lane = lax.broadcasted_iota(jnp.int32, shape, 0)
            lane = lax.broadcasted_iota(jnp.int32, shape, 1)
            bits = small.bit_length() - 1
            lane = lax.shift_right_logical(lane, bits) * chunk + (lane & (small - 1))
            for group in range(8):
                pair = jnp.where(source_lane == lane + group * small, 1.0, 0.0).astype(bf16)
                value = jnp.dot(tail, pair, preferred_element_type=f32)
                pad = ropes_held.shape[1] - value.shape[1]
                value = jnp.concatenate([value, jnp.zeros((value.shape[0], pad), f32)], axis=1)
                ropes_held[pl.ds(group, sections * few, stride=8), :] = value
        at = slice(prompt * rows, (prompt + 1) * rows)
        for section in range(sections):
            pieces = [block_ref[i * sections + section, at, :] for i in range(experts)]
            to = slice(section * rows, (section + 1) * rows)
            query_ref[prompt, to, :] = jnp.concatenate(
                [piece[:, :chunk] for piece in pieces], axis=1
            )
            if whole:
                rope = ropes_held[to, : cosine.shape[1]]
            else:
                rope = jnp.concatenate(
                    [piece[:, chunk:].astype(f32) for piece in pieces], axis=1
                )
            query_rope_ref[prompt, to, :] = turn(rope, cosine, sine).astype(bf16)
        lines = 0
        for section in range(sections):
            lines = lines + block_ref[
                owner * sections + section, prompts * rows + extra :, :
            ].astype(f32)
        recent, recent_rope = [], []
        for step in range(steps):
            parts = [lines[step * experts + part :][:1] for part in range(experts)]
            if whole:
                end = cosine.shape[1]
                parts.append(
                    lines[steps * experts :][:1, step * end : (step + 1) * end]
                )
            line = jnp.concatenate(parts, axis=1)
            recent.append(scaled(line[:, :latent], gain))
            at = slice(step * heads, step * heads + 1)
            recent_rope.append(turn(line[:, latent:], cosine[at], sine[at]))
        spare = recent_ref.shape[1] - steps
        recent.append(jnp.zeros((spare, latent), f32))
        recent_rope.append(jnp.zeros((spare, recent_rope[0].shape[1]), f32))
        recent_ref[prompt] = jnp.concatenate(recent, axis=0).astype(bf16)
        recent_rope_ref[prompt] = jnp.concatenate(recent_rope, axis=0).astype(bf16)


def gather_queries(blocks, lengths, owners, kv_gain, table, prompts, sources, experts, sections,
                   steps, heads):
    latent = kv_gain.shape[0]
    rope = table[0].shape[1]
    rows = sections * steps * heads
    spare = steps + -steps % 16
    shape = lambda *sizes: jax.ShapeDtypeStruct((prompts,) + sizes, jnp.bfloat16)
    held = pl.BlockSpec(memory_space=pltpu.VMEM)
    return pl.pallas_call(
        functools.partial(
            gather_kernel, prompts, experts, sections, sources, heads, steps, latent
        ),
        out_shape=[shape(rows, latent), shape(rows, rope), shape(spare, latent), shape(spare, rope)],
        in_specs=[pl.BlockSpec(memory_space=pltpu.SMEM)] * 2 + [held] * 4,
        out_specs=[held] * 4,
        scratch_shapes=[pltpu.VMEM((steps * heads, rope), jnp.float32)] * 2
        + [pltpu.VMEM((rows, 128), jnp.float32)],
        compiler_params=params(blocks, scale=4),
        name="gather_queries",
    )(*at_home(lengths, owners, kv_gain, *table), blocks)


def attend_kernel(parts, positions, sections, sources, heads, steps, score_scale, *refs):
    part_refs = refs[:parts]
    (length_ref, gain_ref, cosine_ref, sine_ref, query_ref, query_rope_ref, recent_ref,
     recent_rope_ref) = refs[parts : parts + 8]
    out_refs, token_ref, held = refs[-2 - sections : -2], refs[-2], refs[-1]
    token_ref[...] = jnp.zeros_like(token_ref)
    f32, bf16 = jnp.float32, jnp.bfloat16
    nt = (((1,), (1,)), ((), ()))
    prompts, _, latent = query_ref.shape
    rows = steps * heads
    section_rank = lax.axis_index("section")
    first = lax.axis_index("expert") * sources + section_rank * prompts
    for prompt in range(prompts):
        at = slice(prompt * positions, (prompt + 1) * positions)
        projected = part_refs[0][at].astype(f32)
        for ref in part_refs[1:]:
            projected = projected + ref[at].astype(f32)
        keys = scaled(projected[:, :latent], gain_ref[...][None]).astype(bf16)
        key_rope = turn(
            projected[:, latent:], cosine_ref[:positions], sine_ref[:positions]
        ).astype(bf16)
        query, query_rope = query_ref[prompt], query_rope_ref[prompt]
        recent, recent_rope = recent_ref[prompt], recent_rope_ref[prompt]
        scores = lax.dot_general(query, keys, nt, preferred_element_type=f32)
        scores = scores + lax.dot_general(query_rope, key_rope, nt, preferred_element_type=f32)
        fresh = lax.dot_general(query, recent, nt, preferred_element_type=f32)
        fresh = fresh + lax.dot_general(query_rope, recent_rope, nt, preferred_element_type=f32)
        place = lax.broadcasted_iota(jnp.int32, scores.shape, 1)
        scores = jnp.where(
            place < length_ref[first + prompt], scores * score_scale, masked_value
        )
        row = lax.broadcasted_iota(jnp.int32, (rows, fresh.shape[1]), 0)
        place = lax.broadcasted_iota(jnp.int32, (rows, fresh.shape[1]), 1)
        seen = jnp.where(place < 1, 1.0, 0.0)
        for step in range(1, steps):
            seen = jnp.where((place <= step) & (row >= step * heads), 1.0, seen)
        seen = jnp.concatenate([seen] * sections, axis=0)
        fresh = jnp.where(seen > 0.5, fresh * score_scale, masked_value)
        most = jnp.maximum(
            jnp.max(scores, axis=-1, keepdims=True), jnp.max(fresh, axis=-1, keepdims=True)
        )
        scores = jnp.exp(scores - most)
        fresh = jnp.exp(fresh - most)
        total = jnp.sum(scores, axis=-1, keepdims=True) + jnp.sum(fresh, axis=-1, keepdims=True)
        scores = (scores / total).astype(bf16)
        fresh = (fresh / total).astype(bf16)
        mixed = jnp.dot(scores, keys, preferred_element_type=f32)
        mixed = mixed + jnp.dot(fresh, recent, preferred_element_type=f32)
        mixed = mixed.astype(bf16)
        for section in range(sections):
            held[section] = mixed[section * rows : (section + 1) * rows]
        for mask, ref in enumerate(out_refs):
            ref[prompt * rows : (prompt + 1) * rows, :] = held[section_rank ^ mask]


def attend(
    parts, positions, lengths, kv_gain, table, gathered, sources, steps, sections, score_scale,
    after
):
    prompts, rows, latent = gathered[0].shape
    out = (rows // sections, latent)
    held = pl.BlockSpec(memory_space=pltpu.VMEM)
    return pl.pallas_call(
        functools.partial(
            attend_kernel, len(parts), positions, sections, sources, out[0] // steps, steps,
            score_scale
        ),
        out_shape=[jax.ShapeDtypeStruct((prompts * out[0], latent), jnp.bfloat16)] * sections
        + [jax.ShapeDtypeStruct((8, 128), jnp.bfloat16)],
        in_specs=[held] * len(parts)
        + [pl.BlockSpec(memory_space=pltpu.SMEM)]
        + [held] * 7
        + [pl.BlockSpec(memory_space=pl.ANY)] * len(after),
        out_specs=[held] * (sections + 1),
        scratch_shapes=[pltpu.VMEM((sections,) + out, jnp.bfloat16)],
        compiler_params=params(*parts, *gathered, scale=6),
        name="attend",
    )(*parts, *at_home(lengths, kv_gain, *table), *gathered, *after)


def value_kernel(experts, sections, heads, steps, sources, count, *refs):
    owner_ref, latent_refs, uv_refs = refs[0], refs[1 : 1 + sections], refs[1 + sections :]
    name_ref, score_ref = uv_refs[count : count + 2]
    uv_refs = list(uv_refs[:count])
    out_ref, held = refs[-2:]
    group_rank, groups = lax.axis_index("groups"), lax.axis_size("groups")
    weights = []
    while uv_refs:
        if uv_refs[0].shape[0] == heads:
            weights.append(uv_refs[:1])
        else:
            weights.append(uv_refs[:groups])
        uv_refs = uv_refs[len(weights[-1]) :]
    f32, bf16 = jnp.float32, jnp.bfloat16
    chunk = weights[0][0].shape[2]
    rows = latent_refs[0].shape[0]
    for mask, ref in enumerate(latent_refs):
        for index in range(experts):
            held[index, mask * rows : (mask + 1) * rows, :chunk] = ref[
                :, index * chunk : (index + 1) * chunk
            ].astype(f32)
    rank = lax.axis_index("expert")
    values = []
    for head in range(heads):
        at = pl.ds(head, sections * rows // heads, stride=heads)
        total = 0
        for mask, shares in enumerate(weights):
            size = shares[0].shape[0]
            weight = shares[0][head % size]
            for other in range(1, len(shares)):
                mine = (group_rank ^ other) == head // size
                weight = jnp.where(mine, shares[other][head % size], weight)
            total = total + lax.dot_general(
                held[rank ^ mask, at, :][:, :chunk].astype(bf16),
                weight,
                (((1,), (1,)), ((), ())),
                preferred_element_type=f32,
            )
        values.append(total.astype(bf16))
    values = jnp.concatenate(values, axis=1)
    prompts = sources // sections
    section_rank = lax.axis_index("section")
    size = sources * steps
    to = lax.broadcasted_iota(jnp.int32, (size, size), 0)
    row = lax.broadcasted_iota(jnp.int32, (size, size), 1)
    order = jnp.zeros((size, size), f32)
    for mask in range(sections):
        for prompt in range(prompts):
            owner = owner_ref[
                rank * sources + (section_rank ^ mask) * prompts + prompt
            ]
            for step in range(steps):
                index = (mask * prompts + prompt) * steps + step
                order = jnp.where((row == index) & (to == owner * steps + step), 1.0, order)
    width = values.shape[1]
    out_ref[:, :width] = jnp.dot(
        order.astype(bf16), values, preferred_element_type=f32
    ).astype(bf16)
    names = jnp.concatenate([name_ref[step] for step in range(steps)], axis=0).astype(f32)
    scores = jnp.concatenate([score_ref[step] for step in range(steps)], axis=0)
    high = scores.astype(bf16).astype(f32)
    spare = jnp.zeros((size, out_ref.shape[1] - width - 3 * names.shape[1]), f32)
    route = jnp.concatenate([names, high, scores - high, spare], axis=1)
    out_ref[:, width:] = route.astype(bf16)


def head_products(owners, latents, uv_parts, names, scores, steps, sources, after):
    rows, width = latents[0].shape
    heads, value, _ = uv_parts[0][0].shape
    experts = len(uv_parts)
    uv_parts = [share for part in uv_parts for share in part]
    held = pl.BlockSpec(memory_space=pltpu.VMEM)
    total = rows * len(latents)
    return pl.pallas_call(
        functools.partial(
            value_kernel, experts, len(latents), heads, steps, sources, len(uv_parts)
        ),
        out_shape=jax.ShapeDtypeStruct(
            (total // heads, heads * value + 128), jnp.bfloat16
        ),
        in_specs=[pl.BlockSpec(memory_space=pltpu.SMEM)]
        + [held] * (len(latents) + len(uv_parts) + 2)
        + [pl.BlockSpec(memory_space=pl.ANY)] * len(after),
        out_specs=held,
        scratch_shapes=[
            pltpu.VMEM((experts, total, max(width // experts, 128)), jnp.float32)
        ],
        compiler_params=params(*latents, *uv_parts, scale=4),
        name="head_products",
    )(*at_home(owners), *latents, *uv_parts, *at_home(names, scores), *after)


def output_kernel(experts, *refs):
    value_refs = refs[:experts]
    weight_ref, out_ref = refs[experts:]
    depth = weight_ref.shape[0]
    values = jnp.concatenate([ref[:, :depth] for ref in value_refs], axis=0)
    rows = values.shape[0]
    to = lax.broadcasted_iota(jnp.int32, (rows, rows), 0)
    row = lax.broadcasted_iota(jnp.int32, (rows, rows), 1)
    source = (to & (experts - 1)) ^ lax.axis_index("expert")
    rest = lax.shift_right_logical(to, experts.bit_length() - 1)
    order = jnp.where(row == source * (rows // experts) + rest, 1.0, 0.0).astype(jnp.bfloat16)
    values = jnp.dot(order, values, preferred_element_type=jnp.float32).astype(jnp.bfloat16)
    out_ref[...] = jnp.dot(
        values, weight_ref[...], preferred_element_type=jnp.float32
    ).astype(out_ref.dtype)


def output_product(values, weight):
    rows = sum(value.shape[0] for value in values)
    held = pl.BlockSpec(memory_space=pltpu.VMEM)
    return pl.pallas_call(
        functools.partial(output_kernel, len(values)),
        out_shape=jax.ShapeDtypeStruct((rows, weight.shape[1]), jnp.bfloat16),
        in_specs=[held] * (len(values) + 1),
        out_specs=held,
        compiler_params=params(*values, scale=8),
        name="output_product",
    )(*values, weight)


def mix_kernel(count, owners, rows, *refs):
    part_refs, own_refs = refs[:count], refs[count : count + owners]
    out_ref, held = refs[-2:]
    f32 = jnp.float32
    total = part_refs[0][...].astype(f32)
    for ref in part_refs[1:]:
        total = total + ref[...].astype(f32)
    block, column = held.shape[1:]
    for owner in range(owners):
        held[owner] = total[owner * block : (owner + 1) * block]
    rank = lax.axis_index("expert")
    for mask, ref in enumerate(own_refs):
        lines = []
        for line, at in enumerate(range(0, column, ref.shape[1])):
            end = min(at + ref.shape[1], column)
            to = rows + line * block
            lines.append(ref[to : to + block, : end - at].astype(f32))
        lines = lines[0] if len(lines) == 1 else jnp.concatenate(lines, axis=1)
        out_ref[rank ^ mask] = (held[rank ^ mask] + lines).astype(out_ref.dtype)


def mix(parts, owns, rows, after):
    total, width = parts[0].shape
    owners = len(owns)
    held = pl.BlockSpec(memory_space=pltpu.VMEM)
    shape = (owners, total // owners, width)
    return pl.pallas_call(
        functools.partial(mix_kernel, len(parts), owners, rows),
        out_shape=jax.ShapeDtypeStruct(shape, parts[0].dtype),
        in_specs=[held] * (len(parts) + owners)
        + [pl.BlockSpec(memory_space=pl.ANY)] * len(after),
        out_specs=held,
        scratch_shapes=[pltpu.VMEM(shape, jnp.float32)],
        compiler_params=params(*parts, *owns, scale=4),
        name="mix",
    )(*parts, *owns, *after)


def expert_kernel(experts, sections, picks, *refs):
    mixed_refs, route_refs = refs[:experts], refs[experts : 2 * experts]
    gain_ref, gate_ref, up_ref, down_ref, out_ref, near_ref, columns = refs[2 * experts :]
    f32, bf16 = jnp.float32, jnp.bfloat16
    count = gate_ref.shape[0]
    rank = lax.axis_index("expert")
    width = gain_ref.shape[0]
    block = mixed_refs[0].shape[1]
    for mask, ref in enumerate(mixed_refs):
        columns[rank ^ mask] = ref[...]
    mixed, route = [], []
    for mask, ref in enumerate(route_refs):
        mixed.append(
            jnp.concatenate([columns[i, rank ^ mask] for i in range(experts)], axis=1).astype(f32)
        )
        route.append(ref[:, ref.shape[1] - 128 :].astype(f32))
    near = mixed[0]
    mixed = jnp.concatenate(mixed, axis=0)
    route = jnp.concatenate(route, axis=0)
    named = route[:, :picks]
    weights = route[:, picks : 2 * picks] + route[:, 2 * picks : 3 * picks]
    weights = route_scale * weights / jnp.sum(weights, axis=-1, keepdims=True)
    scale = lax.rsqrt(jnp.mean(mixed * mixed, axis=-1, keepdims=True) + epsilon)
    rows_in = (mixed * scale * gain_ref[...][None].astype(f32)).astype(bf16)
    column = width // sections
    total = 0
    for x in range(count):
        mine = (rank * count + x).astype(f32)
        weight = jnp.sum(jnp.where(named == mine, weights, 0.0), axis=-1, keepdims=True)
        gate = jnp.dot(rows_in, gate_ref[x], preferred_element_type=f32)
        up = jnp.dot(rows_in, up_ref[x], preferred_element_type=f32)
        inner = gate / (1.0 + jnp.exp(-gate)) * up * weight
        total = total + jnp.dot(inner.astype(bf16), down_ref[x], preferred_element_type=f32)
    for section in range(sections):
        at = slice(section * column, (section + 1) * column)
        near_ref[section] = near[:, at].astype(bf16)
        for mask in range(experts):
            out_ref[(rank ^ mask) * sections + section] = total[
                mask * block : (mask + 1) * block, at
            ].astype(bf16)


def run_experts(mixed, routes, gain, w_gate, w_up, w_down, picks, sections):
    experts = len(mixed)
    block = (mixed[0].shape[1], gain.shape[0] // sections)
    held = pl.BlockSpec(memory_space=pltpu.VMEM)
    return pl.pallas_call(
        functools.partial(expert_kernel, experts, sections, picks),
        out_shape=[
            jax.ShapeDtypeStruct((experts * sections,) + block, jnp.bfloat16),
            jax.ShapeDtypeStruct((sections,) + block, jnp.bfloat16),
        ],
        in_specs=[held] * (2 * experts + 4),
        out_specs=[held] * 2,
        scratch_shapes=[pltpu.VMEM((experts,) + mixed[0].shape, jnp.bfloat16)],
        compiler_params=params(*mixed, scale=32),
        name="run_experts",
    )(*mixed, *routes, *at_home(gain), w_gate, w_up, w_down)


def finish_kernel(block_ref, near_ref, out_ref):
    f32 = jnp.float32
    steps, sources, _ = out_ref.shape
    total = near_ref[lax.axis_index("section")].astype(f32)
    for index in range(block_ref.shape[0]):
        total = total + block_ref[index].astype(f32)
    for step in range(steps):
        out_ref[step] = total[step * sources : (step + 1) * sources].astype(out_ref.dtype)


def finish(blocks, near, steps):
    held = pl.BlockSpec(memory_space=pltpu.VMEM)
    _, rows, column = near.shape
    return pl.pallas_call(
        finish_kernel,
        out_shape=jax.ShapeDtypeStruct((steps, rows // steps, column), near.dtype),
        in_specs=[held] * 2,
        out_specs=held,
        compiler_params=params(blocks, near, scale=4),
        name="finish",
    )(blocks, near)


def local(
    prompts,
    owners,
    lengths,
    residual,
    queries,
    expert_ids,
    route_scores,
    attn_gain,
    w_dkv,
    kv_gain,
    w_uk,
    w_uv,
    w_o,
    moe_gain,
    w_gate,
    w_up,
    w_down,
):
    bf16, f32 = jnp.bfloat16, jnp.float32
    expert_rank = lax.axis_index("expert")
    section_rank = lax.axis_index("section")
    experts = lax.axis_size("expert")
    sections = lax.axis_size("section")
    groups = lax.axis_size("groups")
    prompt_count, full_length, width = prompts.shape
    steps, tokens_here, heads, _ = queries.shape
    depth = w_dkv.shape[0]
    piece = depth // experts
    latent = kv_gain.shape[0]
    cache_width = w_dkv.shape[1]
    rows = prompt_count * full_length
    own_rows = steps * tokens_here

    w_turned = w_dkv.T
    masks = [1 << bit for bit in range(experts.bit_length() - 1)]
    far = masks[-1]
    uv_share, w_piece, *cut = cut_columns(
        prompts.reshape(rows, width), queries, w_uv, w_turned, sections, experts, groups
    )
    w_parts = spread(w_piece, "section")
    uv_share = swap(uv_share, "expert", far)
    cut = deliver(cut, "expert")

    blocks, riders, token = absorb_queries(
        owners, cut, queries.shape, w_uk, residual, attn_gain, w_turned, prompt_count, sections,
        [uv_share],
    )
    blocks = lax.all_to_all(blocks, ("expert", "section"), 0, 0, tiled=True)

    away = list(project(cut[1:], riders, w_parts, 1, rows, piece, [token]))
    near = list(project(cut[:1], riders, w_parts, 0, rows, piece, away[:1]))
    parts = deliver(near + away, "expert")
    table = rotation(full_length + steps + -(full_length + steps) % 8, cache_width - latent)
    gathered = list(gather_queries(
        blocks, lengths, owners, kv_gain, table, prompt_count, tokens_here, experts, sections,
        steps, heads
    ))
    uv_shares = spread(uv_share, "groups")
    later = masks[1:-1] + masks[:1]
    held = [doubled({far: share}, "expert", later) for share in uv_shares]
    uv_parts = {mask: [share[mask] for share in held] for mask in held[0]}
    for mask, part in doubled({0: w_uv}, "expert", later).items():
        uv_parts[mask] = [part]
    *out_latent, token = attend(
        parts, full_length, lengths, kv_gain, table, gathered, tokens_here, steps, sections,
        queries.shape[-1] ** (-0.5),
        [share for mask in range(1, experts) for share in uv_parts[mask]],
    )

    (w_gate,) = fetch([w_gate], [token])
    out_latent = deliver(out_latent, "section")
    head_values = head_products(
        owners, out_latent, [uv_parts[mask] for mask in range(experts)], expert_ids,
        route_scores, steps, tokens_here, [w_gate],
    )
    head_values = spread(head_values, "expert")

    (w_o,) = fetch([w_o], [])
    attended = output_product(head_values, w_o)
    (w_up,) = fetch([w_up], [attended])
    mixed = mix(spread(attended, "section"), parts, rows, [w_up])
    (w_down,) = fetch([w_down], [mixed])
    blocks, near = run_experts(
        spread(mixed, "expert"),
        head_values,
        moe_gain,
        w_gate,
        w_up,
        w_down,
        expert_ids.shape[2],
        sections,
    )
    blocks = lax.all_to_all(blocks, ("expert", "section"), 0, 0, tiled=True)
    return finish(blocks, near, steps)


def solution(mesh):
    placed = (
        P(("groups", "expert", "section"), None, None),
        P("groups"),
        P("groups"),
        P(None, ("groups", "expert"), None),
        P(None, ("groups", "expert"), "section", None),
        P(None, ("groups", "expert"), None),
        P(None, ("groups", "expert"), None),
        P(),
        P("section", None),
        P(),
        P("section", None, "expert"),
        P("section", None, "expert"),
        P("section", "expert"),
        P(),
        P("expert", None, "section"),
        P("expert", None, "section"),
        P("expert", "section", None),
    )
    return jax.shard_map(
        local,
        mesh=mesh,
        in_specs=placed,
        out_specs=P(None, ("groups", "expert"), "section"),
        check_vma=False,
    )
```
